32 devices in a mesh: seg: 8 (over y, x, core), fsdp: 4 (over z).
Axes of the slice: x: 2, y: 2, z: 4, core: 2. Of those that a mesh axis runs over, the one named last changes fastest.
Arguments:
- tokens: bfloat16 [4, 2048, 4096], P('fsdp', 'seg')
- w_query: bfloat16 [4096, 2048], P(('seg', 'fsdp'))
- w_key: bfloat16 [4096, 512], P(('seg', 'fsdp'))
- value_weight: bfloat16 [4096, 512], P(('seg', 'fsdp')), may hold values from -0.09375 to 0.09375
- gate_bias: float32 [16], replicated, may hold values from -2 to 2
- block_mask: int32 [4, 8, 2, 2], P('fsdp', 'seg'), may hold values from 0 to 1, as said below
- valid_len: int32 [4, 8], P('fsdp', 'seg'), may hold values from 1 to 256, as said below
Outputs:
- attended: bfloat16 [4, 2048, 2048], P('fsdp', 'seg')
The draws below stay inside these ranges and needn't reach their ends.
Inputs may be any that keep to these rules, and one draw needn't show every extreme that they name: block_mask[b, s] is 1 on its diagonal, 0 above it, and 0 or 1 below it. `valid_len`: the first segment of every book is full.
All inputs are finite; a program needn't handle non-finite values.
Results may differ from the reference program's by a relative error of at most 0.0095.
Values may be sent and summed in bfloat16 or wider, within the bound.
No kernel may reach another device: no remote copies, remote signals or barrier semaphores. Data moves between devices by JAX's collectives and lax.ppermute only.
A program may use at most 128 MiB of HBM per device.

```python
import jax
import jax.numpy as jnp
from jax import lax

MODEL_WIDTH = 4096
HEAD_SIZE = 128
QUERY_HEADS = 16
KEY_VALUE_HEADS = 4
BLK = 128
SEG_LEN = 256
NB = 2
SEGS = 8
BOOKS = 4


def query_weight_matrix(key):
    return jax.random.normal(jax.random.fold_in(key, 11), (MODEL_WIDTH, QUERY_HEADS * HEAD_SIZE), jnp.float32) * MODEL_WIDTH ** (-0.5)


def draw_w_query(key, part):
    return query_weight_matrix(key).astype(jnp.bfloat16)


def draw_w_key(key, part):
    own_part = jax.random.normal(jax.random.fold_in(key, 12), (MODEL_WIDTH, KEY_VALUE_HEADS * HEAD_SIZE), jnp.float32) * MODEL_WIDTH ** (-0.5)
    result = own_part
    return result.astype(jnp.bfloat16)


def draw_tokens(key, part):
    length = SEGS * SEG_LEN
    offset = jax.random.normal(jax.random.fold_in(key, 21), (BOOKS, SEGS, 1, MODEL_WIDTH), jnp.float32) * 1.5
    offset = jnp.broadcast_to(offset, (BOOKS, SEGS, SEG_LEN, MODEL_WIDTH)).reshape(BOOKS, length, MODEL_WIDTH)
    noise = jax.random.normal(jax.random.fold_in(key, 22), (BOOKS, length, MODEL_WIDTH), jnp.float32)
    result = noise + offset
    return result.astype(jnp.bfloat16)


def draw_block_mask(key, part):
    bits = jax.random.randint(jax.random.fold_in(key, 31), (BOOKS, SEGS, NB, NB), 0, 2, jnp.int32)
    rows = jnp.arange(NB, dtype=jnp.int32)[:, None]
    cols = jnp.arange(NB, dtype=jnp.int32)[None, :]
    return jnp.where(rows == cols, 1, jnp.where(cols < rows, bits, 0)).astype(jnp.int32)


def draw_valid_len(key, part):
    pick = jax.random.randint(jax.random.fold_in(key, 41), (BOOKS, SEGS), 0, 4, jnp.int32)
    short = jax.random.randint(jax.random.fold_in(key, 42), (BOOKS, SEGS), 1, SEG_LEN + 1, jnp.int32)
    lengths = jnp.where(pick > 0, SEG_LEN, short)
    first = jnp.arange(SEGS, dtype=jnp.int32)[None, :] == 0
    return jnp.where(first, SEG_LEN, lengths).astype(jnp.int32)


def steps_of(rng, extent, shards, low, top_value):
    factor_of, own = 1.0, jax.random.fold_in(rng, 6)
    for position, parts in shards:
        heights = jnp.exp(jax.random.uniform(jax.random.fold_in(own, position), (parts,), jnp.float32, low / len(shards), top_value / len(shards)))
        factor_of = factor_of * jnp.repeat(heights, extent[position] // parts).reshape([-1 if axis == position else 1 for axis in range(len(extent))])
    return factor_of


def bell_draw(own_key, shape, scale, most, pieces=(), kind=jnp.bfloat16):
    values = scale * jax.random.normal(own_key, shape, jnp.float32)
    if pieces:
        values = values * steps_of(own_key, shape, pieces, -0.22, 0.18)
    return jnp.clip(values, -most, most).astype(kind)


def setup_inputs(seed: int = 0) -> dict:
    arg_keys = jax.random.split(jax.random.key(seed), 8)
    tokens = draw_tokens(jax.random.fold_in(arg_keys[7], 71), 0)
    w_query = draw_w_query(jax.random.fold_in(arg_keys[7], 71), 0)
    w_key = draw_w_key(jax.random.fold_in(arg_keys[7], 71), 0)
    value_weight = bell_draw(arg_keys[3], (MODEL_WIDTH, KEY_VALUE_HEADS * HEAD_SIZE), MODEL_WIDTH ** -0.5, 0.09375, ((0, 32),))
    gate_bias = jnp.clip(jax.random.uniform(arg_keys[4], (QUERY_HEADS,), jnp.float32, -2.0, 2.0), -2.0, 2.0)
    block_mask = draw_block_mask(jax.random.fold_in(arg_keys[7], 71), 0)
    valid_len = draw_valid_len(jax.random.fold_in(arg_keys[7], 71), 0)
    return dict(tokens=tokens, w_query=w_query, w_key=w_key, value_weight=value_weight, gate_bias=gate_bias, block_mask=block_mask, valid_len=valid_len)


def sigma_plus(v):
    return jax.nn.elu(v) + 1.0


def segment_delta(keys, values, valid):
    length = keys.shape[0]
    heads_kv = keys.shape[1] // HEAD_SIZE
    live = (jnp.arange(length, dtype=jnp.int32) < valid)[:, None, None]
    sig_keys = jnp.where(live, sigma_plus(keys.reshape(length, heads_kv, HEAD_SIZE).astype(jnp.float32)), 0.0)
    delta_m = jnp.einsum("jgd,jge->gde", sig_keys, values.reshape(length, heads_kv, HEAD_SIZE).astype(jnp.float32), precision=lax.Precision.HIGHEST)
    delta_z = jnp.sum(sig_keys, axis=0)
    return delta_m, delta_z


def segment_output(queries, keys, values, gate_bias, mask_blocks, valid, memory, normalizer):
    length = queries.shape[0]
    heads_kv = memory.shape[0]
    group = queries.shape[1] // (heads_kv * HEAD_SIZE)
    nblocks = mask_blocks.shape[0]
    q_heads = queries.reshape(length, heads_kv, group, HEAD_SIZE)
    k_heads = keys.reshape(length, heads_kv, HEAD_SIZE)
    v_heads = values.reshape(length, heads_kv, HEAD_SIZE)
    scores = jnp.einsum("igxd,jgd->gxij", q_heads.astype(jnp.float32), k_heads.astype(jnp.float32), precision=lax.Precision.HIGHEST) * (HEAD_SIZE ** -0.5)
    full = jnp.broadcast_to(mask_blocks[:, None, :, None], (nblocks, BLK, nblocks, BLK)).reshape(length, length)
    pos = jnp.arange(length, dtype=jnp.int32)
    allowed = (full > 0) & (pos[None, :] <= pos[:, None]) & (pos[None, :] < valid)
    masked = jnp.where(allowed, scores, -1e30)
    top = jnp.max(masked, axis=-1, keepdims=True)
    expo = jnp.where(allowed, jnp.exp(masked - top), 0.0)
    total = jnp.maximum(jnp.sum(expo, axis=-1, keepdims=True), 1.0)
    weights = (expo / total).astype(jnp.bfloat16)
    local = jnp.einsum("gxij,jgd->igxd", weights.astype(jnp.float32), v_heads.astype(jnp.float32), precision=lax.Precision.HIGHEST)
    sig_q = sigma_plus(q_heads.astype(jnp.float32))
    numer = jnp.einsum("igxd,gde->igxe", sig_q, memory, precision=lax.Precision.HIGHEST)
    denom = jnp.einsum("igxd,gd->igx", sig_q, normalizer, precision=lax.Precision.HIGHEST) + 1.0
    gate = jax.nn.sigmoid(gate_bias).reshape(heads_kv, group)[None, :, :, None]
    mixed = gate * (numer / denom[..., None]) + (1.0 - gate) * local
    live = (pos < valid)[:, None, None, None]
    return jnp.where(live, mixed, 0.0).reshape(length, -1).astype(jnp.bfloat16)


def reference(tokens, w_query, w_key, value_weight, gate_bias, block_mask, valid_len):
    heads_kv = w_key.shape[1] // HEAD_SIZE

    def one_book(book):
        book_tokens, book_masks, book_valid = book
        segs = book_tokens.reshape(SEGS, SEG_LEN, MODEL_WIDTH)

        def step(carry, item):
            memory, normalizer = carry
            seg_tokens, mask_blocks, valid = item
            queries = jnp.dot(seg_tokens, w_query, preferred_element_type=jnp.float32).astype(jnp.bfloat16)
            keys = jnp.dot(seg_tokens, w_key, preferred_element_type=jnp.float32).astype(jnp.bfloat16)
            values = jnp.dot(seg_tokens, value_weight, preferred_element_type=jnp.float32).astype(jnp.bfloat16)
            output = segment_output(queries, keys, values, gate_bias, mask_blocks, valid, memory, normalizer)
            delta_m, delta_z = segment_delta(keys, values, valid)
            return (memory + delta_m, normalizer + delta_z), output

        start = (jnp.zeros((heads_kv, HEAD_SIZE, HEAD_SIZE), jnp.float32), jnp.zeros((heads_kv, HEAD_SIZE), jnp.float32))
        carry, outputs = lax.scan(step, start, (segs, book_masks, book_valid))
        return outputs.reshape(SEGS * SEG_LEN, -1)

    return lax.map(one_book, (tokens, block_mask, valid_len))
```

```python
import functools

import jax
import jax.numpy as jnp
from jax import lax
from jax.experimental import pallas as pl
from jax.experimental.pallas import tpu as pltpu
from jax.sharding import PartitionSpec as P

HEAD_SIZE = 128
BLK = 128
MEMBERS = 4
META_ROWS = 16
AXES = ("seg", "fsdp")

VMEM = pl.BlockSpec(memory_space=pltpu.VMEM)
SMEM = pl.BlockSpec(memory_space=pltpu.SMEM)


def call(body, outs, n_smem, n_vmem, flops=0, scratch=(), limit=48 << 20):
    return pl.pallas_call(
        body,
        out_shape=outs,
        in_specs=[SMEM] * n_smem + [VMEM] * n_vmem,
        out_specs=[VMEM] * len(outs),
        scratch_shapes=list(scratch),
        compiler_params=pltpu.CompilerParams(vmem_limit_bytes=limit),
        cost_estimate=pl.CostEstimate(flops=flops, bytes_accessed=8 << 20, transcendentals=0),
    )


def aligned(offset):
    return pl.multiple_of(offset, HEAD_SIZE)


def pack_body(group, here_ref, meta_ref, wq_ref, wk_ref, wv_ref, *outs):
    rows = wk_ref.shape[0]
    half = group * HEAD_SIZE // 2
    lane = lax.broadcasted_iota(jnp.int32, (META_ROWS, 2 * HEAD_SIZE), 1)
    facts = jnp.zeros((META_ROWS, 2 * HEAD_SIZE), jnp.float32)
    for place in range(5):
        facts = jnp.where(lane == place, meta_ref[place].astype(jnp.float32), facts)
    for k in range(MEMBERS):
        head = here_ref[0] ^ k
        kv, q0, q1 = outs[3 * k : 3 * k + 3]
        at = aligned(head * HEAD_SIZE)
        kv[0:rows, 0:HEAD_SIZE] = wk_ref[:, pl.ds(at, HEAD_SIZE)]
        kv[0:rows, HEAD_SIZE:] = wv_ref[:, pl.ds(at, HEAD_SIZE)]
        kv[rows:, :] = facts.astype(jnp.bfloat16)
        q0[...] = wq_ref[:, pl.ds(aligned(head * 2 * half), half)]
        q1[...] = wq_ref[:, pl.ds(aligned(head * 2 * half + half), half)]


def project(tokens_ref, pieces, offs_ref):
    total = None
    for p, piece in enumerate(pieces):
        parts = [
            tokens_ref[:, pl.ds(aligned(offs_ref[p * MEMBERS + k]), HEAD_SIZE)]
            for k in range(MEMBERS)
        ]
        term = jnp.dot(
            jnp.concatenate(parts, axis=1), piece[...], preferred_element_type=jnp.float32
        )
        total = term if total is None else total + term
    return total


def sigma_plus(v):
    return jnp.where(v > 0, v + 1.0, jnp.exp(jnp.minimum(v, 0.0)))


def kv_body(n_pieces, segs, offs_ref, meta_ref, *refs):
    tokens, pieces, outs = refs[: len(segs)], refs[len(segs) : len(segs) + n_pieces], refs[len(segs) + n_pieces :]
    for n, seg in enumerate(segs):
        kv = project(tokens[n], pieces, offs_ref).astype(jnp.bfloat16)
        outs[2 * n][...] = kv
        length = kv.shape[0]
        row = lax.broadcasted_iota(jnp.int32, (length, HEAD_SIZE), 0)
        keys = kv[:, :HEAD_SIZE].astype(jnp.float32)
        sig = jnp.where(row < meta_ref[5 * seg], sigma_plus(keys), 0.0)
        wide = jnp.concatenate(
            [kv[:, HEAD_SIZE:], jnp.ones((length, HEAD_SIZE), jnp.bfloat16)], axis=1
        )
        high = sig.astype(jnp.bfloat16)
        low = (sig - high.astype(jnp.float32)).astype(jnp.bfloat16)
        over = (((0,), (0,)), ((), ()))
        delta = lax.dot_general(high, wide, over, preferred_element_type=jnp.float32)
        delta += lax.dot_general(low, wide, over, preferred_element_type=jnp.float32)
        outs[2 * n + 1][...] = delta


def attend_body(
    n_pieces, heads, first_head, group, here_ref, offs_ref, meta_ref, gate_ref, *refs
):
    tokens = refs[:MEMBERS]
    pieces = refs[MEMBERS : MEMBERS + n_pieces]
    rest = refs[MEMBERS + n_pieces :]
    kvs, deltas, base = rest[:MEMBERS], rest[MEMBERS : 2 * MEMBERS], rest[2 * MEMBERS]
    outs = rest[2 * MEMBERS + 1 :]
    me = here_ref[0]
    for seg in range(MEMBERS):
        queries = project(tokens[seg], pieces, offs_ref).astype(jnp.bfloat16)
        length = queries.shape[0]
        stacked = jnp.concatenate(
            [queries[:, h * HEAD_SIZE : (h + 1) * HEAD_SIZE] for h in range(heads)], axis=0
        )
        rows = heads * length
        keys = kvs[seg][:, :HEAD_SIZE]
        values = kvs[seg][:, HEAD_SIZE:]
        scores = lax.dot_general(
            stacked, keys, (((1,), (1,)), ((), ())), preferred_element_type=jnp.float32
        ) * HEAD_SIZE ** (-0.5)
        i = lax.broadcasted_iota(jnp.int32, (rows, length), 0) % length
        j = lax.broadcasted_iota(jnp.int32, (rows, length), 1)
        valid = meta_ref[5 * seg]
        top_block, left_block = i < BLK, j < BLK
        seen = jnp.where(
            top_block,
            jnp.where(left_block, meta_ref[5 * seg + 1], meta_ref[5 * seg + 2]),
            jnp.where(left_block, meta_ref[5 * seg + 3], meta_ref[5 * seg + 4]),
        )
        allowed = (seen == 1) & (j <= i) & (j < valid)
        masked = jnp.where(allowed, scores, -1e30)
        top = jnp.max(masked, axis=-1, keepdims=True)
        expo = jnp.where(allowed, jnp.exp(masked - top), 0.0)
        total = jnp.maximum(jnp.sum(expo, axis=-1, keepdims=True), 1.0)
        weights = (expo / total).astype(jnp.bfloat16)
        local = jnp.dot(weights, values, preferred_element_type=jnp.float32)

        memory = base[...].astype(jnp.float32)
        for other in range(MEMBERS):
            earlier = jnp.where((me ^ other) < (me ^ seg), 1.0, 0.0)
            if other != seg:
                memory = memory + earlier * deltas[other][...]
        sig = sigma_plus(stacked.astype(jnp.float32))
        high = sig.astype(jnp.bfloat16)
        low = (sig - high.astype(jnp.float32)).astype(jnp.bfloat16)
        mem_high = memory.astype(jnp.bfloat16)
        mem_low = (memory - mem_high.astype(jnp.float32)).astype(jnp.bfloat16)
        numer = jnp.dot(high, mem_high, preferred_element_type=jnp.float32)
        numer += jnp.dot(high, mem_low, preferred_element_type=jnp.float32)
        numer += jnp.dot(low, mem_high, preferred_element_type=jnp.float32)
        retrieved = numer[:, :HEAD_SIZE] / (numer[:, HEAD_SIZE:] + 1.0)
        live = lax.broadcasted_iota(jnp.int32, (length, HEAD_SIZE), 0) < valid
        for h in range(heads):
            span = slice(h * length, (h + 1) * length)
            logit = jnp.full((1, HEAD_SIZE), gate_ref[me * group + first_head + h], jnp.float32)
            gate = 1.0 / (1.0 + jnp.exp(-logit))
            mixed = gate * retrieved[span] + (1.0 - gate) * local[span]
            outs[seg][:, h * HEAD_SIZE : (h + 1) * HEAD_SIZE] = jnp.where(live, mixed, 0.0).astype(
                jnp.bfloat16
            )


def assemble_body(group, here_ref, *refs):
    parts, out = refs[:-1], refs[-1]
    half = group * HEAD_SIZE // 2
    for k in range(MEMBERS):
        at = (here_ref[0] ^ k) * 2 * half
        for c in range(2):
            out[:, pl.ds(aligned(at + c * half), half)] = parts[2 * k + c][...]


def shards(sizes, tokens, w_query, w_key, value_weight, gate_bias, block_mask, valid_len):
    n_seg, n_z = sizes
    n_groups = n_seg // MEMBERS
    heads_kv = w_key.shape[1] // HEAD_SIZE
    group = w_query.shape[1] // w_key.shape[1]
    half = group * HEAD_SIZE // 2
    rows = w_query.shape[0]
    length, width = tokens.shape[1], tokens.shape[2]
    assert heads_kv == MEMBERS and group % 2 == 0
    seg = lax.axis_index("seg")
    z = lax.axis_index("fsdp")
    g, m = seg // MEMBERS, seg % MEMBERS
    here = jnp.reshape(m, (1,)).astype(jnp.int32)

    def permute(array, to):
        pairs = []
        for gg in range(n_groups):
            for mm in range(MEMBERS):
                for zz in range(n_z):
                    target = to(gg, mm, zz)
                    if target is not None:
                        index = lambda t: (t[0] * MEMBERS + t[1]) * n_z + t[2]
                        pairs.append((index((gg, mm, zz)), index(target)))
        return lax.ppermute(array, AXES, pairs)

    def to_member(array, k):
        return permute(array, lambda gg, mm, zz: (gg, mm ^ k, zz))

    bf16 = jnp.bfloat16
    shape = jax.ShapeDtypeStruct
    mine = jnp.concatenate([valid_len.reshape(1), block_mask.reshape(4)]).astype(jnp.int32)
    packed = call(
        functools.partial(pack_body, group),
        [shape((rows + META_ROWS, 2 * HEAD_SIZE), bf16), shape((rows, half), bf16), shape((rows, half), bf16)]
        * MEMBERS,
        2,
        3,
    )(here, mine, w_query, w_key, value_weight)
    received = [packed[:3]] + [
        [to_member(part, k) for part in packed[3 * k : 3 * k + 3]] for k in range(1, MEMBERS)
    ]
    meta = jnp.concatenate([part[0][rows, :5] for part in received]).astype(jnp.int32)

    own = tokens[0]
    sibling = to_member(own, 1)
    across = to_member(own, 2)
    diagonal = to_member(across, 1)
    books = [own, sibling, across, diagonal]

    def gathered(piece):
        if n_groups == 2 and n_z == 4:
            flip = lambda b: lambda gg, mm, zz: (gg, mm, zz ^ b)
            one = permute(piece, flip(1))
            two = permute(piece, flip(2))
            inner = permute(piece, lambda gg, mm, zz: (gg, mm, zz ^ 3) if zz in (1, 2) else None)
            outer = permute(two, lambda gg, mm, zz: (gg, mm, zz ^ 1) if zz in (1, 2) else None)
            three = jnp.where((z == 1) | (z == 2), inner, outer)
            line = [piece, one, two, three]
            return line + [permute(part, lambda gg, mm, zz: (gg ^ 1, mm, zz)) for part in line]
        index = lambda gg, mm, zz: (gg * MEMBERS + mm) * n_z + zz
        everything = lax.all_gather(
            piece,
            AXES,
            axis_index_groups=[
                [index(gg, mm, zz) for gg in range(n_groups) for zz in range(n_z)]
                for mm in range(MEMBERS)
            ],
        )
        columns = piece.shape[1]
        natural = everything.reshape(n_groups, n_z, MEMBERS, rows, columns)
        members = jnp.arange(MEMBERS, dtype=jnp.int32) ^ m
        natural = jnp.take(natural, members, axis=2).transpose(0, 2, 1, 3, 4)
        return list(natural.reshape(-1, MEMBERS * HEAD_SIZE, columns))

    if n_groups == 2 and n_z == 4:
        assert rows == HEAD_SIZE
        n_pieces = n_groups * n_z
        a, b, k = jnp.meshgrid(
            jnp.arange(n_groups), jnp.arange(n_z), jnp.arange(MEMBERS), indexing="ij"
        )
        offs = ((((g ^ a) * MEMBERS + (m ^ k)) * n_z + (z ^ b)) * rows).reshape(-1).astype(jnp.int32)
    else:
        n_pieces = width // (MEMBERS * HEAD_SIZE)
        offs = jnp.arange(n_pieces * MEMBERS, dtype=jnp.int32) * HEAD_SIZE

    chunks = [
        gathered(jnp.concatenate([part[c][:rows] for part in received], axis=0)) for c in range(3)
    ]

    kvs, deltas = [], []
    for segs in ((0, 1), (2, 3)):
        found = call(
            functools.partial(kv_body, n_pieces, segs),
            [shape((length, 2 * HEAD_SIZE), bf16), shape((HEAD_SIZE, 2 * HEAD_SIZE), jnp.float32)] * 2,
            2,
            2 + n_pieces,
            flops=2 * 2 * length * width * 2 * HEAD_SIZE,
        )(offs, meta, *[books[s] for s in segs], *chunks[0])
        kvs += found[0::2]
        deltas += found[1::2]

    total = (deltas[0] + deltas[1] + deltas[2] + deltas[3]).astype(bf16)
    base = None
    for a in range(1, n_groups):
        term = permute(total, lambda gg, mm, zz: (gg ^ a, mm, zz) if gg < gg ^ a else None)
        base = term if base is None else base.astype(jnp.float32) + term.astype(jnp.float32)

    sent = []
    for c in range(2):
        attended = call(
            functools.partial(attend_body, n_pieces, group // 2, c * (group // 2), group),
            [shape((length, half), bf16)] * MEMBERS,
            4,
            3 * MEMBERS + 1 + n_pieces,
            flops=2 * MEMBERS * length * width * half,
        )(here, offs, meta, gate_bias, *books, *chunks[1 + c], *kvs, *deltas, base)
        sent.append([attended[0]] + [to_member(attended[k], k) for k in range(1, MEMBERS)])

    (output,) = call(
        functools.partial(assemble_body, group),
        [shape((length, w_query.shape[1]), bf16)],
        1,
        2 * MEMBERS,
    )(here, *[sent[c][k] for k in range(MEMBERS) for c in range(2)])
    return output[None]


def solution(mesh):
    in_specs = (
        P("fsdp", "seg", None),
        P(("seg", "fsdp"), None),
        P(("seg", "fsdp"), None),
        P(("seg", "fsdp"), None),
        P(),
        P("fsdp", "seg", None, None),
        P("fsdp", "seg"),
    )
    out_specs = P("fsdp", "seg", None)
    body = functools.partial(shards, (mesh.shape["seg"], mesh.shape["fsdp"]))
    return jax.shard_map(body, mesh=mesh, in_specs=in_specs, out_specs=out_specs, check_vma=False)
```

```python
import functools

import jax
import jax.numpy as jnp
from jax import lax
from jax.experimental import pallas as pl
from jax.experimental.pallas import tpu as pltpu
from jax.sharding import PartitionSpec as P

HEAD_SIZE = 128
BLK = 128
MEMBERS = 4
META_ROWS = 16
FACTS = 2
AXES = ("seg", "fsdp")

VMEM = pl.BlockSpec(memory_space=pltpu.VMEM)
SMEM = pl.BlockSpec(memory_space=pltpu.SMEM)
HBM = pl.BlockSpec(memory_space=pl.ANY)


def call(body, outs, in_specs, flops=0, scratch=(), out_spec=VMEM, limit=28 << 20):
    return pl.pallas_call(
        body,
        out_shape=outs,
        in_specs=in_specs,
        out_specs=[out_spec] * len(outs),
        scratch_shapes=list(scratch),
        compiler_params=pltpu.CompilerParams(vmem_limit_bytes=limit),
        cost_estimate=pl.CostEstimate(flops=flops, bytes_accessed=4 << 20, transcendentals=0),
    )


def aligned(offset):
    return pl.multiple_of(offset, HEAD_SIZE)


def pack_body(
    group, early, here_ref, valid_ref, mask_ref, wq_ref, wk_ref, wv_ref, *refs
):
    outs, facts_ref, sems = refs[: 2 * MEMBERS], refs[-2], refs[-1]
    rows = wk_ref.shape[0]
    lane = lax.broadcasted_iota(jnp.int32, facts_ref.shape, 1)
    facts = jnp.where(lane == 0, valid_ref[0, 0], mask_ref[0, 0, 1, 0])
    facts_ref[...] = facts.astype(jnp.float32).astype(jnp.bfloat16)
    copies = []

    def copy(source, target):
        copies.append(pltpu.make_async_copy(source, target, sems.at[len(copies)]))
        copies[-1].start()

    for k in range(MEMBERS):
        head = here_ref[0] ^ k
        first, second = outs[2 * k : 2 * k + 2]
        at = aligned(head * HEAD_SIZE)
        wide = group * HEAD_SIZE
        copy(wk_ref.at[:, pl.ds(at, HEAD_SIZE)], first.at[pl.ds(0, rows), pl.ds(0, HEAD_SIZE)])
        copy(wv_ref.at[:, pl.ds(at, HEAD_SIZE)], first.at[pl.ds(0, rows), pl.ds(HEAD_SIZE, HEAD_SIZE)])
        if early:
            copy(
                wq_ref.at[:, pl.ds(aligned(head * wide), early * HEAD_SIZE)],
                first.at[pl.ds(0, rows), pl.ds(2 * HEAD_SIZE, early * HEAD_SIZE)],
            )
        copy(facts_ref, first.at[pl.ds(rows, META_ROWS), :])
        copy(
            wq_ref.at[:, pl.ds(aligned(head * wide + early * HEAD_SIZE), (group - early) * HEAD_SIZE)],
            second,
        )
    for one in copies:
        one.wait()


def columns_of(tokens_ref, offs_ref, piece):
    parts = [
        tokens_ref[:, pl.ds(aligned(offs_ref[piece * MEMBERS + k]), HEAD_SIZE)]
        for k in range(MEMBERS)
    ]
    return jnp.concatenate(parts, axis=1)


def project_body(n_segs, n_pieces, keep_last, offs_ref, *refs):
    tokens, pieces = refs[:n_segs], refs[n_segs : n_segs + n_pieces - 1]
    outs = refs[n_segs + n_pieces - 1 :]
    for n in range(n_segs):
        total = None
        for p in range(n_pieces - 1):
            term = jnp.dot(
                columns_of(tokens[n], offs_ref, p), pieces[p][...], preferred_element_type=jnp.float32
            )
            total = term if total is None else total + term
        outs[n][...] = total
        if keep_last:
            outs[n_segs + n][...] = columns_of(tokens[n], offs_ref, n_pieces - 1)


def sigma_plus(v):
    return jnp.where(v > 0, v + 1.0, jnp.exp(jnp.minimum(v, 0.0)))


def split(values):
    high = values.astype(jnp.bfloat16)
    return high, (values - high.astype(jnp.float32)).astype(jnp.bfloat16)


def kv_body(meta_ref, piece_ref, *refs):
    sums, lasts = refs[:MEMBERS], refs[MEMBERS : 2 * MEMBERS]
    outs = refs[2 * MEMBERS :]
    whole = None
    for seg in range(MEMBERS):
        total = sums[seg][...] + jnp.dot(
            lasts[seg][...], piece_ref[...], preferred_element_type=jnp.float32
        )
        kvq = total.astype(jnp.bfloat16)
        outs[2 * seg][...] = kvq
        length = kvq.shape[0]
        row = lax.broadcasted_iota(jnp.int32, (length, HEAD_SIZE), 0)
        keys = kvq[:, :HEAD_SIZE].astype(jnp.float32)
        sig = jnp.where(row < meta_ref[FACTS * seg], sigma_plus(keys), 0.0)
        wide = jnp.concatenate(
            [kvq[:, HEAD_SIZE : 2 * HEAD_SIZE], jnp.ones((length, HEAD_SIZE), jnp.bfloat16)], axis=1
        )
        high, low = split(sig)
        over = (((0,), (0,)), ((), ()))
        delta = lax.dot_general(high, wide, over, preferred_element_type=jnp.float32)
        delta += lax.dot_general(low, wide, over, preferred_element_type=jnp.float32)
        outs[2 * seg + 1][...] = delta
        whole = delta if whole is None else whole + delta
    outs[-1][...] = whole.astype(jnp.bfloat16)


def attend_body(
    segs, heads, first_head, group, ready, here_ref, meta_ref, gate_ref, base_ref, *refs
):
    kvqs, deltas = refs[:MEMBERS], refs[MEMBERS : 2 * MEMBERS]
    rest = refs[2 * MEMBERS :]
    n = len(segs)
    if not ready:
        piece, sums, lasts = rest[0], rest[1 : 1 + n], rest[1 + n : 1 + 2 * n]
        rest = rest[1 + 2 * n :]
    outs = rest
    me = here_ref[0]
    for at, seg in enumerate(segs):
        if ready:
            queries = kvqs[seg][:, 2 * HEAD_SIZE : (2 + heads) * HEAD_SIZE]
        else:
            queries = (
                sums[at][...]
                + jnp.dot(lasts[at][...], piece[...], preferred_element_type=jnp.float32)
            ).astype(jnp.bfloat16)
        length = queries.shape[0]
        blocks = length // BLK
        valid = meta_ref[FACTS * seg]
        seen = meta_ref[FACTS * seg + 1] == 1

        memory = base_ref[...].astype(jnp.float32)
        for other in range(MEMBERS):
            if other != seg:
                earlier = jnp.where((me ^ other) < (me ^ seg), 1.0, 0.0)
                memory = memory + earlier * deltas[other][...]
        mem_high, mem_low = split(memory)

        for block in range(blocks):
            span = slice(block * BLK, (block + 1) * BLK)
            stacked = jnp.concatenate(
                [queries[span, h * HEAD_SIZE : (h + 1) * HEAD_SIZE] for h in range(heads)], axis=0
            )
            width = (block + 1) * BLK
            keys = kvqs[seg][0:width, :HEAD_SIZE]
            values = kvqs[seg][0:width, HEAD_SIZE : 2 * HEAD_SIZE]
            scores = lax.dot_general(
                stacked, keys, (((1,), (1,)), ((), ())), preferred_element_type=jnp.float32
            ) * HEAD_SIZE ** (-0.5)
            i = lax.broadcasted_iota(jnp.int32, (BLK, width), 0) + block * BLK
            j = lax.broadcasted_iota(jnp.int32, (BLK, width), 1)
            allowed = (j <= i) & (j < valid)
            if block:
                allowed = allowed & ((j >= block * BLK) | seen)
            allowed = jnp.concatenate([jnp.where(allowed, 0.0, -1e30)] * heads, axis=0)
            masked = jnp.where(allowed < 0, -1e30, scores)
            top = jnp.max(masked, axis=-1, keepdims=True)
            expo = jnp.exp(masked - top)
            total = jnp.maximum(jnp.sum(expo, axis=-1, keepdims=True), 1.0)
            weights = (expo / total).astype(jnp.bfloat16)
            local = jnp.dot(weights, values, preferred_element_type=jnp.float32)

            high, low = split(sigma_plus(stacked.astype(jnp.float32)))
            numer = jnp.dot(high, mem_high, preferred_element_type=jnp.float32)
            numer += jnp.dot(high, mem_low, preferred_element_type=jnp.float32)
            numer += jnp.dot(low, mem_high, preferred_element_type=jnp.float32)
            retrieved = numer[:, :HEAD_SIZE] / (numer[:, HEAD_SIZE:] + 1.0)
            live = lax.broadcasted_iota(jnp.int32, (BLK, HEAD_SIZE), 0) + block * BLK < valid
            for h in range(heads):
                part = slice(h * BLK, (h + 1) * BLK)
                logit = jnp.full((1, HEAD_SIZE), gate_ref[me * group + first_head + h], jnp.float32)
                gate = 1.0 / (1.0 + jnp.exp(-logit))
                mixed = gate * retrieved[part] + (1.0 - gate) * local[part]
                outs[at][span, h * HEAD_SIZE : (h + 1) * HEAD_SIZE] = jnp.where(
                    live, mixed, 0.0
                ).astype(jnp.bfloat16)


def assemble_body(group, widths, here_ref, *refs):
    parts, out = refs[:-1], refs[-1]
    for k in range(MEMBERS):
        at = (here_ref[0] ^ k) * group * HEAD_SIZE
        for c, width in enumerate(widths):
            out[:, pl.ds(aligned(at), width)] = parts[len(widths) * k + c][...]
            at = at + width


def after(array, *others):
    return lax.optimization_barrier((array,) + others)[0]


def shards(sizes, tokens, w_query, w_key, value_weight, gate_bias, block_mask, valid_len):
    n_seg, n_z = sizes
    n_groups = n_seg // MEMBERS
    heads_kv = w_key.shape[1] // HEAD_SIZE
    group = w_query.shape[1] // w_key.shape[1]
    early = group // 2
    rows = w_query.shape[0]
    length, width = tokens.shape[1], tokens.shape[2]
    assert heads_kv == MEMBERS and length == 2 * BLK
    seg = lax.axis_index("seg")
    z = lax.axis_index("fsdp")
    g, m = seg // MEMBERS, seg % MEMBERS
    here = jnp.reshape(m, (1,)).astype(jnp.int32)
    bf16, f32 = jnp.bfloat16, jnp.float32
    shape = jax.ShapeDtypeStruct

    def permute(array, to):
        pairs = []
        for gg in range(n_groups):
            for mm in range(MEMBERS):
                for zz in range(n_z):
                    target = to(gg, mm, zz)
                    if target is not None:
                        index = lambda t: (t[0] * MEMBERS + t[1]) * n_z + t[2]
                        pairs.append((index((gg, mm, zz)), index(target)))
        return lax.ppermute(array, AXES, pairs)

    def to_member(array, k):
        return permute(array, lambda gg, mm, zz: (gg, mm ^ k, zz))

    wide = [(2 + early) * HEAD_SIZE, (group - early) * HEAD_SIZE]
    packed = call(
        functools.partial(pack_body, group, early),
        [shape((rows + META_ROWS, wide[0]), bf16), shape((rows, wide[1]), bf16)] * MEMBERS,
        [SMEM] * 3 + [HBM] * 3,
        scratch=[pltpu.VMEM((META_ROWS, wide[0]), bf16), pltpu.SemaphoreType.DMA((5 * MEMBERS,))],
        out_spec=HBM,
    )(here, valid_len, block_mask, w_query, w_key, value_weight)
    order = (2, 3, 1)
    first = {0: packed[0]}
    second = {0: packed[1]}
    for k in order:
        first[k] = to_member(packed[2 * k], k)
    for k in order:
        second[k] = to_member(packed[2 * k + 1], k)
    meta = jnp.concatenate([first[k][rows, :FACTS] for k in range(MEMBERS)]).astype(jnp.int32)

    own = after(tokens[0], first[2], first[3])
    across = to_member(own, 2)
    sibling = to_member(own, 1)
    diagonal = to_member(across, 1)
    books = [tokens[0], sibling, across, diagonal]

    def gathered(piece):
        if n_groups == 2 and n_z == 4:
            inside = (z == 1) | (z == 2)
            over = lambda part: permute(part, lambda gg, mm, zz: (gg ^ 1, mm, zz))
            outward = lambda part: permute(
                part, lambda gg, mm, zz: (gg, mm, zz ^ 1) if zz in (1, 2) else None
            )
            inward = lambda part: permute(
                part, lambda gg, mm, zz: (gg, mm, zz ^ 3) if zz in (1, 2) else None
            )
            one = permute(piece, lambda gg, mm, zz: (gg, mm, zz ^ 1))
            inner = inward(piece)
            far = [over(piece)]
            middle = inward(one)
            outer = outward(inner)
            far.append(over(one))
            two = jnp.where(inside, inner, outer)
            last = outward(middle)
            far.append(over(two))
            three = jnp.where(inside, middle, last)
            far.append(over(three))
            return [piece, one, two, three] + far
        index = lambda gg, mm, zz: (gg * MEMBERS + mm) * n_z + zz
        everything = lax.all_gather(
            piece,
            AXES,
            axis_index_groups=[
                [index(gg, mm, zz) for gg in range(n_groups) for zz in range(n_z)]
                for mm in range(MEMBERS)
            ],
        )
        columns = piece.shape[1]
        natural = everything.reshape(n_groups, n_z, MEMBERS, rows, columns)
        members = jnp.arange(MEMBERS, dtype=jnp.int32) ^ m
        natural = jnp.take(natural, members, axis=2).transpose(0, 2, 1, 3, 4)
        return list(natural.reshape(-1, MEMBERS * HEAD_SIZE, columns))

    if n_groups == 2 and n_z == 4:
        assert rows == HEAD_SIZE
        n_pieces = n_groups * n_z
        inside = (z == 1) | (z == 2)
        steps = jnp.stack([z, z ^ 1, jnp.where(inside, z ^ 3, z ^ 2), jnp.where(inside, z ^ 2, z ^ 3)])
        a, b, k = jnp.meshgrid(
            jnp.arange(n_groups), jnp.arange(n_z), jnp.arange(MEMBERS), indexing="ij"
        )
        offs = ((((g ^ a) * MEMBERS + (m ^ k)) * n_z + steps[b]) * rows).reshape(-1).astype(jnp.int32)
    else:
        n_pieces = width // (MEMBERS * HEAD_SIZE)
        offs = jnp.arange(n_pieces * MEMBERS, dtype=jnp.int32) * HEAD_SIZE

    chunks = [
        gathered(jnp.concatenate([part[k][:rows] for k in range(MEMBERS)], axis=0))
        for part in (first, second)
    ]

    sums, lasts = [[], []], []
    for c in range(2):
        for segs in ((0, 1), (2, 3)):
            n = len(segs)
            found = call(
                functools.partial(project_body, n, n_pieces, c == 0),
                [shape((length, wide[c]), f32)] * n
                + [shape((length, MEMBERS * HEAD_SIZE), bf16)] * (n if c == 0 else 0),
                [SMEM] + [VMEM] * (n + n_pieces - 1),
                flops=2 * n * length * width * wide[c],
            )(offs, *[books[s] for s in segs], *chunks[c][:-1])
            sums[c] += found[:n]
            lasts += found[n:]

    found = call(
        kv_body,
        [shape((length, wide[0]), bf16), shape((HEAD_SIZE, 2 * HEAD_SIZE), f32)] * MEMBERS
        + [shape((HEAD_SIZE, 2 * HEAD_SIZE), bf16)],
        [SMEM] + [VMEM] * (1 + 2 * MEMBERS),
        flops=2 * MEMBERS * length * MEMBERS * HEAD_SIZE * wide[0],
    )(meta, chunks[0][-1], *sums[0], *lasts)
    kvqs, deltas, total = found[0:-1:2], found[1:-1:2], found[-1]

    base = None
    for a in range(1, n_groups):
        term = permute(total, lambda gg, mm, zz: (gg ^ a, mm, zz) if gg < gg ^ a else None)
        base = term if base is None else base.astype(f32) + term.astype(f32)

    sent = {}

    def attend(c, segs):
        heads = wide[c] // HEAD_SIZE - (0 if c else 2)
        extra = [] if c == 0 else [chunks[1][-1], *[sums[1][s] for s in segs], *[lasts[s] for s in segs]]
        attended = call(
            functools.partial(attend_body, segs, heads, c * early, group, c == 0),
            [shape((length, heads * HEAD_SIZE), bf16)] * len(segs),
            [SMEM] * 3 + [VMEM] * (1 + 2 * MEMBERS + len(extra)),
            flops=2 * len(segs) * length * length * HEAD_SIZE * heads * 3,
        )(here, meta, gate_bias, base, *kvqs, *deltas, *extra)
        for seg_at, part in zip(segs, attended):
            sent[c, seg_at] = to_member(part, seg_at) if seg_at else part

    attend(0, (2, 3))
    attend(0, (1, 0))
    attend(1, (2, 3))
    attend(1, (1, 0))
    (output,) = call(
        functools.partial(assemble_body, group, (early * HEAD_SIZE, wide[1])),
        [shape((length, w_query.shape[1]), bf16)],
        [SMEM] + [VMEM] * (2 * MEMBERS),
    )(here, *[sent[c, k] for k in range(MEMBERS) for c in range(2)])
    return output[None]


def solution(mesh):
    in_specs = (
        P("fsdp", "seg", None),
        P(("seg", "fsdp"), None),
        P(("seg", "fsdp"), None),
        P(("seg", "fsdp"), None),
        P(),
        P("fsdp", "seg", None, None),
        P("fsdp", "seg"),
    )
    out_specs = P("fsdp", "seg", None)
    body = functools.partial(shards, (mesh.shape["seg"], mesh.shape["fsdp"]))
    return jax.shard_map(body, mesh=mesh, in_specs=in_specs, out_specs=out_specs, check_vma=False)
```

```python
import functools

import jax
import jax.numpy as jnp
from jax import lax
from jax.experimental import pallas as pl
from jax.experimental.pallas import tpu as pltpu
from jax.sharding import PartitionSpec as P

HEAD_SIZE = 128
BLK = 128
MEMBERS = 4
META_ROWS = 16
HALF = META_ROWS // 2
AXES = ("seg", "fsdp")

VMEM = pl.BlockSpec(memory_space=pltpu.VMEM)
SMEM = pl.BlockSpec(memory_space=pltpu.SMEM)
ANY = pl.BlockSpec(memory_space=pl.ANY)
HBM = pl.BlockSpec(memory_space=pltpu.HBM)


def call(body, outs, in_specs, flops=0, scratch=(), out_spec=VMEM, limit=28 << 20):
    return pl.pallas_call(
        body,
        out_shape=outs,
        in_specs=in_specs,
        out_specs=[out_spec] * len(outs),
        scratch_shapes=list(scratch),
        compiler_params=pltpu.CompilerParams(vmem_limit_bytes=limit),
        cost_estimate=pl.CostEstimate(flops=flops, bytes_accessed=4 << 20, transcendentals=0),
    )


def aligned(offset):
    return pl.multiple_of(offset, HEAD_SIZE)


def pack_body(
    group, early, here_ref, valid_ref, mask_ref, wq_ref, wk_ref, wv_ref, *refs
):
    outs, facts_ref, sems = refs[: 2 * MEMBERS], refs[-2], refs[-1]
    rows = wk_ref.shape[0]
    row = lax.broadcasted_iota(jnp.int32, facts_ref.shape, 0)
    facts = jnp.where(row < HALF, valid_ref[0, 0], mask_ref[0, 0, 1, 0])
    facts_ref[...] = facts.astype(jnp.float32).astype(jnp.bfloat16)
    copies = []

    def copy(source, target):
        copies.append(pltpu.make_async_copy(source, target, sems.at[len(copies)]))
        copies[-1].start()

    for k in range(MEMBERS):
        head = here_ref[1] ^ k
        first, second = outs[2 * k : 2 * k + 2]
        at = aligned(head * HEAD_SIZE)
        wide = group * HEAD_SIZE
        copy(wk_ref.at[:, pl.ds(at, HEAD_SIZE)], first.at[pl.ds(0, rows), pl.ds(0, HEAD_SIZE)])
        copy(wv_ref.at[:, pl.ds(at, HEAD_SIZE)], first.at[pl.ds(0, rows), pl.ds(HEAD_SIZE, HEAD_SIZE)])
        if early:
            copy(
                wq_ref.at[:, pl.ds(aligned(head * wide), early * HEAD_SIZE)],
                first.at[pl.ds(0, rows), pl.ds(2 * HEAD_SIZE, early * HEAD_SIZE)],
            )
        copy(facts_ref, first.at[pl.ds(rows, META_ROWS), :])
        copy(
            wq_ref.at[:, pl.ds(aligned(head * wide + early * HEAD_SIZE), (group - early) * HEAD_SIZE)],
            second,
        )
    for one in copies:
        one.wait()


def columns_of(tokens_ref, here_ref, piece, line):
    if not line:
        return tokens_ref[:, pl.ds(piece * MEMBERS * HEAD_SIZE, MEMBERS * HEAD_SIZE)]
    g, m, z = here_ref[0] ^ (piece // line), here_ref[1], here_ref[2]
    inside = (z == 1) | (z == 2)
    step = piece % line
    if step < 2:
        z = z ^ step
    else:
        z = jnp.where(inside, z ^ (5 - step), z ^ step)
    parts = [
        tokens_ref[:, pl.ds(aligned(((g * MEMBERS + (m ^ k)) * line + z) * HEAD_SIZE), HEAD_SIZE)]
        for k in range(MEMBERS)
    ]
    return jnp.concatenate(parts, axis=1)


def facts_of(message_ref):
    rows = message_ref.shape[0] - META_ROWS
    facts = message_ref[rows:, : 2 * HEAD_SIZE].astype(jnp.float32)
    return facts[0:1, :], facts[HALF : HALF + 1, :]


def iota(shape, dimension):
    return lax.broadcasted_iota(jnp.int32, shape, dimension).astype(jnp.float32)


def project_body(n_segs, n_pieces, keep_last, line, here_ref, *refs):
    tokens, pieces = refs[:n_segs], refs[n_segs : n_segs + n_pieces - 1]
    outs = refs[n_segs + n_pieces - 1 :]
    for n in range(n_segs):
        total = None
        for p in range(n_pieces - 1):
            term = jnp.dot(
                columns_of(tokens[n], here_ref, p, line), pieces[p][...], preferred_element_type=jnp.float32
            )
            total = term if total is None else total + term
        outs[n][...] = total
        if keep_last:
            outs[n_segs + n][...] = columns_of(tokens[n], here_ref, n_pieces - 1, line)


def sigma_plus(v):
    return jnp.where(v > 0, v + 1.0, jnp.exp(jnp.minimum(v, 0.0)))


def split(values):
    high = values.astype(jnp.bfloat16)
    return high, (values - high.astype(jnp.float32)).astype(jnp.bfloat16)


def kv_body(piece_ref, *refs):
    sums, lasts, messages = refs[:MEMBERS], refs[MEMBERS : 2 * MEMBERS], refs[2 * MEMBERS : 3 * MEMBERS]
    outs = refs[3 * MEMBERS :]
    whole = None
    for seg in range(MEMBERS):
        total = sums[seg][...] + jnp.dot(
            lasts[seg][...], piece_ref[...], preferred_element_type=jnp.float32
        )
        kvq = total.astype(jnp.bfloat16)
        outs[2 * seg][...] = kvq
        length = kvq.shape[0]
        valid, _ = facts_of(messages[seg])
        keys = kvq[:, :HEAD_SIZE].astype(jnp.float32)
        live = iota((length, HEAD_SIZE), 0) < valid[:, :HEAD_SIZE]
        sig = jnp.where(live, sigma_plus(keys), 0.0)
        wide = jnp.concatenate(
            [kvq[:, HEAD_SIZE : 2 * HEAD_SIZE], jnp.ones((length, HEAD_SIZE), jnp.bfloat16)], axis=1
        )
        high, low = split(sig)
        over = (((0,), (0,)), ((), ()))
        delta = lax.dot_general(high, wide, over, preferred_element_type=jnp.float32)
        delta += lax.dot_general(low, wide, over, preferred_element_type=jnp.float32)
        outs[2 * seg + 1][...] = delta
        whole = delta if whole is None else whole + delta
    outs[-1][...] = whole.astype(jnp.bfloat16)


def attend_body(segs, early, late, first_head, group, here_ref, gate_ref, base_ref, *refs):
    kvqs, deltas, messages = refs[:MEMBERS], refs[MEMBERS : 2 * MEMBERS], refs[2 * MEMBERS : 3 * MEMBERS]
    rest = refs[3 * MEMBERS :]
    n = len(segs)
    piece, sums, lasts, outs = rest[0], rest[1 : 1 + n], rest[1 + n : 1 + 2 * n], rest[1 + 2 * n :]
    me = here_ref[1]
    heads = early + late[1] - late[0]
    at_late = slice(late[0] * HEAD_SIZE, late[1] * HEAD_SIZE)
    for at, seg in enumerate(segs):
        queries = (
            sums[at][:, at_late]
            + jnp.dot(lasts[at][...], piece[:, at_late], preferred_element_type=jnp.float32)
        ).astype(jnp.bfloat16)
        if early:
            queries = jnp.concatenate(
                [kvqs[seg][:, 2 * HEAD_SIZE : (2 + early) * HEAD_SIZE], queries], axis=1
            )
        length = queries.shape[0]
        blocks = length // BLK
        valid, seen = facts_of(messages[seg])

        memory = base_ref[...].astype(jnp.float32)
        for other in range(MEMBERS):
            if other != seg:
                earlier = jnp.where((me ^ other) < (me ^ seg), 1.0, 0.0)
                memory = memory + earlier * deltas[other][...]
        mem_high, mem_low = split(memory)

        for block in range(blocks):
            span = slice(block * BLK, (block + 1) * BLK)
            stacked = jnp.concatenate(
                [queries[span, h * HEAD_SIZE : (h + 1) * HEAD_SIZE] for h in range(heads)], axis=0
            )
            width = (block + 1) * BLK
            keys = kvqs[seg][0:width, :HEAD_SIZE]
            values = kvqs[seg][0:width, HEAD_SIZE : 2 * HEAD_SIZE]
            scores = lax.dot_general(
                stacked, keys, (((1,), (1,)), ((), ())), preferred_element_type=jnp.float32
            ) * HEAD_SIZE ** (-0.5)
            i, j = iota((BLK, width), 0) + block * BLK, iota((BLK, width), 1)
            limit = valid[:, :width]
            if block:
                limit = jnp.where((j[0:1] >= block * BLK) | (seen[:, :width] > 0), limit, 0.0)
            allowed = (j <= i) & (j < limit)
            masked = jnp.concatenate(
                [
                    jnp.where(allowed, scores[h * BLK : (h + 1) * BLK], -1e30)
                    for h in range(heads)
                ],
                axis=0,
            )
            top = jnp.max(masked, axis=-1, keepdims=True)
            expo = jnp.exp(masked - top)
            total = jnp.maximum(jnp.sum(expo, axis=-1, keepdims=True), 1.0)
            weights = (expo / total).astype(jnp.bfloat16)
            local = jnp.dot(weights, values, preferred_element_type=jnp.float32)

            high, low = split(sigma_plus(stacked.astype(jnp.float32)))
            numer = jnp.dot(high, mem_high, preferred_element_type=jnp.float32)
            numer += jnp.dot(high, mem_low, preferred_element_type=jnp.float32)
            numer += jnp.dot(low, mem_high, preferred_element_type=jnp.float32)
            retrieved = numer[:, :HEAD_SIZE] / (numer[:, HEAD_SIZE:] + 1.0)
            live = iota((BLK, HEAD_SIZE), 0) + block * BLK < valid[:, :HEAD_SIZE]
            for h in range(heads):
                part = slice(h * BLK, (h + 1) * BLK)
                logit = jnp.full((1, HEAD_SIZE), gate_ref[me * group + first_head + h], jnp.float32)
                gate = 1.0 / (1.0 + jnp.exp(-logit))
                mixed = gate * retrieved[part] + (1.0 - gate) * local[part]
                outs[at][span, h * HEAD_SIZE : (h + 1) * HEAD_SIZE] = jnp.where(
                    live, mixed, 0.0
                ).astype(jnp.bfloat16)


def assemble_body(group, widths, here_ref, *refs):
    parts, out = refs[:-1], refs[-1]
    for k in range(MEMBERS):
        at = (here_ref[1] ^ k) * group * HEAD_SIZE
        for c, width in enumerate(widths):
            out[:, pl.ds(aligned(at), width)] = parts[len(widths) * k + c][...]
            at = at + width


def after(array, *others):
    return lax.optimization_barrier((array,) + others)[0]


def shards(sizes, tokens, w_query, w_key, value_weight, gate_bias, block_mask, valid_len):
    n_seg, n_z = sizes
    n_groups = n_seg // MEMBERS
    heads_kv = w_key.shape[1] // HEAD_SIZE
    group = w_query.shape[1] // w_key.shape[1]
    early = 1
    rows = w_query.shape[0]
    length, width = tokens.shape[1], tokens.shape[2]
    assert heads_kv == MEMBERS and length == 2 * BLK
    seg = lax.axis_index("seg")
    z = lax.axis_index("fsdp")
    g, m = seg // MEMBERS, seg % MEMBERS
    here = jnp.stack([g, m, z]).astype(jnp.int32)
    bf16, f32 = jnp.bfloat16, jnp.float32
    shape = jax.ShapeDtypeStruct

    def permute(array, to):
        pairs = []
        for gg in range(n_groups):
            for mm in range(MEMBERS):
                for zz in range(n_z):
                    target = to(gg, mm, zz)
                    if target is not None:
                        index = lambda t: (t[0] * MEMBERS + t[1]) * n_z + t[2]
                        pairs.append((index((gg, mm, zz)), index(target)))
        return lax.ppermute(array, AXES, pairs)

    def to_member(array, k):
        return permute(array, lambda gg, mm, zz: (gg, mm ^ k, zz))

    wide = [(2 + early) * HEAD_SIZE, (group - early) * HEAD_SIZE]
    packed = call(
        functools.partial(pack_body, group, early),
        [shape((rows + META_ROWS, wide[0]), bf16), shape((rows, wide[1]), bf16)] * MEMBERS,
        [SMEM] * 3 + [HBM] * 3,
        scratch=[pltpu.VMEM((META_ROWS, wide[0]), bf16), pltpu.SemaphoreType.DMA((5 * MEMBERS,))],
        out_spec=ANY,
    )(here, valid_len, block_mask, w_query, w_key, value_weight)
    order = (2, 3, 1)
    first = {0: packed[0]}
    second = {0: packed[1]}
    for k in order:
        first[k] = to_member(packed[2 * k], k)
    for k in order:
        second[k] = to_member(packed[2 * k + 1], k)
    messages = [first[k] for k in range(MEMBERS)]

    own = after(tokens[0], first[2], first[3], second[2], second[3])
    across = to_member(own, 2)
    sibling = to_member(own, 1)
    diagonal = to_member(across, 1)
    books = [tokens[0], sibling, across, diagonal]

    def lines(pieces):
        inside = (z == 1) | (z == 2)
        over = lambda part: permute(part, lambda gg, mm, zz: (gg ^ 1, mm, zz))
        pair = lambda part: permute(part, lambda gg, mm, zz: (gg, mm, zz ^ 1))
        outward = lambda part: permute(
            part, lambda gg, mm, zz: (gg, mm, zz ^ 1) if zz in (1, 2) else None
        )
        inward = lambda part: permute(
            part, lambda gg, mm, zz: (gg, mm, zz ^ 3) if zz in (1, 2) else None
        )
        locked = lambda *parts: lax.optimization_barrier(parts)
        states = [(pair(piece), inward(piece), over(piece)) for piece in pieces]
        found = [[] for _ in pieces]
        for n, piece in enumerate(pieces):
            one, inner, far0 = locked(*states[n])
            found[n] = [piece, one, far0]
            states[n] = (inward(one), outward(inner), over(one), inner)
        for n in range(len(pieces)):
            middle, outer, far1, inner = locked(*states[n])
            two = jnp.where(inside, inner, outer)
            states[n] = (outward(middle), over(two), middle, two, far1)
        for n in range(len(pieces)):
            last, far2, middle, two, far1 = locked(*states[n])
            three = jnp.where(inside, middle, last)
            piece, one, far0 = found[n]
            found[n] = [piece, one, two, three, far0, far1, far2, over(three)]
        return found

    def gathered(piece):
        index = lambda gg, mm, zz: (gg * MEMBERS + mm) * n_z + zz
        everything = lax.all_gather(
            piece,
            AXES,
            axis_index_groups=[
                [index(gg, mm, zz) for gg in range(n_groups) for zz in range(n_z)]
                for mm in range(MEMBERS)
            ],
        )
        columns = piece.shape[1]
        natural = everything.reshape(n_groups, n_z, MEMBERS, rows, columns)
        members = jnp.arange(MEMBERS, dtype=jnp.int32) ^ m
        natural = jnp.take(natural, members, axis=2).transpose(0, 2, 1, 3, 4)
        return list(natural.reshape(-1, MEMBERS * HEAD_SIZE, columns))

    pieces = [
        jnp.concatenate([part[k][:rows] for k in range(MEMBERS)], axis=0) for part in (first, second)
    ]
    if n_groups == 2 and n_z == 4:
        assert rows == HEAD_SIZE
        line, chunks = n_z, lines(pieces)
    else:
        line, chunks = 0, [gathered(piece) for piece in pieces]
    n_pieces = width // (MEMBERS * HEAD_SIZE)

    sums, lasts = [[], []], []
    for c in range(2):
        for segs in ((0, 1), (2, 3)):
            n = len(segs)
            found = call(
                functools.partial(project_body, n, n_pieces, c == 0, line),
                [shape((length, wide[c]), f32)] * n
                + [shape((length, MEMBERS * HEAD_SIZE), bf16)] * (n if c == 0 else 0),
                [SMEM] + [VMEM] * (n + n_pieces - 1),
                flops=2 * n * length * width * wide[c],
            )(here, *[books[s] for s in segs], *chunks[c][:-1])
            sums[c] += found[:n]
            lasts += found[n:]

    found = call(
        kv_body,
        [shape((length, wide[0]), bf16), shape((HEAD_SIZE, 2 * HEAD_SIZE), f32)] * MEMBERS
        + [shape((HEAD_SIZE, 2 * HEAD_SIZE), bf16)],
        [VMEM] * (1 + 3 * MEMBERS),
        flops=2 * MEMBERS * length * MEMBERS * HEAD_SIZE * wide[0],
    )(chunks[0][-1], *sums[0], *lasts, *messages)
    kvqs, deltas, total = found[0:-1:2], found[1:-1:2], found[-1]

    base = None
    for a in range(1, n_groups):
        term = permute(total, lambda gg, mm, zz: (gg ^ a, mm, zz) if gg < gg ^ a else None)
        base = term if base is None else base.astype(f32) + term.astype(f32)

    sent = {}
    half = group // 2
    picks = [(early, (0, half - early)), (0, (half - early, group - early))]

    def attend(c, segs, base):
        attended = call(
            functools.partial(attend_body, segs, *picks[c], c * half, group),
            [shape((length, half * HEAD_SIZE), bf16)] * len(segs),
            [SMEM] * 2 + [VMEM] * (2 + 3 * MEMBERS + 2 * len(segs)),
            flops=2 * len(segs) * length * length * HEAD_SIZE * half * 3,
        )(
            here, gate_bias, base, *kvqs, *deltas, *messages, chunks[1][-1],
            *[sums[1][s] for s in segs], *[lasts[s] for s in segs],
        )
        for seg_at, part in zip(segs, attended):
            sent[c, seg_at] = to_member(part, seg_at) if seg_at else part
        return attended

    far = attend(0, (2, 3), base)
    far = attend(1, (2, 3), after(base, *far))
    near = attend(0, (1, 0), after(base, *far))
    attend(1, (1, 0), after(base, *near))
    (output,) = call(
        functools.partial(assemble_body, group, (half * HEAD_SIZE,) * 2),
        [shape((length, w_query.shape[1]), bf16)],
        [SMEM] + [VMEM] * (2 * MEMBERS),
    )(here, *[sent[c, k] for k in range(MEMBERS) for c in range(2)])
    return output[None]


def solution(mesh):
    in_specs = (
        P("fsdp", "seg", None),
        P(("seg", "fsdp"), None),
        P(("seg", "fsdp"), None),
        P(("seg", "fsdp"), None),
        P(),
        P("fsdp", "seg", None, None),
        P("fsdp", "seg"),
    )
    out_specs = P("fsdp", "seg", None)
    body = functools.partial(shards, (mesh.shape["seg"], mesh.shape["fsdp"]))
    return jax.shard_map(body, mesh=mesh, in_specs=in_specs, out_specs=out_specs, check_vma=False)
```

```python
import functools

import jax
import jax.numpy as jnp
from jax import lax
from jax.experimental import pallas as pl
from jax.experimental.pallas import tpu as pltpu
from jax.sharding import PartitionSpec as P

HEAD_SIZE = 128
BLK = 128
MEMBERS = 4
META_ROWS = 16
HALF = META_ROWS // 2
AXES = ("seg", "fsdp")

VMEM = pl.BlockSpec(memory_space=pltpu.VMEM)
SMEM = pl.BlockSpec(memory_space=pltpu.SMEM)
ANY = pl.BlockSpec(memory_space=pl.ANY)
HBM = pl.BlockSpec(memory_space=pltpu.HBM)


def call(body, outs, in_specs, flops=0, scratch=(), out_spec=VMEM, limit=28 << 20):
    return pl.pallas_call(
        body,
        out_shape=outs,
        in_specs=in_specs,
        out_specs=[out_spec] * len(outs),
        scratch_shapes=list(scratch),
        compiler_params=pltpu.CompilerParams(vmem_limit_bytes=limit),
        cost_estimate=pl.CostEstimate(flops=flops, bytes_accessed=4 << 20, transcendentals=0),
    )


def aligned(offset):
    return pl.multiple_of(offset, HEAD_SIZE)


def pack_body(group, here_ref, valid_ref, mask_ref, wq_ref, wk_ref, wv_ref, *refs):
    outs, facts_ref, sems = refs[:MEMBERS], refs[-2], refs[-1]
    rows = wk_ref.shape[0]
    row = lax.broadcasted_iota(jnp.int32, facts_ref.shape, 0)
    facts = jnp.where(row < HALF, valid_ref[0, 0], mask_ref[0, 0, 1, 0])
    facts_ref[...] = facts.astype(jnp.float32).astype(jnp.bfloat16)
    copies = []

    def copy(source, target):
        copies.append(pltpu.make_async_copy(source, target, sems.at[len(copies)]))
        copies[-1].start()

    for k in (2, 3, 1, 0):
        head, out = here_ref[1] ^ k, outs[k]
        at = aligned(head * HEAD_SIZE)
        top = pl.ds(0, rows)
        copy(wk_ref.at[:, pl.ds(at, HEAD_SIZE)], out.at[top, pl.ds(0, HEAD_SIZE)])
        copy(wv_ref.at[:, pl.ds(at, HEAD_SIZE)], out.at[top, pl.ds(HEAD_SIZE, HEAD_SIZE)])
        wide = group * HEAD_SIZE
        copy(wq_ref.at[:, pl.ds(aligned(head * wide), wide)], out.at[top, pl.ds(2 * HEAD_SIZE, wide)])
        copy(facts_ref, out.at[pl.ds(rows, META_ROWS), :])
    for one in copies:
        one.wait()


def columns_of(tokens_ref, here_ref, piece, members, line):
    if not line:
        first = (piece * MEMBERS + members[0]) * HEAD_SIZE
        return tokens_ref[:, pl.ds(first, len(members) * HEAD_SIZE)]
    g, m, z = here_ref[0] ^ (piece // line), here_ref[1], here_ref[2]
    inside = (z == 1) | (z == 2)
    step = piece % line
    if step < 2:
        z = z ^ step
    else:
        z = jnp.where(inside, z ^ (5 - step), z ^ step)
    parts = [
        tokens_ref[:, pl.ds(aligned(((g * MEMBERS + (m ^ k)) * line + z) * HEAD_SIZE), HEAD_SIZE)]
        for k in members
    ]
    return jnp.concatenate(parts, axis=1)


def facts_of(message_ref):
    rows = message_ref.shape[0] - META_ROWS
    facts = message_ref[rows:, : 2 * HEAD_SIZE].astype(jnp.float32)
    return facts[0:1, :], facts[HALF : HALF + 1, :]


def iota(shape, dimension):
    return lax.broadcasted_iota(jnp.int32, shape, dimension).astype(jnp.float32)


def project_body(places, line, n_pieces, first, here_ref, *refs):
    tokens, pieces = refs[:2], refs[2 : 2 + 2 * len(places)]
    rest = refs[2 + 2 * len(places) :]
    length = tokens[0].shape[0]
    total = None if first else jnp.concatenate([rest[0][...], rest[1][...]], axis=0)
    outs = rest if first else rest[2:]
    for half in range(2):
        members = (0, 1) if half == 0 else (2, 3)
        for n, place in enumerate(places):
            columns = jnp.concatenate(
                [columns_of(one, here_ref, place, members, line) for one in tokens], axis=0
            )
            term = jnp.dot(columns, pieces[2 * n + half][...], preferred_element_type=jnp.float32)
            total = term if total is None else total + term
    for n in range(2):
        outs[n][...] = total[n * length : (n + 1) * length]
        if first:
            outs[2 + n][...] = columns_of(tokens[n], here_ref, n_pieces - 1, range(MEMBERS), line)


def sigma_plus(v):
    return jnp.where(v > 0, v + 1.0, jnp.exp(jnp.minimum(v, 0.0)))


def split(values):
    high = values.astype(jnp.bfloat16)
    return high, (values - high.astype(jnp.float32)).astype(jnp.bfloat16)


def last_piece(columns_ref, upper_ref, lower_ref, start, width):
    half = upper_ref.shape[0]
    at = slice(start, start + width)
    lost = 2 * HEAD_SIZE if start else 0
    term = jnp.dot(columns_ref[:, :half], upper_ref[:, at], preferred_element_type=jnp.float32)
    return term + jnp.dot(columns_ref[:, half:], lower_ref[:, start - lost : start - lost + width], preferred_element_type=jnp.float32)


def kv_body(upper_ref, lower_ref, *refs):
    sums, lasts, messages = refs[:MEMBERS], refs[MEMBERS : 2 * MEMBERS], refs[2 * MEMBERS : 3 * MEMBERS]
    outs = refs[3 * MEMBERS :]
    whole = None
    for seg in range(MEMBERS):
        at = 2 * HEAD_SIZE
        total = sums[seg][:, :at] + last_piece(lasts[seg], upper_ref, lower_ref, 0, at)
        kv = total.astype(jnp.bfloat16)
        outs[2 * seg][...] = kv
        length = kv.shape[0]
        valid, _ = facts_of(messages[seg])
        keys = kv[:, :HEAD_SIZE].astype(jnp.float32)
        live = iota((length, HEAD_SIZE), 0) < valid[:, :HEAD_SIZE]
        sig = jnp.where(live, sigma_plus(keys), 0.0)
        wide = jnp.concatenate(
            [kv[:, HEAD_SIZE:], jnp.ones((length, HEAD_SIZE), jnp.bfloat16)], axis=1
        )
        high, low = split(sig)
        over = (((0,), (0,)), ((), ()))
        delta = lax.dot_general(high, wide, over, preferred_element_type=jnp.float32)
        delta += lax.dot_general(low, wide, over, preferred_element_type=jnp.float32)
        outs[2 * seg + 1][...] = delta
        whole = delta if whole is None else whole + delta
    outs[-1][...] = whole.astype(jnp.bfloat16)


def attend_body(segs, heads, first_head, group, here_ref, gate_ref, base_ref, upper_ref, lower_ref, *refs):
    kvs, deltas, messages = refs[:MEMBERS], refs[MEMBERS : 2 * MEMBERS], refs[2 * MEMBERS : 3 * MEMBERS]
    rest = refs[3 * MEMBERS :]
    n = len(segs)
    sums, lasts, outs = rest[:n], rest[n : 2 * n], rest[2 * n :]
    me = here_ref[1]
    start, across = (2 + first_head) * HEAD_SIZE, heads * HEAD_SIZE
    for at, seg in enumerate(segs):
        queries = sums[at][:, start : start + across]
        queries += last_piece(lasts[at], upper_ref, lower_ref, start, across)
        queries = queries.astype(jnp.bfloat16)
        length = queries.shape[0]
        blocks = length // BLK
        valid, seen = facts_of(messages[seg])

        memory = base_ref[...].astype(jnp.float32)
        for other in range(MEMBERS):
            if other != seg:
                earlier = jnp.where((me ^ other) < (me ^ seg), 1.0, 0.0)
                memory = memory + earlier * deltas[other][...]
        mem_high, mem_low = split(memory)

        for block in range(blocks):
            span = slice(block * BLK, (block + 1) * BLK)
            stacked = jnp.concatenate(
                [queries[span, h * HEAD_SIZE : (h + 1) * HEAD_SIZE] for h in range(heads)], axis=0
            )
            width = (block + 1) * BLK
            keys = kvs[seg][0:width, :HEAD_SIZE]
            values = kvs[seg][0:width, HEAD_SIZE:]
            scores = lax.dot_general(
                stacked, keys, (((1,), (1,)), ((), ())), preferred_element_type=jnp.float32
            ) * HEAD_SIZE ** (-0.5)
            i, j = iota((BLK, width), 0) + block * BLK, iota((BLK, width), 1)
            limit = valid[:, :width]
            if block:
                limit = jnp.where((j[0:1] >= block * BLK) | (seen[:, :width] > 0), limit, 0.0)
            allowed = (j <= i) & (j < limit)
            masked = jnp.concatenate(
                [
                    jnp.where(allowed, scores[h * BLK : (h + 1) * BLK], -1e30)
                    for h in range(heads)
                ],
                axis=0,
            )
            top = jnp.max(masked, axis=-1, keepdims=True)
            expo = jnp.exp(masked - top)
            total = jnp.maximum(jnp.sum(expo, axis=-1, keepdims=True), 1.0)
            weights = (expo / total).astype(jnp.bfloat16)
            local = jnp.dot(weights, values, preferred_element_type=jnp.float32)

            high, low = split(sigma_plus(stacked.astype(jnp.float32)))
            numer = jnp.dot(high, mem_high, preferred_element_type=jnp.float32)
            numer += jnp.dot(high, mem_low, preferred_element_type=jnp.float32)
            numer += jnp.dot(low, mem_high, preferred_element_type=jnp.float32)
            retrieved = numer[:, :HEAD_SIZE] / (numer[:, HEAD_SIZE:] + 1.0)
            live = iota((BLK, HEAD_SIZE), 0) + block * BLK < valid[:, :HEAD_SIZE]
            for h in range(heads):
                part = slice(h * BLK, (h + 1) * BLK)
                logit = jnp.full((1, HEAD_SIZE), gate_ref[me * group + first_head + h], jnp.float32)
                gate = 1.0 / (1.0 + jnp.exp(-logit))
                mixed = gate * retrieved[part] + (1.0 - gate) * local[part]
                outs[at][span, h * HEAD_SIZE : (h + 1) * HEAD_SIZE] = jnp.where(
                    live, mixed, 0.0
                ).astype(jnp.bfloat16)


def assemble_body(group, widths, here_ref, *refs):
    parts, out = refs[:-1], refs[-1]
    for k in range(MEMBERS):
        at = (here_ref[1] ^ k) * group * HEAD_SIZE
        for c, width in enumerate(widths):
            out[:, pl.ds(aligned(at), width)] = parts[len(widths) * k + c][...]
            at = at + width


def after(array, *others):
    return lax.optimization_barrier((array,) + others)[0]


def shards(sizes, tokens, w_query, w_key, value_weight, gate_bias, block_mask, valid_len):
    n_seg, n_z = sizes
    n_groups = n_seg // MEMBERS
    heads_kv = w_key.shape[1] // HEAD_SIZE
    group = w_query.shape[1] // w_key.shape[1]
    half = group // 2
    rows = w_query.shape[0]
    length, width = tokens.shape[1], tokens.shape[2]
    assert heads_kv == MEMBERS and length == 2 * BLK
    seg = lax.axis_index("seg")
    z = lax.axis_index("fsdp")
    g, m = seg // MEMBERS, seg % MEMBERS
    here = jnp.stack([g, m, z]).astype(jnp.int32)
    bf16, f32 = jnp.bfloat16, jnp.float32
    shape = jax.ShapeDtypeStruct

    def permute(array, to):
        pairs = []
        for gg in range(n_groups):
            for mm in range(MEMBERS):
                for zz in range(n_z):
                    target = to(gg, mm, zz)
                    if target is not None:
                        index = lambda t: (t[0] * MEMBERS + t[1]) * n_z + t[2]
                        pairs.append((index((gg, mm, zz)), index(target)))
        return lax.ppermute(array, AXES, pairs)

    def to_member(array, k):
        return permute(array, lambda gg, mm, zz: (gg, mm ^ k, zz))

    wide = (2 + group) * HEAD_SIZE
    packed = call(
        functools.partial(pack_body, group),
        [shape((rows + META_ROWS, wide), bf16)] * MEMBERS,
        [SMEM] * 3 + [HBM] * 3,
        scratch=[pltpu.VMEM((META_ROWS, wide), bf16), pltpu.SemaphoreType.DMA((4 * MEMBERS,))],
        out_spec=ANY,
    )(here, valid_len, block_mask, w_query, w_key, value_weight)
    messages = [packed[0], *[to_member(packed[k], k) for k in (1, 2, 3)]]

    own = after(tokens[0], *messages)
    across = to_member(own, 2)
    sibling = to_member(own, 1)

    def lines(pieces):
        inside = (z == 1) | (z == 2)
        over = lambda part: permute(part, lambda gg, mm, zz: (gg ^ 1, mm, zz))
        pair = lambda part: permute(part, lambda gg, mm, zz: (gg, mm, zz ^ 1))
        outward = lambda part: permute(
            part, lambda gg, mm, zz: (gg, mm, zz ^ 1) if zz in (1, 2) else None
        )
        inward = lambda part: permute(
            part, lambda gg, mm, zz: (gg, mm, zz ^ 3) if zz in (1, 2) else None
        )
        locked = lambda *parts: lax.optimization_barrier(parts)
        states = [(pair(piece), inward(piece), over(piece)) for piece in pieces]
        found, marks = [[] for _ in pieces], []
        for n, piece in enumerate(pieces):
            one, inner, far0 = locked(*states[n])
            found[n] = [piece, one, far0]
            states[n] = (inward(one), outward(inner), over(one), inner)
        for n in range(len(pieces)):
            middle, outer, far1, inner = locked(*states[n])
            marks.append(far1)
            two = jnp.where(inside, inner, outer)
            states[n] = (outward(middle), over(two), middle, two, far1)
        for n in range(len(pieces)):
            last, far2, middle, two, far1 = locked(*states[n])
            three = jnp.where(inside, middle, last)
            piece, one, far0 = found[n]
            found[n] = [piece, one, two, three, far0, far1, far2]
            if n == 0:
                final = over(three)
                found[n] += [final, final]
            else:
                at = 2 * HEAD_SIZE
                found[n] += [over(jnp.where(inside, middle[:, cut], last[:, cut])) for cut in (slice(0, at), slice(at, None))]
        return found, marks[-1]

    def gathered(piece):
        index = lambda gg, mm, zz: (gg * MEMBERS + mm) * n_z + zz
        everything = lax.all_gather(
            piece,
            AXES,
            axis_index_groups=[
                [index(gg, mm, zz) for gg in range(n_groups) for zz in range(n_z)]
                for mm in range(MEMBERS)
            ],
        )
        columns = piece.shape[1]
        natural = everything.reshape(n_groups, n_z, MEMBERS, rows, columns)
        members = jnp.arange(MEMBERS, dtype=jnp.int32) ^ m
        natural = jnp.take(natural, members, axis=2).transpose(0, 2, 1, 3, 4)
        return list(natural.reshape(-1, MEMBERS * HEAD_SIZE, columns))

    pieces = [
        jnp.concatenate([messages[k][:rows] for k in members], axis=0) for members in ((0, 1), (2, 3))
    ]
    n_pieces = width // (MEMBERS * HEAD_SIZE)
    if n_groups == 2 and n_z == 4:
        assert rows == HEAD_SIZE
        line = n_z
        (upper, lower), mark = lines(pieces)
        across_late = after(across, mark)
        parts = [(0, 1, 4, 5), (2, 3, 6)]
    else:
        line = 0
        full = gathered(jnp.concatenate(pieces, axis=0))
        cut = MEMBERS * HEAD_SIZE // 2
        upper, lower = [part[:cut] for part in full], [part[cut:] for part in full]
        upper.append(upper[-1])
        lower[-1:] = [lower[-1][:, : 2 * HEAD_SIZE], lower[-1][:, 2 * HEAD_SIZE :]]
        across_late = across
        parts = [tuple(range(n_pieces - 1))]
    diagonal = to_member(across_late, 1)
    books = [tokens[0], sibling, across, diagonal]

    sums, lasts = [None] * MEMBERS, [None] * MEMBERS
    for c, places in enumerate(parts):
        for segs in ((0, 1), (2, 3)):
            found = call(
                functools.partial(project_body, places, line, n_pieces, c == 0),
                [shape((length, wide), f32)] * 2
                + [shape((length, MEMBERS * HEAD_SIZE), bf16)] * (2 if c == 0 else 0),
                [SMEM] + [VMEM] * (2 + 2 * len(places) + (0 if c == 0 else 2)),
                flops=2 * 2 * length * len(places) * MEMBERS * HEAD_SIZE * wide,
            )(
                here,
                *[books[s] for s in segs],
                *[part[p] for p in places for part in (upper, lower)],
                *([] if c == 0 else [sums[s] for s in segs]),
            )
            for at, s in enumerate(segs):
                sums[s] = found[at]
                if c == 0:
                    lasts[s] = found[2 + at]

    found = call(
        kv_body,
        [shape((length, 2 * HEAD_SIZE), bf16), shape((HEAD_SIZE, 2 * HEAD_SIZE), f32)] * MEMBERS
        + [shape((HEAD_SIZE, 2 * HEAD_SIZE), bf16)],
        [VMEM] * (2 + 3 * MEMBERS),
        flops=2 * MEMBERS * length * MEMBERS * HEAD_SIZE * 2 * HEAD_SIZE,
    )(upper[-2], lower[-2], *sums, *lasts, *messages)
    kvs, deltas, total = found[0:-1:2], found[1:-1:2], found[-1]

    base = None
    for a in range(1, n_groups):
        term = permute(total, lambda gg, mm, zz: (gg ^ a, mm, zz) if gg < gg ^ a else None)
        base = term if base is None else base.astype(f32) + term.astype(f32)

    sent = {}

    def attend(c, segs, base):
        attended = call(
            functools.partial(attend_body, segs, half, c * half, group),
            [shape((length, half * HEAD_SIZE), bf16)] * len(segs),
            [SMEM] * 2 + [VMEM] * (3 + 3 * MEMBERS + 2 * len(segs)),
            flops=2 * len(segs) * length * length * HEAD_SIZE * half * 3,
        )(
            here, gate_bias, base, upper[-1], lower[-1], *kvs, *deltas, *messages,
            *[sums[s] for s in segs], *[lasts[s] for s in segs],
        )
        for seg_at, part in zip(segs, attended):
            sent[c, seg_at] = to_member(part, seg_at) if seg_at else part
        return attended

    far = attend(0, (2, 3), base)
    far = attend(1, (2, 3), after(base, *far))
    near = attend(0, (1, 0), after(base, *far))
    attend(1, (1, 0), after(base, *near))
    (output,) = call(
        functools.partial(assemble_body, group, (half * HEAD_SIZE,) * 2),
        [shape((length, w_query.shape[1]), bf16)],
        [SMEM] + [VMEM] * (2 * MEMBERS),
    )(here, *[sent[c, k] for k in range(MEMBERS) for c in range(2)])
    return output[None]


def solution(mesh):
    in_specs = (
        P("fsdp", "seg", None),
        P(("seg", "fsdp"), None),
        P(("seg", "fsdp"), None),
        P(("seg", "fsdp"), None),
        P(),
        P("fsdp", "seg", None, None),
        P("fsdp", "seg"),
    )
    out_specs = P("fsdp", "seg", None)
    body = functools.partial(shards, (mesh.shape["seg"], mesh.shape["fsdp"]))
    return jax.shard_map(body, mesh=mesh, in_specs=in_specs, out_specs=out_specs, check_vma=False)
```

```python
import functools

import jax
import jax.numpy as jnp
from jax import lax
from jax.experimental import pallas as pl
from jax.experimental.pallas import tpu as pltpu
from jax.sharding import PartitionSpec as P

HEAD_SIZE = 128
BLK = 128
MEMBERS = 4
META_ROWS = 16
HALF = META_ROWS // 2
AXES = ("seg", "fsdp")

VMEM = pl.BlockSpec(memory_space=pltpu.VMEM)
SMEM = pl.BlockSpec(memory_space=pltpu.SMEM)
ANY = pl.BlockSpec(memory_space=pl.ANY)
HBM = pl.BlockSpec(memory_space=pltpu.HBM)


def call(body, outs, in_specs, flops=0, scratch=(), out_spec=VMEM, limit=28 << 20):
    return pl.pallas_call(
        body,
        out_shape=outs,
        in_specs=in_specs,
        out_specs=[out_spec] * len(outs),
        scratch_shapes=list(scratch),
        compiler_params=pltpu.CompilerParams(vmem_limit_bytes=limit),
        cost_estimate=pl.CostEstimate(flops=flops, bytes_accessed=4 << 20, transcendentals=0),
    )


def aligned(offset):
    return pl.multiple_of(offset, HEAD_SIZE)


def pack_body(group, here_ref, valid_ref, mask_ref, wq_ref, wk_ref, wv_ref, *refs):
    outs, facts_ref, sems = refs[:MEMBERS], refs[-2], refs[-1]
    rows = wk_ref.shape[0]
    row = lax.broadcasted_iota(jnp.int32, facts_ref.shape, 0)
    facts = jnp.where(row < HALF, valid_ref[0, 0], mask_ref[0, 0, 1, 0])
    facts_ref[...] = facts.astype(jnp.float32).astype(jnp.bfloat16)
    copies = []

    def copy(source, target):
        copies.append(pltpu.make_async_copy(source, target, sems.at[len(copies)]))
        copies[-1].start()

    for k in (2, 3, 1, 0):
        head, out = here_ref[1] ^ k, outs[k]
        at = aligned(head * HEAD_SIZE)
        top = pl.ds(0, rows)
        copy(wk_ref.at[:, pl.ds(at, HEAD_SIZE)], out.at[top, pl.ds(0, HEAD_SIZE)])
        copy(wv_ref.at[:, pl.ds(at, HEAD_SIZE)], out.at[top, pl.ds(HEAD_SIZE, HEAD_SIZE)])
        wide = group * HEAD_SIZE
        copy(wq_ref.at[:, pl.ds(aligned(head * wide), wide)], out.at[top, pl.ds(2 * HEAD_SIZE, wide)])
        copy(facts_ref, out.at[pl.ds(rows, META_ROWS), :])
    for one in copies:
        one.wait()


def columns_of(tokens_ref, here_ref, piece, members, line):
    if not line:
        first = (piece * MEMBERS + members[0]) * HEAD_SIZE
        return tokens_ref[:, pl.ds(first, len(members) * HEAD_SIZE)]
    g, m, z = here_ref[0] ^ (piece // line), here_ref[1], here_ref[2]
    inside = (z == 1) | (z == 2)
    step = piece % line
    if step < 2:
        z = z ^ step
    else:
        z = jnp.where(inside, z ^ (5 - step), z ^ step)
    parts = [
        tokens_ref[:, pl.ds(aligned(((g * MEMBERS + (m ^ k)) * line + z) * HEAD_SIZE), HEAD_SIZE)]
        for k in members
    ]
    return jnp.concatenate(parts, axis=1)


def facts_of(message_ref):
    rows = message_ref.shape[0] - META_ROWS
    facts = message_ref[rows:, : 2 * HEAD_SIZE].astype(jnp.float32)
    return facts[0:1, :], facts[HALF : HALF + 1, :]


def iota(shape, dimension):
    return lax.broadcasted_iota(jnp.int32, shape, dimension).astype(jnp.float32)


def project_body(places, line, n_pieces, first, here_ref, *refs):
    tokens, pieces = refs[:2], refs[2 : 2 + 2 * len(places)]
    rest = refs[2 + 2 * len(places) :]
    length = tokens[0].shape[0]
    total = None if first else jnp.concatenate([rest[0][...], rest[1][...]], axis=0)
    outs = rest if first else rest[2:]
    for half in range(2):
        members = (0, 1) if half == 0 else (2, 3)
        for n, place in enumerate(places):
            columns = jnp.concatenate(
                [columns_of(one, here_ref, place, members, line) for one in tokens], axis=0
            )
            term = jnp.dot(columns, pieces[2 * n + half][...], preferred_element_type=jnp.float32)
            total = term if total is None else total + term
    for n in range(2):
        outs[n][...] = total[n * length : (n + 1) * length]
        if first:
            outs[2 + n][...] = columns_of(tokens[n], here_ref, n_pieces - 1, range(MEMBERS), line)


def sigma_plus(v):
    return jnp.where(v > 0, v + 1.0, jnp.exp(jnp.minimum(v, 0.0)))


def split(values):
    high = values.astype(jnp.bfloat16)
    return high, (values - high.astype(jnp.float32)).astype(jnp.bfloat16)


def last_piece(columns_ref, upper_ref, lower_ref, start, width):
    half = upper_ref.shape[0]
    at = slice(start, start + width)
    lost = 2 * HEAD_SIZE if start else 0
    term = jnp.dot(columns_ref[:, :half], upper_ref[:, at], preferred_element_type=jnp.float32)
    return term + jnp.dot(columns_ref[:, half:], lower_ref[:, start - lost : start - lost + width], preferred_element_type=jnp.float32)


def kv_body(upper_ref, lower_ref, *refs):
    sums, lasts, messages = refs[:MEMBERS], refs[MEMBERS : 2 * MEMBERS], refs[2 * MEMBERS : 3 * MEMBERS]
    outs = refs[3 * MEMBERS :]
    whole = None
    for seg in range(MEMBERS):
        at = 2 * HEAD_SIZE
        total = sums[seg][:, :at] + last_piece(lasts[seg], upper_ref, lower_ref, 0, at)
        kv = total.astype(jnp.bfloat16)
        outs[2 * seg][...] = kv
        length = kv.shape[0]
        valid, _ = facts_of(messages[seg])
        keys = kv[:, :HEAD_SIZE].astype(jnp.float32)
        live = iota((length, HEAD_SIZE), 0) < valid[:, :HEAD_SIZE]
        sig = jnp.where(live, sigma_plus(keys), 0.0)
        wide = jnp.concatenate(
            [kv[:, HEAD_SIZE:], jnp.ones((length, HEAD_SIZE), jnp.bfloat16)], axis=1
        )
        high, low = split(sig)
        over = (((0,), (0,)), ((), ()))
        delta = lax.dot_general(high, wide, over, preferred_element_type=jnp.float32)
        delta += lax.dot_general(low, wide, over, preferred_element_type=jnp.float32)
        outs[2 * seg + 1][...] = delta
        whole = delta if whole is None else whole + delta
    outs[-1][...] = whole.astype(jnp.bfloat16)


def attend_body(segs, heads, first_head, group, here_ref, gate_ref, base_ref, upper_ref, lower_ref, *refs):
    kvs, deltas, messages = refs[:MEMBERS], refs[MEMBERS : 2 * MEMBERS], refs[2 * MEMBERS : 3 * MEMBERS]
    rest = refs[3 * MEMBERS :]
    n = len(segs)
    sums, lasts, outs = rest[:n], rest[n : 2 * n], rest[2 * n :]
    me = here_ref[1]
    start, across = (2 + first_head) * HEAD_SIZE, heads * HEAD_SIZE
    for at, seg in enumerate(segs):
        queries = sums[at][:, start : start + across]
        queries += last_piece(lasts[at], upper_ref, lower_ref, start, across)
        queries = queries.astype(jnp.bfloat16)
        length = queries.shape[0]
        blocks = length // BLK
        valid, seen = facts_of(messages[seg])

        memory = base_ref[...].astype(jnp.float32)
        for other in range(MEMBERS):
            if other != seg:
                earlier = jnp.where((me ^ other) < (me ^ seg), 1.0, 0.0)
                memory = memory + earlier * deltas[other][...]
        mem_high, mem_low = split(memory)

        for block in range(blocks):
            span = slice(block * BLK, (block + 1) * BLK)
            stacked = jnp.concatenate(
                [queries[span, h * HEAD_SIZE : (h + 1) * HEAD_SIZE] for h in range(heads)], axis=0
            )
            width = (block + 1) * BLK
            keys = kvs[seg][0:width, :HEAD_SIZE]
            values = kvs[seg][0:width, HEAD_SIZE:]
            scores = lax.dot_general(
                stacked, keys, (((1,), (1,)), ((), ())), preferred_element_type=jnp.float32
            ) * HEAD_SIZE ** (-0.5)
            i, j = iota((BLK, width), 0) + block * BLK, iota((BLK, width), 1)
            limit = valid[:, :width]
            if block:
                limit = jnp.where((j[0:1] >= block * BLK) | (seen[:, :width] > 0), limit, 0.0)
            allowed = (j <= i) & (j < limit)
            masked = jnp.concatenate(
                [
                    jnp.where(allowed, scores[h * BLK : (h + 1) * BLK], -1e30)
                    for h in range(heads)
                ],
                axis=0,
            )
            top = jnp.max(masked, axis=-1, keepdims=True)
            expo = jnp.exp(masked - top)
            total = jnp.maximum(jnp.sum(expo, axis=-1, keepdims=True), 1.0)
            weights = (expo / total).astype(jnp.bfloat16)
            local = jnp.dot(weights, values, preferred_element_type=jnp.float32)

            high, low = split(sigma_plus(stacked.astype(jnp.float32)))
            numer = jnp.dot(high, mem_high, preferred_element_type=jnp.float32)
            numer += jnp.dot(high, mem_low, preferred_element_type=jnp.float32)
            numer += jnp.dot(low, mem_high, preferred_element_type=jnp.float32)
            retrieved = numer[:, :HEAD_SIZE] / (numer[:, HEAD_SIZE:] + 1.0)
            live = iota((BLK, HEAD_SIZE), 0) + block * BLK < valid[:, :HEAD_SIZE]
            for h in range(heads):
                part = slice(h * BLK, (h + 1) * BLK)
                logit = jnp.full((1, HEAD_SIZE), gate_ref[me * group + first_head + h], jnp.float32)
                gate = 1.0 / (1.0 + jnp.exp(-logit))
                mixed = gate * retrieved[part] + (1.0 - gate) * local[part]
                outs[at][span, h * HEAD_SIZE : (h + 1) * HEAD_SIZE] = jnp.where(
                    live, mixed, 0.0
                ).astype(jnp.bfloat16)


def assemble_body(group, widths, here_ref, *refs):
    parts, out = refs[:-1], refs[-1]
    for k in range(MEMBERS):
        at = (here_ref[1] ^ k) * group * HEAD_SIZE
        for c, width in enumerate(widths):
            out[:, pl.ds(aligned(at), width)] = parts[len(widths) * k + c][...]
            at = at + width


def after(array, *others):
    return lax.optimization_barrier((array,) + others)[0]


def shards(sizes, tokens, w_query, w_key, value_weight, gate_bias, block_mask, valid_len):
    n_seg, n_z = sizes
    n_groups = n_seg // MEMBERS
    heads_kv = w_key.shape[1] // HEAD_SIZE
    group = w_query.shape[1] // w_key.shape[1]
    half = group // 2
    rows = w_query.shape[0]
    length, width = tokens.shape[1], tokens.shape[2]
    assert heads_kv == MEMBERS and length == 2 * BLK
    seg = lax.axis_index("seg")
    z = lax.axis_index("fsdp")
    g, m = seg // MEMBERS, seg % MEMBERS
    here = jnp.stack([g, m, z]).astype(jnp.int32)
    bf16, f32 = jnp.bfloat16, jnp.float32
    shape = jax.ShapeDtypeStruct

    def permute(array, to):
        pairs = []
        for gg in range(n_groups):
            for mm in range(MEMBERS):
                for zz in range(n_z):
                    target = to(gg, mm, zz)
                    if target is not None:
                        index = lambda t: (t[0] * MEMBERS + t[1]) * n_z + t[2]
                        pairs.append((index((gg, mm, zz)), index(target)))
        return lax.ppermute(array, AXES, pairs)

    def to_member(array, k):
        return permute(array, lambda gg, mm, zz: (gg, mm ^ k, zz))

    wide = (2 + group) * HEAD_SIZE
    packed = call(
        functools.partial(pack_body, group),
        [shape((rows + META_ROWS, wide), bf16)] * MEMBERS,
        [SMEM] * 3 + [HBM] * 3,
        scratch=[pltpu.VMEM((META_ROWS, wide), bf16), pltpu.SemaphoreType.DMA((4 * MEMBERS,))],
        out_spec=ANY,
    )(here, valid_len, block_mask, w_query, w_key, value_weight)
    messages = [packed[0], *[to_member(packed[k], k) for k in (1, 2, 3)]]

    def gathered(piece):
        index = lambda gg, mm, zz: (gg * MEMBERS + mm) * n_z + zz
        everything = lax.all_gather(
            piece,
            AXES,
            axis_index_groups=[
                [index(gg, mm, zz) for gg in range(n_groups) for zz in range(n_z)]
                for mm in range(MEMBERS)
            ],
        )
        columns = piece.shape[1]
        natural = everything.reshape(n_groups, n_z, MEMBERS, rows, columns)
        members = jnp.arange(MEMBERS, dtype=jnp.int32) ^ m
        natural = jnp.take(natural, members, axis=2).transpose(0, 2, 1, 3, 4)
        return list(natural.reshape(-1, MEMBERS * HEAD_SIZE, columns))

    pieces = [
        jnp.concatenate([messages[k][:rows] for k in members], axis=0) for members in ((0, 1), (2, 3))
    ]
    n_pieces = width // (MEMBERS * HEAD_SIZE)
    sums, lasts = [None] * MEMBERS, [None] * MEMBERS

    def project(segs, places, upper, lower, line, first):
        found = call(
            functools.partial(project_body, places, line, n_pieces, first),
            [shape((length, wide), f32)] * 2
            + [shape((length, MEMBERS * HEAD_SIZE), bf16)] * (2 if first else 0),
            [SMEM] + [VMEM] * (2 + 2 * len(places) + (0 if first else 2)),
            flops=2 * 2 * length * len(places) * MEMBERS * HEAD_SIZE * wide,
        )(
            here,
            *[books[s] for s in segs],
            *[part[p] for p in places for part in (upper, lower)],
            *([] if first else [sums[s] for s in segs]),
        )
        for at, s in enumerate(segs):
            sums[s] = found[at]
            if first:
                lasts[s] = found[2 + at]

    cut = 2 * HEAD_SIZE
    if n_groups == 2 and n_z == 4:
        assert rows == HEAD_SIZE
        inside = (z == 1) | (z == 2)
        over = lambda part: permute(part, lambda gg, mm, zz: (gg ^ 1, mm, zz))
        pair = lambda part: permute(part, lambda gg, mm, zz: (gg, mm, zz ^ 1))
        outward = lambda part: permute(
            part, lambda gg, mm, zz: (gg, mm, zz ^ 1) if zz in (1, 2) else None
        )
        inward = lambda part: permute(
            part, lambda gg, mm, zz: (gg, mm, zz ^ 3) if zz in (1, 2) else None
        )
        locked = lambda *parts: lax.optimization_barrier(parts)
        stage1 = lambda piece: (pair(piece), inward(piece), over(piece))
        stage2 = lambda one, inner: (inward(one), outward(inner), over(one))
        stage3 = lambda middle, two: (outward(middle), over(two))

        a, b, own, sibling = locked(*pieces, tokens[0], to_member(tokens[0], 1))
        across = to_member(own, 2)
        a_one, a_inner, a_far0 = locked(*stage1(a))
        b_one, b_inner, b_far0 = locked(*stage1(b))
        a_middle, a_outer, a_far1 = locked(*stage2(a_one, a_inner))
        b_middle, b_outer, b_far1 = locked(*stage2(b_one, b_inner))
        a_two = jnp.where(inside, a_inner, a_outer)
        a_last, a_far2 = stage3(a_middle, a_two)
        b_two = jnp.where(inside, b_inner, b_outer)
        b_last, b_far2 = stage3(b_middle, b_two)
        (
            a_last, a_far2, a_middle, a_two, a_far1, b_last, b_middle, b_two, b_far1, across, sibling, own
        ) = locked(
            a_last, a_far2, a_middle, a_two, a_far1, b_last, b_middle, b_two, b_far1, across, sibling, own
        )
        diagonal = to_member(across, 1)
        a_three = jnp.where(inside, a_middle, a_last)
        a_far3 = over(a_three)
        b_three = jnp.where(inside, b_middle, b_last)
        b_far3 = [
            over(jnp.where(inside, b_middle[:, at], b_last[:, at]))
            for at in (slice(0, cut), slice(cut, None))
        ]
        books = [own, sibling, across, diagonal]
        upper = [a, a_one, a_two, a_three, a_far0, a_far1, a_far2, a_far3, a_far3]
        lower = [b, b_one, b_two, b_three, b_far0, b_far1, b_far2] + b_far3
        project((0, 1), (0, 1, 4, 5), upper, lower, n_z, True)
        project((0, 1), (2, 3, 6), upper, lower, n_z, False)
        project((2, 3), (0, 1, 4, 5), upper, lower, n_z, True)
        project((2, 3), (2, 3, 6), upper, lower, n_z, False)
    else:
        across, sibling = to_member(tokens[0], 2), to_member(tokens[0], 1)
        books = [tokens[0], sibling, across, to_member(across, 1)]
        full = gathered(jnp.concatenate(pieces, axis=0))
        deep = MEMBERS * HEAD_SIZE // 2
        upper, lower = [part[:deep] for part in full], [part[deep:] for part in full]
        upper.append(upper[-1])
        lower[-1:] = [lower[-1][:, :cut], lower[-1][:, cut:]]
        for segs in ((0, 1), (2, 3)):
            project(segs, tuple(range(n_pieces - 1)), upper, lower, 0, True)

    found = call(
        kv_body,
        [shape((length, 2 * HEAD_SIZE), bf16), shape((HEAD_SIZE, 2 * HEAD_SIZE), f32)] * MEMBERS
        + [shape((HEAD_SIZE, 2 * HEAD_SIZE), bf16)],
        [VMEM] * (2 + 3 * MEMBERS),
        flops=2 * MEMBERS * length * MEMBERS * HEAD_SIZE * 2 * HEAD_SIZE,
    )(upper[-2], lower[-2], *sums, *lasts, *messages)
    kvs, deltas, total = found[0:-1:2], found[1:-1:2], found[-1]

    base = None
    for a in range(1, n_groups):
        term = permute(total, lambda gg, mm, zz: (gg ^ a, mm, zz) if gg < gg ^ a else None)
        base = term if base is None else base.astype(f32) + term.astype(f32)

    sent = {}

    def attend(c, segs, base):
        attended = call(
            functools.partial(attend_body, segs, half, c * half, group),
            [shape((length, half * HEAD_SIZE), bf16)] * len(segs),
            [SMEM] * 2 + [VMEM] * (3 + 3 * MEMBERS + 2 * len(segs)),
            flops=2 * len(segs) * length * length * HEAD_SIZE * half * 3,
        )(
            here, gate_bias, base, upper[-1], lower[-1], *kvs, *deltas, *messages,
            *[sums[s] for s in segs], *[lasts[s] for s in segs],
        )
        for seg_at, part in zip(segs, attended):
            sent[c, seg_at] = to_member(part, seg_at) if seg_at else part
        return attended

    far = attend(0, (2, 3), base)
    far = attend(1, (2, 3), after(base, *far))
    near = attend(0, (1, 0), after(base, *far))
    attend(1, (1, 0), after(base, *near))
    (output,) = call(
        functools.partial(assemble_body, group, (half * HEAD_SIZE,) * 2),
        [shape((length, w_query.shape[1]), bf16)],
        [SMEM] + [VMEM] * (2 * MEMBERS),
    )(here, *[sent[c, k] for k in range(MEMBERS) for c in range(2)])
    return output[None]


def solution(mesh):
    in_specs = (
        P("fsdp", "seg", None),
        P(("seg", "fsdp"), None),
        P(("seg", "fsdp"), None),
        P(("seg", "fsdp"), None),
        P(),
        P("fsdp", "seg", None, None),
        P("fsdp", "seg"),
    )
    out_specs = P("fsdp", "seg", None)
    body = functools.partial(shards, (mesh.shape["seg"], mesh.shape["fsdp"]))
    return jax.shard_map(body, mesh=mesh, in_specs=in_specs, out_specs=out_specs, check_vma=False)
```

```python
import functools

import jax
import jax.numpy as jnp
from jax import lax
from jax.experimental import pallas as pl
from jax.experimental.pallas import tpu as pltpu
from jax.sharding import PartitionSpec as P

HEAD_SIZE = 128
BLK = 128
MEMBERS = 4
META_ROWS = 16
HALF = META_ROWS // 2
AXES = ("seg", "fsdp")

VMEM = pl.BlockSpec(memory_space=pltpu.VMEM)
SMEM = pl.BlockSpec(memory_space=pltpu.SMEM)
ANY = pl.BlockSpec(memory_space=pl.ANY)
HBM = pl.BlockSpec(memory_space=pltpu.HBM)


def call(body, outs, in_specs, flops=0, scratch=(), out_spec=VMEM, limit=16 << 20):
    return pl.pallas_call(
        body,
        out_shape=outs,
        in_specs=in_specs,
        out_specs=[out_spec] * len(outs),
        scratch_shapes=list(scratch),
        compiler_params=pltpu.CompilerParams(vmem_limit_bytes=limit),
        cost_estimate=pl.CostEstimate(flops=flops, bytes_accessed=4 << 20, transcendentals=0),
    )


def aligned(offset):
    return pl.multiple_of(offset, HEAD_SIZE)


def pack_body(group, here_ref, valid_ref, mask_ref, wq_ref, wk_ref, wv_ref, *refs):
    outs, facts_ref, sems = refs[:MEMBERS], refs[-2], refs[-1]
    rows = wk_ref.shape[0]
    row = lax.broadcasted_iota(jnp.int32, facts_ref.shape, 0)
    facts = jnp.where(row < HALF, valid_ref[0, 0], mask_ref[0, 0, 1, 0])
    facts_ref[...] = facts.astype(jnp.float32).astype(jnp.bfloat16)
    copies = []

    def copy(source, target):
        copies.append(pltpu.make_async_copy(source, target, sems.at[len(copies)]))
        copies[-1].start()

    for k in (2, 3, 1, 0):
        head, out = here_ref[1] ^ k, outs[k]
        at = aligned(head * HEAD_SIZE)
        top = pl.ds(0, rows)
        copy(wk_ref.at[:, pl.ds(at, HEAD_SIZE)], out.at[top, pl.ds(0, HEAD_SIZE)])
        copy(wv_ref.at[:, pl.ds(at, HEAD_SIZE)], out.at[top, pl.ds(HEAD_SIZE, HEAD_SIZE)])
        wide = group * HEAD_SIZE
        copy(wq_ref.at[:, pl.ds(aligned(head * wide), wide)], out.at[top, pl.ds(2 * HEAD_SIZE, wide)])
        copy(facts_ref, out.at[pl.ds(rows, META_ROWS), :])
    for one in copies:
        one.wait()


def columns_of(tokens_ref, here_ref, piece, members, line):
    if not line:
        first = (piece * MEMBERS + members[0]) * HEAD_SIZE
        return tokens_ref[:, pl.ds(first, len(members) * HEAD_SIZE)]
    g, m, z = here_ref[0] ^ (piece // line), here_ref[1], here_ref[2]
    inside = (z == 1) | (z == 2)
    step = piece % line
    if step < 2:
        z = z ^ step
    else:
        z = jnp.where(inside, z ^ (5 - step), z ^ step)
    parts = [
        tokens_ref[:, pl.ds(aligned(((g * MEMBERS + (m ^ k)) * line + z) * HEAD_SIZE), HEAD_SIZE)]
        for k in members
    ]
    return jnp.concatenate(parts, axis=1)


def facts_of(message_ref):
    rows = message_ref.shape[0] - META_ROWS
    facts = message_ref[rows:, : 2 * HEAD_SIZE].astype(jnp.float32)
    return facts[0:1, :], facts[HALF : HALF + 1, :]


def iota(shape, dimension):
    return lax.broadcasted_iota(jnp.int32, shape, dimension).astype(jnp.float32)


def project_body(places, line, n_pieces, first, here_ref, *refs):
    tokens, pieces = refs[:2], refs[2 : 2 + 2 * len(places)]
    rest = refs[2 + 2 * len(places) :]
    length = tokens[0].shape[0]
    total = None if first else jnp.concatenate([rest[0][...], rest[1][...]], axis=0)
    outs = rest if first else rest[2:]
    for half in range(2):
        members = (0, 1) if half == 0 else (2, 3)
        for n, place in enumerate(places):
            columns = jnp.concatenate(
                [columns_of(one, here_ref, place, members, line) for one in tokens], axis=0
            )
            term = jnp.dot(columns, pieces[2 * n + half][...], preferred_element_type=jnp.float32)
            total = term if total is None else total + term
    for n in range(2):
        outs[n][...] = total[n * length : (n + 1) * length]
        if first:
            outs[2 + n][...] = columns_of(tokens[n], here_ref, n_pieces - 1, range(MEMBERS), line)


def sigma_plus(v):
    return jnp.where(v > 0, v + 1.0, jnp.exp(jnp.minimum(v, 0.0)))


def split(values):
    high = values.astype(jnp.bfloat16)
    return high, (values - high.astype(jnp.float32)).astype(jnp.bfloat16)


def last_piece(columns_ref, upper_ref, lower_ref, start, width):
    half = upper_ref.shape[0]
    at = slice(start, start + width)
    lost = 2 * HEAD_SIZE if start else 0
    term = jnp.dot(columns_ref[:, :half], upper_ref[:, at], preferred_element_type=jnp.float32)
    return term + jnp.dot(columns_ref[:, half:], lower_ref[:, start - lost : start - lost + width], preferred_element_type=jnp.float32)


def kv_body(upper_ref, lower_ref, *refs):
    sums, lasts, messages = refs[:MEMBERS], refs[MEMBERS : 2 * MEMBERS], refs[2 * MEMBERS : 3 * MEMBERS]
    outs = refs[3 * MEMBERS :]
    whole = None
    for seg in range(MEMBERS):
        at = 2 * HEAD_SIZE
        total = sums[seg][:, :at] + last_piece(lasts[seg], upper_ref, lower_ref, 0, at)
        kv = total.astype(jnp.bfloat16)
        outs[2 * seg][...] = kv
        length = kv.shape[0]
        valid, _ = facts_of(messages[seg])
        keys = kv[:, :HEAD_SIZE].astype(jnp.float32)
        live = iota((length, HEAD_SIZE), 0) < valid[:, :HEAD_SIZE]
        sig = jnp.where(live, sigma_plus(keys), 0.0)
        wide = jnp.concatenate(
            [kv[:, HEAD_SIZE:], jnp.ones((length, HEAD_SIZE), jnp.bfloat16)], axis=1
        )
        high, low = split(sig)
        over = (((0,), (0,)), ((), ()))
        delta = lax.dot_general(high, wide, over, preferred_element_type=jnp.float32)
        delta += lax.dot_general(low, wide, over, preferred_element_type=jnp.float32)
        outs[2 * seg + 1][...] = delta
        whole = delta if whole is None else whole + delta
    outs[-1][...] = whole.astype(jnp.bfloat16)


def local_body(segs, heads, upper_ref, lower_ref, *refs):
    n = len(segs)
    kvs, messages, sums, lasts = refs[:n], refs[n : 2 * n], refs[2 * n : 3 * n], refs[3 * n : 4 * n]
    outs = refs[4 * n :]
    start, across = 2 * HEAD_SIZE, heads * HEAD_SIZE
    for at in range(n):
        queries = sums[at][:, start:] + last_piece(lasts[at], upper_ref, lower_ref, start, across)
        queries = queries.astype(jnp.bfloat16)
        outs[2 * at][...] = queries
        blocks = queries.shape[0] // BLK
        valid, seen = facts_of(messages[at])
        for block in range(blocks):
            span = slice(block * BLK, (block + 1) * BLK)
            stacked = jnp.concatenate(
                [queries[span, h * HEAD_SIZE : (h + 1) * HEAD_SIZE] for h in range(heads)], axis=0
            )
            width = (block + 1) * BLK
            keys = kvs[at][0:width, :HEAD_SIZE]
            values = kvs[at][0:width, HEAD_SIZE:]
            scores = lax.dot_general(
                stacked, keys, (((1,), (1,)), ((), ())), preferred_element_type=jnp.float32
            ) * HEAD_SIZE ** (-0.5)
            i, j = iota((BLK, width), 0) + block * BLK, iota((BLK, width), 1)
            limit = valid[:, :width]
            if block:
                limit = jnp.where((j[0:1] >= block * BLK) | (seen[:, :width] > 0), limit, 0.0)
            allowed = (j <= i) & (j < limit)
            masked = jnp.concatenate(
                [
                    jnp.where(allowed, scores[h * BLK : (h + 1) * BLK], -1e30)
                    for h in range(heads)
                ],
                axis=0,
            )
            top = jnp.max(masked, axis=-1, keepdims=True)
            expo = jnp.exp(masked - top)
            total = jnp.maximum(jnp.sum(expo, axis=-1, keepdims=True), 1.0)
            weights = (expo / total).astype(jnp.bfloat16)
            local = jnp.dot(weights, values, preferred_element_type=jnp.float32)
            for h in range(heads):
                outs[2 * at + 1][span, h * HEAD_SIZE : (h + 1) * HEAD_SIZE] = local[
                    h * BLK : (h + 1) * BLK
                ]


def mix_body(segs, heads, here_ref, gate_ref, base_ref, *refs):
    n = len(segs)
    deltas, rest = refs[:MEMBERS], refs[MEMBERS:]
    messages, queries, locals_, outs = rest[:n], rest[n : 2 * n], rest[2 * n : 3 * n], rest[3 * n :]
    me = here_ref[1]
    for at, seg in enumerate(segs):
        memory = base_ref[...].astype(jnp.float32)
        for other in range(MEMBERS):
            if other != seg:
                earlier = jnp.where((me ^ other) < (me ^ seg), 1.0, 0.0)
                memory = memory + earlier * deltas[other][...]
        mem_high, mem_low = split(memory)
        valid, _ = facts_of(messages[at])
        length = queries[at].shape[0]
        live = iota((length, HEAD_SIZE), 0) < valid[:, :HEAD_SIZE]
        for h in range(heads):
            columns = slice(h * HEAD_SIZE, (h + 1) * HEAD_SIZE)
            high, low = split(sigma_plus(queries[at][:, columns].astype(jnp.float32)))
            numer = jnp.dot(high, mem_high, preferred_element_type=jnp.float32)
            numer += jnp.dot(high, mem_low, preferred_element_type=jnp.float32)
            numer += jnp.dot(low, mem_high, preferred_element_type=jnp.float32)
            retrieved = numer[:, :HEAD_SIZE] / (numer[:, HEAD_SIZE:] + 1.0)
            logit = jnp.full((1, HEAD_SIZE), gate_ref[me * heads + h], jnp.float32)
            gate = 1.0 / (1.0 + jnp.exp(-logit))
            mixed = gate * retrieved + (1.0 - gate) * locals_[at][:, columns]
            outs[at][:, columns] = jnp.where(live, mixed, 0.0).astype(jnp.bfloat16)


def assemble_body(here_ref, *refs):
    parts, out = refs[:-1], refs[-1]
    width = parts[0].shape[1]
    for k in range(MEMBERS):
        out[:, pl.ds(aligned((here_ref[1] ^ k) * width), width)] = parts[k][...]


def after(array, *others):
    return lax.optimization_barrier((array,) + others)[0]


def shards(sizes, tokens, w_query, w_key, value_weight, gate_bias, block_mask, valid_len):
    n_seg, n_z = sizes
    n_groups = n_seg // MEMBERS
    heads_kv = w_key.shape[1] // HEAD_SIZE
    group = w_query.shape[1] // w_key.shape[1]
    rows = w_query.shape[0]
    length, width = tokens.shape[1], tokens.shape[2]
    assert heads_kv == MEMBERS and length == 2 * BLK
    seg = lax.axis_index("seg")
    z = lax.axis_index("fsdp")
    g, m = seg // MEMBERS, seg % MEMBERS
    here = jnp.stack([g, m, z]).astype(jnp.int32)
    bf16, f32 = jnp.bfloat16, jnp.float32
    shape = jax.ShapeDtypeStruct

    def permute(array, to):
        pairs = []
        for gg in range(n_groups):
            for mm in range(MEMBERS):
                for zz in range(n_z):
                    target = to(gg, mm, zz)
                    if target is not None:
                        index = lambda t: (t[0] * MEMBERS + t[1]) * n_z + t[2]
                        pairs.append((index((gg, mm, zz)), index(target)))
        return lax.ppermute(array, AXES, pairs)

    def to_member(array, k):
        return permute(array, lambda gg, mm, zz: (gg, mm ^ k, zz))

    wide = (2 + group) * HEAD_SIZE
    packed = call(
        functools.partial(pack_body, group),
        [shape((rows + META_ROWS, wide), bf16)] * MEMBERS,
        [SMEM] * 3 + [HBM] * 3,
        scratch=[pltpu.VMEM((META_ROWS, wide), bf16), pltpu.SemaphoreType.DMA((4 * MEMBERS,))],
        out_spec=ANY,
        limit=60 << 20,
    )(here, valid_len, block_mask, w_query, w_key, value_weight)
    messages = [packed[0], *[to_member(packed[k], k) for k in (1, 2, 3)]]

    def gathered(piece):
        index = lambda gg, mm, zz: (gg * MEMBERS + mm) * n_z + zz
        everything = lax.all_gather(
            piece,
            AXES,
            axis_index_groups=[
                [index(gg, mm, zz) for gg in range(n_groups) for zz in range(n_z)]
                for mm in range(MEMBERS)
            ],
        )
        columns = piece.shape[1]
        natural = everything.reshape(n_groups, n_z, MEMBERS, rows, columns)
        members = jnp.arange(MEMBERS, dtype=jnp.int32) ^ m
        natural = jnp.take(natural, members, axis=2).transpose(0, 2, 1, 3, 4)
        return list(natural.reshape(-1, MEMBERS * HEAD_SIZE, columns))

    pieces = [
        jnp.concatenate([messages[k][:rows] for k in members], axis=0) for members in ((0, 1), (2, 3))
    ]
    n_pieces = width // (MEMBERS * HEAD_SIZE)
    sums, lasts = [None] * MEMBERS, [None] * MEMBERS

    def project(segs, places, upper, lower, line, first):
        found = call(
            functools.partial(project_body, places, line, n_pieces, first),
            [shape((length, wide), f32)] * 2
            + [shape((length, MEMBERS * HEAD_SIZE), bf16)] * (2 if first else 0),
            [SMEM] + [VMEM] * (2 + 2 * len(places) + (0 if first else 2)),
            flops=2 * 2 * length * len(places) * MEMBERS * HEAD_SIZE * wide,
        )(
            here,
            *[books[s] for s in segs],
            *[part[p] for p in places for part in (upper, lower)],
            *([] if first else [sums[s] for s in segs]),
        )
        for at, s in enumerate(segs):
            sums[s] = found[at]
            if first:
                lasts[s] = found[2 + at]

    cut = 2 * HEAD_SIZE
    if n_groups == 2 and n_z == 4:
        assert rows == HEAD_SIZE
        inside = (z == 1) | (z == 2)
        over = lambda part: permute(part, lambda gg, mm, zz: (gg ^ 1, mm, zz))
        pair = lambda part: permute(part, lambda gg, mm, zz: (gg, mm, zz ^ 1))
        outward = lambda part: permute(
            part, lambda gg, mm, zz: (gg, mm, zz ^ 1) if zz in (1, 2) else None
        )
        inward = lambda part: permute(
            part, lambda gg, mm, zz: (gg, mm, zz ^ 3) if zz in (1, 2) else None
        )
        locked = lambda *parts: lax.optimization_barrier(parts)
        stage1 = lambda piece: (pair(piece), inward(piece), over(piece))
        stage2 = lambda one, inner: (inward(one), outward(inner), over(one))
        stage3 = lambda middle, two: (outward(middle), over(two))

        a, b, own, sibling = locked(*pieces, tokens[0], to_member(tokens[0], 1))
        across = to_member(own, 2)
        a_one, a_inner, a_far0 = locked(*stage1(a))
        b_one, b_inner, b_far0 = locked(*stage1(b))
        a_middle, a_outer, a_far1 = locked(*stage2(a_one, a_inner))
        b_middle, b_outer, b_far1 = locked(*stage2(b_one, b_inner))
        a_two = jnp.where(inside, a_inner, a_outer)
        a_last, a_far2 = stage3(a_middle, a_two)
        b_two = jnp.where(inside, b_inner, b_outer)
        b_last, b_far2 = stage3(b_middle, b_two)
        a_last, a_far2, a_middle = locked(a_last, a_far2, a_middle)
        a_three = jnp.where(inside, a_middle, a_last)
        a_far3 = over(a_three)
        books = [own, sibling]
        upper = [a, a_one, a_two, a_three, a_far0, a_far1, a_far2, a_far3, a_far3]
        lower = [b, b_one, b_two, None, b_far0, b_far1]
        project((0, 1), (0, 1, 4, 5), upper, lower, n_z, True)
        b_last, b_far2, b_middle, a_far3, across, sums[0], sums[1] = locked(
            b_last, b_far2, b_middle, a_far3, across, sums[0], sums[1]
        )
        b_far3 = [
            over(jnp.where(inside, b_middle[:, at], b_last[:, at]))
            for at in (slice(0, cut), slice(cut, None))
        ]
        books += [across, to_member(across, 1)]
        upper[7:] = [a_far3, a_far3]
        lower[3:] = [jnp.where(inside, b_middle, b_last), b_far0, b_far1, b_far2] + b_far3
        project((0, 1), (2, 3, 6), upper, lower, n_z, False)
        project((2, 3), (0, 1, 4, 5), upper, lower, n_z, True)
        project((2, 3), (2, 3, 6), upper, lower, n_z, False)
    else:
        across, sibling = to_member(tokens[0], 2), to_member(tokens[0], 1)
        books = [tokens[0], sibling, across, to_member(across, 1)]
        full = gathered(jnp.concatenate(pieces, axis=0))
        deep = MEMBERS * HEAD_SIZE // 2
        upper, lower = [part[:deep] for part in full], [part[deep:] for part in full]
        upper.append(upper[-1])
        lower[-1:] = [lower[-1][:, :cut], lower[-1][:, cut:]]
        for segs in ((0, 1), (2, 3)):
            project(segs, tuple(range(n_pieces - 1)), upper, lower, 0, True)

    found = call(
        kv_body,
        [shape((length, 2 * HEAD_SIZE), bf16), shape((HEAD_SIZE, 2 * HEAD_SIZE), f32)] * MEMBERS
        + [shape((HEAD_SIZE, 2 * HEAD_SIZE), bf16)],
        [VMEM] * (2 + 3 * MEMBERS),
        flops=2 * MEMBERS * length * MEMBERS * HEAD_SIZE * 2 * HEAD_SIZE,
    )(upper[-2], lower[-2], *sums, *lasts, *messages)
    kvs, deltas, total = found[0:-1:2], found[1:-1:2], found[-1]

    base = None
    for a in range(1, n_groups):
        term = permute(total, lambda gg, mm, zz: (gg ^ a, mm, zz) if gg < gg ^ a else None)
        base = term if base is None else base.astype(f32) + term.astype(f32)

    heads_wide = group * HEAD_SIZE

    def local(segs, piece):
        found = call(
            functools.partial(local_body, segs, group),
            [shape((length, heads_wide), bf16), shape((length, heads_wide), f32)] * len(segs),
            [VMEM] * (2 + 4 * len(segs)),
            flops=4 * len(segs) * length * length * heads_wide,
        )(piece, lower[-1], *[one[s] for one in (kvs, messages, sums, lasts) for s in segs])
        return found[0::2], found[1::2]

    def mix(segs, base, queries, locals_):
        return call(
            functools.partial(mix_body, segs, group),
            [shape((length, heads_wide), bf16)] * len(segs),
            [SMEM] * 2 + [VMEM] * (1 + MEMBERS + 3 * len(segs)),
            flops=0,
        )(here, gate_bias, base, *deltas, *[messages[s] for s in segs], *queries, *locals_)

    queries, locals_ = local((2, 3), upper[-1])
    near = local((1, 0), after(upper[-1], *queries))
    base = after(base, *near[0])
    (two,) = mix((2,), base, queries[:1], locals_[:1])
    (three,) = mix((3,), after(base, two), queries[1:], locals_[1:])
    near = mix((1, 0), after(base, three), *near)
    sent = [near[1], to_member(near[0], 1), to_member(two, 2), to_member(three, 3)]
    (output,) = call(
        assemble_body,
        [shape((length, w_query.shape[1]), bf16)],
        [SMEM] + [VMEM] * MEMBERS,
    )(here, *sent)
    return output[None]


def solution(mesh):
    in_specs = (
        P("fsdp", "seg", None),
        P(("seg", "fsdp"), None),
        P(("seg", "fsdp"), None),
        P(("seg", "fsdp"), None),
        P(),
        P("fsdp", "seg", None, None),
        P("fsdp", "seg"),
    )
    out_specs = P("fsdp", "seg", None)
    body = functools.partial(shards, (mesh.shape["seg"], mesh.shape["fsdp"]))
    return jax.shard_map(body, mesh=mesh, in_specs=in_specs, out_specs=out_specs, check_vma=False)
```

```python
import functools

import jax
import jax.numpy as jnp
from jax import lax
from jax.experimental import pallas as pl
from jax.experimental.pallas import tpu as pltpu
from jax.sharding import PartitionSpec as P

HEAD_SIZE = 128
BLK = 128
MEMBERS = 4
META_ROWS = 16
HALF = META_ROWS // 2
AXES = ("seg", "fsdp")

VMEM = pl.BlockSpec(memory_space=pltpu.VMEM)
SMEM = pl.BlockSpec(memory_space=pltpu.SMEM)
ANY = pl.BlockSpec(memory_space=pl.ANY)
HBM = pl.BlockSpec(memory_space=pltpu.HBM)


def call(body, outs, in_specs, flops=0, scratch=(), out_spec=VMEM, limit=16 << 20):
    return pl.pallas_call(
        body,
        out_shape=outs,
        in_specs=in_specs,
        out_specs=[out_spec] * len(outs),
        scratch_shapes=list(scratch),
        compiler_params=pltpu.CompilerParams(vmem_limit_bytes=limit),
        cost_estimate=pl.CostEstimate(flops=flops, bytes_accessed=4 << 20, transcendentals=0),
    )


def aligned(offset):
    return pl.multiple_of(offset, HEAD_SIZE)


def pack_body(group, here_ref, valid_ref, mask_ref, wq_ref, wk_ref, wv_ref, *outs):
    rows, wide = wk_ref.shape[0], group * HEAD_SIZE
    row = lax.broadcasted_iota(jnp.int32, (META_ROWS, outs[0].shape[1]), 0)
    facts = jnp.where(row < HALF, valid_ref[0, 0], mask_ref[0, 0, 1, 0])
    facts = facts.astype(jnp.float32).astype(jnp.bfloat16)
    for k in range(MEMBERS):
        head, out = here_ref[1] ^ k, outs[k]
        at = aligned(head * HEAD_SIZE)
        out[:rows, :HEAD_SIZE] = wk_ref[:, pl.ds(at, HEAD_SIZE)]
        out[:rows, HEAD_SIZE : 2 * HEAD_SIZE] = wv_ref[:, pl.ds(at, HEAD_SIZE)]
        out[:rows, 2 * HEAD_SIZE :] = wq_ref[:, pl.ds(aligned(head * wide), wide)]
        out[rows:, :] = facts


def spans_of(here_ref, piece, line):
    if not line:
        return [(piece * MEMBERS * HEAD_SIZE, MEMBERS * HEAD_SIZE)]
    g, m, z = here_ref[0] ^ (piece // line), here_ref[1], here_ref[2]
    inside = (z == 1) | (z == 2)
    step = piece % line
    if step < 2:
        z = z ^ step
    else:
        z = jnp.where(inside, z ^ (5 - step), z ^ step)
    return [
        (aligned(((g * MEMBERS + (m ^ k)) * line + z) * HEAD_SIZE), HEAD_SIZE) for k in range(MEMBERS)
    ]


def facts_of(message_ref):
    rows = message_ref.shape[0] - META_ROWS
    facts = message_ref[rows:, : 2 * HEAD_SIZE].astype(jnp.float32)
    return facts[0:1, :], facts[HALF : HALF + 1, :]


def iota(shape, dimension):
    return lax.broadcasted_iota(jnp.int32, shape, dimension).astype(jnp.float32)


def project_body(places, line, n_pieces, first, here_ref, *refs):
    tokens, pieces = refs[:2], refs[2 : 2 + 2 * len(places)]
    rest = refs[2 + 2 * len(places) : -2]
    columns_ref, sems = refs[-2:]
    length = tokens[0].shape[0]
    deep = MEMBERS * HEAD_SIZE
    outs = rest if first else rest[2:]
    copies = []

    def bring(n, piece, target, rows, at):
        for start, width in spans_of(here_ref, piece, line):
            one = pltpu.make_async_copy(
                tokens[n].at[:, pl.ds(start, width)],
                target.at[rows, pl.ds(at, width)],
                sems.at[len(copies)],
            )
            one.start()
            copies.append(one)
            at += width

    marks = []
    for p, place in enumerate(places):
        for n in range(2):
            bring(n, place, columns_ref, pl.ds(n * length, length), p * deep)
        marks.append(len(copies))
    if first:
        for n in range(2):
            bring(n, n_pieces - 1, outs[2 + n], pl.ds(0, length), 0)
    total = None if first else jnp.concatenate([rest[0][...], rest[1][...]], axis=0)
    done = 0
    for p in range(len(places)):
        for one in copies[done : marks[p]]:
            one.wait()
        done = marks[p]
        for half in range(2):
            at = p * deep + half * deep // 2
            term = jnp.dot(
                columns_ref[:, at : at + deep // 2],
                pieces[2 * p + half][...],
                preferred_element_type=jnp.float32,
            )
            total = term if total is None else total + term
    for n in range(2):
        outs[n][...] = total[n * length : (n + 1) * length]
    for one in copies[done:]:
        one.wait()


def sigma_plus(v):
    return jnp.where(v > 0, v + 1.0, jnp.exp(jnp.minimum(v, 0.0)))


def split(values):
    high = values.astype(jnp.bfloat16)
    return high, (values - high.astype(jnp.float32)).astype(jnp.bfloat16)


def last_piece(columns_ref, upper_ref, lower_ref, start):
    half, width = upper_ref.shape[0], lower_ref.shape[1]
    term = jnp.dot(
        columns_ref[:, :half], upper_ref[:, start : start + width], preferred_element_type=jnp.float32
    )
    return term + jnp.dot(columns_ref[:, half:], lower_ref[...], preferred_element_type=jnp.float32)


def kv_body(upper_ref, lower_ref, *refs):
    sums, lasts, messages = refs[:MEMBERS], refs[MEMBERS : 2 * MEMBERS], refs[2 * MEMBERS : 3 * MEMBERS]
    outs = refs[3 * MEMBERS :]
    whole = None
    for seg in range(MEMBERS):
        at = 2 * HEAD_SIZE
        total = sums[seg][:, :at] + last_piece(lasts[seg], upper_ref, lower_ref, 0)
        kv = total.astype(jnp.bfloat16)
        outs[2 * seg][...] = kv
        length = kv.shape[0]
        valid, _ = facts_of(messages[seg])
        keys = kv[:, :HEAD_SIZE].astype(jnp.float32)
        live = iota((length, HEAD_SIZE), 0) < valid[:, :HEAD_SIZE]
        sig = jnp.where(live, sigma_plus(keys), 0.0)
        wide = jnp.concatenate(
            [kv[:, HEAD_SIZE:], jnp.ones((length, HEAD_SIZE), jnp.bfloat16)], axis=1
        )
        high, low = split(sig)
        over = (((0,), (0,)), ((), ()))
        delta = lax.dot_general(high, wide, over, preferred_element_type=jnp.float32)
        delta += lax.dot_general(low, wide, over, preferred_element_type=jnp.float32)
        outs[2 * seg + 1][...] = delta
        whole = delta if whole is None else whole + delta
    outs[-1][...] = whole.astype(jnp.bfloat16)


def attend_body(
    segs, parts, heads, here_ref, gate_ref, base_ref, upper_ref, *refs
):
    n = len(segs)
    lowers, refs = refs[: len(parts)], refs[len(parts) :]
    deltas, refs = refs[:MEMBERS], refs[MEMBERS:]
    kvs, messages, sums, lasts, outs = [refs[k * n : (k + 1) * n] for k in range(5)]
    all_heads = upper_ref.shape[1] // HEAD_SIZE - 2
    me = here_ref[1]
    across = len(parts) * heads * HEAD_SIZE
    first = 2 * HEAD_SIZE + parts[0] * heads * HEAD_SIZE
    heads = len(parts) * heads
    first_head = first // HEAD_SIZE - 2
    for at, seg in enumerate(segs):
        terms = []
        for p, lower_ref in enumerate(lowers):
            terms.append(last_piece(lasts[at], upper_ref, lower_ref, first + p * lower_ref.shape[1]))
        queries = sums[at][:, first : first + across] + jnp.concatenate(terms, axis=1)
        queries = queries.astype(jnp.bfloat16)

        memory = base_ref[...].astype(jnp.float32)
        for other in range(MEMBERS):
            if other != seg:
                earlier = jnp.where((me ^ other) < (me ^ seg), 1.0, 0.0)
                memory = memory + earlier * deltas[other][...]
        mem_high, mem_low = split(memory)
        blocks = queries.shape[0] // BLK
        valid, seen = facts_of(messages[at])
        for block in range(blocks):
            span = slice(block * BLK, (block + 1) * BLK)
            stacked = jnp.concatenate(
                [queries[span, h * HEAD_SIZE : (h + 1) * HEAD_SIZE] for h in range(heads)], axis=0
            )
            width = (block + 1) * BLK
            keys = kvs[at][0:width, :HEAD_SIZE]
            values = kvs[at][0:width, HEAD_SIZE:]
            scores = lax.dot_general(
                stacked, keys, (((1,), (1,)), ((), ())), preferred_element_type=jnp.float32
            ) * HEAD_SIZE ** (-0.5)
            i, j = iota((BLK, width), 0) + block * BLK, iota((BLK, width), 1)
            limit = valid[:, :width]
            if block:
                limit = jnp.where((j[0:1] >= block * BLK) | (seen[:, :width] > 0), limit, 0.0)
            allowed = (j <= i) & (j < limit)
            masked = jnp.concatenate(
                [
                    jnp.where(allowed, scores[h * BLK : (h + 1) * BLK], -1e30)
                    for h in range(heads)
                ],
                axis=0,
            )
            top = jnp.max(masked, axis=-1, keepdims=True)
            expo = jnp.exp(masked - top)
            total = jnp.maximum(jnp.sum(expo, axis=-1, keepdims=True), 1.0)
            weights = (expo / total).astype(jnp.bfloat16)
            local = jnp.dot(weights, values, preferred_element_type=jnp.float32)

            high, low = split(sigma_plus(stacked.astype(jnp.float32)))
            numer = jnp.dot(high, mem_high, preferred_element_type=jnp.float32)
            numer += jnp.dot(high, mem_low, preferred_element_type=jnp.float32)
            numer += jnp.dot(low, mem_high, preferred_element_type=jnp.float32)
            retrieved = numer[:, :HEAD_SIZE] / (numer[:, HEAD_SIZE:] + 1.0)
            live = iota((BLK, HEAD_SIZE), 0) + block * BLK < valid[:, :HEAD_SIZE]
            for h in range(heads):
                part = slice(h * BLK, (h + 1) * BLK)
                logit = jnp.full((1, HEAD_SIZE), gate_ref[me * all_heads + first_head + h], jnp.float32)
                gate = 1.0 / (1.0 + jnp.exp(-logit))
                mixed = gate * retrieved[part] + (1.0 - gate) * local[part]
                outs[at][span, h * HEAD_SIZE : (h + 1) * HEAD_SIZE] = jnp.where(
                    live, mixed, 0.0
                ).astype(jnp.bfloat16)


def assemble_body(counts, here_ref, *refs):
    parts, out = list(refs[:-1]), refs[-1]
    width = out.shape[1] // MEMBERS
    for k, count in enumerate(counts):
        for c in range(count):
            at = (here_ref[1] ^ k) * width + c * (width // count)
            out[:, pl.ds(aligned(at), width // count)] = parts.pop(0)[...]


def after(array, *others):
    return lax.optimization_barrier((array,) + others)[0]


def shards(sizes, tokens, w_query, w_key, value_weight, gate_bias, block_mask, valid_len):
    n_seg, n_z = sizes
    n_groups = n_seg // MEMBERS
    heads_kv = w_key.shape[1] // HEAD_SIZE
    group = w_query.shape[1] // w_key.shape[1]
    rows = w_query.shape[0]
    length, width = tokens.shape[1], tokens.shape[2]
    assert heads_kv == MEMBERS and group == 4 and length == 2 * BLK
    seg = lax.axis_index("seg")
    z = lax.axis_index("fsdp")
    g, m = seg // MEMBERS, seg % MEMBERS
    here = jnp.stack([g, m, z]).astype(jnp.int32)
    bf16, f32 = jnp.bfloat16, jnp.float32
    shape = jax.ShapeDtypeStruct

    def permute(array, to):
        pairs = []
        for gg in range(n_groups):
            for mm in range(MEMBERS):
                for zz in range(n_z):
                    target = to(gg, mm, zz)
                    if target is not None:
                        index = lambda t: (t[0] * MEMBERS + t[1]) * n_z + t[2]
                        pairs.append((index((gg, mm, zz)), index(target)))
        return lax.ppermute(array, AXES, pairs)

    def to_member(array, k):
        return permute(array, lambda gg, mm, zz: (gg, mm ^ k, zz))

    wide = (2 + group) * HEAD_SIZE
    packed = call(
        functools.partial(pack_body, group),
        [shape((rows + META_ROWS, wide), bf16)] * MEMBERS,
        [SMEM] * 3 + [VMEM] * 3,
    )(here, valid_len, block_mask, w_query, w_key, value_weight)
    messages = [packed[0], *[to_member(packed[k], k) for k in (1, 2, 3)]]

    def gathered(piece):
        index = lambda gg, mm, zz: (gg * MEMBERS + mm) * n_z + zz
        everything = lax.all_gather(
            piece,
            AXES,
            axis_index_groups=[
                [index(gg, mm, zz) for gg in range(n_groups) for zz in range(n_z)]
                for mm in range(MEMBERS)
            ],
        )
        columns = piece.shape[1]
        natural = everything.reshape(n_groups, n_z, MEMBERS, rows, columns)
        members = jnp.arange(MEMBERS, dtype=jnp.int32) ^ m
        natural = jnp.take(natural, members, axis=2).transpose(0, 2, 1, 3, 4)
        return list(natural.reshape(-1, MEMBERS * HEAD_SIZE, columns))

    pieces = [
        jnp.concatenate([messages[k][:rows] for k in members], axis=0) for members in ((0, 1), (2, 3))
    ]
    n_pieces = width // (MEMBERS * HEAD_SIZE)
    sums, lasts = [None] * MEMBERS, [None] * MEMBERS

    def project(segs, places, upper, lower, line, first):
        found = call(
            functools.partial(project_body, places, line, n_pieces, first),
            [shape((length, wide), f32)] * 2
            + [shape((length, MEMBERS * HEAD_SIZE), bf16)] * (2 if first else 0),
            [SMEM] + [ANY] * 2 + [VMEM] * (2 * len(places) + (0 if first else 2)),
            flops=2 * 2 * length * len(places) * MEMBERS * HEAD_SIZE * wide,
            scratch=[
                pltpu.VMEM((2 * length, len(places) * MEMBERS * HEAD_SIZE), bf16),
                pltpu.SemaphoreType.DMA((2 * MEMBERS * (len(places) + 1),)),
            ],
        )(
            here,
            *[books[s] for s in segs],
            *[part[p] for p in places for part in (upper, lower)],
            *([] if first else [sums[s] for s in segs]),
        )
        for at, s in enumerate(segs):
            sums[s] = found[at]
            if first:
                lasts[s] = found[2 + at]

    if n_groups == 2 and n_z == 4:
        assert rows == HEAD_SIZE
        inside = (z == 1) | (z == 2)
        over = lambda part: permute(part, lambda gg, mm, zz: (gg ^ 1, mm, zz))
        pair = lambda part: permute(part, lambda gg, mm, zz: (gg, mm, zz ^ 1))
        outward = lambda part: permute(
            part, lambda gg, mm, zz: (gg, mm, zz ^ 1) if zz in (1, 2) else None
        )
        inward = lambda part: permute(
            part, lambda gg, mm, zz: (gg, mm, zz ^ 3) if zz in (1, 2) else None
        )
        locked = lambda *parts: lax.optimization_barrier(parts)
        stage1 = lambda piece: (pair(piece), inward(piece), over(piece))
        stage2 = lambda one, inner: (inward(one), outward(inner), over(one))
        stage3 = lambda middle, two: (outward(middle), over(two))

        a, b, own, sibling = locked(*pieces, tokens[0], to_member(tokens[0], 1))
        across = to_member(own, 2)
        a_one, a_inner, a_far0 = locked(*stage1(a))
        b_one, b_inner, b_far0 = locked(*stage1(b))
        a_middle, a_outer, a_far1 = locked(*stage2(a_one, a_inner))
        b_middle, b_outer, b_far1 = locked(*stage2(b_one, b_inner))
        a_two = jnp.where(inside, a_inner, a_outer)
        a_last, a_far2 = stage3(a_middle, a_two)
        b_two = jnp.where(inside, b_inner, b_outer)
        b_last, b_far2 = stage3(b_middle, b_two)
        a_last, a_far2, a_middle, across, b_middle, b_two, b_far1 = locked(
            a_last, a_far2, a_middle, across, b_middle, b_two, b_far1
        )
        a_three = jnp.where(inside, a_middle, a_last)
        a_far3 = over(a_three)
        books = [own, sibling, across, to_member(across, 1)]
        upper = [a, a_one, a_two, a_three, a_far0, a_far1, a_far2, a_far3]
        lower = [b, b_one, b_two, None, b_far0, b_far1]
        project((0, 1), (0, 1, 4, 5), upper, lower, n_z, True)
        project((2, 3), (0, 1, 4, 5), upper, lower, n_z, True)
        b_last, b_far2, b_middle, a_far3, *sums = locked(b_last, b_far2, b_middle, a_far3, *sums)
        b_three = jnp.where(inside, b_middle, b_last)
        upper[7] = a_far3
        lower[3:] = [b_three, b_far0, b_far1, b_far2]
        finish = lambda at, *others: over(after(b_three[:, at], *others))
        project((0, 1), (2, 3, 6), upper, lower, n_z, False)
        project((2, 3), (2, 3, 6), upper, lower, n_z, False)
    else:
        across, sibling = to_member(tokens[0], 2), to_member(tokens[0], 1)
        books = [tokens[0], sibling, across, to_member(across, 1)]
        full = gathered(jnp.concatenate(pieces, axis=0))
        deep = MEMBERS * HEAD_SIZE // 2
        upper, lower = [part[:deep] for part in full], [part[deep:] for part in full]
        finish = lambda at, *others: lower[n_pieces - 1][:, at]
        for segs in ((0, 1), (2, 3)):
            project(segs, tuple(range(n_pieces - 1)), upper, lower, 0, True)

    halves = [slice(k * HEAD_SIZE, (k + 2) * HEAD_SIZE) for k in (0, 2, 4)]
    lower_kv, lower_q0 = finish(halves[0]), finish(halves[1])
    found = call(
        kv_body,
        [shape((length, 2 * HEAD_SIZE), bf16), shape((HEAD_SIZE, 2 * HEAD_SIZE), f32)] * MEMBERS
        + [shape((HEAD_SIZE, 2 * HEAD_SIZE), bf16)],
        [VMEM] * (2 + 3 * MEMBERS),
        flops=2 * MEMBERS * length * MEMBERS * HEAD_SIZE * 2 * HEAD_SIZE,
    )(upper[-1], lower_kv, *sums, *lasts, *messages)
    kvs, deltas, total = found[0:-1:2], found[1:-1:2], found[-1]

    base = None
    for a in range(1, n_groups):
        term = permute(total, lambda gg, mm, zz: (gg ^ a, mm, zz) if gg < gg ^ a else None)
        base = term if base is None else base.astype(f32) + term.astype(f32)

    lower_q1 = finish(halves[2], total)

    def attend(segs, parts, base, *lowers):
        across = len(parts) * 2 * HEAD_SIZE
        return call(
            functools.partial(attend_body, segs, parts, 2),
            [shape((length, across), bf16)] * len(segs),
            [SMEM] * 2 + [VMEM] * (2 + len(lowers) + MEMBERS + 4 * len(segs)),
            flops=4 * len(segs) * length * length * across,
        )(
            here, gate_bias, base, upper[-1], *lowers, *deltas,
            *[one[s] for one in (kvs, messages, sums, lasts) for s in segs],
        )

    two0, three0 = attend((2, 3), (0,), base, lower_q0)
    two1, three1 = attend((2, 3), (1,), after(base, two0, three0), lower_q1)
    one0, mine0 = attend((1, 0), (0,), after(base, two1, three1), lower_q0)
    one1, mine1 = attend((1, 0), (1,), after(base, one0), lower_q1)
    sent = [mine0, mine1]
    for k, parts in ((1, (one0, one1)), (2, (two0, two1)), (3, (three0, three1))):
        sent += [to_member(part, k) for part in parts]
    (output,) = call(
        functools.partial(assemble_body, (2,) * MEMBERS),
        [shape((length, w_query.shape[1]), bf16)],
        [SMEM] + [VMEM] * len(sent),
    )(here, *sent)
    return output[None]


def solution(mesh):
    in_specs = (
        P("fsdp", "seg", None),
        P(("seg", "fsdp"), None),
        P(("seg", "fsdp"), None),
        P(("seg", "fsdp"), None),
        P(),
        P("fsdp", "seg", None, None),
        P("fsdp", "seg"),
    )
    out_specs = P("fsdp", "seg", None)
    body = functools.partial(shards, (mesh.shape["seg"], mesh.shape["fsdp"]))
    return jax.shard_map(body, mesh=mesh, in_specs=in_specs, out_specs=out_specs, check_vma=False)
```

```python
import functools

import jax
import jax.numpy as jnp
from jax import lax
from jax.experimental import pallas as pl
from jax.experimental.pallas import tpu as pltpu
from jax.sharding import PartitionSpec as P

HEAD_SIZE = 128
BLK = 128
MEMBERS = 4
META_ROWS = 16
HALF = META_ROWS // 2
AXES = ("seg", "fsdp")

VMEM = pl.BlockSpec(memory_space=pltpu.VMEM)
SMEM = pl.BlockSpec(memory_space=pltpu.SMEM)
ANY = pl.BlockSpec(memory_space=pl.ANY)
HBM = pl.BlockSpec(memory_space=pltpu.HBM)


def call(body, outs, in_specs, flops=0, scratch=(), out_spec=VMEM, limit=16 << 20):
    return pl.pallas_call(
        body,
        out_shape=outs,
        in_specs=in_specs,
        out_specs=[out_spec] * len(outs),
        scratch_shapes=list(scratch),
        compiler_params=pltpu.CompilerParams(vmem_limit_bytes=limit),
        cost_estimate=pl.CostEstimate(flops=flops, bytes_accessed=4 << 20, transcendentals=0),
    )


def aligned(offset):
    return pl.multiple_of(offset, HEAD_SIZE)


def pack_body(group, here_ref, valid_ref, mask_ref, wq_ref, wk_ref, wv_ref, *outs):
    rows, wide = wk_ref.shape[0], group * HEAD_SIZE
    row = lax.broadcasted_iota(jnp.int32, (META_ROWS, outs[0].shape[1]), 0)
    facts = jnp.where(row < HALF, valid_ref[0, 0], mask_ref[0, 0, 1, 0])
    facts = facts.astype(jnp.float32).astype(jnp.bfloat16)
    for k in range(MEMBERS):
        head, out = here_ref[1] ^ k, outs[k]
        at = aligned(head * HEAD_SIZE)
        out[:rows, :HEAD_SIZE] = wk_ref[:, pl.ds(at, HEAD_SIZE)]
        out[:rows, HEAD_SIZE : 2 * HEAD_SIZE] = wv_ref[:, pl.ds(at, HEAD_SIZE)]
        out[:rows, 2 * HEAD_SIZE :] = wq_ref[:, pl.ds(aligned(head * wide), wide)]
        out[rows:, :] = facts


def columns_of(tokens_ref, here_ref, piece, half, line):
    deep = MEMBERS * HEAD_SIZE // 2
    if not line:
        return tokens_ref[:, pl.ds((2 * piece + half) * deep, deep)]
    g, m, z = here_ref[0] ^ (piece // line), here_ref[1], here_ref[2]
    inside = (z == 1) | (z == 2)
    step = piece % line
    if step < 2:
        z = z ^ step
    else:
        z = jnp.where(inside, z ^ (5 - step), z ^ step)
    parts = [
        tokens_ref[:, pl.ds(aligned(((g * MEMBERS + (m ^ k)) * line + z) * HEAD_SIZE), HEAD_SIZE)]
        for k in (2 * half, 2 * half + 1)
    ]
    return jnp.concatenate(parts, axis=1)


def facts_of(message_ref):
    rows = message_ref.shape[0] - META_ROWS
    facts = message_ref[rows:, : 2 * HEAD_SIZE].astype(jnp.float32)
    return facts[0:1, :], facts[HALF : HALF + 1, :]


def iota(shape, dimension):
    return lax.broadcasted_iota(jnp.int32, shape, dimension).astype(jnp.float32)


def project_body(early, late, line, here_ref, *refs):
    tokens, pieces, outs = refs[:2], refs[2 : 2 + len(early)], refs[2 + len(early) :]
    length = tokens[0].shape[0]
    total = None
    for place, piece in zip(early, pieces):
        columns = jnp.concatenate([columns_of(one, here_ref, *place, line) for one in tokens], axis=0)
        term = jnp.dot(columns, piece[...], preferred_element_type=jnp.float32)
        total = term if total is None else total + term
    for n in range(2):
        outs[n][...] = total[n * length : (n + 1) * length]
        for k, place in enumerate(late):
            columns = columns_of(tokens[n], here_ref, *place, line)
            deep = columns.shape[1]
            outs[2 + n][:, k * deep : (k + 1) * deep] = columns


def sigma_plus(v):
    return jnp.where(v > 0, v + 1.0, jnp.exp(jnp.minimum(v, 0.0)))


def split(values):
    high = values.astype(jnp.bfloat16)
    return high, (values - high.astype(jnp.float32)).astype(jnp.bfloat16)


def late_rows(pieces, start):
    width = pieces[-1].shape[1]
    rows = [piece[:, start : start + width] for piece in pieces[:-1]]
    return jnp.concatenate(rows + [pieces[-1][...]], axis=0)


def kv_body(n_late, *refs):
    pieces, refs = refs[:n_late], refs[n_late:]
    sums, lates, messages = refs[:MEMBERS], refs[MEMBERS : 2 * MEMBERS], refs[2 * MEMBERS : 3 * MEMBERS]
    outs = refs[3 * MEMBERS :]
    rows = late_rows(pieces, 0)
    kvs = []
    for seg in range(MEMBERS):
        total = sums[seg][:, : 2 * HEAD_SIZE]
        total += jnp.dot(lates[seg][...], rows, preferred_element_type=jnp.float32)
        kvs.append(total.astype(jnp.bfloat16))
        outs[2 * seg][...] = kvs[seg]
    whole = None
    for seg, kv in enumerate(kvs):
        length = kv.shape[0]
        valid, _ = facts_of(messages[seg])
        keys = kv[:, :HEAD_SIZE].astype(jnp.float32)
        live = iota((length, HEAD_SIZE), 0) < valid[:, :HEAD_SIZE]
        sig = jnp.where(live, sigma_plus(keys), 0.0)
        wide = jnp.concatenate(
            [kv[:, HEAD_SIZE:], jnp.ones((length, HEAD_SIZE), jnp.bfloat16)], axis=1
        )
        high, low = split(sig)
        over = (((0,), (0,)), ((), ()))
        delta = lax.dot_general(high, wide, over, preferred_element_type=jnp.float32)
        delta += lax.dot_general(low, wide, over, preferred_element_type=jnp.float32)
        outs[2 * seg + 1][...] = delta
        whole = delta if whole is None else whole + delta
    outs[-1][...] = whole.astype(jnp.bfloat16)


def local_body(n, n_late, start, heads, *refs):
    pieces, refs = refs[:n_late], refs[n_late:]
    kvs, messages, sums, lates, outs = [refs[k * n : (k + 1) * n] for k in range(4)] + [refs[4 * n :]]
    rows = late_rows(pieces, start)
    columns = slice(start, start + heads * HEAD_SIZE)
    queries = []
    for at in range(n):
        total = sums[at][:, columns] + jnp.dot(
            lates[at][...], rows, preferred_element_type=jnp.float32
        )
        queries.append(total.astype(jnp.bfloat16))
        outs[2 * at][...] = queries[at]
    work = [(at, block) for at in range(n) for block in range(queries[0].shape[0] // BLK)]
    span = lambda block: slice(block * BLK, (block + 1) * BLK)
    scores = []
    for at, block in work:
        stacked = jnp.concatenate(
            [queries[at][span(block), h * HEAD_SIZE : (h + 1) * HEAD_SIZE] for h in range(heads)], axis=0
        )
        keys = kvs[at][0 : (block + 1) * BLK, :HEAD_SIZE]
        scores.append(
            lax.dot_general(
                stacked, keys, (((1,), (1,)), ((), ())), preferred_element_type=jnp.float32
            )
        )
    weights = []
    for (at, block), score in zip(work, scores):
        width = (block + 1) * BLK
        valid, seen = facts_of(messages[at])
        i, j = iota((BLK, width), 0) + block * BLK, iota((BLK, width), 1)
        limit = valid[:, :width]
        if block:
            limit = jnp.where((j[0:1] >= block * BLK) | (seen[:, :width] > 0), limit, 0.0)
        allowed = (j <= i) & (j < limit)
        masked = jnp.concatenate(
            [jnp.where(allowed, score[span(h)] * HEAD_SIZE ** (-0.5), -1e30) for h in range(heads)],
            axis=0,
        )
        top = jnp.max(masked, axis=-1, keepdims=True)
        expo = jnp.exp(masked - top)
        total = jnp.maximum(jnp.sum(expo, axis=-1, keepdims=True), 1.0)
        weights.append((expo * (1.0 / total)).astype(jnp.bfloat16))
    for (at, block), weight in zip(work, weights):
        values = kvs[at][0 : (block + 1) * BLK, HEAD_SIZE:]
        local = jnp.dot(weight, values, preferred_element_type=jnp.float32)
        for h in range(heads):
            outs[2 * at + 1][span(block), h * HEAD_SIZE : (h + 1) * HEAD_SIZE] = local[span(h)]


def mix_body(segs, parts, group, here_ref, gate_ref, base_ref, *refs):
    deltas, messages, refs = refs[:MEMBERS], refs[MEMBERS : MEMBERS + len(segs)], refs[MEMBERS + len(segs) :]
    n = len(segs) * len(parts)
    queries, locals_, outs = refs[:n], refs[n : 2 * n], refs[2 * n :]
    me = here_ref[1]
    heads = queries[0].shape[1] // HEAD_SIZE
    length = queries[0].shape[0]
    work = [(at, p, h) for at in range(len(segs)) for p in range(len(parts)) for h in range(heads)]
    memories = []
    for seg in segs:
        memory = base_ref[...].astype(jnp.float32)
        for other in range(MEMBERS):
            if other != seg:
                earlier = jnp.where((me ^ other) < (me ^ seg), 1.0, 0.0)
                memory = memory + earlier * deltas[other][...]
        memories.append(split(memory))
    columns = lambda h: slice(h * HEAD_SIZE, (h + 1) * HEAD_SIZE)
    numers = []
    for at, p, h in work:
        mem_high, mem_low = memories[at]
        high, low = split(sigma_plus(queries[at * len(parts) + p][:, columns(h)].astype(jnp.float32)))
        numer = jnp.dot(high, mem_high, preferred_element_type=jnp.float32)
        numer += jnp.dot(high, mem_low, preferred_element_type=jnp.float32)
        numer += jnp.dot(low, mem_high, preferred_element_type=jnp.float32)
        numers.append(numer)
    for (at, p, h), numer in zip(work, numers):
        valid, _ = facts_of(messages[at])
        live = iota((length, HEAD_SIZE), 0) < valid[:, :HEAD_SIZE]
        retrieved = numer[:, :HEAD_SIZE] / (numer[:, HEAD_SIZE:] + 1.0)
        logit = jnp.full((1, HEAD_SIZE), gate_ref[me * group + parts[p] * heads + h], jnp.float32)
        gate = 1.0 / (1.0 + jnp.exp(-logit))
        mixed = gate * retrieved + (1.0 - gate) * locals_[at * len(parts) + p][:, columns(h)]
        outs[at * len(parts) + p][:, columns(h)] = jnp.where(live, mixed, 0.0).astype(jnp.bfloat16)


def assemble_body(counts, here_ref, *refs):
    parts, out = list(refs[:-1]), refs[-1]
    width = out.shape[1] // MEMBERS
    for k, count in enumerate(counts):
        for c in range(count):
            at = (here_ref[1] ^ k) * width + c * (width // count)
            out[:, pl.ds(aligned(at), width // count)] = parts.pop(0)[...]


def after(array, *others):
    return lax.optimization_barrier((array,) + others)[0]


def shards(sizes, tokens, w_query, w_key, value_weight, gate_bias, block_mask, valid_len):
    n_seg, n_z = sizes
    n_groups = n_seg // MEMBERS
    heads_kv = w_key.shape[1] // HEAD_SIZE
    group = w_query.shape[1] // w_key.shape[1]
    rows = w_query.shape[0]
    length, width = tokens.shape[1], tokens.shape[2]
    assert heads_kv == MEMBERS and group == 4 and length == 2 * BLK
    seg = lax.axis_index("seg")
    z = lax.axis_index("fsdp")
    g, m = seg // MEMBERS, seg % MEMBERS
    here = jnp.stack([g, m, z]).astype(jnp.int32)
    bf16, f32 = jnp.bfloat16, jnp.float32
    shape = jax.ShapeDtypeStruct

    def permute(array, to):
        pairs = []
        for gg in range(n_groups):
            for mm in range(MEMBERS):
                for zz in range(n_z):
                    target = to(gg, mm, zz)
                    if target is not None:
                        index = lambda t: (t[0] * MEMBERS + t[1]) * n_z + t[2]
                        pairs.append((index((gg, mm, zz)), index(target)))
        return lax.ppermute(array, AXES, pairs)

    def to_member(array, k):
        return permute(array, lambda gg, mm, zz: (gg, mm ^ k, zz))

    wide = (2 + group) * HEAD_SIZE
    packed = call(
        functools.partial(pack_body, group),
        [shape((rows + META_ROWS, wide), bf16)] * MEMBERS,
        [SMEM] * 3 + [VMEM] * 3,
    )(here, valid_len, block_mask, w_query, w_key, value_weight)
    messages = [packed[0], *[to_member(packed[k], k) for k in (1, 2, 3)]]

    def gathered(piece):
        index = lambda gg, mm, zz: (gg * MEMBERS + mm) * n_z + zz
        everything = lax.all_gather(
            piece,
            AXES,
            axis_index_groups=[
                [index(gg, mm, zz) for gg in range(n_groups) for zz in range(n_z)]
                for mm in range(MEMBERS)
            ],
        )
        columns = piece.shape[1]
        natural = everything.reshape(n_groups, n_z, MEMBERS, rows, columns)
        members = jnp.arange(MEMBERS, dtype=jnp.int32) ^ m
        natural = jnp.take(natural, members, axis=2).transpose(0, 2, 1, 3, 4)
        return list(natural.reshape(-1, MEMBERS * HEAD_SIZE, columns))

    pieces = [
        jnp.concatenate([messages[k][:rows] for k in members], axis=0) for members in ((0, 1), (2, 3))
    ]
    n_pieces = width // (MEMBERS * HEAD_SIZE)
    sums, lates = [None] * MEMBERS, [None] * MEMBERS

    def project(segs, early, late, halves, line):
        deep = MEMBERS * HEAD_SIZE // 2
        found = call(
            functools.partial(project_body, early, late, line),
            [shape((length, wide), f32)] * 2 + [shape((length, len(late) * deep), bf16)] * 2,
            [SMEM] + [VMEM] * (2 + len(early)),
            flops=2 * 2 * length * len(early) * deep * wide,
        )(here, *[books[s] for s in segs], *[halves[half][piece] for piece, half in early])
        for at, s in enumerate(segs):
            sums[s], lates[s] = found[at], found[2 + at]

    if n_groups == 2 and n_z == 4:
        assert rows == HEAD_SIZE
        inside = (z == 1) | (z == 2)
        over = lambda part: permute(part, lambda gg, mm, zz: (gg ^ 1, mm, zz))
        pair = lambda part: permute(part, lambda gg, mm, zz: (gg, mm, zz ^ 1))
        outward = lambda part: permute(
            part, lambda gg, mm, zz: (gg, mm, zz ^ 1) if zz in (1, 2) else None
        )
        inward = lambda part: permute(
            part, lambda gg, mm, zz: (gg, mm, zz ^ 3) if zz in (1, 2) else None
        )
        locked = lambda *parts: lax.optimization_barrier(parts)
        stage1 = lambda piece: (pair(piece), inward(piece), over(piece))
        stage2 = lambda one, inner: (inward(one), outward(inner), over(one))
        stage3 = lambda middle, two: (outward(middle), over(two))

        a, b, own, sibling = locked(*pieces, tokens[0], to_member(tokens[0], 1))
        across = to_member(own, 2)
        a_one, a_inner, a_far0 = locked(*stage1(a))
        b_one, b_inner, b_far0 = locked(*stage1(b))
        a_middle, a_outer, a_far1 = locked(*stage2(a_one, a_inner))
        b_middle, b_outer, b_far1 = locked(*stage2(b_one, b_inner))
        a_two = jnp.where(inside, a_inner, a_outer)
        a_last, a_far2 = stage3(a_middle, a_two)
        b_two = jnp.where(inside, b_inner, b_outer)
        b_last, b_far2 = stage3(b_middle, b_two)
        a_last, a_far2, a_middle = locked(a_last, a_far2, a_middle)
        a_three = jnp.where(inside, a_middle, a_last)
        a_far3 = over(a_three)
        books = [own, sibling]
        upper = [a, a_one, a_two, a_three, a_far0, a_far1, a_far2]
        lower = [b, b_one, b_two, None, b_far0, b_far1]
        late = [(7, 0), (3, 1), (6, 1), (7, 1)]
        early = [(k, half) for half in range(2) for k in range(8) if (k, half) not in late]
        project((0, 1), early, late, (upper, lower), n_z)
        b_last, b_far2, b_middle, sums[0], sums[1], across = locked(
            b_last, b_far2, b_middle, sums[0], sums[1], after(across, a_last, a_far2)
        )
        books += [across, to_member(across, 1)]
        project((2, 3), early, late, (upper, lower), n_z)
        b_three = jnp.where(inside, b_middle, b_last)
        pieces = [a_far3, b_three, b_far2]
        finish = lambda at, *others: over(after(b_three[:, at], *others))
    else:
        across, sibling = to_member(tokens[0], 2), to_member(tokens[0], 1)
        books = [tokens[0], sibling, across, to_member(across, 1)]
        full = gathered(jnp.concatenate(pieces, axis=0))
        deep = MEMBERS * HEAD_SIZE // 2
        upper, lower = [part[:deep] for part in full], [part[deep:] for part in full]
        late = [(n_pieces - 1, 0), (n_pieces - 1, 1)]
        early = [(k, half) for half in range(2) for k in range(n_pieces - 1)]
        for segs in ((0, 1), (2, 3)):
            project(segs, early, late, (upper, lower), 0)
        pieces = [upper[-1]]
        finish = lambda at, *others: lower[-1][:, at]

    halves = [slice(k * HEAD_SIZE, (k + 2) * HEAD_SIZE) for k in (0, 2, 4)]
    lower_kv, lower_q0 = finish(halves[0]), finish(halves[1])
    found = call(
        functools.partial(kv_body, len(pieces) + 1),
        [shape((length, 2 * HEAD_SIZE), bf16), shape((HEAD_SIZE, 2 * HEAD_SIZE), f32)] * MEMBERS
        + [shape((HEAD_SIZE, 2 * HEAD_SIZE), bf16)],
        [VMEM] * (len(pieces) + 1 + 3 * MEMBERS),
        flops=2 * MEMBERS * length * len(late) * MEMBERS * HEAD_SIZE * HEAD_SIZE,
    )(*pieces, lower_kv, *sums, *lates, *messages)
    kvs, deltas, total = found[0:-1:2], found[1:-1:2], found[-1]

    base = None
    for a in range(1, n_groups):
        term = permute(total, lambda gg, mm, zz: (gg ^ a, mm, zz) if gg < gg ^ a else None)
        base = term if base is None else base.astype(f32) + term.astype(f32)

    lower_q1 = finish(halves[2], total)
    half = group // 2

    def local(segs, part, lower_q):
        found = call(
            functools.partial(local_body, len(segs), len(pieces) + 1, halves[1 + part].start, half),
            [shape((length, half * HEAD_SIZE), bf16), shape((length, half * HEAD_SIZE), f32)] * len(segs),
            [VMEM] * (len(pieces) + 1 + 4 * len(segs)),
            flops=4 * len(segs) * length * length * half * HEAD_SIZE,
        )(*pieces, lower_q, *[one[s] for one in (kvs, messages, sums, lates) for s in segs])
        return {(s, part): (found[2 * at], found[2 * at + 1]) for at, s in enumerate(segs)}

    def mix(segs, parts, base, ready):
        keys = [(s, part) for s in segs for part in parts]
        return call(
            functools.partial(mix_body, segs, parts, group),
            [shape((length, half * HEAD_SIZE), bf16)] * len(keys),
            [SMEM] * 2 + [VMEM] * (1 + MEMBERS + len(segs) + 2 * len(keys)),
            flops=2 * len(keys) * length * half * HEAD_SIZE * HEAD_SIZE * 6,
        )(
            here, gate_bias, base, *deltas, *[messages[s] for s in segs],
            *[ready[key][0] for key in keys], *[ready[key][1] for key in keys],
        )

    ready = local((2, 3, 1, 0), 0, lower_q0)
    base = after(base, *ready[2, 0])
    two0, three0 = mix((2, 3), (0,), base, ready)
    ready |= local((2, 3), 1, after(lower_q1, two0, three0))
    two1, three1 = mix((2, 3), (1,), base, ready)
    ready |= local((1, 0), 1, after(lower_q1, two1, three1))
    one0, one1, mine0, mine1 = mix((1, 0), (0, 1), after(base, two1, three1), ready)
    sent = [mine0, mine1]
    for k, parts in ((1, (one0, one1)), (2, (two0, two1)), (3, (three0, three1))):
        sent += [to_member(part, k) for part in parts]
    (output,) = call(
        functools.partial(assemble_body, (2,) * MEMBERS),
        [shape((length, w_query.shape[1]), bf16)],
        [SMEM] + [VMEM] * len(sent),
    )(here, *sent)
    return output[None]


def solution(mesh):
    in_specs = (
        P("fsdp", "seg", None),
        P(("seg", "fsdp"), None),
        P(("seg", "fsdp"), None),
        P(("seg", "fsdp"), None),
        P(),
        P("fsdp", "seg", None, None),
        P("fsdp", "seg"),
    )
    out_specs = P("fsdp", "seg", None)
    body = functools.partial(shards, (mesh.shape["seg"], mesh.shape["fsdp"]))
    return jax.shard_map(body, mesh=mesh, in_specs=in_specs, out_specs=out_specs, check_vma=False)
```

```python
import functools

import jax
import jax.numpy as jnp
from jax import lax
from jax.experimental import pallas as pl
from jax.experimental.pallas import tpu as pltpu
from jax.sharding import PartitionSpec as P

HEAD_SIZE = 128
BLK = 128
MEMBERS = 4
META_ROWS = 16
HALF = META_ROWS // 2
AXES = ("seg", "fsdp")

VMEM = pl.BlockSpec(memory_space=pltpu.VMEM)
SMEM = pl.BlockSpec(memory_space=pltpu.SMEM)
ANY = pl.BlockSpec(memory_space=pl.ANY)
HBM = pl.BlockSpec(memory_space=pltpu.HBM)


def call(body, outs, in_specs, flops=0, scratch=(), out_spec=VMEM, limit=16 << 20):
    return pl.pallas_call(
        body,
        out_shape=outs,
        in_specs=in_specs,
        out_specs=[out_spec] * len(outs),
        scratch_shapes=list(scratch),
        compiler_params=pltpu.CompilerParams(vmem_limit_bytes=limit),
        cost_estimate=pl.CostEstimate(flops=flops, bytes_accessed=4 << 20, transcendentals=0),
    )


def aligned(offset):
    return pl.multiple_of(offset, HEAD_SIZE)


def pack_body(group, here_ref, valid_ref, mask_ref, wq_ref, wk_ref, wv_ref, *outs):
    rows, wide = wk_ref.shape[0], group * HEAD_SIZE
    row = lax.broadcasted_iota(jnp.int32, (META_ROWS, outs[0].shape[1]), 0)
    facts = jnp.where(row < HALF, valid_ref[0, 0], mask_ref[0, 0, 1, 0])
    facts = facts.astype(jnp.float32).astype(jnp.bfloat16)
    for k in range(MEMBERS):
        head, out = here_ref[1] ^ k, outs[k]
        at = aligned(head * HEAD_SIZE)
        out[:rows, :HEAD_SIZE] = wk_ref[:, pl.ds(at, HEAD_SIZE)]
        out[:rows, HEAD_SIZE : 2 * HEAD_SIZE] = wv_ref[:, pl.ds(at, HEAD_SIZE)]
        out[:rows, 2 * HEAD_SIZE :] = wq_ref[:, pl.ds(aligned(head * wide), wide)]
        out[rows:, :] = facts


def columns_of(tokens_ref, here_ref, piece, half, line):
    deep = MEMBERS * HEAD_SIZE // 2
    if not line:
        return tokens_ref[:, pl.ds((2 * piece + half) * deep, deep)]
    g, m, z = here_ref[0] ^ (piece // line), here_ref[1], here_ref[2]
    inside = (z == 1) | (z == 2)
    step = piece % line
    if step < 2:
        z = z ^ step
    else:
        z = jnp.where(inside, z ^ (5 - step), z ^ step)
    parts = [
        tokens_ref[:, pl.ds(aligned(((g * MEMBERS + (m ^ k)) * line + z) * HEAD_SIZE), HEAD_SIZE)]
        for k in (2 * half, 2 * half + 1)
    ]
    return jnp.concatenate(parts, axis=1)


def facts_of(message_ref):
    rows = message_ref.shape[0] - META_ROWS
    facts = message_ref[rows:, : 2 * HEAD_SIZE].astype(jnp.float32)
    return facts[0:1, :], facts[HALF : HALF + 1, :]


def iota(shape, dimension):
    return lax.broadcasted_iota(jnp.int32, shape, dimension).astype(jnp.float32)


def project_body(early, late, line, here_ref, *refs):
    tokens, pieces, outs = refs[:2], refs[2 : 2 + len(early)], refs[2 + len(early) :]
    length = tokens[0].shape[0]
    total = None
    for place, piece in zip(early, pieces):
        columns = jnp.concatenate([columns_of(one, here_ref, *place, line) for one in tokens], axis=0)
        term = jnp.dot(columns, piece[...], preferred_element_type=jnp.float32)
        total = term if total is None else total + term
    for n in range(2):
        outs[n][...] = total[n * length : (n + 1) * length]
        for k, place in enumerate(late):
            columns = columns_of(tokens[n], here_ref, *place, line)
            deep = columns.shape[1]
            outs[2 + n][:, k * deep : (k + 1) * deep] = columns


def sigma_plus(v):
    return jnp.where(v > 0, v + 1.0, jnp.exp(jnp.minimum(v, 0.0)))


def split(values):
    high = values.astype(jnp.bfloat16)
    return high, (values - high.astype(jnp.float32)).astype(jnp.bfloat16)


def late_rows(here_ref, last_ref, start, width, *pieces):
    *whole, upper, inner, outer = pieces
    rows = [piece[:, start : start + width] for piece in whole]
    lost = whole[0].shape[1] - upper.shape[1] if start else 0
    rows.append(upper[:, start - lost : start - lost + width])
    inside = (here_ref[2] == 1) | (here_ref[2] == 2)

    @pl.when(inside)
    def _():
        last_ref[...] = inner[:, start : start + width]

    @pl.when(jnp.logical_not(inside))
    def _():
        last_ref[...] = outer[...]

    return jnp.concatenate(rows + [last_ref[...]], axis=0)


def kv_body(n_late, here_ref, *refs):
    pieces, refs, last_ref = refs[:n_late], refs[n_late:-1], refs[-1]
    sums, lates, messages = refs[:MEMBERS], refs[MEMBERS : 2 * MEMBERS], refs[2 * MEMBERS : 3 * MEMBERS]
    outs = refs[3 * MEMBERS :]
    rows = late_rows(here_ref, last_ref, 0, 2 * HEAD_SIZE, *pieces)
    kvs = []
    for seg in range(MEMBERS):
        total = sums[seg][:, : 2 * HEAD_SIZE]
        total += jnp.dot(lates[seg][...], rows, preferred_element_type=jnp.float32)
        kvs.append(total.astype(jnp.bfloat16))
        outs[2 * seg][...] = kvs[seg]
    whole = None
    for seg, kv in enumerate(kvs):
        length = kv.shape[0]
        valid, _ = facts_of(messages[seg])
        keys = kv[:, :HEAD_SIZE].astype(jnp.float32)
        live = iota((length, HEAD_SIZE), 0) < valid[:, :HEAD_SIZE]
        sig = jnp.where(live, sigma_plus(keys), 0.0)
        wide = jnp.concatenate(
            [kv[:, HEAD_SIZE:], jnp.ones((length, HEAD_SIZE), jnp.bfloat16)], axis=1
        )
        high, low = split(sig)
        over = (((0,), (0,)), ((), ()))
        delta = lax.dot_general(high, wide, over, preferred_element_type=jnp.float32)
        delta += lax.dot_general(low, wide, over, preferred_element_type=jnp.float32)
        outs[2 * seg + 1][...] = delta
        whole = delta if whole is None else whole + delta
    outs[-1][...] = whole.astype(jnp.bfloat16)


def local_body(n, n_late, start, heads, here_ref, *refs):
    pieces, refs, last_ref = refs[:n_late], refs[n_late:-1], refs[-1]
    kvs, messages, sums, lates, outs = [refs[k * n : (k + 1) * n] for k in range(4)] + [refs[4 * n :]]
    rows = late_rows(here_ref, last_ref, start, heads * HEAD_SIZE, *pieces)
    columns = slice(start, start + heads * HEAD_SIZE)
    queries = []
    for at in range(n):
        total = sums[at][:, columns] + jnp.dot(
            lates[at][...], rows, preferred_element_type=jnp.float32
        )
        queries.append(total.astype(jnp.bfloat16))
        outs[2 * at][...] = queries[at]
    work = [(at, block) for at in range(n) for block in range(queries[0].shape[0] // BLK)]
    span = lambda block: slice(block * BLK, (block + 1) * BLK)
    scores = []
    for at, block in work:
        stacked = jnp.concatenate(
            [queries[at][span(block), h * HEAD_SIZE : (h + 1) * HEAD_SIZE] for h in range(heads)], axis=0
        )
        keys = kvs[at][0 : (block + 1) * BLK, :HEAD_SIZE]
        scores.append(
            lax.dot_general(
                stacked, keys, (((1,), (1,)), ((), ())), preferred_element_type=jnp.float32
            )
        )
    weights = []
    for (at, block), score in zip(work, scores):
        width = (block + 1) * BLK
        valid, seen = facts_of(messages[at])
        i, j = iota((BLK, width), 0) + block * BLK, iota((BLK, width), 1)
        limit = valid[:, :width]
        if block:
            limit = jnp.where((j[0:1] >= block * BLK) | (seen[:, :width] > 0), limit, 0.0)
        allowed = (j <= i) & (j < limit)
        masked = jnp.concatenate(
            [jnp.where(allowed, score[span(h)] * HEAD_SIZE ** (-0.5), -1e30) for h in range(heads)],
            axis=0,
        )
        top = jnp.max(masked, axis=-1, keepdims=True)
        expo = jnp.exp(masked - top)
        total = jnp.maximum(jnp.sum(expo, axis=-1, keepdims=True), 1.0)
        weights.append((expo * (1.0 / total)).astype(jnp.bfloat16))
    for (at, block), weight in zip(work, weights):
        values = kvs[at][0 : (block + 1) * BLK, HEAD_SIZE:]
        local = jnp.dot(weight, values, preferred_element_type=jnp.float32)
        for h in range(heads):
            outs[2 * at + 1][span(block), h * HEAD_SIZE : (h + 1) * HEAD_SIZE] = local[span(h)]


def mix_body(segs, parts, group, here_ref, gate_ref, base_ref, *refs):
    deltas, messages, refs = refs[:MEMBERS], refs[MEMBERS : MEMBERS + len(segs)], refs[MEMBERS + len(segs) :]
    n = len(segs) * len(parts)
    queries, locals_, outs = refs[:n], refs[n : 2 * n], refs[2 * n :]
    me = here_ref[1]
    heads = queries[0].shape[1] // HEAD_SIZE
    length = queries[0].shape[0]
    work = [(at, p, h) for at in range(len(segs)) for p in range(len(parts)) for h in range(heads)]
    memories = []
    for seg in segs:
        memory = base_ref[...].astype(jnp.float32)
        for other in range(MEMBERS):
            if other != seg:
                earlier = jnp.where((me ^ other) < (me ^ seg), 1.0, 0.0)
                memory = memory + earlier * deltas[other][...]
        memories.append(split(memory))
    columns = lambda h: slice(h * HEAD_SIZE, (h + 1) * HEAD_SIZE)
    numers = []
    for at, p, h in work:
        mem_high, mem_low = memories[at]
        high, low = split(sigma_plus(queries[at * len(parts) + p][:, columns(h)].astype(jnp.float32)))
        numer = jnp.dot(high, mem_high, preferred_element_type=jnp.float32)
        numer += jnp.dot(high, mem_low, preferred_element_type=jnp.float32)
        numer += jnp.dot(low, mem_high, preferred_element_type=jnp.float32)
        numers.append(numer)
    for (at, p, h), numer in zip(work, numers):
        valid, _ = facts_of(messages[at])
        live = iota((length, HEAD_SIZE), 0) < valid[:, :HEAD_SIZE]
        retrieved = numer[:, :HEAD_SIZE] / (numer[:, HEAD_SIZE:] + 1.0)
        logit = jnp.full((1, HEAD_SIZE), gate_ref[me * group + parts[p] * heads + h], jnp.float32)
        gate = 1.0 / (1.0 + jnp.exp(-logit))
        mixed = gate * retrieved + (1.0 - gate) * locals_[at * len(parts) + p][:, columns(h)]
        outs[at * len(parts) + p][:, columns(h)] = jnp.where(live, mixed, 0.0).astype(jnp.bfloat16)


def assemble_body(counts, here_ref, *refs):
    parts, out = list(refs[:-1]), refs[-1]
    width = out.shape[1] // MEMBERS
    for k, count in enumerate(counts):
        for c in range(count):
            at = (here_ref[1] ^ k) * width + c * (width // count)
            out[:, pl.ds(aligned(at), width // count)] = parts.pop(0)[...]


def after(array, *others):
    return lax.optimization_barrier((array,) + others)[0]


def shards(sizes, tokens, w_query, w_key, value_weight, gate_bias, block_mask, valid_len):
    n_seg, n_z = sizes
    n_groups = n_seg // MEMBERS
    heads_kv = w_key.shape[1] // HEAD_SIZE
    group = w_query.shape[1] // w_key.shape[1]
    rows = w_query.shape[0]
    length, width = tokens.shape[1], tokens.shape[2]
    assert heads_kv == MEMBERS and group == 4 and length == 2 * BLK
    seg = lax.axis_index("seg")
    z = lax.axis_index("fsdp")
    g, m = seg // MEMBERS, seg % MEMBERS
    here = jnp.stack([g, m, z]).astype(jnp.int32)
    bf16, f32 = jnp.bfloat16, jnp.float32
    shape = jax.ShapeDtypeStruct

    def permute(array, to):
        pairs = []
        for gg in range(n_groups):
            for mm in range(MEMBERS):
                for zz in range(n_z):
                    target = to(gg, mm, zz)
                    if target is not None:
                        index = lambda t: (t[0] * MEMBERS + t[1]) * n_z + t[2]
                        pairs.append((index((gg, mm, zz)), index(target)))
        return lax.ppermute(array, AXES, pairs)

    def to_member(array, k):
        return permute(array, lambda gg, mm, zz: (gg, mm ^ k, zz))

    wide = (2 + group) * HEAD_SIZE
    packed = call(
        functools.partial(pack_body, group),
        [shape((rows + META_ROWS, wide), bf16)] * MEMBERS,
        [SMEM] * 3 + [VMEM] * 3,
    )(here, valid_len, block_mask, w_query, w_key, value_weight)
    messages = [packed[0], *[to_member(packed[k], k) for k in (1, 2, 3)]]

    def gathered(piece):
        index = lambda gg, mm, zz: (gg * MEMBERS + mm) * n_z + zz
        everything = lax.all_gather(
            piece,
            AXES,
            axis_index_groups=[
                [index(gg, mm, zz) for gg in range(n_groups) for zz in range(n_z)]
                for mm in range(MEMBERS)
            ],
        )
        columns = piece.shape[1]
        natural = everything.reshape(n_groups, n_z, MEMBERS, rows, columns)
        members = jnp.arange(MEMBERS, dtype=jnp.int32) ^ m
        natural = jnp.take(natural, members, axis=2).transpose(0, 2, 1, 3, 4)
        return list(natural.reshape(-1, MEMBERS * HEAD_SIZE, columns))

    pieces = [
        jnp.concatenate([messages[k][:rows] for k in members], axis=0) for members in ((0, 1), (2, 3))
    ]
    n_pieces = width // (MEMBERS * HEAD_SIZE)
    sums, lates = [None] * MEMBERS, [None] * MEMBERS

    def project(segs, early, late, halves, line):
        deep = MEMBERS * HEAD_SIZE // 2
        found = call(
            functools.partial(project_body, early, late, line),
            [shape((length, wide), f32)] * 2 + [shape((length, len(late) * deep), bf16)] * 2,
            [SMEM] + [VMEM] * (2 + len(early)),
            flops=2 * 2 * length * len(early) * deep * wide,
        )(here, *[books[s] for s in segs], *[halves[half][piece] for piece, half in early])
        for at, s in enumerate(segs):
            sums[s], lates[s] = found[at], found[2 + at]

    cut = 2 * HEAD_SIZE
    if n_groups == 2 and n_z == 4:
        assert rows == HEAD_SIZE
        inside = (z == 1) | (z == 2)
        over = lambda part: permute(part, lambda gg, mm, zz: (gg ^ 1, mm, zz))
        pair = lambda part: permute(part, lambda gg, mm, zz: (gg, mm, zz ^ 1))
        outward = lambda part: permute(
            part, lambda gg, mm, zz: (gg, mm, zz ^ 1) if zz in (1, 2) else None
        )
        inward = lambda part: permute(
            part, lambda gg, mm, zz: (gg, mm, zz ^ 3) if zz in (1, 2) else None
        )
        locked = lambda *parts: lax.optimization_barrier(parts)
        stage1 = lambda piece: (pair(piece), inward(piece), over(piece))
        stage2 = lambda one, inner: (inward(one), outward(inner), over(one))
        stage3 = lambda middle, two: (outward(middle), over(two))

        a, b, own, sibling = locked(*pieces, tokens[0], to_member(tokens[0], 1))
        across = to_member(own, 2)
        a_one, a_inner, a_far0 = locked(*stage1(a))
        b_one, b_inner, b_far0 = locked(*stage1(b))
        a_middle, a_outer, a_far1 = locked(*stage2(a_one, a_inner))
        b_middle, b_outer, b_far1 = locked(*stage2(b_one, b_inner))
        a_two = jnp.where(inside, a_inner, a_outer)
        a_last, a_far2 = stage3(a_middle, a_two)
        b_two = jnp.where(inside, b_inner, b_outer)
        b_last, b_far2, b_inner = *stage3(b_middle, b_two), inward(b_far1)
        a_last, a_far2, a_middle = locked(a_last, a_far2, a_middle)
        a_three = jnp.where(inside, a_middle, a_last)
        books = [own, sibling]
        upper = [a, a_one, a_two, None, a_far0, a_far1]
        lower = [b, b_one, b_two, None, b_far0, b_far1]
        early = [(k, half) for half in range(2) for k in (0, 1, 2, 4, 5)]
        late = [(3, 0), (6, 0), (3, 1), (6, 1), (7, 0), (7, 1)]
        project((0, 1), early, late, (upper, lower), n_z)
        b_last, b_far2, b_middle, b_inner, sums[0], sums[1], across = locked(
            b_last, b_far2, b_middle, b_inner, sums[0], sums[1], after(across, a_last, a_far2)
        )
        books += [across, to_member(across, 1)]
        project((2, 3), early, late, (upper, lower), n_z)
        b_three = jnp.where(inside, b_middle, b_last)
        pieces = [a_three, a_far2, b_three, b_far2]
        upper_kv, upper_q = [over(a_three[:, at]) for at in (slice(0, cut), slice(cut, None))]
        inner = b_inner
        finish = lambda at, *others: outward(after(b_inner[:, at], *others))
    else:
        across, sibling = to_member(tokens[0], 2), to_member(tokens[0], 1)
        books = [tokens[0], sibling, across, to_member(across, 1)]
        full = gathered(jnp.concatenate(pieces, axis=0))
        deep = MEMBERS * HEAD_SIZE // 2
        upper, lower = [part[:deep] for part in full], [part[deep:] for part in full]
        late = [(n_pieces - 1, 0), (n_pieces - 1, 1)]
        early = [(k, half) for half in range(2) for k in range(n_pieces - 1)]
        late = [(n_pieces - 2, 1)] + late
        early.remove(late[0])
        for segs in ((0, 1), (2, 3)):
            project(segs, early, late, (upper, lower), 0)
        pieces = [lower[-2]]
        upper_kv, upper_q = upper[-1][:, :cut], upper[-1][:, cut:]
        inner = lower[-1]
        finish = lambda at, *others: inner[:, at]

    halves = [slice(k * HEAD_SIZE, (k + 2) * HEAD_SIZE) for k in (0, 2, 4)]
    lower_kv, lower_q0 = finish(halves[0]), finish(halves[1])
    found = call(
        functools.partial(kv_body, len(late) + 1),
        [shape((length, 2 * HEAD_SIZE), bf16), shape((HEAD_SIZE, 2 * HEAD_SIZE), f32)] * MEMBERS
        + [shape((HEAD_SIZE, 2 * HEAD_SIZE), bf16)],
        [SMEM] + [VMEM] * (len(late) + 1 + 3 * MEMBERS),
        flops=2 * MEMBERS * length * len(late) * MEMBERS * HEAD_SIZE * HEAD_SIZE,
        scratch=[pltpu.VMEM((MEMBERS * HEAD_SIZE // 2, cut), bf16)],
    )(here, *pieces, upper_kv, inner, lower_kv, *sums, *lates, *messages)
    kvs, deltas, total = found[0:-1:2], found[1:-1:2], found[-1]

    base = None
    for a in range(1, n_groups):
        term = permute(total, lambda gg, mm, zz: (gg ^ a, mm, zz) if gg < gg ^ a else None)
        base = term if base is None else base.astype(f32) + term.astype(f32)

    lower_q1 = finish(halves[2], total)
    half = group // 2

    def local(segs, part, lower_q):
        found = call(
            functools.partial(local_body, len(segs), len(late) + 1, halves[1 + part].start, half),
            [shape((length, half * HEAD_SIZE), bf16), shape((length, half * HEAD_SIZE), f32)] * len(segs),
            [SMEM] + [VMEM] * (len(late) + 1 + 4 * len(segs)),
            flops=4 * len(segs) * length * length * half * HEAD_SIZE,
            scratch=[pltpu.VMEM((MEMBERS * HEAD_SIZE // 2, half * HEAD_SIZE), bf16)],
        )(here, *pieces, upper_q, inner, lower_q, *[one[s] for one in (kvs, messages, sums, lates) for s in segs])
        return {(s, part): (found[2 * at], found[2 * at + 1]) for at, s in enumerate(segs)}

    def mix(segs, parts, base, ready):
        keys = [(s, part) for s in segs for part in parts]
        return call(
            functools.partial(mix_body, segs, parts, group),
            [shape((length, half * HEAD_SIZE), bf16)] * len(keys),
            [SMEM] * 2 + [VMEM] * (1 + MEMBERS + len(segs) + 2 * len(keys)),
            flops=2 * len(keys) * length * half * HEAD_SIZE * HEAD_SIZE * 6,
        )(
            here, gate_bias, base, *deltas, *[messages[s] for s in segs],
            *[ready[key][0] for key in keys], *[ready[key][1] for key in keys],
        )

    ready = local((2, 3, 1, 0), 0, lower_q0)
    base = after(base, *ready[2, 0])
    two0, three0 = mix((2, 3), (0,), base, ready)
    ready |= local((2, 3), 1, after(lower_q1, two0, three0))
    two1, three1 = mix((2, 3), (1,), base, ready)
    ready |= local((1, 0), 1, after(lower_q1, two1, three1))
    one0, one1, mine0, mine1 = mix((1, 0), (0, 1), after(base, two1, three1), ready)
    sent = [mine0, mine1]
    for k, parts in ((1, (one0, one1)), (2, (two0, two1)), (3, (three0, three1))):
        sent += [to_member(part, k) for part in parts]
    (output,) = call(
        functools.partial(assemble_body, (2,) * MEMBERS),
        [shape((length, w_query.shape[1]), bf16)],
        [SMEM] + [VMEM] * len(sent),
    )(here, *sent)
    return output[None]


def solution(mesh):
    in_specs = (
        P("fsdp", "seg", None),
        P(("seg", "fsdp"), None),
        P(("seg", "fsdp"), None),
        P(("seg", "fsdp"), None),
        P(),
        P("fsdp", "seg", None, None),
        P("fsdp", "seg"),
    )
    out_specs = P("fsdp", "seg", None)
    body = functools.partial(shards, (mesh.shape["seg"], mesh.shape["fsdp"]))
    return jax.shard_map(body, mesh=mesh, in_specs=in_specs, out_specs=out_specs, check_vma=False)
```

```python
import functools

import jax
import jax.numpy as jnp
from jax import lax
from jax.experimental import pallas as pl
from jax.experimental.pallas import tpu as pltpu
from jax.sharding import PartitionSpec as P

HEAD_SIZE = 128
BLK = 128
MEMBERS = 4
META_ROWS = 16
HALF = META_ROWS // 2
AXES = ("seg", "fsdp")

VMEM = pl.BlockSpec(memory_space=pltpu.VMEM)
SMEM = pl.BlockSpec(memory_space=pltpu.SMEM)
ANY = pl.BlockSpec(memory_space=pl.ANY)
HBM = pl.BlockSpec(memory_space=pltpu.HBM)


def call(body, outs, in_specs, flops=0, scratch=(), out_spec=VMEM, limit=16 << 20):
    return pl.pallas_call(
        body,
        out_shape=outs,
        in_specs=in_specs,
        out_specs=[out_spec] * len(outs),
        scratch_shapes=list(scratch),
        compiler_params=pltpu.CompilerParams(vmem_limit_bytes=limit),
        cost_estimate=pl.CostEstimate(flops=flops, bytes_accessed=4 << 20, transcendentals=0),
    )


def aligned(offset):
    return pl.multiple_of(offset, HEAD_SIZE)


def pack_body(group, here_ref, valid_ref, mask_ref, wq_ref, wk_ref, wv_ref, *outs):
    rows, wide = wk_ref.shape[0], group * HEAD_SIZE
    row = lax.broadcasted_iota(jnp.int32, (META_ROWS, outs[0].shape[1]), 0)
    facts = jnp.where(row < HALF, valid_ref[0, 0], mask_ref[0, 0, 1, 0])
    facts = facts.astype(jnp.float32).astype(jnp.bfloat16)
    for k in range(MEMBERS):
        head, out = here_ref[1] ^ k, outs[k]
        at = aligned(head * HEAD_SIZE)
        out[:rows, :HEAD_SIZE] = wk_ref[:, pl.ds(at, HEAD_SIZE)]
        out[:rows, HEAD_SIZE : 2 * HEAD_SIZE] = wv_ref[:, pl.ds(at, HEAD_SIZE)]
        out[:rows, 2 * HEAD_SIZE :] = wq_ref[:, pl.ds(aligned(head * wide), wide)]
        out[rows:, :] = facts


def columns_of(tokens_ref, here_ref, piece, half, line):
    deep = MEMBERS * HEAD_SIZE // 2
    if not line:
        return tokens_ref[:, pl.ds((2 * piece + half) * deep, deep)]
    g, m, z = here_ref[0] ^ (piece // line), here_ref[1], here_ref[2]
    inside = (z == 1) | (z == 2)
    step = piece % line
    if step < 2:
        z = z ^ step
    else:
        z = jnp.where(inside, z ^ (5 - step), z ^ step)
    parts = [
        tokens_ref[:, pl.ds(aligned(((g * MEMBERS + (m ^ k)) * line + z) * HEAD_SIZE), HEAD_SIZE)]
        for k in (2 * half, 2 * half + 1)
    ]
    return jnp.concatenate(parts, axis=1)


def facts_of(message_ref):
    rows = message_ref.shape[0] - META_ROWS
    facts = message_ref[rows:, : 2 * HEAD_SIZE].astype(jnp.float32)
    return facts[0:1, :], facts[HALF : HALF + 1, :]


def iota(shape, dimension):
    return lax.broadcasted_iota(jnp.int32, shape, dimension).astype(jnp.float32)


def project_body(early, late, line, here_ref, *refs):
    tokens, pieces, outs = refs[:2], refs[2 : 2 + len(early)], refs[2 + len(early) :]
    length = tokens[0].shape[0]
    total = None
    for place, piece in zip(early, pieces):
        columns = jnp.concatenate([columns_of(one, here_ref, *place, line) for one in tokens], axis=0)
        term = jnp.dot(columns, piece[...], preferred_element_type=jnp.float32)
        total = term if total is None else total + term
    for n in range(2):
        outs[n][...] = total[n * length : (n + 1) * length]
        for k, place in enumerate(late):
            columns = columns_of(tokens[n], here_ref, *place, line)
            deep = columns.shape[1]
            outs[2 + n][:, k * deep : (k + 1) * deep] = columns


def sigma_plus(v):
    return jnp.where(v > 0, v + 1.0, jnp.exp(jnp.minimum(v, 0.0)))


def split(values):
    high = values.astype(jnp.bfloat16)
    return high, (values - high.astype(jnp.float32)).astype(jnp.bfloat16)


def late_rows(here_ref, chosen_ref, start, width, *pieces):
    *whole, inner, outer, part = pieces
    lost = inner.shape[1] - outer.shape[1] if start else 0
    inside = (here_ref[2] == 1) | (here_ref[2] == 2)

    @pl.when(inside)
    def _():
        chosen_ref[...] = inner[:, start : start + width]

    @pl.when(jnp.logical_not(inside))
    def _():
        chosen_ref[...] = outer[:, start - lost : start - lost + width]

    rows = [piece[:, start : start + width] for piece in whole]
    return jnp.concatenate(rows + [chosen_ref[...], part[...]], axis=0)


def kv_body(n_late, here_ref, *refs):
    pieces, refs, chosen_ref = refs[:n_late], refs[n_late:-1], refs[-1]
    sums, lates, messages = refs[:MEMBERS], refs[MEMBERS : 2 * MEMBERS], refs[2 * MEMBERS : 3 * MEMBERS]
    outs = refs[3 * MEMBERS :]
    rows = late_rows(here_ref, chosen_ref, 0, 2 * HEAD_SIZE, *pieces)
    kvs = []
    for seg in range(MEMBERS):
        total = sums[seg][:, : 2 * HEAD_SIZE]
        total += jnp.dot(lates[seg][...], rows, preferred_element_type=jnp.float32)
        kvs.append(total.astype(jnp.bfloat16))
        outs[2 * seg][...] = kvs[seg]
    whole = None
    for seg, kv in enumerate(kvs):
        length = kv.shape[0]
        valid, _ = facts_of(messages[seg])
        keys = kv[:, :HEAD_SIZE].astype(jnp.float32)
        live = iota((length, HEAD_SIZE), 0) < valid[:, :HEAD_SIZE]
        sig = jnp.where(live, sigma_plus(keys), 0.0)
        wide = jnp.concatenate(
            [kv[:, HEAD_SIZE:], jnp.ones((length, HEAD_SIZE), jnp.bfloat16)], axis=1
        )
        high, low = split(sig)
        over = (((0,), (0,)), ((), ()))
        delta = lax.dot_general(high, wide, over, preferred_element_type=jnp.float32)
        delta += lax.dot_general(low, wide, over, preferred_element_type=jnp.float32)
        outs[2 * seg + 1][...] = delta
        whole = delta if whole is None else whole + delta
    outs[-1][...] = whole.astype(jnp.bfloat16)


def local_body(n, n_late, start, heads, here_ref, *refs):
    pieces, refs, chosen_ref = refs[:n_late], refs[n_late:-1], refs[-1]
    kvs, messages, sums, lates, outs = [refs[k * n : (k + 1) * n] for k in range(4)] + [refs[4 * n :]]
    rows = late_rows(here_ref, chosen_ref, start, heads * HEAD_SIZE, *pieces)
    columns = slice(start, start + heads * HEAD_SIZE)
    queries = []
    for at in range(n):
        total = sums[at][:, columns] + jnp.dot(
            lates[at][...], rows, preferred_element_type=jnp.float32
        )
        queries.append(total.astype(jnp.bfloat16))
        outs[2 * at][...] = queries[at]
    work = [(at, block) for at in range(n) for block in range(queries[0].shape[0] // BLK)]
    span = lambda block: slice(block * BLK, (block + 1) * BLK)
    scores = []
    for at, block in work:
        stacked = jnp.concatenate(
            [queries[at][span(block), h * HEAD_SIZE : (h + 1) * HEAD_SIZE] for h in range(heads)], axis=0
        )
        keys = kvs[at][0 : (block + 1) * BLK, :HEAD_SIZE]
        scores.append(
            lax.dot_general(
                stacked, keys, (((1,), (1,)), ((), ())), preferred_element_type=jnp.float32
            )
        )
    weights = []
    for (at, block), score in zip(work, scores):
        width = (block + 1) * BLK
        valid, seen = facts_of(messages[at])
        i, j = iota((BLK, width), 0) + block * BLK, iota((BLK, width), 1)
        limit = valid[:, :width]
        if block:
            limit = jnp.where((j[0:1] >= block * BLK) | (seen[:, :width] > 0), limit, 0.0)
        allowed = (j <= i) & (j < limit)
        masked = jnp.concatenate(
            [jnp.where(allowed, score[span(h)] * HEAD_SIZE ** (-0.5), -1e30) for h in range(heads)],
            axis=0,
        )
        top = jnp.max(masked, axis=-1, keepdims=True)
        expo = jnp.exp(masked - top)
        total = jnp.maximum(jnp.sum(expo, axis=-1, keepdims=True), 1.0)
        weights.append((expo * (1.0 / total)).astype(jnp.bfloat16))
    for (at, block), weight in zip(work, weights):
        values = kvs[at][0 : (block + 1) * BLK, HEAD_SIZE:]
        local = jnp.dot(weight, values, preferred_element_type=jnp.float32)
        for h in range(heads):
            outs[2 * at + 1][span(block), h * HEAD_SIZE : (h + 1) * HEAD_SIZE] = local[span(h)]


def mix_body(segs, parts, group, here_ref, gate_ref, base_ref, *refs):
    deltas, messages, refs = refs[:MEMBERS], refs[MEMBERS : MEMBERS + len(segs)], refs[MEMBERS + len(segs) :]
    n = len(segs) * len(parts)
    queries, locals_, outs = refs[:n], refs[n : 2 * n], refs[2 * n :]
    me = here_ref[1]
    heads = queries[0].shape[1] // HEAD_SIZE
    length = queries[0].shape[0]
    work = [(at, p, h) for at in range(len(segs)) for p in range(len(parts)) for h in range(heads)]
    memories = []
    for seg in segs:
        memory = base_ref[...].astype(jnp.float32)
        for other in range(MEMBERS):
            if other != seg:
                earlier = jnp.where((me ^ other) < (me ^ seg), 1.0, 0.0)
                memory = memory + earlier * deltas[other][...]
        memories.append(split(memory))
    columns = lambda h: slice(h * HEAD_SIZE, (h + 1) * HEAD_SIZE)
    numers = []
    for at, p, h in work:
        mem_high, mem_low = memories[at]
        high, low = split(sigma_plus(queries[at * len(parts) + p][:, columns(h)].astype(jnp.float32)))
        numer = jnp.dot(high, mem_high, preferred_element_type=jnp.float32)
        numer += jnp.dot(high, mem_low, preferred_element_type=jnp.float32)
        numer += jnp.dot(low, mem_high, preferred_element_type=jnp.float32)
        numers.append(numer)
    for (at, p, h), numer in zip(work, numers):
        valid, _ = facts_of(messages[at])
        live = iota((length, HEAD_SIZE), 0) < valid[:, :HEAD_SIZE]
        retrieved = numer[:, :HEAD_SIZE] / (numer[:, HEAD_SIZE:] + 1.0)
        logit = jnp.full((1, HEAD_SIZE), gate_ref[me * group + parts[p] * heads + h], jnp.float32)
        gate = 1.0 / (1.0 + jnp.exp(-logit))
        mixed = gate * retrieved + (1.0 - gate) * locals_[at * len(parts) + p][:, columns(h)]
        outs[at * len(parts) + p][:, columns(h)] = jnp.where(live, mixed, 0.0).astype(jnp.bfloat16)


def assemble_body(counts, here_ref, *refs):
    parts, out = list(refs[:-1]), refs[-1]
    width = out.shape[1] // MEMBERS
    for k, count in enumerate(counts):
        for c in range(count):
            at = (here_ref[1] ^ k) * width + c * (width // count)
            out[:, pl.ds(aligned(at), width // count)] = parts.pop(0)[...]


def after(array, *others):
    return lax.optimization_barrier((array,) + others)[0]


def shards(sizes, tokens, w_query, w_key, value_weight, gate_bias, block_mask, valid_len):
    n_seg, n_z = sizes
    n_groups = n_seg // MEMBERS
    heads_kv = w_key.shape[1] // HEAD_SIZE
    group = w_query.shape[1] // w_key.shape[1]
    rows = w_query.shape[0]
    length, width = tokens.shape[1], tokens.shape[2]
    assert heads_kv == MEMBERS and group == 4 and length == 2 * BLK
    seg = lax.axis_index("seg")
    z = lax.axis_index("fsdp")
    g, m = seg // MEMBERS, seg % MEMBERS
    here = jnp.stack([g, m, z]).astype(jnp.int32)
    bf16, f32 = jnp.bfloat16, jnp.float32
    shape = jax.ShapeDtypeStruct

    def permute(array, to):
        pairs = []
        for gg in range(n_groups):
            for mm in range(MEMBERS):
                for zz in range(n_z):
                    target = to(gg, mm, zz)
                    if target is not None:
                        index = lambda t: (t[0] * MEMBERS + t[1]) * n_z + t[2]
                        pairs.append((index((gg, mm, zz)), index(target)))
        return lax.ppermute(array, AXES, pairs)

    def to_member(array, k):
        return permute(array, lambda gg, mm, zz: (gg, mm ^ k, zz))

    wide = (2 + group) * HEAD_SIZE
    packed = call(
        functools.partial(pack_body, group),
        [shape((rows + META_ROWS, wide), bf16)] * MEMBERS,
        [SMEM] * 3 + [VMEM] * 3,
    )(here, valid_len, block_mask, w_query, w_key, value_weight)
    messages = [packed[0], *[to_member(packed[k], k) for k in (1, 2, 3)]]

    def gathered(piece):
        index = lambda gg, mm, zz: (gg * MEMBERS + mm) * n_z + zz
        everything = lax.all_gather(
            piece,
            AXES,
            axis_index_groups=[
                [index(gg, mm, zz) for gg in range(n_groups) for zz in range(n_z)]
                for mm in range(MEMBERS)
            ],
        )
        columns = piece.shape[1]
        natural = everything.reshape(n_groups, n_z, MEMBERS, rows, columns)
        members = jnp.arange(MEMBERS, dtype=jnp.int32) ^ m
        natural = jnp.take(natural, members, axis=2).transpose(0, 2, 1, 3, 4)
        return list(natural.reshape(-1, MEMBERS * HEAD_SIZE, columns))

    pieces = [
        jnp.concatenate([messages[k][:rows] for k in members], axis=0) for members in ((0, 1), (2, 3))
    ]
    n_pieces = width // (MEMBERS * HEAD_SIZE)
    sums, lates = [None] * MEMBERS, [None] * MEMBERS

    def project(segs, early, late, halves, line):
        deep = MEMBERS * HEAD_SIZE // 2
        found = call(
            functools.partial(project_body, early, late, line),
            [shape((length, wide), f32)] * 2 + [shape((length, len(late) * deep), bf16)] * 2,
            [SMEM] + [VMEM] * (2 + len(early)),
            flops=2 * 2 * length * len(early) * deep * wide,
        )(here, *[books[s] for s in segs], *[halves[half][piece] for piece, half in early])
        for at, s in enumerate(segs):
            sums[s], lates[s] = found[at], found[2 + at]

    cut = 2 * HEAD_SIZE
    if n_groups == 2 and n_z == 4:
        assert rows == HEAD_SIZE
        inside = (z == 1) | (z == 2)
        over = lambda part: permute(part, lambda gg, mm, zz: (gg ^ 1, mm, zz))
        pair = lambda part: permute(part, lambda gg, mm, zz: (gg, mm, zz ^ 1))
        outward = lambda part: permute(
            part, lambda gg, mm, zz: (gg, mm, zz ^ 1) if zz in (1, 2) else None
        )
        inward = lambda part: permute(
            part, lambda gg, mm, zz: (gg, mm, zz ^ 3) if zz in (1, 2) else None
        )
        locked = lambda *parts: lax.optimization_barrier(parts)
        stage1 = lambda piece: (pair(piece), inward(piece), over(piece))
        stage2 = lambda one, inner: (inward(one), outward(inner), over(one))
        stage3 = lambda middle, two: (outward(middle), over(two))

        a, b, own, sibling = locked(*pieces, tokens[0], to_member(tokens[0], 1))
        across = to_member(own, 2)
        a_one, a_inner, a_far0 = locked(*stage1(a))
        b_one, b_inner, b_far0 = locked(*stage1(b))
        a_middle, a_outer, a_far1 = locked(*stage2(a_one, a_inner))
        b_middle, b_outer, b_far1 = locked(*stage2(b_one, b_inner))
        a_two = jnp.where(inside, a_inner, a_outer)
        a_inner, (a_last, a_far2) = inward(a_far1), stage3(a_middle, a_two)
        b_two = jnp.where(inside, b_inner, b_outer)
        b_last, b_far2 = stage3(b_middle, b_two)
        a_last, a_far2, a_middle, a_inner = locked(a_last, a_far2, a_middle, a_inner)
        a_three = jnp.where(inside, a_middle, a_last)
        books = [own, sibling]
        upper = [a, a_one, a_two, None, a_far0, a_far1]
        lower = [b, b_one, b_two, None, b_far0, b_far1]
        early = [(k, half) for half in range(2) for k in (0, 1, 2, 4, 5)]
        late = [(3, 0), (6, 0), (3, 1), (6, 1), (7, 0), (7, 1)]
        project((0, 1), early, late, (upper, lower), n_z)
        b_last, b_far2, b_middle, sums[0], sums[1], across = locked(
            b_last, b_far2, b_middle, sums[0], sums[1], after(across, a_last, a_far2)
        )
        books += [across, to_member(across, 1)]
        project((2, 3), early, late, (upper, lower), n_z)
        b_three = jnp.where(inside, b_middle, b_last)
        pieces = [a_three, a_far2, b_three, b_far2]
        outer_kv, outer_q = [outward(a_inner[:, at]) for at in (slice(0, cut), slice(cut, None))]
        inner = a_inner
        finish = lambda at, *others: over(after(b_three[:, at], *others))
    else:
        across, sibling = to_member(tokens[0], 2), to_member(tokens[0], 1)
        books = [tokens[0], sibling, across, to_member(across, 1)]
        full = gathered(jnp.concatenate(pieces, axis=0))
        deep = MEMBERS * HEAD_SIZE // 2
        upper, lower = [part[:deep] for part in full], [part[deep:] for part in full]
        late = [(n_pieces - 1, 0), (n_pieces - 1, 1)]
        early = [(k, half) for half in range(2) for k in range(n_pieces - 1)]
        late = [(n_pieces - 2, 1)] + late
        early.remove(late[0])
        for segs in ((0, 1), (2, 3)):
            project(segs, early, late, (upper, lower), 0)
        pieces = [lower[-2]]
        outer_kv, outer_q = upper[-1][:, :cut], upper[-1][:, cut:]
        inner = upper[-1]
        finish = lambda at, *others: lower[-1][:, at]

    halves = [slice(k * HEAD_SIZE, (k + 2) * HEAD_SIZE) for k in (0, 2, 4)]
    lower_kv, lower_q0 = finish(halves[0]), finish(halves[1])
    found = call(
        functools.partial(kv_body, len(late) + 1),
        [shape((length, 2 * HEAD_SIZE), bf16), shape((HEAD_SIZE, 2 * HEAD_SIZE), f32)] * MEMBERS
        + [shape((HEAD_SIZE, 2 * HEAD_SIZE), bf16)],
        [SMEM] + [VMEM] * (len(late) + 1 + 3 * MEMBERS),
        flops=2 * MEMBERS * length * len(late) * MEMBERS * HEAD_SIZE * HEAD_SIZE,
        scratch=[pltpu.VMEM((MEMBERS * HEAD_SIZE // 2, cut), bf16)],
    )(here, *pieces, inner, outer_kv, lower_kv, *sums, *lates, *messages)
    kvs, deltas, total = found[0:-1:2], found[1:-1:2], found[-1]

    base = None
    for a in range(1, n_groups):
        term = permute(total, lambda gg, mm, zz: (gg ^ a, mm, zz) if gg < gg ^ a else None)
        base = term if base is None else base.astype(f32) + term.astype(f32)

    lower_q1 = finish(halves[2], total)
    half = group // 2

    def local(segs, part, lower_q):
        found = call(
            functools.partial(local_body, len(segs), len(late) + 1, halves[1 + part].start, half),
            [shape((length, half * HEAD_SIZE), bf16), shape((length, half * HEAD_SIZE), f32)] * len(segs),
            [SMEM] + [VMEM] * (len(late) + 1 + 4 * len(segs)),
            flops=4 * len(segs) * length * length * half * HEAD_SIZE,
            scratch=[pltpu.VMEM((MEMBERS * HEAD_SIZE // 2, half * HEAD_SIZE), bf16)],
        )(here, *pieces, inner, outer_q, lower_q, *[one[s] for one in (kvs, messages, sums, lates) for s in segs])
        return {(s, part): (found[2 * at], found[2 * at + 1]) for at, s in enumerate(segs)}

    def mix(segs, parts, base, ready):
        keys = [(s, part) for s in segs for part in parts]
        return call(
            functools.partial(mix_body, segs, parts, group),
            [shape((length, half * HEAD_SIZE), bf16)] * len(keys),
            [SMEM] * 2 + [VMEM] * (1 + MEMBERS + len(segs) + 2 * len(keys)),
            flops=2 * len(keys) * length * half * HEAD_SIZE * HEAD_SIZE * 6,
        )(
            here, gate_bias, base, *deltas, *[messages[s] for s in segs],
            *[ready[key][0] for key in keys], *[ready[key][1] for key in keys],
        )

    ready = local((2, 3, 1, 0), 0, lower_q0)
    base = after(base, *ready[2, 0])
    two0, three0 = mix((2, 3), (0,), base, ready)
    ready |= local((2, 3), 1, after(lower_q1, two0, three0))
    two1, three1 = mix((2, 3), (1,), base, ready)
    ready |= local((1, 0), 1, after(lower_q1, two1, three1))
    one0, one1, mine0, mine1 = mix((1, 0), (0, 1), after(base, two1, three1), ready)
    sent = [mine0, mine1]
    for k, parts in ((1, (one0, one1)), (2, (two0, two1)), (3, (three0, three1))):
        sent += [to_member(part, k) for part in parts]
    (output,) = call(
        functools.partial(assemble_body, (2,) * MEMBERS),
        [shape((length, w_query.shape[1]), bf16)],
        [SMEM] + [VMEM] * len(sent),
    )(here, *sent)
    return output[None]


def solution(mesh):
    in_specs = (
        P("fsdp", "seg", None),
        P(("seg", "fsdp"), None),
        P(("seg", "fsdp"), None),
        P(("seg", "fsdp"), None),
        P(),
        P("fsdp", "seg", None, None),
        P("fsdp", "seg"),
    )
    out_specs = P("fsdp", "seg", None)
    body = functools.partial(shards, (mesh.shape["seg"], mesh.shape["fsdp"]))
    return jax.shard_map(body, mesh=mesh, in_specs=in_specs, out_specs=out_specs, check_vma=False)
```

```python
import functools

import jax
import jax.numpy as jnp
from jax import lax
from jax.experimental import pallas as pl
from jax.experimental.pallas import tpu as pltpu
from jax.sharding import PartitionSpec as P

HEAD_SIZE = 128
BLK = 128
MEMBERS = 4
META_ROWS = 16
HALF = META_ROWS // 2
AXES = ("seg", "fsdp")

VMEM = pl.BlockSpec(memory_space=pltpu.VMEM)
SMEM = pl.BlockSpec(memory_space=pltpu.SMEM)
ANY = pl.BlockSpec(memory_space=pl.ANY)
HBM = pl.BlockSpec(memory_space=pltpu.HBM)


def call(body, outs, in_specs, flops=0, scratch=(), out_spec=VMEM, limit=16 << 20):
    return pl.pallas_call(
        body,
        out_shape=outs,
        in_specs=in_specs,
        out_specs=[out_spec] * len(outs),
        scratch_shapes=list(scratch),
        compiler_params=pltpu.CompilerParams(vmem_limit_bytes=limit),
        cost_estimate=pl.CostEstimate(flops=flops, bytes_accessed=4 << 20, transcendentals=0),
    )


def aligned(offset):
    return pl.multiple_of(offset, HEAD_SIZE)


def pack_body(group, here_ref, valid_ref, mask_ref, wq_ref, wk_ref, wv_ref, *outs):
    rows, wide = wk_ref.shape[0], group * HEAD_SIZE
    row = lax.broadcasted_iota(jnp.int32, (META_ROWS, outs[0].shape[1]), 0)
    facts = jnp.where(row < HALF, valid_ref[0, 0], mask_ref[0, 0, 1, 0])
    facts = facts.astype(jnp.float32).astype(jnp.bfloat16)
    for k in range(MEMBERS):
        head, out = here_ref[1] ^ k, outs[k]
        at = aligned(head * HEAD_SIZE)
        out[:rows, :HEAD_SIZE] = wk_ref[:, pl.ds(at, HEAD_SIZE)]
        out[:rows, HEAD_SIZE : 2 * HEAD_SIZE] = wv_ref[:, pl.ds(at, HEAD_SIZE)]
        out[:rows, 2 * HEAD_SIZE :] = wq_ref[:, pl.ds(aligned(head * wide), wide)]
        out[rows:, :] = facts


def columns_of(tokens_ref, here_ref, piece, half, line):
    deep = MEMBERS * HEAD_SIZE // 2
    if not line:
        return tokens_ref[:, pl.ds((2 * piece + half) * deep, deep)]
    g, m, z = here_ref[0] ^ (piece // line), here_ref[1], here_ref[2]
    inside = (z == 1) | (z == 2)
    step = piece % line
    if step < 2:
        z = z ^ step
    else:
        z = jnp.where(inside, z ^ (5 - step), z ^ step)
    parts = [
        tokens_ref[:, pl.ds(aligned(((g * MEMBERS + (m ^ k)) * line + z) * HEAD_SIZE), HEAD_SIZE)]
        for k in (2 * half, 2 * half + 1)
    ]
    return jnp.concatenate(parts, axis=1)


def facts_of(message_ref):
    rows = message_ref.shape[0] - META_ROWS
    facts = message_ref[rows:, : 2 * HEAD_SIZE].astype(jnp.float32)
    return facts[0:1, :], facts[HALF : HALF + 1, :]


def iota(shape, dimension):
    return lax.broadcasted_iota(jnp.int32, shape, dimension).astype(jnp.float32)


def project_body(early, late, line, here_ref, *refs):
    tokens, pieces, outs = refs[:2], refs[2 : 2 + len(early)], refs[2 + len(early) :]
    length = tokens[0].shape[0]
    total = None
    for place, piece in zip(early, pieces):
        columns = jnp.concatenate([columns_of(one, here_ref, *place, line) for one in tokens], axis=0)
        term = jnp.dot(columns, piece[...], preferred_element_type=jnp.float32)
        total = term if total is None else total + term
    for n in range(2):
        outs[n][...] = total[n * length : (n + 1) * length]
        for k, place in enumerate(late):
            columns = columns_of(tokens[n], here_ref, *place, line)
            deep = columns.shape[1]
            outs[2 + n][:, k * deep : (k + 1) * deep] = columns


def sigma_plus(v):
    return jnp.where(v > 0, v + 1.0, jnp.exp(jnp.minimum(v, 0.0)))


def split(values):
    high = values.astype(jnp.bfloat16)
    return high, (values - high.astype(jnp.float32)).astype(jnp.bfloat16)


def late_rows(here_ref, chosen_ref, start, width, *pieces):
    *whole, inner, outer, part = pieces
    lost = inner.shape[1] - outer.shape[1] if start else 0
    inside = (here_ref[2] == 1) | (here_ref[2] == 2)

    @pl.when(inside)
    def _():
        chosen_ref[...] = inner[:, start : start + width]

    @pl.when(jnp.logical_not(inside))
    def _():
        chosen_ref[...] = outer[:, start - lost : start - lost + width]

    rows = [piece[:, start : start + width] for piece in whole]
    return jnp.concatenate(rows + [chosen_ref[...], part[...]], axis=0)


def kv_body(n_late, here_ref, *refs):
    pieces, refs, chosen_ref = refs[:n_late], refs[n_late:-1], refs[-1]
    sums, lates, messages = refs[:MEMBERS], refs[MEMBERS : 2 * MEMBERS], refs[2 * MEMBERS : 3 * MEMBERS]
    outs = refs[3 * MEMBERS :]
    rows = late_rows(here_ref, chosen_ref, 0, 2 * HEAD_SIZE, *pieces)
    kvs = []
    for seg in range(MEMBERS):
        total = sums[seg][:, : 2 * HEAD_SIZE]
        total += jnp.dot(lates[seg][...], rows, preferred_element_type=jnp.float32)
        kvs.append(total.astype(jnp.bfloat16))
        outs[2 * seg][...] = kvs[seg]
    whole = None
    for seg, kv in enumerate(kvs):
        length = kv.shape[0]
        valid, _ = facts_of(messages[seg])
        keys = kv[:, :HEAD_SIZE].astype(jnp.float32)
        live = iota((length, HEAD_SIZE), 0) < valid[:, :HEAD_SIZE]
        sig = jnp.where(live, sigma_plus(keys), 0.0)
        wide = jnp.concatenate(
            [kv[:, HEAD_SIZE:], jnp.ones((length, HEAD_SIZE), jnp.bfloat16)], axis=1
        )
        high, low = split(sig)
        over = (((0,), (0,)), ((), ()))
        delta = lax.dot_general(high, wide, over, preferred_element_type=jnp.float32)
        delta += lax.dot_general(low, wide, over, preferred_element_type=jnp.float32)
        outs[2 * seg + 1][...] = delta
        whole = delta if whole is None else whole + delta
    outs[-1][...] = whole.astype(jnp.bfloat16)


def local_body(n, n_late, start, heads, here_ref, *refs):
    pieces, refs, chosen_ref = refs[:n_late], refs[n_late:-1], refs[-1]
    kvs, messages, sums, lates, outs = [refs[k * n : (k + 1) * n] for k in range(4)] + [refs[4 * n :]]
    rows = late_rows(here_ref, chosen_ref, start, heads * HEAD_SIZE, *pieces)
    columns = slice(start, start + heads * HEAD_SIZE)
    queries = []
    for at in range(n):
        total = sums[at][:, columns] + jnp.dot(
            lates[at][...], rows, preferred_element_type=jnp.float32
        )
        queries.append(total.astype(jnp.bfloat16))
        outs[2 * at][...] = queries[at]
    work = [(at, block) for at in range(n) for block in range(queries[0].shape[0] // BLK)]
    span = lambda block: slice(block * BLK, (block + 1) * BLK)
    scores = []
    for at, block in work:
        stacked = jnp.concatenate(
            [queries[at][span(block), h * HEAD_SIZE : (h + 1) * HEAD_SIZE] for h in range(heads)], axis=0
        )
        keys = kvs[at][0 : (block + 1) * BLK, :HEAD_SIZE]
        scores.append(
            lax.dot_general(
                stacked, keys, (((1,), (1,)), ((), ())), preferred_element_type=jnp.float32
            )
        )
    weights = []
    for (at, block), score in zip(work, scores):
        width = (block + 1) * BLK
        valid, seen = facts_of(messages[at])
        i, j = iota((BLK, width), 0) + block * BLK, iota((BLK, width), 1)
        limit = valid[:, :width]
        if block:
            limit = jnp.where((j[0:1] >= block * BLK) | (seen[:, :width] > 0), limit, 0.0)
        allowed = (j <= i) & (j < limit)
        masked = jnp.concatenate(
            [jnp.where(allowed, score[span(h)] * HEAD_SIZE ** (-0.5), -1e30) for h in range(heads)],
            axis=0,
        )
        top = jnp.max(masked, axis=-1, keepdims=True)
        expo = jnp.exp(masked - top)
        total = jnp.maximum(jnp.sum(expo, axis=-1, keepdims=True), 1.0)
        weights.append((expo * (1.0 / total)).astype(jnp.bfloat16))
    for (at, block), weight in zip(work, weights):
        values = kvs[at][0 : (block + 1) * BLK, HEAD_SIZE:]
        local = jnp.dot(weight, values, preferred_element_type=jnp.float32)
        for h in range(heads):
            outs[2 * at + 1][span(block), h * HEAD_SIZE : (h + 1) * HEAD_SIZE] = local[span(h)]


def mix_body(segs, parts, group, here_ref, gate_ref, base_ref, *refs):
    deltas, messages, refs = refs[:MEMBERS], refs[MEMBERS : MEMBERS + len(segs)], refs[MEMBERS + len(segs) :]
    n = len(segs) * len(parts)
    queries, locals_, outs = refs[:n], refs[n : 2 * n], refs[2 * n :]
    me = here_ref[1]
    heads = queries[0].shape[1] // HEAD_SIZE
    length = queries[0].shape[0]
    work = [(at, p, h) for at in range(len(segs)) for p in range(len(parts)) for h in range(heads)]
    memories = []
    for seg in segs:
        memory = jnp.where(here_ref[3] > 0, 1.0, 0.0) * base_ref[...].astype(jnp.float32)
        for other in range(MEMBERS):
            if other != seg:
                earlier = jnp.where((me ^ other) < (me ^ seg), 1.0, 0.0)
                memory = memory + earlier * deltas[other][...]
        memories.append(split(memory))
    columns = lambda h: slice(h * HEAD_SIZE, (h + 1) * HEAD_SIZE)
    numers = []
    for at, p, h in work:
        mem_high, mem_low = memories[at]
        high, low = split(sigma_plus(queries[at * len(parts) + p][:, columns(h)].astype(jnp.float32)))
        numer = jnp.dot(high, mem_high, preferred_element_type=jnp.float32)
        numer += jnp.dot(high, mem_low, preferred_element_type=jnp.float32)
        numer += jnp.dot(low, mem_high, preferred_element_type=jnp.float32)
        numers.append(numer)
    for (at, p, h), numer in zip(work, numers):
        valid, _ = facts_of(messages[at])
        live = iota((length, HEAD_SIZE), 0) < valid[:, :HEAD_SIZE]
        retrieved = numer[:, :HEAD_SIZE] / (numer[:, HEAD_SIZE:] + 1.0)
        logit = jnp.full((1, HEAD_SIZE), gate_ref[me * group + parts[p] * heads + h], jnp.float32)
        gate = 1.0 / (1.0 + jnp.exp(-logit))
        mixed = gate * retrieved + (1.0 - gate) * locals_[at * len(parts) + p][:, columns(h)]
        outs[at * len(parts) + p][:, columns(h)] = jnp.where(live, mixed, 0.0).astype(jnp.bfloat16)


def assemble_body(places, here_ref, *refs):
    out = refs[-1]
    for (k, c), part in zip(places, refs):
        width = part.shape[1]
        at = (here_ref[1] ^ k) * 2 * width + c * width
        out[:, pl.ds(aligned(at), width)] = part[...]


def finish_body(places, here_ref, *refs):
    out, sems = refs[-2:]
    copies = []
    for n, ((k, c), part) in enumerate(zip(places, refs)):
        width = part.shape[1]
        at = (here_ref[1] ^ k) * 2 * width + c * width
        copies.append(
            pltpu.make_async_copy(part, out.at[:, pl.ds(aligned(at), width)], sems.at[n])
        )
        copies[-1].start()
    for one in copies:
        one.wait()


def after(array, *others):
    return lax.optimization_barrier((array,) + others)[0]


def shards(sizes, tokens, w_query, w_key, value_weight, gate_bias, block_mask, valid_len):
    n_seg, n_z = sizes
    n_groups = n_seg // MEMBERS
    heads_kv = w_key.shape[1] // HEAD_SIZE
    group = w_query.shape[1] // w_key.shape[1]
    rows = w_query.shape[0]
    length, width = tokens.shape[1], tokens.shape[2]
    assert heads_kv == MEMBERS and group == 4 and length == 2 * BLK
    seg = lax.axis_index("seg")
    z = lax.axis_index("fsdp")
    g, m = seg // MEMBERS, seg % MEMBERS
    here = jnp.stack([g, m, z, g if n_groups == 2 else 1]).astype(jnp.int32)
    bf16, f32 = jnp.bfloat16, jnp.float32
    shape = jax.ShapeDtypeStruct

    def permute(array, to):
        pairs = []
        for gg in range(n_groups):
            for mm in range(MEMBERS):
                for zz in range(n_z):
                    target = to(gg, mm, zz)
                    if target is not None:
                        index = lambda t: (t[0] * MEMBERS + t[1]) * n_z + t[2]
                        pairs.append((index((gg, mm, zz)), index(target)))
        return lax.ppermute(array, AXES, pairs)

    def to_member(array, k):
        return permute(array, lambda gg, mm, zz: (gg, mm ^ k, zz))

    wide = (2 + group) * HEAD_SIZE
    sibling = to_member(tokens[0], 1)
    packed = call(
        functools.partial(pack_body, group),
        [shape((rows + META_ROWS, wide), bf16)] * MEMBERS,
        [SMEM] * 3 + [VMEM] * 3,
    )(after(here, sibling), valid_len, block_mask, w_query, w_key, value_weight)
    messages = [packed[0], *[to_member(packed[k], k) for k in (1, 2, 3)]]

    def gathered(piece):
        index = lambda gg, mm, zz: (gg * MEMBERS + mm) * n_z + zz
        everything = lax.all_gather(
            piece,
            AXES,
            axis_index_groups=[
                [index(gg, mm, zz) for gg in range(n_groups) for zz in range(n_z)]
                for mm in range(MEMBERS)
            ],
        )
        columns = piece.shape[1]
        natural = everything.reshape(n_groups, n_z, MEMBERS, rows, columns)
        members = jnp.arange(MEMBERS, dtype=jnp.int32) ^ m
        natural = jnp.take(natural, members, axis=2).transpose(0, 2, 1, 3, 4)
        return list(natural.reshape(-1, MEMBERS * HEAD_SIZE, columns))

    pieces = [
        jnp.concatenate([messages[k][:rows] for k in members], axis=0) for members in ((0, 1), (2, 3))
    ]
    n_pieces = width // (MEMBERS * HEAD_SIZE)
    sums, lates = [None] * MEMBERS, [None] * MEMBERS

    def project(segs, early, late, halves, line):
        deep = MEMBERS * HEAD_SIZE // 2
        found = call(
            functools.partial(project_body, early, late, line),
            [shape((length, wide), f32)] * 2 + [shape((length, len(late) * deep), bf16)] * 2,
            [SMEM] + [VMEM] * (2 + len(early)),
            flops=2 * 2 * length * len(early) * deep * wide,
        )(here, *[books[s] for s in segs], *[halves[half][piece] for piece, half in early])
        for at, s in enumerate(segs):
            sums[s], lates[s] = found[at], found[2 + at]

    cut = 2 * HEAD_SIZE
    if n_groups == 2 and n_z == 4:
        assert rows == HEAD_SIZE
        inside = (z == 1) | (z == 2)
        over = lambda part: permute(part, lambda gg, mm, zz: (gg ^ 1, mm, zz))
        pair = lambda part: permute(part, lambda gg, mm, zz: (gg, mm, zz ^ 1))
        outward = lambda part: permute(
            part, lambda gg, mm, zz: (gg, mm, zz ^ 1) if zz in (1, 2) else None
        )
        inward = lambda part: permute(
            part, lambda gg, mm, zz: (gg, mm, zz ^ 3) if zz in (1, 2) else None
        )
        locked = lambda *parts: lax.optimization_barrier(parts)
        stage1 = lambda piece: (pair(piece), inward(piece), over(piece))
        stage2 = lambda one, inner: (inward(one), outward(inner), over(one))
        stage3 = lambda middle, two: (outward(middle), over(two))

        a = pieces[0]
        a_one, a_inner, a_far0 = locked(*stage1(a))
        own = after(tokens[0], messages[2], messages[3])
        across = to_member(own, 2)
        b = after(pieces[1], a_one)
        b_one, b_inner, b_far0 = locked(*stage1(b))
        a_middle, a_outer, a_far1 = locked(*stage2(a_one, a_inner))
        b_middle, b_outer, b_far1 = locked(*stage2(b_one, b_inner))
        a_two = jnp.where(inside, a_inner, a_outer)
        a_inner, (a_last, a_far2) = inward(a_far1), stage3(a_middle, a_two)
        b_two = jnp.where(inside, b_inner, b_outer)
        b_last, b_far2 = stage3(b_middle, b_two)
        a_last, a_far2, a_middle, a_inner = locked(a_last, a_far2, a_middle, a_inner)
        a_three = jnp.where(inside, a_middle, a_last)
        books = [own, sibling]
        upper = [a, a_one, a_two, None, a_far0, a_far1]
        lower = [b, b_one, b_two, None, b_far0, b_far1]
        early = [(k, half) for half in range(2) for k in (0, 1, 2, 4, 5)]
        late = [(3, 0), (6, 0), (3, 1), (6, 1), (7, 0), (7, 1)]
        project((0, 1), early, late, (upper, lower), n_z)
        b_last, b_far2, b_middle, sums[0], sums[1], across = locked(
            b_last, b_far2, b_middle, sums[0], sums[1], after(across, a_last, a_far2)
        )
        books += [across, to_member(across, 1)]
        project((2, 3), early, late, (upper, lower), n_z)
        b_three = jnp.where(inside, b_middle, b_last)
        pieces = [a_three, a_far2, b_three, b_far2]
        outer_kv, outer_q = [outward(a_inner[:, at]) for at in (slice(0, cut), slice(cut, None))]
        inner = a_inner
        finish = lambda at, *others: over(after(b_three[:, at], *others))
    else:
        across = to_member(tokens[0], 2)
        books = [tokens[0], sibling, across, to_member(across, 1)]
        full = gathered(jnp.concatenate(pieces, axis=0))
        deep = MEMBERS * HEAD_SIZE // 2
        upper, lower = [part[:deep] for part in full], [part[deep:] for part in full]
        late = [(n_pieces - 1, 0), (n_pieces - 1, 1)]
        early = [(k, half) for half in range(2) for k in range(n_pieces - 1)]
        late = [(n_pieces - 2, 1)] + late
        early.remove(late[0])
        for segs in ((0, 1), (2, 3)):
            project(segs, early, late, (upper, lower), 0)
        pieces = [lower[-2]]
        outer_kv, outer_q = upper[-1][:, :cut], upper[-1][:, cut:]
        inner = upper[-1]
        finish = lambda at, *others: lower[-1][:, at]

    halves = [slice(k * HEAD_SIZE, (k + 2) * HEAD_SIZE) for k in (0, 2, 4)]
    lower_kv, lower_q0 = finish(halves[0]), finish(halves[1])
    found = call(
        functools.partial(kv_body, len(late) + 1),
        [shape((length, 2 * HEAD_SIZE), bf16), shape((HEAD_SIZE, 2 * HEAD_SIZE), f32)] * MEMBERS
        + [shape((HEAD_SIZE, 2 * HEAD_SIZE), bf16)],
        [SMEM] + [VMEM] * (len(late) + 1 + 3 * MEMBERS),
        flops=2 * MEMBERS * length * len(late) * MEMBERS * HEAD_SIZE * HEAD_SIZE,
        scratch=[pltpu.VMEM((MEMBERS * HEAD_SIZE // 2, cut), bf16)],
    )(here, *pieces, inner, outer_kv, lower_kv, *sums, *lates, *messages)
    kvs, deltas, total = found[0:-1:2], found[1:-1:2], found[-1]

    base = None
    for a in range(1, n_groups):
        term = permute(total, lambda gg, mm, zz: (gg ^ a, mm, zz))
        if n_groups > 2:
            term = jnp.where((g ^ a) < g, term, 0).astype(f32)
        base = term if base is None else base + term

    lower_q1 = finish(halves[2], total)
    half = group // 2

    def local(segs, part, lower_q):
        found = call(
            functools.partial(local_body, len(segs), len(late) + 1, halves[1 + part].start, half),
            [shape((length, half * HEAD_SIZE), bf16), shape((length, half * HEAD_SIZE), f32)] * len(segs),
            [SMEM] + [VMEM] * (len(late) + 1 + 4 * len(segs)),
            flops=4 * len(segs) * length * length * half * HEAD_SIZE,
            scratch=[pltpu.VMEM((MEMBERS * HEAD_SIZE // 2, half * HEAD_SIZE), bf16)],
        )(here, *pieces, inner, outer_q, lower_q, *[one[s] for one in (kvs, messages, sums, lates) for s in segs])
        return {(s, part): (found[2 * at], found[2 * at + 1]) for at, s in enumerate(segs)}

    def mix(segs, parts, base, ready):
        keys = [(s, part) for s in segs for part in parts]
        return call(
            functools.partial(mix_body, segs, parts, group),
            [shape((length, half * HEAD_SIZE), bf16)] * len(keys),
            [SMEM] * 2 + [VMEM] * (1 + MEMBERS + len(segs) + 2 * len(keys)),
            flops=2 * len(keys) * length * half * HEAD_SIZE * HEAD_SIZE * 6,
        )(
            here, gate_bias, base, *deltas, *[messages[s] for s in segs],
            *[ready[key][0] for key in keys], *[ready[key][1] for key in keys],
        )

    ready = local((2, 3), 0, lower_q0)
    base = after(base, *ready[2, 0])
    two0, three0 = mix((2, 3), (0,), base, ready)
    ready |= local((2, 3), 1, after(lower_q1, two0, three0))
    two1, three1 = mix((2, 3), (1,), base, ready)
    ready |= local((1, 0), 0, after(lower_q0, two1, three1))
    ready |= local((1, 0), 1, after(lower_q1, two1, three1))
    one0, one1, mine0, mine1 = mix((1, 0), (0, 1), after(base, two1, three1), ready)
    parts = {(0, 0): mine0, (0, 1): mine1}
    for k, mixed in ((1, (one0, one1)), (2, (two0, two1)), (3, (three0, three1))):
        for c in range(2):
            parts[k, c] = to_member(mixed[c], k)
    last = [(1, 0), (1, 1)]
    first = [key for key in parts if key not in last]
    out_shape = shape((length, w_query.shape[1]), bf16)
    (output,) = call(
        functools.partial(assemble_body, first), [out_shape], [SMEM] + [VMEM] * len(first)
    )(here, *[parts[key] for key in first])
    output = pl.pallas_call(
        functools.partial(finish_body, last),
        out_shape=out_shape,
        in_specs=[SMEM] + [VMEM] * len(last) + [ANY],
        out_specs=ANY,
        scratch_shapes=[pltpu.SemaphoreType.DMA((len(last),))],
        input_output_aliases={1 + len(last): 0},
        cost_estimate=pl.CostEstimate(flops=0, bytes_accessed=1 << 20, transcendentals=0),
    )(here, *[parts[key] for key in last], output)
    return output[None]


def solution(mesh):
    in_specs = (
        P("fsdp", "seg", None),
        P(("seg", "fsdp"), None),
        P(("seg", "fsdp"), None),
        P(("seg", "fsdp"), None),
        P(),
        P("fsdp", "seg", None, None),
        P("fsdp", "seg"),
    )
    out_specs = P("fsdp", "seg", None)
    body = functools.partial(shards, (mesh.shape["seg"], mesh.shape["fsdp"]))
    return jax.shard_map(body, mesh=mesh, in_specs=in_specs, out_specs=out_specs, check_vma=False)
```

```python
import functools

import jax
import jax.numpy as jnp
from jax import lax
from jax.experimental import pallas as pl
from jax.experimental.pallas import tpu as pltpu
from jax.sharding import PartitionSpec as P

HEAD_SIZE = 128
BLK = 128
MEMBERS = 4
META_ROWS = 16
HALF = META_ROWS // 2
AXES = ("seg", "fsdp")

VMEM = pl.BlockSpec(memory_space=pltpu.VMEM)
SMEM = pl.BlockSpec(memory_space=pltpu.SMEM)
ANY = pl.BlockSpec(memory_space=pl.ANY)
HBM = pl.BlockSpec(memory_space=pltpu.HBM)


def call(body, outs, in_specs, flops=0, scratch=(), out_spec=VMEM, limit=16 << 20, moved=4 << 20):
    return pl.pallas_call(
        body,
        out_shape=outs,
        in_specs=in_specs,
        out_specs=[out_spec] * len(outs),
        scratch_shapes=list(scratch),
        compiler_params=pltpu.CompilerParams(vmem_limit_bytes=limit),
        cost_estimate=pl.CostEstimate(flops=flops, bytes_accessed=moved, transcendentals=0),
    )


def aligned(offset):
    return pl.multiple_of(offset, HEAD_SIZE)


def pack_body(group, here_ref, valid_ref, mask_ref, wq_ref, wk_ref, wv_ref, *outs):
    rows, wide = wk_ref.shape[0], group * HEAD_SIZE
    row = lax.broadcasted_iota(jnp.int32, (META_ROWS, outs[0].shape[1]), 0)
    facts = jnp.where(row < HALF, valid_ref[0, 0], mask_ref[0, 0, 1, 0])
    facts = facts.astype(jnp.float32).astype(jnp.bfloat16)
    for k, out, first in ((2, outs[2], 0), (3, outs[2], rows), (0, outs[0], 0), (1, outs[1], 0)):
        head = here_ref[1] ^ k
        at, to = aligned(head * HEAD_SIZE), slice(first, first + rows)
        out[to, :HEAD_SIZE] = wk_ref[:, pl.ds(at, HEAD_SIZE)]
        out[to, HEAD_SIZE : 2 * HEAD_SIZE] = wv_ref[:, pl.ds(at, HEAD_SIZE)]
        out[to, 2 * HEAD_SIZE :] = wq_ref[:, pl.ds(aligned(head * wide), wide)]
    for out in outs:
        out[out.shape[0] - META_ROWS :, :] = facts


def columns_of(tokens_ref, here_ref, piece, half, line):
    deep = MEMBERS * HEAD_SIZE // 2
    if not line:
        return tokens_ref[:, pl.ds((2 * piece + half) * deep, deep)]
    g, m, z = here_ref[0] ^ (piece // line), here_ref[1], here_ref[2]
    inside = (z == 1) | (z == 2)
    step = piece % line
    if step < 2:
        z = z ^ step
    else:
        z = jnp.where(inside, z ^ (5 - step), z ^ step)
    parts = [
        tokens_ref[:, pl.ds(aligned(((g * MEMBERS + (m ^ k)) * line + z) * HEAD_SIZE), HEAD_SIZE)]
        for k in (2 * half, 2 * half + 1)
    ]
    return jnp.concatenate(parts, axis=1)


def facts_of(message_ref):
    rows = message_ref.shape[0] - META_ROWS
    facts = message_ref[rows:, : 2 * HEAD_SIZE].astype(jnp.float32)
    return facts[0:1, :], facts[HALF : HALF + 1, :]


def iota(shape, dimension):
    return lax.broadcasted_iota(jnp.int32, shape, dimension).astype(jnp.float32)


def project_body(early, late, line, here_ref, *refs):
    tokens, pieces, outs = refs[:2], refs[2 : 2 + len(early)], refs[2 + len(early) :]
    length = tokens[0].shape[0]
    total = None
    for place, piece in zip(early, pieces):
        columns = jnp.concatenate([columns_of(one, here_ref, *place, line) for one in tokens], axis=0)
        term = jnp.dot(columns, piece[...], preferred_element_type=jnp.float32)
        total = term if total is None else total + term
    for n in range(2):
        outs[n][...] = total[n * length : (n + 1) * length]
        for k, place in enumerate(late):
            columns = columns_of(tokens[n], here_ref, *place, line)
            deep = columns.shape[1]
            outs[2 + n][:, k * deep : (k + 1) * deep] = columns


def sigma_plus(v):
    return jnp.where(v > 0, v + 1.0, jnp.exp(jnp.minimum(v, 0.0)))


def split(values):
    high = values.astype(jnp.bfloat16)
    return high, (values - high.astype(jnp.float32)).astype(jnp.bfloat16)


def late_rows(here_ref, chosen_ref, start, width, *pieces):
    *whole, inner, outer, part = pieces
    lost = inner.shape[1] - outer.shape[1] if start else 0
    inside = (here_ref[2] == 1) | (here_ref[2] == 2)

    @pl.when(inside)
    def _():
        chosen_ref[...] = inner[:, start : start + width]

    @pl.when(jnp.logical_not(inside))
    def _():
        chosen_ref[...] = outer[:, start - lost : start - lost + width]

    rows = [piece[:, start : start + width] for piece in whole]
    return jnp.concatenate(rows + [chosen_ref[...], part[...]], axis=0)


def kv_body(n_late, here_ref, *refs):
    pieces, refs, chosen_ref = refs[:n_late], refs[n_late:-1], refs[-1]
    sums, lates, messages = refs[:MEMBERS], refs[MEMBERS : 2 * MEMBERS], refs[2 * MEMBERS : 3 * MEMBERS]
    outs = refs[3 * MEMBERS :]
    rows = late_rows(here_ref, chosen_ref, 0, 2 * HEAD_SIZE, *pieces)
    kvs = []
    for seg in range(MEMBERS):
        total = sums[seg][:, : 2 * HEAD_SIZE]
        total += jnp.dot(lates[seg][...], rows, preferred_element_type=jnp.float32)
        kvs.append(total.astype(jnp.bfloat16))
        outs[2 * seg][...] = kvs[seg]
    whole = None
    for seg, kv in enumerate(kvs):
        length = kv.shape[0]
        valid, _ = facts_of(messages[seg])
        keys = kv[:, :HEAD_SIZE].astype(jnp.float32)
        live = iota((length, HEAD_SIZE), 0) < valid[:, :HEAD_SIZE]
        sig = jnp.where(live, sigma_plus(keys), 0.0)
        wide = jnp.concatenate(
            [kv[:, HEAD_SIZE:], jnp.ones((length, HEAD_SIZE), jnp.bfloat16)], axis=1
        )
        high, low = split(sig)
        over = (((0,), (0,)), ((), ()))
        delta = lax.dot_general(high, wide, over, preferred_element_type=jnp.float32)
        delta += lax.dot_general(low, wide, over, preferred_element_type=jnp.float32)
        outs[2 * seg + 1][...] = delta
        whole = delta if whole is None else whole + delta
    outs[-1][...] = whole.astype(jnp.bfloat16)


def local_body(n, n_late, start, heads, here_ref, *refs):
    pieces, refs, chosen_ref = refs[:n_late], refs[n_late:-1], refs[-1]
    kvs, messages, sums, lates, outs = [refs[k * n : (k + 1) * n] for k in range(4)] + [refs[4 * n :]]
    rows = late_rows(here_ref, chosen_ref, start, heads * HEAD_SIZE, *pieces)
    columns = slice(start, start + heads * HEAD_SIZE)
    queries = []
    for at in range(n):
        total = sums[at][:, columns] + jnp.dot(
            lates[at][...], rows, preferred_element_type=jnp.float32
        )
        queries.append(total.astype(jnp.bfloat16))
        outs[2 * at][...] = queries[at]
    work = [(at, block) for at in range(n) for block in range(queries[0].shape[0] // BLK)]
    span = lambda block: slice(block * BLK, (block + 1) * BLK)
    scores = []
    for at, block in work:
        stacked = jnp.concatenate(
            [queries[at][span(block), h * HEAD_SIZE : (h + 1) * HEAD_SIZE] for h in range(heads)], axis=0
        )
        keys = kvs[at][0 : (block + 1) * BLK, :HEAD_SIZE]
        scores.append(
            lax.dot_general(
                stacked, keys, (((1,), (1,)), ((), ())), preferred_element_type=jnp.float32
            )
        )
    weights = []
    for (at, block), score in zip(work, scores):
        width = (block + 1) * BLK
        valid, seen = facts_of(messages[at])
        i, j = iota((BLK, width), 0) + block * BLK, iota((BLK, width), 1)
        limit = valid[:, :width]
        if block:
            limit = jnp.where((j[0:1] >= block * BLK) | (seen[:, :width] > 0), limit, 0.0)
        allowed = (j <= i) & (j < limit)
        masked = jnp.concatenate(
            [jnp.where(allowed, score[span(h)] * HEAD_SIZE ** (-0.5), -1e30) for h in range(heads)],
            axis=0,
        )
        top = jnp.max(masked, axis=-1, keepdims=True)
        expo = jnp.exp(masked - top)
        total = jnp.maximum(jnp.sum(expo, axis=-1, keepdims=True), 1.0)
        weights.append((expo * (1.0 / total)).astype(jnp.bfloat16))
    for (at, block), weight in zip(work, weights):
        values = kvs[at][0 : (block + 1) * BLK, HEAD_SIZE:]
        local = jnp.dot(weight, values, preferred_element_type=jnp.float32)
        for h in range(heads):
            outs[2 * at + 1][span(block), h * HEAD_SIZE : (h + 1) * HEAD_SIZE] = local[span(h)]


def mix_body(segs, parts, group, here_ref, gate_ref, base_ref, *refs):
    deltas, messages, refs = refs[:MEMBERS], refs[MEMBERS : MEMBERS + len(segs)], refs[MEMBERS + len(segs) :]
    n = len(segs) * len(parts)
    queries, locals_, outs = refs[:n], refs[n : 2 * n], refs[2 * n :]
    me = here_ref[1]
    heads = queries[0].shape[1] // HEAD_SIZE
    length = queries[0].shape[0]
    work = [(at, p, h) for at in range(len(segs)) for p in range(len(parts)) for h in range(heads)]
    memories = []
    for seg in segs:
        memory = jnp.where(here_ref[3] > 0, 1.0, 0.0) * base_ref[...].astype(jnp.float32)
        for other in range(MEMBERS):
            if other != seg:
                earlier = jnp.where((me ^ other) < (me ^ seg), 1.0, 0.0)
                memory = memory + earlier * deltas[other][...]
        memories.append(split(memory))
    columns = lambda h: slice(h * HEAD_SIZE, (h + 1) * HEAD_SIZE)
    numers = []
    for at, p, h in work:
        mem_high, mem_low = memories[at]
        high, low = split(sigma_plus(queries[at * len(parts) + p][:, columns(h)].astype(jnp.float32)))
        numer = jnp.dot(high, mem_high, preferred_element_type=jnp.float32)
        numer += jnp.dot(high, mem_low, preferred_element_type=jnp.float32)
        numer += jnp.dot(low, mem_high, preferred_element_type=jnp.float32)
        numers.append(numer)
    for (at, p, h), numer in zip(work, numers):
        valid, _ = facts_of(messages[at])
        live = iota((length, HEAD_SIZE), 0) < valid[:, :HEAD_SIZE]
        retrieved = numer[:, :HEAD_SIZE] / (numer[:, HEAD_SIZE:] + 1.0)
        logit = jnp.full((1, HEAD_SIZE), gate_ref[me * group + parts[p] * heads + h], jnp.float32)
        gate = 1.0 / (1.0 + jnp.exp(-logit))
        mixed = gate * retrieved + (1.0 - gate) * locals_[at * len(parts) + p][:, columns(h)]
        outs[at * len(parts) + p][:, columns(h)] = jnp.where(live, mixed, 0.0).astype(jnp.bfloat16)


def assemble_body(counts, here_ref, *refs):
    parts, out = list(refs[:-1]), refs[-1]
    width = out.shape[1] // MEMBERS
    for k, count in enumerate(counts):
        for c in range(count):
            at = (here_ref[1] ^ k) * width + c * (width // count)
            out[:, pl.ds(aligned(at), width // count)] = parts.pop(0)[...]


def stack_body(first, upper_ref, lower_ref, out_ref):
    rows = out_ref.shape[0] // 2
    out_ref[:rows] = upper_ref[:rows]
    out_ref[rows:] = lower_ref[first : first + rows]


def gate_body(here_ref, *refs):
    out = refs[-1]
    for n in range(out.shape[0]):
        out[n] = here_ref[n]


def after(array, *others):
    return lax.optimization_barrier((array,) + others)[0]


def shards(sizes, tokens, w_query, w_key, value_weight, gate_bias, block_mask, valid_len):
    n_seg, n_z = sizes
    n_groups = n_seg // MEMBERS
    heads_kv = w_key.shape[1] // HEAD_SIZE
    group = w_query.shape[1] // w_key.shape[1]
    rows = w_query.shape[0]
    length, width = tokens.shape[1], tokens.shape[2]
    assert heads_kv == MEMBERS and group == 4 and length == 2 * BLK
    seg = lax.axis_index("seg")
    z = lax.axis_index("fsdp")
    g, m = seg // MEMBERS, seg % MEMBERS
    here = jnp.stack([g, m, z, g if n_groups == 2 else 1]).astype(jnp.int32)
    bf16, f32 = jnp.bfloat16, jnp.float32
    shape = jax.ShapeDtypeStruct

    def permute(array, to):
        pairs = []
        for gg in range(n_groups):
            for mm in range(MEMBERS):
                for zz in range(n_z):
                    target = to(gg, mm, zz)
                    if target is not None:
                        index = lambda t: (t[0] * MEMBERS + t[1]) * n_z + t[2]
                        pairs.append((index((gg, mm, zz)), index(target)))
        return lax.ppermute(array, AXES, pairs)

    def to_member(array, k):
        return permute(array, lambda gg, mm, zz: (gg, mm ^ k, zz))

    wide = (2 + group) * HEAD_SIZE
    packed = call(
        functools.partial(pack_body, group),
        [shape((n * rows + META_ROWS, wide), bf16) for n in (1, 1, 2)],
        [SMEM] * 3 + [VMEM] * 3,
    )(here, valid_len, block_mask, w_query, w_key, value_weight)
    messages = [packed[0], to_member(packed[1], 1), to_member(packed[2], 2)]

    def gathered(piece):
        index = lambda gg, mm, zz: (gg * MEMBERS + mm) * n_z + zz
        everything = lax.all_gather(
            piece,
            AXES,
            axis_index_groups=[
                [index(gg, mm, zz) for gg in range(n_groups) for zz in range(n_z)]
                for mm in range(MEMBERS)
            ],
        )
        columns = piece.shape[1]
        natural = everything.reshape(n_groups, n_z, MEMBERS, rows, columns)
        members = jnp.arange(MEMBERS, dtype=jnp.int32) ^ m
        natural = jnp.take(natural, members, axis=2).transpose(0, 2, 1, 3, 4)
        return list(natural.reshape(-1, MEMBERS * HEAD_SIZE, columns))

    stack = lambda first, *pair: call(
        functools.partial(stack_body, first), [shape((2 * rows, wide), bf16)], [VMEM] * 2, moved=1 << 20
    )(*pair)[0]
    n_pieces = width // (MEMBERS * HEAD_SIZE)
    sums, lates = [None] * MEMBERS, [None] * MEMBERS

    def project(segs, early, late, halves, line):
        deep = MEMBERS * HEAD_SIZE // 2
        found = call(
            functools.partial(project_body, early, late, line),
            [shape((length, wide), f32)] * 2 + [shape((length, len(late) * deep), bf16)] * 2,
            [SMEM] + [VMEM] * (2 + len(early)),
            flops=2 * 2 * length * len(early) * deep * wide,
        )(here, *[books[s] for s in segs], *[halves[half][piece] for piece, half in early])
        for at, s in enumerate(segs):
            sums[s], lates[s] = found[at], found[2 + at]

    cut = 2 * HEAD_SIZE
    if n_groups == 2 and n_z == 4:
        assert rows == HEAD_SIZE
        inside = (z == 1) | (z == 2)
        over = lambda part: permute(part, lambda gg, mm, zz: (gg ^ 1, mm, zz))
        pair = lambda part: permute(part, lambda gg, mm, zz: (gg, mm, zz ^ 1))
        outward = lambda part: permute(
            part, lambda gg, mm, zz: (gg, mm, zz ^ 1) if zz in (1, 2) else None
        )
        inward = lambda part: permute(
            part, lambda gg, mm, zz: (gg, mm, zz ^ 3) if zz in (1, 2) else None
        )
        locked = lambda *parts: lax.optimization_barrier(parts)
        stage1 = lambda piece: (pair(piece), inward(piece), over(piece))
        stage2 = lambda one, inner: (inward(one), outward(inner), over(one))
        stage3 = lambda middle, two: (outward(middle), over(two))

        a = stack(0, *messages[:2])
        a_one, a_inner, a_far0 = locked(*stage1(a))
        messages.append(to_member(after(messages[2], a_one), 1))
        own = after(tokens[0], messages[2], a_one)
        across = to_member(own, 2)
        b, sibling = locked(stack(rows, *messages[2:]), to_member(own, 1))
        b_one, b_inner, b_far0 = locked(*stage1(b))
        a_middle, a_outer, a_far1 = locked(*stage2(a_one, a_inner))
        b_middle, b_outer, b_far1 = locked(*stage2(b_one, b_inner))
        a_two = jnp.where(inside, a_inner, a_outer)
        a_inner, (a_last, a_far2) = inward(a_far1), stage3(a_middle, a_two)
        b_two = jnp.where(inside, b_inner, b_outer)
        b_last, b_far2 = stage3(b_middle, b_two)
        a_last, a_far2, a_middle, a_inner = locked(a_last, a_far2, a_middle, a_inner)
        a_three = jnp.where(inside, a_middle, a_last)
        books = [own, sibling]
        upper = [a, a_one, a_two, None, a_far0, a_far1]
        lower = [b, b_one, b_two, None, b_far0, b_far1]
        early = [(k, half) for half in range(2) for k in (0, 1, 2, 4, 5)]
        late = [(3, 0), (6, 0), (3, 1), (6, 1), (7, 0), (7, 1)]
        project((0, 1), early, late, (upper, lower), n_z)
        b_last, b_far2, b_middle, sums[0], sums[1], across = locked(
            b_last, b_far2, b_middle, sums[0], sums[1], after(across, a_last, a_far2)
        )
        books += [across, to_member(across, 1)]
        project((2, 3), early, late, (upper, lower), n_z)
        b_three = jnp.where(inside, b_middle, b_last)
        pieces = [a_three, a_far2, b_three, b_far2]
        outer_kv, outer_q = [outward(a_inner[:, at]) for at in (slice(0, cut), slice(cut, None))]
        inner = a_inner
        finish = lambda at: over(b_three[:, at])
    else:
        across, sibling = to_member(tokens[0], 2), to_member(tokens[0], 1)
        books = [tokens[0], sibling, across, to_member(across, 1)]
        messages.append(to_member(messages[2], 1))
        full = gathered(jnp.concatenate([stack(0, *messages[:2]), stack(rows, *messages[2:])], axis=0))
        deep = MEMBERS * HEAD_SIZE // 2
        upper, lower = [part[:deep] for part in full], [part[deep:] for part in full]
        late = [(n_pieces - 1, 0), (n_pieces - 1, 1)]
        early = [(k, half) for half in range(2) for k in range(n_pieces - 1)]
        late = [(n_pieces - 2, 1)] + late
        early.remove(late[0])
        for segs in ((0, 1), (2, 3)):
            project(segs, early, late, (upper, lower), 0)
        pieces = [lower[-2]]
        outer_kv, outer_q = upper[-1][:, :cut], upper[-1][:, cut:]
        inner = upper[-1]
        finish = lambda at: lower[-1][:, at]

    halves = [slice(k * HEAD_SIZE, (k + 2) * HEAD_SIZE) for k in (0, 2, 4)]
    lower_kv, lower_q0, lower_q1 = [finish(at) for at in halves]
    found = call(
        functools.partial(kv_body, len(late) + 1),
        [shape((length, 2 * HEAD_SIZE), bf16), shape((HEAD_SIZE, 2 * HEAD_SIZE), f32)] * MEMBERS
        + [shape((HEAD_SIZE, 2 * HEAD_SIZE), bf16)],
        [SMEM] + [VMEM] * (len(late) + 1 + 3 * MEMBERS),
        flops=2 * MEMBERS * length * len(late) * MEMBERS * HEAD_SIZE * HEAD_SIZE,
        scratch=[pltpu.VMEM((MEMBERS * HEAD_SIZE // 2, cut), bf16)],
    )(here, *pieces, inner, outer_kv, lower_kv, *sums, *lates, *messages)
    kvs, deltas, total = found[0:-1:2], found[1:-1:2], found[-1]

    base = None
    for a in range(1, n_groups):
        term = permute(total, lambda gg, mm, zz: (gg ^ a, mm, zz))
        if n_groups > 2:
            term = jnp.where((g ^ a) < g, term, 0).astype(f32)
        base = term if base is None else base + term

    half = group // 2

    def local(segs, part, lower_q):
        found = call(
            functools.partial(local_body, len(segs), len(late) + 1, halves[1 + part].start, half),
            [shape((length, half * HEAD_SIZE), bf16), shape((length, half * HEAD_SIZE), f32)] * len(segs),
            [SMEM] + [VMEM] * (len(late) + 1 + 4 * len(segs)),
            flops=4 * len(segs) * length * length * half * HEAD_SIZE,
            scratch=[pltpu.VMEM((MEMBERS * HEAD_SIZE // 2, half * HEAD_SIZE), bf16)],
        )(here, *pieces, inner, outer_q, lower_q, *[one[s] for one in (kvs, messages, sums, lates) for s in segs])
        return {(s, part): (found[2 * at], found[2 * at + 1]) for at, s in enumerate(segs)}

    def mix(segs, parts, base, ready):
        keys = [(s, part) for s in segs for part in parts]
        return call(
            functools.partial(mix_body, segs, parts, group),
            [shape((length, half * HEAD_SIZE), bf16)] * len(keys),
            [SMEM] * 2 + [VMEM] * (1 + MEMBERS + len(segs) + 2 * len(keys)),
            flops=2 * len(keys) * length * half * HEAD_SIZE * HEAD_SIZE * 6,
        )(
            here, gate_bias, base, *deltas, *[messages[s] for s in segs],
            *[ready[key][0] for key in keys], *[ready[key][1] for key in keys],
        )

    ready = local((2, 3, 1, 0), 0, lower_q0)
    base = after(base, *ready[2, 0])
    two0, three0 = mix((2, 3), (0,), base, ready)
    ready |= local((2, 3), 1, after(lower_q1, two0, three0))
    two1, three1 = mix((2, 3), (1,), base, ready)
    ready |= local((1, 0), 1, after(lower_q1, two1, three1))
    one0, one1, mine0, mine1 = mix((1, 0), (0, 1), after(base, two1, three1), ready)
    sent = [mine0, mine1]
    for k, parts in ((1, (one0, one1)), (2, (two0, two1)), (3, (three0, three1))):
        sent += [to_member(part, k) for part in parts]
    far = sent[4:]
    (there,) = call(
        gate_body, [shape((4,), jnp.int32)], [SMEM] + [ANY] * len(far), out_spec=SMEM, moved=16 << 20
    )(here, *far)
    (output,) = call(
        functools.partial(assemble_body, (2,) * MEMBERS),
        [shape((length, w_query.shape[1]), bf16)],
        [SMEM] + [VMEM] * len(sent),
    )(there, *sent)
    return output[None]


def solution(mesh):
    in_specs = (
        P("fsdp", "seg", None),
        P(("seg", "fsdp"), None),
        P(("seg", "fsdp"), None),
        P(("seg", "fsdp"), None),
        P(),
        P("fsdp", "seg", None, None),
        P("fsdp", "seg"),
    )
    out_specs = P("fsdp", "seg", None)
    body = functools.partial(shards, (mesh.shape["seg"], mesh.shape["fsdp"]))
    return jax.shard_map(body, mesh=mesh, in_specs=in_specs, out_specs=out_specs, check_vma=False)
```

```python
import functools

import jax
import jax.numpy as jnp
from jax import lax
from jax.experimental import pallas as pl
from jax.experimental.pallas import tpu as pltpu
from jax.sharding import PartitionSpec as P

HEAD_SIZE = 128
BLK = 128
MEMBERS = 4
META_ROWS = 16
HALF = META_ROWS // 2
AXES = ("seg", "fsdp")

VMEM = pl.BlockSpec(memory_space=pltpu.VMEM)
SMEM = pl.BlockSpec(memory_space=pltpu.SMEM)
ANY = pl.BlockSpec(memory_space=pl.ANY)
HBM = pl.BlockSpec(memory_space=pltpu.HBM)


def call(body, outs, in_specs, flops=0, scratch=(), out_spec=VMEM, limit=16 << 20, moved=4 << 20):
    return pl.pallas_call(
        body,
        out_shape=outs,
        in_specs=in_specs,
        out_specs=[out_spec] * len(outs),
        scratch_shapes=list(scratch),
        compiler_params=pltpu.CompilerParams(vmem_limit_bytes=limit),
        cost_estimate=pl.CostEstimate(flops=flops, bytes_accessed=moved, transcendentals=0),
    )


def aligned(offset):
    return pl.multiple_of(offset, HEAD_SIZE)


def pack_body(group, here_ref, valid_ref, mask_ref, wq_ref, wk_ref, wv_ref, *outs):
    rows, wide = wk_ref.shape[0], group * HEAD_SIZE
    row = lax.broadcasted_iota(jnp.int32, (META_ROWS, outs[0].shape[1]), 0)
    facts = jnp.where(row < HALF, valid_ref[0, 0], mask_ref[0, 0, 1, 0])
    facts = facts.astype(jnp.float32).astype(jnp.bfloat16)
    for k, out, first in ((2, outs[2], 0), (3, outs[2], rows), (0, outs[0], 0), (1, outs[1], 0)):
        head = here_ref[1] ^ k
        at, to = aligned(head * HEAD_SIZE), slice(first, first + rows)
        out[to, :HEAD_SIZE] = wk_ref[:, pl.ds(at, HEAD_SIZE)]
        out[to, HEAD_SIZE : 2 * HEAD_SIZE] = wv_ref[:, pl.ds(at, HEAD_SIZE)]
        out[to, 2 * HEAD_SIZE :] = wq_ref[:, pl.ds(aligned(head * wide), wide)]
    for out in outs:
        out[out.shape[0] - META_ROWS :, :] = facts


def columns_of(tokens_ref, here_ref, piece, half, line):
    deep = MEMBERS * HEAD_SIZE // 2
    if not line:
        return tokens_ref[:, pl.ds((2 * piece + half) * deep, deep)]
    g, m, z = here_ref[0] ^ (piece // line), here_ref[1], here_ref[2]
    inside = (z == 1) | (z == 2)
    step = piece % line
    if step < 2:
        z = z ^ step
    else:
        z = jnp.where(inside, z ^ (5 - step), z ^ step)
    parts = [
        tokens_ref[:, pl.ds(aligned(((g * MEMBERS + (m ^ k)) * line + z) * HEAD_SIZE), HEAD_SIZE)]
        for k in (2 * half, 2 * half + 1)
    ]
    return jnp.concatenate(parts, axis=1)


def facts_of(message_ref):
    rows = message_ref.shape[0] - META_ROWS
    facts = message_ref[rows:, : 2 * HEAD_SIZE].astype(jnp.float32)
    return facts[0:1, :], facts[HALF : HALF + 1, :]


def iota(shape, dimension):
    return lax.broadcasted_iota(jnp.int32, shape, dimension).astype(jnp.float32)


def project_body(early, late, line, far, here_ref, *refs):
    if far:
        *refs, books_ref, sems = refs
        copies = [
            pltpu.make_async_copy(refs[0].at[here_ref[1] ^ k], books_ref.at[n], sems.at[n])
            for n, k in enumerate(far)
        ]
        for one in copies:
            one.start()
        for one in copies:
            one.wait()
        refs = [books_ref.at[0], books_ref.at[1], *refs[1:]]
    tokens, pieces, outs = refs[:2], refs[2 : 2 + len(early)], refs[2 + len(early) :]
    length = tokens[0].shape[0]
    total = None
    for place, piece in zip(early, pieces):
        columns = jnp.concatenate([columns_of(one, here_ref, *place, line) for one in tokens], axis=0)
        term = jnp.dot(columns, piece[...], preferred_element_type=jnp.float32)
        total = term if total is None else total + term
    for n in range(2):
        outs[n][...] = total[n * length : (n + 1) * length]
        for k, place in enumerate(late):
            columns = columns_of(tokens[n], here_ref, *place, line)
            deep = columns.shape[1]
            outs[2 + n][:, k * deep : (k + 1) * deep] = columns


def sigma_plus(v):
    return jnp.where(v > 0, v + 1.0, jnp.exp(jnp.minimum(v, 0.0)))


def split(values):
    high = values.astype(jnp.bfloat16)
    return high, (values - high.astype(jnp.float32)).astype(jnp.bfloat16)


def late_rows(here_ref, chosen_ref, start, width, *pieces):
    *whole, inner, outer, part = pieces
    lost = inner.shape[1] - outer.shape[1] if start else 0
    inside = (here_ref[2] == 1) | (here_ref[2] == 2)

    @pl.when(inside)
    def _():
        chosen_ref[...] = inner[:, start : start + width]

    @pl.when(jnp.logical_not(inside))
    def _():
        chosen_ref[...] = outer[:, start - lost : start - lost + width]

    rows = [piece[:, start : start + width] for piece in whole]
    return jnp.concatenate(rows + [chosen_ref[...], part[...]], axis=0)


def kv_body(n_late, here_ref, *refs):
    pieces, refs, chosen_ref = refs[:n_late], refs[n_late:-1], refs[-1]
    sums, lates, messages = refs[:MEMBERS], refs[MEMBERS : 2 * MEMBERS], refs[2 * MEMBERS : 3 * MEMBERS]
    outs = refs[3 * MEMBERS :]
    rows = late_rows(here_ref, chosen_ref, 0, 2 * HEAD_SIZE, *pieces)
    kvs = []
    for seg in range(MEMBERS):
        total = sums[seg][:, : 2 * HEAD_SIZE]
        total += jnp.dot(lates[seg][...], rows, preferred_element_type=jnp.float32)
        kvs.append(total.astype(jnp.bfloat16))
        outs[2 * seg][...] = kvs[seg]
    whole = None
    for seg, kv in enumerate(kvs):
        length = kv.shape[0]
        valid, _ = facts_of(messages[seg])
        keys = kv[:, :HEAD_SIZE].astype(jnp.float32)
        live = iota((length, HEAD_SIZE), 0) < valid[:, :HEAD_SIZE]
        sig = jnp.where(live, sigma_plus(keys), 0.0)
        wide = jnp.concatenate(
            [kv[:, HEAD_SIZE:], jnp.ones((length, HEAD_SIZE), jnp.bfloat16)], axis=1
        )
        high, low = split(sig)
        over = (((0,), (0,)), ((), ()))
        delta = lax.dot_general(high, wide, over, preferred_element_type=jnp.float32)
        delta += lax.dot_general(low, wide, over, preferred_element_type=jnp.float32)
        outs[2 * seg + 1][...] = delta
        whole = delta if whole is None else whole + delta
    outs[-1][...] = whole.astype(jnp.bfloat16)


def local_body(n, n_late, start, heads, here_ref, *refs):
    pieces, refs, chosen_ref = refs[:n_late], refs[n_late:-1], refs[-1]
    kvs, messages, sums, lates, outs = [refs[k * n : (k + 1) * n] for k in range(4)] + [refs[4 * n :]]
    rows = late_rows(here_ref, chosen_ref, start, heads * HEAD_SIZE, *pieces)
    columns = slice(start, start + heads * HEAD_SIZE)
    queries = []
    for at in range(n):
        total = sums[at][:, columns] + jnp.dot(
            lates[at][...], rows, preferred_element_type=jnp.float32
        )
        queries.append(total.astype(jnp.bfloat16))
        outs[2 * at][...] = queries[at]
    work = [(at, block) for at in range(n) for block in range(queries[0].shape[0] // BLK)]
    span = lambda block: slice(block * BLK, (block + 1) * BLK)
    scores = []
    for at, block in work:
        stacked = jnp.concatenate(
            [queries[at][span(block), h * HEAD_SIZE : (h + 1) * HEAD_SIZE] for h in range(heads)], axis=0
        )
        keys = kvs[at][0 : (block + 1) * BLK, :HEAD_SIZE]
        scores.append(
            lax.dot_general(
                stacked, keys, (((1,), (1,)), ((), ())), preferred_element_type=jnp.float32
            )
        )
    weights = []
    for (at, block), score in zip(work, scores):
        width = (block + 1) * BLK
        valid, seen = facts_of(messages[at])
        i, j = iota((BLK, width), 0) + block * BLK, iota((BLK, width), 1)
        limit = valid[:, :width]
        if block:
            limit = jnp.where((j[0:1] >= block * BLK) | (seen[:, :width] > 0), limit, 0.0)
        allowed = (j <= i) & (j < limit)
        masked = jnp.concatenate(
            [jnp.where(allowed, score[span(h)] * HEAD_SIZE ** (-0.5), -1e30) for h in range(heads)],
            axis=0,
        )
        top = jnp.max(masked, axis=-1, keepdims=True)
        expo = jnp.exp(masked - top)
        total = jnp.maximum(jnp.sum(expo, axis=-1, keepdims=True), 1.0)
        weights.append((expo * (1.0 / total)).astype(jnp.bfloat16))
    for (at, block), weight in zip(work, weights):
        values = kvs[at][0 : (block + 1) * BLK, HEAD_SIZE:]
        local = jnp.dot(weight, values, preferred_element_type=jnp.float32)
        for h in range(heads):
            outs[2 * at + 1][span(block), h * HEAD_SIZE : (h + 1) * HEAD_SIZE] = local[span(h)]


def mix_body(segs, parts, group, here_ref, gate_ref, base_ref, *refs):
    deltas, messages, refs = refs[:MEMBERS], refs[MEMBERS : MEMBERS + len(segs)], refs[MEMBERS + len(segs) :]
    n = len(segs) * len(parts)
    queries, locals_, outs = refs[:n], refs[n : 2 * n], refs[2 * n :]
    me = here_ref[1]
    heads = queries[0].shape[1] // HEAD_SIZE
    length = queries[0].shape[0]
    work = [(at, p, h) for at in range(len(segs)) for p in range(len(parts)) for h in range(heads)]
    memories = []
    for seg in segs:
        memory = jnp.where(here_ref[3] > 0, 1.0, 0.0) * base_ref[...].astype(jnp.float32)
        for other in range(MEMBERS):
            if other != seg:
                earlier = jnp.where((me ^ other) < (me ^ seg), 1.0, 0.0)
                memory = memory + earlier * deltas[other][...]
        memories.append(split(memory))
    columns = lambda h: slice(h * HEAD_SIZE, (h + 1) * HEAD_SIZE)
    numers = []
    for at, p, h in work:
        mem_high, mem_low = memories[at]
        high, low = split(sigma_plus(queries[at * len(parts) + p][:, columns(h)].astype(jnp.float32)))
        numer = jnp.dot(high, mem_high, preferred_element_type=jnp.float32)
        numer += jnp.dot(high, mem_low, preferred_element_type=jnp.float32)
        numer += jnp.dot(low, mem_high, preferred_element_type=jnp.float32)
        numers.append(numer)
    for (at, p, h), numer in zip(work, numers):
        valid, _ = facts_of(messages[at])
        live = iota((length, HEAD_SIZE), 0) < valid[:, :HEAD_SIZE]
        retrieved = numer[:, :HEAD_SIZE] / (numer[:, HEAD_SIZE:] + 1.0)
        logit = jnp.full((1, HEAD_SIZE), gate_ref[me * group + parts[p] * heads + h], jnp.float32)
        gate = 1.0 / (1.0 + jnp.exp(-logit))
        mixed = gate * retrieved + (1.0 - gate) * locals_[at * len(parts) + p][:, columns(h)]
        outs[at * len(parts) + p][:, columns(h)] = jnp.where(live, mixed, 0.0).astype(jnp.bfloat16)


def assemble_body(counts, here_ref, *refs):
    parts, out = list(refs[1:-1]), refs[-1]
    width = out.shape[1] // MEMBERS
    for k, count in enumerate(counts):
        for c in range(count):
            at = (here_ref[1] ^ k) * width + c * (width // count)
            out[:, pl.ds(aligned(at), width // count)] = parts.pop(0)[...]


def stack_body(first, upper_ref, lower_ref, out_ref):
    rows = out_ref.shape[0] // 2
    out_ref[:rows] = upper_ref[:rows]
    out_ref[rows:] = lower_ref[first : first + rows]


def gate_body(*refs):
    refs[-1][...] = jnp.zeros_like(refs[-1])


def after(array, *others):
    return lax.optimization_barrier((array,) + others)[0]


def shards(sizes, tokens, w_query, w_key, value_weight, gate_bias, block_mask, valid_len):
    n_seg, n_z = sizes
    n_groups = n_seg // MEMBERS
    heads_kv = w_key.shape[1] // HEAD_SIZE
    group = w_query.shape[1] // w_key.shape[1]
    rows = w_query.shape[0]
    length, width = tokens.shape[1], tokens.shape[2]
    assert heads_kv == MEMBERS and group == 4 and length == 2 * BLK
    seg = lax.axis_index("seg")
    z = lax.axis_index("fsdp")
    g, m = seg // MEMBERS, seg % MEMBERS
    here = jnp.stack([g, m, z, g if n_groups == 2 else 1]).astype(jnp.int32)
    bf16, f32 = jnp.bfloat16, jnp.float32
    shape = jax.ShapeDtypeStruct

    def permute(array, to):
        pairs = []
        for gg in range(n_groups):
            for mm in range(MEMBERS):
                for zz in range(n_z):
                    target = to(gg, mm, zz)
                    if target is not None:
                        index = lambda t: (t[0] * MEMBERS + t[1]) * n_z + t[2]
                        pairs.append((index((gg, mm, zz)), index(target)))
        return lax.ppermute(array, AXES, pairs)

    def to_member(array, k):
        return permute(array, lambda gg, mm, zz: (gg, mm ^ k, zz))

    wide = (2 + group) * HEAD_SIZE
    packed = call(
        functools.partial(pack_body, group),
        [shape((n * rows + META_ROWS, wide), bf16) for n in (1, 1, 2)],
        [SMEM] * 3 + [VMEM] * 3,
    )(here, valid_len, block_mask, w_query, w_key, value_weight)
    messages = [packed[0], to_member(packed[1], 1), to_member(packed[2], 2)]

    def gathered(piece):
        index = lambda gg, mm, zz: (gg * MEMBERS + mm) * n_z + zz
        everything = lax.all_gather(
            piece,
            AXES,
            axis_index_groups=[
                [index(gg, mm, zz) for gg in range(n_groups) for zz in range(n_z)]
                for mm in range(MEMBERS)
            ],
        )
        columns = piece.shape[1]
        natural = everything.reshape(n_groups, n_z, MEMBERS, rows, columns)
        members = jnp.arange(MEMBERS, dtype=jnp.int32) ^ m
        natural = jnp.take(natural, members, axis=2).transpose(0, 2, 1, 3, 4)
        return list(natural.reshape(-1, MEMBERS * HEAD_SIZE, columns))

    gather_tokens = lambda part: lax.all_gather(
        part,
        "seg",
        axis_index_groups=[[gg * MEMBERS + mm for mm in range(MEMBERS)] for gg in range(n_groups)],
    )
    stack = lambda first, *pair: call(
        functools.partial(stack_body, first), [shape((2 * rows, wide), bf16)], [VMEM] * 2, moved=1 << 20
    )(*pair)[0]
    n_pieces = width // (MEMBERS * HEAD_SIZE)
    sums, lates = [None] * MEMBERS, [None] * MEMBERS

    def project(segs, early, late, halves, line):
        far = segs if segs == (2, 3) else ()
        deep = MEMBERS * HEAD_SIZE // 2
        found = call(
            functools.partial(project_body, early, late, line, far),
            [shape((length, wide), f32)] * 2 + [shape((length, len(late) * deep), bf16)] * 2,
            [SMEM] + ([ANY] if far else [VMEM] * 2) + [VMEM] * len(early),
            flops=2 * 2 * length * len(early) * deep * wide,
            scratch=[pltpu.VMEM((2, length, width), bf16), pltpu.SemaphoreType.DMA((2,))] if far else (),
        )(here, *([group_tokens] if far else books), *[halves[half][piece] for piece, half in early])
        for at, s in enumerate(segs):
            sums[s], lates[s] = found[at], found[2 + at]

    cut = 2 * HEAD_SIZE
    if n_groups == 2 and n_z == 4:
        assert rows == HEAD_SIZE
        inside = (z == 1) | (z == 2)
        over = lambda part: permute(part, lambda gg, mm, zz: (gg ^ 1, mm, zz))
        pair = lambda part: permute(part, lambda gg, mm, zz: (gg, mm, zz ^ 1))
        outward = lambda part: permute(
            part, lambda gg, mm, zz: (gg, mm, zz ^ 1) if zz in (1, 2) else None
        )
        inward = lambda part: permute(
            part, lambda gg, mm, zz: (gg, mm, zz ^ 3) if zz in (1, 2) else None
        )
        locked = lambda *parts: lax.optimization_barrier(parts)
        stage1 = lambda piece: (pair(piece), inward(piece), over(piece))
        stage2 = lambda one, inner: (inward(one), outward(inner), over(one))
        stage3 = lambda middle, two: (outward(middle), over(two))

        a = stack(0, *messages[:2])
        messages.append(to_member(messages[2], 1))
        a, b, sibling, own = locked(
            a, stack(rows, *messages[2:]), to_member(tokens[0], 1), tokens[0]
        )
        group_tokens = gather_tokens(own)
        a_one, a_inner, a_far0 = locked(*stage1(a))
        b_one, b_inner, b_far0 = locked(*stage1(b))
        a_middle, a_outer, a_far1 = locked(*stage2(a_one, a_inner))
        b_middle, b_outer, b_far1 = locked(*stage2(b_one, b_inner))
        a_two = jnp.where(inside, a_inner, a_outer)
        a_inner, (a_last, a_far2) = inward(a_far1), stage3(a_middle, a_two)
        b_two = jnp.where(inside, b_inner, b_outer)
        b_last, b_far2 = stage3(b_middle, b_two)
        a_last, a_far2, a_middle, a_inner = locked(a_last, a_far2, a_middle, a_inner)
        a_three = jnp.where(inside, a_middle, a_last)
        books = [tokens[0], sibling]
        upper = [a, a_one, a_two, None, a_far0, a_far1]
        lower = [b, b_one, b_two, None, b_far0, b_far1]
        early = [(k, half) for half in range(2) for k in (0, 1, 2, 4, 5)]
        late = [(3, 0), (6, 0), (3, 1), (6, 1), (7, 0), (7, 1)]
        project((0, 1), early, late, (upper, lower), n_z)
        b_last, b_far2, b_middle, sums[0], sums[1] = locked(b_last, b_far2, b_middle, sums[0], sums[1])
        project((2, 3), early, late, (upper, lower), n_z)
        b_three = jnp.where(inside, b_middle, b_last)
        pieces = [a_three, a_far2, b_three, b_far2]
        outer_kv, outer_q = [outward(a_inner[:, at]) for at in (slice(0, cut), slice(cut, None))]
        inner = a_inner
        finish = lambda at: over(b_three[:, at])
    else:
        books = [tokens[0], to_member(tokens[0], 1)]
        group_tokens = gather_tokens(tokens[0])
        messages.append(to_member(messages[2], 1))
        full = gathered(jnp.concatenate([stack(0, *messages[:2]), stack(rows, *messages[2:])], axis=0))
        deep = MEMBERS * HEAD_SIZE // 2
        upper, lower = [part[:deep] for part in full], [part[deep:] for part in full]
        late = [(n_pieces - 1, 0), (n_pieces - 1, 1)]
        early = [(k, half) for half in range(2) for k in range(n_pieces - 1)]
        late = [(n_pieces - 2, 1)] + late
        early.remove(late[0])
        for segs in ((0, 1), (2, 3)):
            project(segs, early, late, (upper, lower), 0)
        pieces = [lower[-2]]
        outer_kv, outer_q = upper[-1][:, :cut], upper[-1][:, cut:]
        inner = upper[-1]
        finish = lambda at: lower[-1][:, at]

    halves = [slice(k * HEAD_SIZE, (k + 2) * HEAD_SIZE) for k in (0, 2, 4)]
    lower_kv, lower_q0, lower_q1 = [finish(at) for at in halves]
    found = call(
        functools.partial(kv_body, len(late) + 1),
        [shape((length, 2 * HEAD_SIZE), bf16), shape((HEAD_SIZE, 2 * HEAD_SIZE), f32)] * MEMBERS
        + [shape((HEAD_SIZE, 2 * HEAD_SIZE), bf16)],
        [SMEM] + [VMEM] * (len(late) + 1 + 3 * MEMBERS),
        flops=2 * MEMBERS * length * len(late) * MEMBERS * HEAD_SIZE * HEAD_SIZE,
        scratch=[pltpu.VMEM((MEMBERS * HEAD_SIZE // 2, cut), bf16)],
    )(here, *pieces, inner, outer_kv, lower_kv, *sums, *lates, *messages)
    kvs, deltas, total = found[0:-1:2], found[1:-1:2], found[-1]

    base = None
    for a in range(1, n_groups):
        term = permute(total, lambda gg, mm, zz: (gg ^ a, mm, zz))
        if n_groups > 2:
            term = jnp.where((g ^ a) < g, term, 0).astype(f32)
        base = term if base is None else base + term

    half = group // 2

    def local(segs, part, lower_q):
        found = call(
            functools.partial(local_body, len(segs), len(late) + 1, halves[1 + part].start, half),
            [shape((length, half * HEAD_SIZE), bf16), shape((length, half * HEAD_SIZE), f32)] * len(segs),
            [SMEM] + [VMEM] * (len(late) + 1 + 4 * len(segs)),
            flops=4 * len(segs) * length * length * half * HEAD_SIZE,
            scratch=[pltpu.VMEM((MEMBERS * HEAD_SIZE // 2, half * HEAD_SIZE), bf16)],
        )(here, *pieces, inner, outer_q, lower_q, *[one[s] for one in (kvs, messages, sums, lates) for s in segs])
        return {(s, part): (found[2 * at], found[2 * at + 1]) for at, s in enumerate(segs)}

    def mix(segs, parts, base, ready):
        keys = [(s, part) for s in segs for part in parts]
        return call(
            functools.partial(mix_body, segs, parts, group),
            [shape((length, half * HEAD_SIZE), bf16)] * len(keys),
            [SMEM] * 2 + [VMEM] * (1 + MEMBERS + len(segs) + 2 * len(keys)),
            flops=2 * len(keys) * length * half * HEAD_SIZE * HEAD_SIZE * 6,
        )(
            here, gate_bias, base, *deltas, *[messages[s] for s in segs],
            *[ready[key][0] for key in keys], *[ready[key][1] for key in keys],
        )

    ready = local((2, 3, 1, 0), 0, lower_q0)
    base = after(base, *ready[2, 0])
    two0, three0 = mix((2, 3), (0,), base, ready)
    ready |= local((2, 3), 1, after(lower_q1, two0, three0))
    two1, three1 = mix((2, 3), (1,), base, ready)
    ready |= local((1, 0), 1, after(lower_q1, two1, three1))
    one0, one1, mine0, mine1 = mix((1, 0), (0, 1), after(base, two1, three1), ready)
    sent = [mine0, mine1]
    for k, parts in ((1, (one0, one1)), (2, (two0, two1)), (3, (three0, three1))):
        sent += [to_member(part, k) for part in parts]
    far = sent[4:]
    (gate,) = call(gate_body, [shape((8, HEAD_SIZE), f32)], [ANY] * len(far), moved=16 << 20)(*far)
    (output,) = call(
        functools.partial(assemble_body, (2,) * MEMBERS),
        [shape((length, w_query.shape[1]), bf16)],
        [SMEM] + [VMEM] * (1 + len(sent)),
    )(here, gate, *sent)
    return output[None]


def solution(mesh):
    in_specs = (
        P("fsdp", "seg", None),
        P(("seg", "fsdp"), None),
        P(("seg", "fsdp"), None),
        P(("seg", "fsdp"), None),
        P(),
        P("fsdp", "seg", None, None),
        P("fsdp", "seg"),
    )
    out_specs = P("fsdp", "seg", None)
    body = functools.partial(shards, (mesh.shape["seg"], mesh.shape["fsdp"]))
    return jax.shard_map(body, mesh=mesh, in_specs=in_specs, out_specs=out_specs, check_vma=False)
```

```python
import functools

import jax
import jax.numpy as jnp
from jax import lax
from jax.experimental import pallas as pl
from jax.experimental.pallas import tpu as pltpu
from jax.sharding import PartitionSpec as P

HEAD_SIZE = 128
BLK = 128
MEMBERS = 4
META_ROWS = 16
HALF = META_ROWS // 2
AXES = ("seg", "fsdp")

VMEM = pl.BlockSpec(memory_space=pltpu.VMEM)
SMEM = pl.BlockSpec(memory_space=pltpu.SMEM)
ANY = pl.BlockSpec(memory_space=pl.ANY)
HBM = pl.BlockSpec(memory_space=pltpu.HBM)


def call(body, outs, in_specs, flops=0, scratch=(), out_spec=VMEM, limit=16 << 20, moved=4 << 20):
    return pl.pallas_call(
        body,
        out_shape=outs,
        in_specs=in_specs,
        out_specs=[out_spec] * len(outs),
        scratch_shapes=list(scratch),
        compiler_params=pltpu.CompilerParams(vmem_limit_bytes=limit),
        cost_estimate=pl.CostEstimate(flops=flops, bytes_accessed=moved, transcendentals=0),
    )


def aligned(offset):
    return pl.multiple_of(offset, HEAD_SIZE)


def pack_body(group, here_ref, valid_ref, mask_ref, wq_ref, wk_ref, wv_ref, *outs):
    rows, wide = wk_ref.shape[0], group * HEAD_SIZE
    row = lax.broadcasted_iota(jnp.int32, (META_ROWS, outs[0].shape[1]), 0)
    facts = jnp.where(row < HALF, valid_ref[0, 0], mask_ref[0, 0, 1, 0])
    facts = facts.astype(jnp.float32).astype(jnp.bfloat16)
    for k in range(MEMBERS):
        head, out = here_ref[1] ^ k, outs[k]
        at = aligned(head * HEAD_SIZE)
        out[:rows, :HEAD_SIZE] = wk_ref[:, pl.ds(at, HEAD_SIZE)]
        out[:rows, HEAD_SIZE : 2 * HEAD_SIZE] = wv_ref[:, pl.ds(at, HEAD_SIZE)]
        out[:rows, 2 * HEAD_SIZE :] = wq_ref[:, pl.ds(aligned(head * wide), wide)]
        out[rows:, :] = facts


def columns_of(tokens_ref, here_ref, piece, half, line):
    deep = MEMBERS * HEAD_SIZE // 2
    if not line:
        return tokens_ref[:, pl.ds((2 * piece + half) * deep, deep)]
    g, m, z = here_ref[0] ^ (piece // line), here_ref[1], here_ref[2]
    inside = (z == 1) | (z == 2)
    step = piece % line
    if step < 2:
        z = z ^ step
    else:
        z = jnp.where(inside, z ^ (5 - step), z ^ step)
    parts = [
        tokens_ref[:, pl.ds(aligned(((g * MEMBERS + (m ^ k)) * line + z) * HEAD_SIZE), HEAD_SIZE)]
        for k in (2 * half, 2 * half + 1)
    ]
    return jnp.concatenate(parts, axis=1)


def facts_of(message_ref):
    rows = message_ref.shape[0] - META_ROWS
    facts = message_ref[rows:, : 2 * HEAD_SIZE].astype(jnp.float32)
    return facts[0:1, :], facts[HALF : HALF + 1, :]


def iota(shape, dimension):
    return lax.broadcasted_iota(jnp.int32, shape, dimension).astype(jnp.float32)


def project_body(early, late, line, here_ref, *refs):
    tokens, pieces, outs = refs[:2], refs[2 : 2 + len(early)], refs[2 + len(early) :]
    length = tokens[0].shape[0]
    total = None
    for place, piece in zip(early, pieces):
        columns = jnp.concatenate([columns_of(one, here_ref, *place, line) for one in tokens], axis=0)
        term = jnp.dot(columns, piece[...], preferred_element_type=jnp.float32)
        total = term if total is None else total + term
    for n in range(2):
        outs[n][...] = total[n * length : (n + 1) * length]
        for k, place in enumerate(late):
            columns = columns_of(tokens[n], here_ref, *place, line)
            deep = columns.shape[1]
            outs[2 + n][:, k * deep : (k + 1) * deep] = columns


def sigma_plus(v):
    return jnp.where(v > 0, v + 1.0, jnp.exp(jnp.minimum(v, 0.0)))


def split(values):
    high = values.astype(jnp.bfloat16)
    return high, (values - high.astype(jnp.float32)).astype(jnp.bfloat16)


def late_rows(here_ref, chosen_ref, start, width, *pieces):
    *whole, inner, outer, part = pieces
    lost = inner.shape[1] - outer.shape[1] if start else 0
    at = slice(start - lost, start - lost + width)
    inside = (here_ref[2] == 1) | (here_ref[2] == 2)

    @pl.when(inside)
    def _():
        chosen_ref[...] = inner[:, start : start + width]

    @pl.when(jnp.logical_not(inside))
    def _():
        chosen_ref[...] = outer[:, at]

    rows = [piece[:, start : start + width] for piece in whole]
    return jnp.concatenate(rows + [chosen_ref[...], part[:, at]], axis=0)


def kv_body(n_late, here_ref, *refs):
    pieces, refs, chosen_ref = refs[:n_late], refs[n_late:-1], refs[-1]
    sums, lates, messages = refs[:MEMBERS], refs[MEMBERS : 2 * MEMBERS], refs[2 * MEMBERS : 3 * MEMBERS]
    outs = refs[3 * MEMBERS :]
    rows = late_rows(here_ref, chosen_ref, 0, 2 * HEAD_SIZE, *pieces)
    kvs = []
    for seg in range(MEMBERS):
        total = sums[seg][:, : 2 * HEAD_SIZE]
        total += jnp.dot(lates[seg][...], rows, preferred_element_type=jnp.float32)
        kvs.append(total.astype(jnp.bfloat16))
        outs[2 * seg][...] = kvs[seg]
    whole = None
    for seg, kv in enumerate(kvs):
        length = kv.shape[0]
        valid, _ = facts_of(messages[seg])
        keys = kv[:, :HEAD_SIZE].astype(jnp.float32)
        live = iota((length, HEAD_SIZE), 0) < valid[:, :HEAD_SIZE]
        sig = jnp.where(live, sigma_plus(keys), 0.0)
        wide = jnp.concatenate(
            [kv[:, HEAD_SIZE:], jnp.ones((length, HEAD_SIZE), jnp.bfloat16)], axis=1
        )
        high, low = split(sig)
        over = (((0,), (0,)), ((), ()))
        delta = lax.dot_general(high, wide, over, preferred_element_type=jnp.float32)
        delta += lax.dot_general(low, wide, over, preferred_element_type=jnp.float32)
        outs[2 * seg + 1][...] = delta
        whole = delta if whole is None else whole + delta
    outs[-1][...] = whole.astype(jnp.bfloat16)


def local_body(n, n_late, start, heads, here_ref, *refs):
    pieces, refs, chosen_ref = refs[:n_late], refs[n_late:-1], refs[-1]
    kvs, messages, sums, lates, outs = [refs[k * n : (k + 1) * n] for k in range(4)] + [refs[4 * n :]]
    rows = late_rows(here_ref, chosen_ref, start, heads * HEAD_SIZE, *pieces)
    columns = slice(start, start + heads * HEAD_SIZE)
    queries = []
    for at in range(n):
        total = sums[at][:, columns] + jnp.dot(
            lates[at][...], rows, preferred_element_type=jnp.float32
        )
        queries.append(total.astype(jnp.bfloat16))
        outs[2 * at][...] = queries[at]
    work = [(at, block) for at in range(n) for block in range(queries[0].shape[0] // BLK)]
    span = lambda block: slice(block * BLK, (block + 1) * BLK)
    scores = []
    for at, block in work:
        stacked = jnp.concatenate(
            [queries[at][span(block), h * HEAD_SIZE : (h + 1) * HEAD_SIZE] for h in range(heads)], axis=0
        )
        keys = kvs[at][0 : (block + 1) * BLK, :HEAD_SIZE]
        scores.append(
            lax.dot_general(
                stacked, keys, (((1,), (1,)), ((), ())), preferred_element_type=jnp.float32
            )
        )
    weights = []
    for (at, block), score in zip(work, scores):
        width = (block + 1) * BLK
        valid, seen = facts_of(messages[at])
        i, j = iota((BLK, width), 0) + block * BLK, iota((BLK, width), 1)
        limit = valid[:, :width]
        if block:
            limit = jnp.where((j[0:1] >= block * BLK) | (seen[:, :width] > 0), limit, 0.0)
        allowed = (j <= i) & (j < limit)
        masked = jnp.concatenate(
            [jnp.where(allowed, score[span(h)] * HEAD_SIZE ** (-0.5), -1e30) for h in range(heads)],
            axis=0,
        )
        top = jnp.max(masked, axis=-1, keepdims=True)
        expo = jnp.exp(masked - top)
        total = jnp.maximum(jnp.sum(expo, axis=-1, keepdims=True), 1.0)
        weights.append((expo * (1.0 / total)).astype(jnp.bfloat16))
    for (at, block), weight in zip(work, weights):
        values = kvs[at][0 : (block + 1) * BLK, HEAD_SIZE:]
        local = jnp.dot(weight, values, preferred_element_type=jnp.float32)
        for h in range(heads):
            outs[2 * at + 1][span(block), h * HEAD_SIZE : (h + 1) * HEAD_SIZE] = local[span(h)]


def mix_body(segs, parts, group, here_ref, gate_ref, base_ref, *refs):
    deltas, messages, refs = refs[:MEMBERS], refs[MEMBERS : MEMBERS + len(segs)], refs[MEMBERS + len(segs) :]
    n = len(segs) * len(parts)
    queries, locals_, outs = refs[:n], refs[n : 2 * n], refs[2 * n :]
    me = here_ref[1]
    heads = queries[0].shape[1] // HEAD_SIZE
    length = queries[0].shape[0]
    work = [(at, p, h) for at in range(len(segs)) for p in range(len(parts)) for h in range(heads)]
    memories = []
    for seg in segs:
        memory = jnp.where(here_ref[3] > 0, 1.0, 0.0) * base_ref[...].astype(jnp.float32)
        for other in range(MEMBERS):
            if other != seg:
                earlier = jnp.where((me ^ other) < (me ^ seg), 1.0, 0.0)
                memory = memory + earlier * deltas[other][...]
        memories.append(split(memory))
    columns = lambda h: slice(h * HEAD_SIZE, (h + 1) * HEAD_SIZE)
    numers = []
    for at, p, h in work:
        mem_high, mem_low = memories[at]
        high, low = split(sigma_plus(queries[at * len(parts) + p][:, columns(h)].astype(jnp.float32)))
        numer = jnp.dot(high, mem_high, preferred_element_type=jnp.float32)
        numer += jnp.dot(high, mem_low, preferred_element_type=jnp.float32)
        numer += jnp.dot(low, mem_high, preferred_element_type=jnp.float32)
        numers.append(numer)
    for (at, p, h), numer in zip(work, numers):
        valid, _ = facts_of(messages[at])
        live = iota((length, HEAD_SIZE), 0) < valid[:, :HEAD_SIZE]
        retrieved = numer[:, :HEAD_SIZE] / (numer[:, HEAD_SIZE:] + 1.0)
        logit = jnp.full((1, HEAD_SIZE), gate_ref[me * group + parts[p] * heads + h], jnp.float32)
        gate = 1.0 / (1.0 + jnp.exp(-logit))
        mixed = gate * retrieved + (1.0 - gate) * locals_[at * len(parts) + p][:, columns(h)]
        outs[at * len(parts) + p][:, columns(h)] = jnp.where(live, mixed, 0.0).astype(jnp.bfloat16)


def assemble_body(counts, here_ref, *refs):
    parts, out = list(refs[1:-1]), refs[-1]
    width = out.shape[1] // MEMBERS
    for k, count in enumerate(counts):
        for c in range(count):
            at = (here_ref[1] ^ k) * width + c * (width // count)
            out[:, pl.ds(aligned(at), width // count)] = parts.pop(0)[...]


def gate_body(*refs):
    refs[-1][...] = jnp.zeros_like(refs[-1])


def after(array, *others):
    return lax.optimization_barrier((array,) + others)[0]


def shards(sizes, tokens, w_query, w_key, value_weight, gate_bias, block_mask, valid_len):
    n_seg, n_z = sizes
    n_groups = n_seg // MEMBERS
    heads_kv = w_key.shape[1] // HEAD_SIZE
    group = w_query.shape[1] // w_key.shape[1]
    rows = w_query.shape[0]
    length, width = tokens.shape[1], tokens.shape[2]
    assert heads_kv == MEMBERS and group == 4 and length == 2 * BLK
    seg = lax.axis_index("seg")
    z = lax.axis_index("fsdp")
    g, m = seg // MEMBERS, seg % MEMBERS
    here = jnp.stack([g, m, z, g if n_groups == 2 else 1]).astype(jnp.int32)
    bf16, f32 = jnp.bfloat16, jnp.float32
    shape = jax.ShapeDtypeStruct

    def permute(array, to):
        pairs = []
        for gg in range(n_groups):
            for mm in range(MEMBERS):
                for zz in range(n_z):
                    target = to(gg, mm, zz)
                    if target is not None:
                        index = lambda t: (t[0] * MEMBERS + t[1]) * n_z + t[2]
                        pairs.append((index((gg, mm, zz)), index(target)))
        return lax.ppermute(array, AXES, pairs)

    def to_member(array, k):
        return permute(array, lambda gg, mm, zz: (gg, mm ^ k, zz))

    wide = (2 + group) * HEAD_SIZE
    packed = call(
        functools.partial(pack_body, group),
        [shape((rows + META_ROWS, wide), bf16)] * MEMBERS,
        [SMEM] * 3 + [VMEM] * 3,
        limit=56 << 20,
    )(here, valid_len, block_mask, w_query, w_key, value_weight)
    messages = [packed[0], *[to_member(packed[k], k) for k in (1, 2, 3)]]

    def gathered(piece):
        index = lambda gg, mm, zz: (gg * MEMBERS + mm) * n_z + zz
        everything = lax.all_gather(
            piece,
            AXES,
            axis_index_groups=[
                [index(gg, mm, zz) for gg in range(n_groups) for zz in range(n_z)]
                for mm in range(MEMBERS)
            ],
        )
        columns = piece.shape[1]
        natural = everything.reshape(n_groups, n_z, MEMBERS, rows, columns)
        members = jnp.arange(MEMBERS, dtype=jnp.int32) ^ m
        natural = jnp.take(natural, members, axis=2).transpose(0, 2, 1, 3, 4)
        return list(natural.reshape(-1, MEMBERS * HEAD_SIZE, columns))

    pieces = [
        jnp.concatenate([messages[k][:rows] for k in members], axis=0) for members in ((0, 1), (2, 3))
    ]
    n_pieces = width // (MEMBERS * HEAD_SIZE)
    sums, lates = [None] * MEMBERS, [None] * MEMBERS

    def project(segs, early, late, halves, line):
        deep = MEMBERS * HEAD_SIZE // 2
        found = call(
            functools.partial(project_body, early, late, line),
            [shape((length, wide), f32)] * 2 + [shape((length, len(late) * deep), bf16)] * 2,
            [SMEM] + [VMEM] * (2 + len(early)),
            flops=2 * 2 * length * len(early) * deep * wide,
        )(here, *[books[s] for s in segs], *[halves[half][piece] for piece, half in early])
        for at, s in enumerate(segs):
            sums[s], lates[s] = found[at], found[2 + at]

    cut = 2 * HEAD_SIZE
    if n_groups == 2 and n_z == 4:
        assert rows == HEAD_SIZE
        inside = (z == 1) | (z == 2)
        over = lambda part: permute(part, lambda gg, mm, zz: (gg ^ 1, mm, zz))
        pair = lambda part: permute(part, lambda gg, mm, zz: (gg, mm, zz ^ 1))
        outward = lambda part: permute(
            part, lambda gg, mm, zz: (gg, mm, zz ^ 1) if zz in (1, 2) else None
        )
        inward = lambda part: permute(
            part, lambda gg, mm, zz: (gg, mm, zz ^ 3) if zz in (1, 2) else None
        )
        locked = lambda *parts: lax.optimization_barrier(parts)
        stage1 = lambda piece: (pair(piece), inward(piece), over(piece))
        stage2 = lambda one, inner: (inward(one), outward(inner), over(one))
        stage3 = lambda middle, two: (outward(middle), over(two))

        a, b, own, sibling = locked(*pieces, tokens[0], to_member(tokens[0], 1))
        across = to_member(own, 2)
        a_one, a_inner, a_far0 = locked(*stage1(a))
        b_one, b_inner, b_far0 = locked(*stage1(b))
        a_middle, a_outer, a_far1 = locked(*stage2(a_one, a_inner))
        b_middle, b_outer, b_far1 = locked(*stage2(b_one, b_inner))
        a_two = jnp.where(inside, a_inner, a_outer)
        a_inner, (a_last, a_far2) = inward(a_far1), stage3(a_middle, a_two)
        b_two = jnp.where(inside, b_inner, b_outer)
        b_last, b_far2 = stage3(b_middle, b_two)
        a_last, a_far2, a_middle, a_inner = locked(a_last, a_far2, a_middle, a_inner)
        a_three = jnp.where(inside, a_middle, a_last)
        books = [own, sibling]
        upper = [a, a_one, a_two, a_three, a_far0, a_far1, a_far2]
        lower = [b, b_one, b_two, None, b_far0, b_far1]
        late = [(3, 1), (6, 1), (7, 0), (7, 1)]
        early = [(k, half) for half in range(2) for k in range(8) if (k, half) not in late]
        project((0, 1), early, late, (upper, lower), n_z)
        b_last, b_far2, b_middle, sums[0], sums[1], across = locked(
            b_last, b_far2, b_middle, sums[0], sums[1], after(across, a_last, a_far2)
        )
        books += [across, to_member(across, 1)]
        project((2, 3), early, late, (upper, lower), n_z)
        b_three = jnp.where(inside, b_middle, b_last)
        pieces = [b_three, b_far2]
        outer_kv, outer_q = [outward(a_inner[:, at]) for at in (slice(0, cut), slice(cut, None))]
        inner = a_inner
        finish = lambda at: over(b_three[:, at])
    else:
        across, sibling = to_member(tokens[0], 2), to_member(tokens[0], 1)
        books = [tokens[0], sibling, across, to_member(across, 1)]
        full = gathered(jnp.concatenate(pieces, axis=0))
        deep = MEMBERS * HEAD_SIZE // 2
        upper, lower = [part[:deep] for part in full], [part[deep:] for part in full]
        late = [(n_pieces - 1, 0), (n_pieces - 1, 1)]
        early = [(k, half) for half in range(2) for k in range(n_pieces - 1)]
        late = [(n_pieces - 2, 1)] + late
        early.remove(late[0])
        for segs in ((0, 1), (2, 3)):
            project(segs, early, late, (upper, lower), 0)
        pieces = [lower[-2]]
        outer_kv, outer_q = upper[-1][:, :cut], upper[-1][:, cut:]
        inner = upper[-1]
        finish = lambda at: lower[-1][:, at]

    halves = [slice(k * HEAD_SIZE, (k + 2) * HEAD_SIZE) for k in (0, 2, 4)]
    lower_kv, lower_q = finish(slice(0, cut)), finish(slice(cut, None))
    found = call(
        functools.partial(kv_body, len(late) + 1),
        [shape((length, 2 * HEAD_SIZE), bf16), shape((HEAD_SIZE, 2 * HEAD_SIZE), f32)] * MEMBERS
        + [shape((HEAD_SIZE, 2 * HEAD_SIZE), bf16)],
        [SMEM] + [VMEM] * (len(late) + 1 + 3 * MEMBERS),
        flops=2 * MEMBERS * length * len(late) * MEMBERS * HEAD_SIZE * HEAD_SIZE,
        scratch=[pltpu.VMEM((MEMBERS * HEAD_SIZE // 2, cut), bf16)],
    )(here, *pieces, inner, outer_kv, lower_kv, *sums, *lates, *messages)
    kvs, deltas, total = found[0:-1:2], found[1:-1:2], found[-1]

    base = None
    for a in range(1, n_groups):
        term = permute(total, lambda gg, mm, zz: (gg ^ a, mm, zz))
        if n_groups > 2:
            term = jnp.where((g ^ a) < g, term, 0).astype(f32)
        base = term if base is None else base + term

    half = group // 2

    def local(segs, part, *others):
        found = call(
            functools.partial(local_body, len(segs), len(late) + 1, halves[1 + part].start, half),
            [shape((length, half * HEAD_SIZE), bf16), shape((length, half * HEAD_SIZE), f32)] * len(segs),
            [SMEM] + [VMEM] * (len(late) + 1 + 4 * len(segs)),
            flops=4 * len(segs) * length * length * half * HEAD_SIZE,
            scratch=[pltpu.VMEM((MEMBERS * HEAD_SIZE // 2, half * HEAD_SIZE), bf16)],
        )(here, *pieces, inner, outer_q, after(lower_q, *others), *[one[s] for one in (kvs, messages, sums, lates) for s in segs])
        return {(s, part): (found[2 * at], found[2 * at + 1]) for at, s in enumerate(segs)}

    def mix(segs, parts, base, ready):
        keys = [(s, part) for s in segs for part in parts]
        return call(
            functools.partial(mix_body, segs, parts, group),
            [shape((length, half * HEAD_SIZE), bf16)] * len(keys),
            [SMEM] * 2 + [VMEM] * (1 + MEMBERS + len(segs) + 2 * len(keys)),
            flops=2 * len(keys) * length * half * HEAD_SIZE * HEAD_SIZE * 6,
        )(
            here, gate_bias, base, *deltas, *[messages[s] for s in segs],
            *[ready[key][0] for key in keys], *[ready[key][1] for key in keys],
        )

    ready = local((2, 3, 1, 0), 0)
    base = after(base, *ready[2, 0])
    two0, three0 = mix((2, 3), (0,), base, ready)
    ready |= local((2, 3), 1, two0, three0)
    two1, three1 = mix((2, 3), (1,), base, ready)
    ready |= local((1, 0), 1, two1, three1)
    one0, one1, mine0, mine1 = mix((1, 0), (0, 1), after(base, two1, three1), ready)
    sent = [mine0, mine1]
    for k, parts in ((1, (one0, one1)), (2, (two0, two1)), (3, (three0, three1))):
        sent += [to_member(part, k) for part in parts]
    far = sent[4:]
    (gate,) = call(gate_body, [shape((8, HEAD_SIZE), f32)], [ANY] * len(far), moved=16 << 20)(*far)
    (output,) = call(
        functools.partial(assemble_body, (2,) * MEMBERS),
        [shape((length, w_query.shape[1]), bf16)],
        [SMEM] + [VMEM] * (1 + len(sent)),
    )(here, gate, *sent)
    return output[None]


def solution(mesh):
    in_specs = (
        P("fsdp", "seg", None),
        P(("seg", "fsdp"), None),
        P(("seg", "fsdp"), None),
        P(("seg", "fsdp"), None),
        P(),
        P("fsdp", "seg", None, None),
        P("fsdp", "seg"),
    )
    out_specs = P("fsdp", "seg", None)
    body = functools.partial(shards, (mesh.shape["seg"], mesh.shape["fsdp"]))
    return jax.shard_map(body, mesh=mesh, in_specs=in_specs, out_specs=out_specs, check_vma=False)
```

```python
import functools

import jax
import jax.numpy as jnp
from jax import lax
from jax.experimental import pallas as pl
from jax.experimental.pallas import tpu as pltpu
from jax.sharding import PartitionSpec as P

HEAD_SIZE = 128
BLK = 128
MEMBERS = 4
META_ROWS = 16
HALF = META_ROWS // 2
AXES = ("seg", "fsdp")

VMEM = pl.BlockSpec(memory_space=pltpu.VMEM)
SMEM = pl.BlockSpec(memory_space=pltpu.SMEM)
ANY = pl.BlockSpec(memory_space=pl.ANY)
HBM = pl.BlockSpec(memory_space=pltpu.HBM)


def call(body, outs, in_specs, flops=0, scratch=(), out_spec=VMEM, limit=16 << 20, moved=4 << 20):
    return pl.pallas_call(
        body,
        out_shape=outs,
        in_specs=in_specs,
        out_specs=[out_spec] * len(outs),
        scratch_shapes=list(scratch),
        compiler_params=pltpu.CompilerParams(vmem_limit_bytes=limit),
        cost_estimate=pl.CostEstimate(flops=flops, bytes_accessed=moved, transcendentals=0),
    )


def aligned(offset):
    return pl.multiple_of(offset, HEAD_SIZE)


def pack_body(group, here_ref, valid_ref, mask_ref, wq_ref, wk_ref, wv_ref, *outs):
    rows, wide = wk_ref.shape[0], group * HEAD_SIZE
    row = lax.broadcasted_iota(jnp.int32, (META_ROWS, outs[0].shape[1]), 0)
    facts = jnp.where(row < HALF, valid_ref[0, 0], mask_ref[0, 0, 1, 0])
    facts = facts.astype(jnp.float32).astype(jnp.bfloat16)
    for k in range(MEMBERS):
        head, out = here_ref[1] ^ k, outs[k]
        at = aligned(head * HEAD_SIZE)
        out[:rows, :HEAD_SIZE] = wk_ref[:, pl.ds(at, HEAD_SIZE)]
        out[:rows, HEAD_SIZE : 2 * HEAD_SIZE] = wv_ref[:, pl.ds(at, HEAD_SIZE)]
        out[:rows, 2 * HEAD_SIZE :] = wq_ref[:, pl.ds(aligned(head * wide), wide)]
        out[rows:, :] = facts


def columns_of(tokens_ref, here_ref, piece, half, line):
    deep = MEMBERS * HEAD_SIZE // 2
    if not line:
        return tokens_ref[:, pl.ds((2 * piece + half) * deep, deep)]
    g, m, z = here_ref[0] ^ (piece // line), here_ref[1], here_ref[2]
    inside = (z == 1) | (z == 2)
    step = piece % line
    if step < 2:
        z = z ^ step
    else:
        z = jnp.where(inside, z ^ (5 - step), z ^ step)
    parts = [
        tokens_ref[:, pl.ds(aligned(((g * MEMBERS + (m ^ k)) * line + z) * HEAD_SIZE), HEAD_SIZE)]
        for k in (2 * half, 2 * half + 1)
    ]
    return jnp.concatenate(parts, axis=1)


def facts_of(message_ref):
    rows = message_ref.shape[0] - META_ROWS
    facts = message_ref[rows:, : 2 * HEAD_SIZE].astype(jnp.float32)
    return facts[0:1, :], facts[HALF : HALF + 1, :]


def iota(shape, dimension):
    return lax.broadcasted_iota(jnp.int32, shape, dimension).astype(jnp.float32)


def project_body(early, late, line, here_ref, *refs):
    tokens, pieces, outs = refs[:2], refs[2 : 2 + len(early)], refs[2 + len(early) :]
    length = tokens[0].shape[0]
    total = None
    for place, piece in zip(early, pieces):
        columns = jnp.concatenate([columns_of(one, here_ref, *place, line) for one in tokens], axis=0)
        term = jnp.dot(columns, piece[...], preferred_element_type=jnp.float32)
        total = term if total is None else total + term
    for n in range(2):
        outs[n][...] = total[n * length : (n + 1) * length]
        for k, place in enumerate(late):
            columns = columns_of(tokens[n], here_ref, *place, line)
            deep = columns.shape[1]
            outs[2 + n][:, k * deep : (k + 1) * deep] = columns


def sigma_plus(v):
    return jnp.where(v > 0, v + 1.0, jnp.exp(jnp.minimum(v, 0.0)))


def split(values):
    high = values.astype(jnp.bfloat16)
    return high, (values - high.astype(jnp.float32)).astype(jnp.bfloat16)


def late_rows(here_ref, chosen_ref, start, width, *pieces):
    *whole, inner, outer, part = pieces
    lost = inner.shape[1] - outer.shape[1] if start else 0
    at = slice(start - lost, start - lost + width)
    inside = (here_ref[2] == 1) | (here_ref[2] == 2)

    @pl.when(inside)
    def _():
        chosen_ref[...] = inner[:, start : start + width]

    @pl.when(jnp.logical_not(inside))
    def _():
        chosen_ref[...] = outer[:, at]

    rows = [piece[:, start : start + width] for piece in whole]
    return jnp.concatenate(rows + [chosen_ref[...], part[...]], axis=0)


def kv_body(n_late, here_ref, *refs):
    pieces, refs, chosen_ref = refs[:n_late], refs[n_late:-1], refs[-1]
    sums, lates, messages = refs[:MEMBERS], refs[MEMBERS : 2 * MEMBERS], refs[2 * MEMBERS : 3 * MEMBERS]
    outs = refs[3 * MEMBERS :]
    rows = late_rows(here_ref, chosen_ref, 0, 2 * HEAD_SIZE, *pieces)
    kvs = []
    for seg in range(MEMBERS):
        total = sums[seg][:, : 2 * HEAD_SIZE]
        total += jnp.dot(lates[seg][...], rows, preferred_element_type=jnp.float32)
        kvs.append(total.astype(jnp.bfloat16))
        outs[2 * seg][...] = kvs[seg]
    whole = None
    for seg, kv in enumerate(kvs):
        length = kv.shape[0]
        valid, _ = facts_of(messages[seg])
        keys = kv[:, :HEAD_SIZE].astype(jnp.float32)
        live = iota((length, HEAD_SIZE), 0) < valid[:, :HEAD_SIZE]
        sig = jnp.where(live, sigma_plus(keys), 0.0)
        wide = jnp.concatenate(
            [kv[:, HEAD_SIZE:], jnp.ones((length, HEAD_SIZE), jnp.bfloat16)], axis=1
        )
        high, low = split(sig)
        over = (((0,), (0,)), ((), ()))
        delta = lax.dot_general(high, wide, over, preferred_element_type=jnp.float32)
        delta += lax.dot_general(low, wide, over, preferred_element_type=jnp.float32)
        outs[2 * seg + 1][...] = delta
        whole = delta if whole is None else whole + delta
    outs[-1][...] = whole.astype(jnp.bfloat16)


def local_body(n, n_late, start, heads, here_ref, *refs):
    pieces, refs, chosen_ref = refs[:n_late], refs[n_late:-1], refs[-1]
    kvs, messages, sums, lates, outs = [refs[k * n : (k + 1) * n] for k in range(4)] + [refs[4 * n :]]
    rows = late_rows(here_ref, chosen_ref, start, heads * HEAD_SIZE, *pieces)
    columns = slice(start, start + heads * HEAD_SIZE)
    queries = []
    for at in range(n):
        total = sums[at][:, columns] + jnp.dot(
            lates[at][...], rows, preferred_element_type=jnp.float32
        )
        queries.append(total.astype(jnp.bfloat16))
        outs[2 * at][...] = queries[at]
    work = [(at, block) for at in range(n) for block in range(queries[0].shape[0] // BLK)]
    span = lambda block: slice(block * BLK, (block + 1) * BLK)
    scores = []
    for at, block in work:
        stacked = jnp.concatenate(
            [queries[at][span(block), h * HEAD_SIZE : (h + 1) * HEAD_SIZE] for h in range(heads)], axis=0
        )
        keys = kvs[at][0 : (block + 1) * BLK, :HEAD_SIZE]
        scores.append(
            lax.dot_general(
                stacked, keys, (((1,), (1,)), ((), ())), preferred_element_type=jnp.float32
            )
        )
    weights = []
    for (at, block), score in zip(work, scores):
        width = (block + 1) * BLK
        valid, seen = facts_of(messages[at])
        i, j = iota((BLK, width), 0) + block * BLK, iota((BLK, width), 1)
        limit = valid[:, :width]
        if block:
            limit = jnp.where((j[0:1] >= block * BLK) | (seen[:, :width] > 0), limit, 0.0)
        allowed = (j <= i) & (j < limit)
        masked = jnp.concatenate(
            [jnp.where(allowed, score[span(h)] * HEAD_SIZE ** (-0.5), -1e30) for h in range(heads)],
            axis=0,
        )
        top = jnp.max(masked, axis=-1, keepdims=True)
        expo = jnp.exp(masked - top)
        total = jnp.maximum(jnp.sum(expo, axis=-1, keepdims=True), 1.0)
        weights.append((expo * (1.0 / total)).astype(jnp.bfloat16))
    for (at, block), weight in zip(work, weights):
        values = kvs[at][0 : (block + 1) * BLK, HEAD_SIZE:]
        local = jnp.dot(weight, values, preferred_element_type=jnp.float32)
        for h in range(heads):
            outs[2 * at + 1][span(block), h * HEAD_SIZE : (h + 1) * HEAD_SIZE] = local[span(h)]


def mix_body(segs, parts, group, here_ref, gate_ref, base_ref, *refs):
    deltas, messages, refs = refs[:MEMBERS], refs[MEMBERS : MEMBERS + len(segs)], refs[MEMBERS + len(segs) :]
    n = len(segs) * len(parts)
    queries, locals_, outs = refs[:n], refs[n : 2 * n], refs[2 * n :]
    me = here_ref[1]
    heads = queries[0].shape[1] // HEAD_SIZE
    length = queries[0].shape[0]
    work = [(at, p, h) for at in range(len(segs)) for p in range(len(parts)) for h in range(heads)]
    memories = []
    for seg in segs:
        memory = jnp.where(here_ref[3] > 0, 1.0, 0.0) * base_ref[...].astype(jnp.float32)
        for other in range(MEMBERS):
            if other != seg:
                earlier = jnp.where((me ^ other) < (me ^ seg), 1.0, 0.0)
                memory = memory + earlier * deltas[other][...]
        memories.append(split(memory))
    columns = lambda h: slice(h * HEAD_SIZE, (h + 1) * HEAD_SIZE)
    numers = []
    for at, p, h in work:
        mem_high, mem_low = memories[at]
        high, low = split(sigma_plus(queries[at * len(parts) + p][:, columns(h)].astype(jnp.float32)))
        numer = jnp.dot(high, mem_high, preferred_element_type=jnp.float32)
        numer += jnp.dot(high, mem_low, preferred_element_type=jnp.float32)
        numer += jnp.dot(low, mem_high, preferred_element_type=jnp.float32)
        numers.append(numer)
    for (at, p, h), numer in zip(work, numers):
        valid, _ = facts_of(messages[at])
        live = iota((length, HEAD_SIZE), 0) < valid[:, :HEAD_SIZE]
        retrieved = numer[:, :HEAD_SIZE] / (numer[:, HEAD_SIZE:] + 1.0)
        logit = jnp.full((1, HEAD_SIZE), gate_ref[me * group + parts[p] * heads + h], jnp.float32)
        gate = 1.0 / (1.0 + jnp.exp(-logit))
        mixed = gate * retrieved + (1.0 - gate) * locals_[at * len(parts) + p][:, columns(h)]
        outs[at * len(parts) + p][:, columns(h)] = jnp.where(live, mixed, 0.0).astype(jnp.bfloat16)


def assemble_body(counts, here_ref, *refs):
    parts, out = list(refs[1:-1]), refs[-1]
    width = out.shape[1] // MEMBERS
    for k, count in enumerate(counts):
        for c in range(count):
            at = (here_ref[1] ^ k) * width + c * (width // count)
            out[:, pl.ds(aligned(at), width // count)] = parts.pop(0)[...]


def gate_body(*refs):
    refs[-1][...] = jnp.zeros_like(refs[-1])


def after(array, *others):
    return lax.optimization_barrier((array,) + others)[0]


def shards(sizes, tokens, w_query, w_key, value_weight, gate_bias, block_mask, valid_len):
    n_seg, n_z = sizes
    n_groups = n_seg // MEMBERS
    heads_kv = w_key.shape[1] // HEAD_SIZE
    group = w_query.shape[1] // w_key.shape[1]
    rows = w_query.shape[0]
    length, width = tokens.shape[1], tokens.shape[2]
    assert heads_kv == MEMBERS and group == 4 and length == 2 * BLK
    seg = lax.axis_index("seg")
    z = lax.axis_index("fsdp")
    g, m = seg // MEMBERS, seg % MEMBERS
    here = jnp.stack([g, m, z, g if n_groups == 2 else 1]).astype(jnp.int32)
    bf16, f32 = jnp.bfloat16, jnp.float32
    shape = jax.ShapeDtypeStruct

    def permute(array, to):
        pairs = []
        for gg in range(n_groups):
            for mm in range(MEMBERS):
                for zz in range(n_z):
                    target = to(gg, mm, zz)
                    if target is not None:
                        index = lambda t: (t[0] * MEMBERS + t[1]) * n_z + t[2]
                        pairs.append((index((gg, mm, zz)), index(target)))
        return lax.ppermute(array, AXES, pairs)

    def to_member(array, k):
        return permute(array, lambda gg, mm, zz: (gg, mm ^ k, zz))

    wide = (2 + group) * HEAD_SIZE
    packed = call(
        functools.partial(pack_body, group),
        [shape((rows + META_ROWS, wide), bf16)] * MEMBERS,
        [SMEM] * 3 + [VMEM] * 3,
        limit=56 << 20,
    )(here, valid_len, block_mask, w_query, w_key, value_weight)
    messages = [packed[0], *[to_member(packed[k], k) for k in (1, 2, 3)]]

    def gathered(piece):
        index = lambda gg, mm, zz: (gg * MEMBERS + mm) * n_z + zz
        everything = lax.all_gather(
            piece,
            AXES,
            axis_index_groups=[
                [index(gg, mm, zz) for gg in range(n_groups) for zz in range(n_z)]
                for mm in range(MEMBERS)
            ],
        )
        columns = piece.shape[1]
        natural = everything.reshape(n_groups, n_z, MEMBERS, rows, columns)
        members = jnp.arange(MEMBERS, dtype=jnp.int32) ^ m
        natural = jnp.take(natural, members, axis=2).transpose(0, 2, 1, 3, 4)
        return list(natural.reshape(-1, MEMBERS * HEAD_SIZE, columns))

    pieces = [
        jnp.concatenate([messages[k][:rows] for k in members], axis=0) for members in ((0, 1), (2, 3))
    ]
    n_pieces = width // (MEMBERS * HEAD_SIZE)
    sums, lates = [None] * MEMBERS, [None] * MEMBERS

    def project(segs, early, late, halves, line):
        deep = MEMBERS * HEAD_SIZE // 2
        found = call(
            functools.partial(project_body, early, late, line),
            [shape((length, wide), f32)] * 2 + [shape((length, len(late) * deep), bf16)] * 2,
            [SMEM] + [VMEM] * (2 + len(early)),
            flops=2 * 2 * length * len(early) * deep * wide,
        )(here, *[books[s] for s in segs], *[halves[half][piece] for piece, half in early])
        for at, s in enumerate(segs):
            sums[s], lates[s] = found[at], found[2 + at]

    cut = 2 * HEAD_SIZE
    if n_groups == 2 and n_z == 4:
        assert rows == HEAD_SIZE
        inside = (z == 1) | (z == 2)
        over = lambda part: permute(part, lambda gg, mm, zz: (gg ^ 1, mm, zz))
        pair = lambda part: permute(part, lambda gg, mm, zz: (gg, mm, zz ^ 1))
        outward = lambda part: permute(
            part, lambda gg, mm, zz: (gg, mm, zz ^ 1) if zz in (1, 2) else None
        )
        inward = lambda part: permute(
            part, lambda gg, mm, zz: (gg, mm, zz ^ 3) if zz in (1, 2) else None
        )
        locked = lambda *parts: lax.optimization_barrier(parts)
        stage1 = lambda piece: (pair(piece), inward(piece), over(piece))
        stage2 = lambda one, inner: (inward(one), outward(inner), over(one))
        stage3 = lambda middle, two: (outward(middle), over(two))

        a, b, own, sibling = locked(*pieces, tokens[0], to_member(tokens[0], 1))
        across = to_member(own, 2)
        a_one, a_inner, a_far0 = locked(*stage1(a))
        b_one, b_inner, b_far0 = locked(*stage1(b))
        a_middle, a_outer, a_far1 = locked(*stage2(a_one, a_inner))
        b_middle, b_outer, b_far1 = locked(*stage2(b_one, b_inner))
        a_two = jnp.where(inside, a_inner, a_outer)
        a_inner, (a_last, a_far2) = inward(a_far1), stage3(a_middle, a_two)
        b_two = jnp.where(inside, b_inner, b_outer)
        b_last, b_far2 = stage3(b_middle, b_two)
        a_last, a_far2, a_middle, a_inner = locked(a_last, a_far2, a_middle, a_inner)
        a_three = jnp.where(inside, a_middle, a_last)
        books = [own, sibling]
        upper = [a, a_one, a_two, a_three, a_far0, a_far1, a_far2]
        lower = [b, b_one, b_two, None, b_far0, b_far1]
        late = [(3, 1), (6, 1), (7, 0), (7, 1)]
        early = [(k, half) for half in range(2) for k in range(8) if (k, half) not in late]
        project((0, 1), early, late, (upper, lower), n_z)
        b_last, b_far2, b_middle, sums[0], sums[1], across = locked(
            b_last, b_far2, b_middle, sums[0], sums[1], after(across, a_last, a_far2)
        )
        books += [across, to_member(across, 1)]
        project((2, 3), early, late, (upper, lower), n_z)
        b_three = jnp.where(inside, b_middle, b_last)
        pieces = [b_three, b_far2]
        outer_kv, outer_q = [outward(a_inner[:, at]) for at in (slice(0, cut), slice(cut, None))]
        inner = a_inner
        finish = lambda at, *others: over(after(b_three[:, at], *others))
    else:
        across, sibling = to_member(tokens[0], 2), to_member(tokens[0], 1)
        books = [tokens[0], sibling, across, to_member(across, 1)]
        full = gathered(jnp.concatenate(pieces, axis=0))
        deep = MEMBERS * HEAD_SIZE // 2
        upper, lower = [part[:deep] for part in full], [part[deep:] for part in full]
        late = [(n_pieces - 1, 0), (n_pieces - 1, 1)]
        early = [(k, half) for half in range(2) for k in range(n_pieces - 1)]
        late = [(n_pieces - 2, 1)] + late
        early.remove(late[0])
        for segs in ((0, 1), (2, 3)):
            project(segs, early, late, (upper, lower), 0)
        pieces = [lower[-2]]
        outer_kv, outer_q = upper[-1][:, :cut], upper[-1][:, cut:]
        inner = upper[-1]
        finish = lambda at, *others: lower[-1][:, at]

    halves = [slice(k * HEAD_SIZE, (k + 2) * HEAD_SIZE) for k in (0, 2, 4)]
    lower_kv, lower_q0 = finish(halves[0]), finish(halves[1])
    found = call(
        functools.partial(kv_body, len(late) + 1),
        [shape((length, 2 * HEAD_SIZE), bf16), shape((HEAD_SIZE, 2 * HEAD_SIZE), f32)] * MEMBERS
        + [shape((HEAD_SIZE, 2 * HEAD_SIZE), bf16)],
        [SMEM] + [VMEM] * (len(late) + 1 + 3 * MEMBERS),
        flops=2 * MEMBERS * length * len(late) * MEMBERS * HEAD_SIZE * HEAD_SIZE,
        scratch=[pltpu.VMEM((MEMBERS * HEAD_SIZE // 2, cut), bf16)],
    )(here, *pieces, inner, outer_kv, lower_kv, *sums, *lates, *messages)
    kvs, deltas, total = found[0:-1:2], found[1:-1:2], found[-1]

    base = None
    for a in range(1, n_groups):
        term = permute(total, lambda gg, mm, zz: (gg ^ a, mm, zz))
        if n_groups > 2:
            term = jnp.where((g ^ a) < g, term, 0).astype(f32)
        base = term if base is None else base + term

    half = group // 2

    def local(segs, part, lower_q):
        found = call(
            functools.partial(local_body, len(segs), len(late) + 1, halves[1 + part].start, half),
            [shape((length, half * HEAD_SIZE), bf16), shape((length, half * HEAD_SIZE), f32)] * len(segs),
            [SMEM] + [VMEM] * (len(late) + 1 + 4 * len(segs)),
            flops=4 * len(segs) * length * length * half * HEAD_SIZE,
            scratch=[pltpu.VMEM((MEMBERS * HEAD_SIZE // 2, half * HEAD_SIZE), bf16)],
        )(here, *pieces, inner, outer_q, lower_q, *[one[s] for one in (kvs, messages, sums, lates) for s in segs])
        return {(s, part): (found[2 * at], found[2 * at + 1]) for at, s in enumerate(segs)}

    def mix(segs, parts, base, ready):
        keys = [(s, part) for s in segs for part in parts]
        return call(
            functools.partial(mix_body, segs, parts, group),
            [shape((length, half * HEAD_SIZE), bf16)] * len(keys),
            [SMEM] * 2 + [VMEM] * (1 + MEMBERS + len(segs) + 2 * len(keys)),
            flops=2 * len(keys) * length * half * HEAD_SIZE * HEAD_SIZE * 6,
        )(
            here, gate_bias, base, *deltas, *[messages[s] for s in segs],
            *[ready[key][0] for key in keys], *[ready[key][1] for key in keys],
        )

    ready = local((2, 3, 1, 0), 0, lower_q0)
    base = after(base, *ready[2, 0])
    lower_q1 = finish(halves[2], base)
    two0, three0 = mix((2, 3), (0,), base, ready)
    ready |= local((2, 3), 1, after(lower_q1, two0, three0))
    two1, three1 = mix((2, 3), (1,), base, ready)
    ready |= local((1, 0), 1, after(lower_q1, two1, three1))
    one0, one1, mine0, mine1 = mix((1, 0), (0, 1), after(base, two1, three1), ready)
    sent = [mine0, mine1]
    for k, parts in ((1, (one0, one1)), (2, (two0, two1)), (3, (three0, three1))):
        sent += [to_member(part, k) for part in parts]
    far = sent[4:]
    (gate,) = call(gate_body, [shape((8, HEAD_SIZE), f32)], [ANY] * len(far), moved=16 << 20)(*far)
    (output,) = call(
        functools.partial(assemble_body, (2,) * MEMBERS),
        [shape((length, w_query.shape[1]), bf16)],
        [SMEM] + [VMEM] * (1 + len(sent)),
    )(here, gate, *sent)
    return output[None]


def solution(mesh):
    in_specs = (
        P("fsdp", "seg", None),
        P(("seg", "fsdp"), None),
        P(("seg", "fsdp"), None),
        P(("seg", "fsdp"), None),
        P(),
        P("fsdp", "seg", None, None),
        P("fsdp", "seg"),
    )
    out_specs = P("fsdp", "seg", None)
    body = functools.partial(shards, (mesh.shape["seg"], mesh.shape["fsdp"]))
    return jax.shard_map(body, mesh=mesh, in_specs=in_specs, out_specs=out_specs, check_vma=False)
```

```python
import functools

import jax
import jax.numpy as jnp
from jax import lax
from jax.experimental import pallas as pl
from jax.experimental.pallas import tpu as pltpu
from jax.sharding import PartitionSpec as P

HEAD_SIZE = 128
BLK = 128
MEMBERS = 4
META_ROWS = 16
HALF = META_ROWS // 2
AXES = ("seg", "fsdp")

VMEM = pl.BlockSpec(memory_space=pltpu.VMEM)
SMEM = pl.BlockSpec(memory_space=pltpu.SMEM)
ANY = pl.BlockSpec(memory_space=pl.ANY)
HBM = pl.BlockSpec(memory_space=pltpu.HBM)


def call(body, outs, in_specs, flops=0, scratch=(), out_spec=VMEM, limit=16 << 20, moved=4 << 20):
    return pl.pallas_call(
        body,
        out_shape=outs,
        in_specs=in_specs,
        out_specs=[out_spec] * len(outs),
        scratch_shapes=list(scratch),
        compiler_params=pltpu.CompilerParams(vmem_limit_bytes=limit),
        cost_estimate=pl.CostEstimate(flops=flops, bytes_accessed=moved, transcendentals=0),
    )


def aligned(offset):
    return pl.multiple_of(offset, HEAD_SIZE)


def pack_body(group, here_ref, valid_ref, mask_ref, wq_ref, wk_ref, wv_ref, *outs):
    rows, wide = wk_ref.shape[0], group * HEAD_SIZE
    row = lax.broadcasted_iota(jnp.int32, (META_ROWS, outs[0].shape[1]), 0)
    facts = jnp.where(row < HALF, valid_ref[0, 0], mask_ref[0, 0, 1, 0])
    facts = facts.astype(jnp.float32).astype(jnp.bfloat16)
    for k in range(MEMBERS):
        head, out = here_ref[1] ^ k, outs[k]
        at = aligned(head * HEAD_SIZE)
        out[:rows, :HEAD_SIZE] = wk_ref[:, pl.ds(at, HEAD_SIZE)]
        out[:rows, HEAD_SIZE : 2 * HEAD_SIZE] = wv_ref[:, pl.ds(at, HEAD_SIZE)]
        out[:rows, 2 * HEAD_SIZE :] = wq_ref[:, pl.ds(aligned(head * wide), wide)]
        out[rows:, :] = facts


def columns_of(tokens_ref, here_ref, piece, half, line):
    deep = MEMBERS * HEAD_SIZE // 2
    if not line:
        return tokens_ref[:, pl.ds((2 * piece + half) * deep, deep)]
    g, m, z = here_ref[0] ^ (piece // line), here_ref[1], here_ref[2]
    inside = (z == 1) | (z == 2)
    step = piece % line
    if step < 2:
        z = z ^ step
    else:
        z = jnp.where(inside, z ^ (5 - step), z ^ step)
    parts = [
        tokens_ref[:, pl.ds(aligned(((g * MEMBERS + (m ^ k)) * line + z) * HEAD_SIZE), HEAD_SIZE)]
        for k in (2 * half, 2 * half + 1)
    ]
    return jnp.concatenate(parts, axis=1)


def facts_of(message_ref):
    rows = message_ref.shape[0] - META_ROWS
    facts = message_ref[rows:, : 2 * HEAD_SIZE].astype(jnp.float32)
    return facts[0:1, :], facts[HALF : HALF + 1, :]


def iota(shape, dimension):
    return lax.broadcasted_iota(jnp.int32, shape, dimension).astype(jnp.float32)


def project_body(early, late, line, here_ref, *refs):
    books, pieces, outs = refs[:2], refs[2 : 2 + len(early)], refs[2 + len(early) : -2]
    tokens_ref, sems = refs[-2:]
    length, width = books[0].shape
    deep = width // 2
    mine = here_ref[0] if line else 0
    copies = []
    for side in range(2):
        at = pl.ds(pl.multiple_of((mine ^ side) * deep, deep), deep)
        for n in range(2):
            copies.append(
                pltpu.make_async_copy(books[n].at[:, at], tokens_ref.at[n, :, at], sems.at[2 * side + n])
            )
            copies[-1].start()
    tokens = [tokens_ref.at[n] for n in range(2)]
    total = None
    near = [n for n, (piece, half) in enumerate(early) if piece < line]
    far = [n for n in range(len(early)) if n not in near]
    for side, members in enumerate((near, far)):
        for one in copies[2 * side : 2 * side + 2]:
            one.wait()
        for at in members:
            columns = jnp.concatenate(
                [columns_of(one, here_ref, *early[at], line) for one in tokens], axis=0
            )
            term = jnp.dot(columns, pieces[at][...], preferred_element_type=jnp.float32)
            total = term if total is None else total + term
    for n in range(2):
        outs[n][...] = total[n * length : (n + 1) * length]
        for k, place in enumerate(late):
            columns = columns_of(tokens[n], here_ref, *place, line)
            wide = columns.shape[1]
            outs[2 + n][:, k * wide : (k + 1) * wide] = columns


def sigma_plus(v):
    return jnp.where(v > 0, v + 1.0, jnp.exp(jnp.minimum(v, 0.0)))


def split(values):
    high = values.astype(jnp.bfloat16)
    return high, (values - high.astype(jnp.float32)).astype(jnp.bfloat16)


def late_rows(here_ref, chosen_ref, start, width, *pieces):
    *whole, inner, outer, part = pieces
    lost = inner.shape[1] - outer.shape[1] if start else 0
    at = slice(start - lost, start - lost + width)
    inside = (here_ref[2] == 1) | (here_ref[2] == 2)

    @pl.when(inside)
    def _():
        chosen_ref[...] = inner[:, start : start + width]

    @pl.when(jnp.logical_not(inside))
    def _():
        chosen_ref[...] = outer[:, at]

    rows = [piece[:, start : start + width] for piece in whole]
    return jnp.concatenate(rows + [chosen_ref[...], part[:, at]], axis=0)


def kv_body(n_late, here_ref, *refs):
    pieces, refs, chosen_ref = refs[:n_late], refs[n_late:-1], refs[-1]
    sums, lates, messages = refs[:MEMBERS], refs[MEMBERS : 2 * MEMBERS], refs[2 * MEMBERS : 3 * MEMBERS]
    outs = refs[3 * MEMBERS :]
    rows = late_rows(here_ref, chosen_ref, 0, 2 * HEAD_SIZE, *pieces)
    kvs = []
    for seg in range(MEMBERS):
        total = sums[seg][:, : 2 * HEAD_SIZE]
        total += jnp.dot(lates[seg][...], rows, preferred_element_type=jnp.float32)
        kvs.append(total.astype(jnp.bfloat16))
        outs[2 * seg][...] = kvs[seg]
    whole = None
    for seg, kv in enumerate(kvs):
        length = kv.shape[0]
        valid, _ = facts_of(messages[seg])
        keys = kv[:, :HEAD_SIZE].astype(jnp.float32)
        live = iota((length, HEAD_SIZE), 0) < valid[:, :HEAD_SIZE]
        sig = jnp.where(live, sigma_plus(keys), 0.0)
        wide = jnp.concatenate(
            [kv[:, HEAD_SIZE:], jnp.ones((length, HEAD_SIZE), jnp.bfloat16)], axis=1
        )
        high, low = split(sig)
        over = (((0,), (0,)), ((), ()))
        delta = lax.dot_general(high, wide, over, preferred_element_type=jnp.float32)
        delta += lax.dot_general(low, wide, over, preferred_element_type=jnp.float32)
        outs[2 * seg + 1][...] = delta
        whole = delta if whole is None else whole + delta
    outs[-1][...] = whole.astype(jnp.bfloat16)


def local_body(n, n_late, start, heads, here_ref, *refs):
    pieces, refs, chosen_ref = refs[:n_late], refs[n_late:-1], refs[-1]
    kvs, messages, sums, lates, outs = [refs[k * n : (k + 1) * n] for k in range(4)] + [refs[4 * n :]]
    rows = late_rows(here_ref, chosen_ref, start, heads * HEAD_SIZE, *pieces)
    columns = slice(start, start + heads * HEAD_SIZE)
    queries = []
    for at in range(n):
        total = sums[at][:, columns] + jnp.dot(
            lates[at][...], rows, preferred_element_type=jnp.float32
        )
        queries.append(total.astype(jnp.bfloat16))
        outs[2 * at][...] = queries[at]
    work = [(at, block) for at in range(n) for block in range(queries[0].shape[0] // BLK)]
    span = lambda block: slice(block * BLK, (block + 1) * BLK)
    scores = []
    for at, block in work:
        stacked = jnp.concatenate(
            [queries[at][span(block), h * HEAD_SIZE : (h + 1) * HEAD_SIZE] for h in range(heads)], axis=0
        )
        keys = kvs[at][0 : (block + 1) * BLK, :HEAD_SIZE]
        scores.append(
            lax.dot_general(
                stacked, keys, (((1,), (1,)), ((), ())), preferred_element_type=jnp.float32
            )
        )
    weights = []
    for (at, block), score in zip(work, scores):
        width = (block + 1) * BLK
        valid, seen = facts_of(messages[at])
        i, j = iota((BLK, width), 0) + block * BLK, iota((BLK, width), 1)
        limit = valid[:, :width]
        if block:
            limit = jnp.where((j[0:1] >= block * BLK) | (seen[:, :width] > 0), limit, 0.0)
        allowed = (j <= i) & (j < limit)
        masked = jnp.concatenate(
            [jnp.where(allowed, score[span(h)] * HEAD_SIZE ** (-0.5), -1e30) for h in range(heads)],
            axis=0,
        )
        top = jnp.max(masked, axis=-1, keepdims=True)
        expo = jnp.exp(masked - top)
        total = jnp.maximum(jnp.sum(expo, axis=-1, keepdims=True), 1.0)
        weights.append((expo * (1.0 / total)).astype(jnp.bfloat16))
    for (at, block), weight in zip(work, weights):
        values = kvs[at][0 : (block + 1) * BLK, HEAD_SIZE:]
        local = jnp.dot(weight, values, preferred_element_type=jnp.float32)
        for h in range(heads):
            outs[2 * at + 1][span(block), h * HEAD_SIZE : (h + 1) * HEAD_SIZE] = local[span(h)]


def mix_body(segs, parts, group, here_ref, gate_ref, base_ref, *refs):
    deltas, messages, refs = refs[:MEMBERS], refs[MEMBERS : MEMBERS + len(segs)], refs[MEMBERS + len(segs) :]
    n = len(segs) * len(parts)
    queries, locals_, outs = refs[:n], refs[n : 2 * n], refs[2 * n :]
    me = here_ref[1]
    heads = queries[0].shape[1] // HEAD_SIZE
    length = queries[0].shape[0]
    work = [(at, p, h) for at in range(len(segs)) for p in range(len(parts)) for h in range(heads)]
    memories = []
    for seg in segs:
        memory = jnp.where(here_ref[3] > 0, 1.0, 0.0) * base_ref[...].astype(jnp.float32)
        for other in range(MEMBERS):
            if other != seg:
                earlier = jnp.where((me ^ other) < (me ^ seg), 1.0, 0.0)
                memory = memory + earlier * deltas[other][...]
        memories.append(split(memory))
    columns = lambda h: slice(h * HEAD_SIZE, (h + 1) * HEAD_SIZE)
    numers = []
    for at, p, h in work:
        mem_high, mem_low = memories[at]
        high, low = split(sigma_plus(queries[at * len(parts) + p][:, columns(h)].astype(jnp.float32)))
        numer = jnp.dot(high, mem_high, preferred_element_type=jnp.float32)
        numer += jnp.dot(high, mem_low, preferred_element_type=jnp.float32)
        numer += jnp.dot(low, mem_high, preferred_element_type=jnp.float32)
        numers.append(numer)
    for (at, p, h), numer in zip(work, numers):
        valid, _ = facts_of(messages[at])
        live = iota((length, HEAD_SIZE), 0) < valid[:, :HEAD_SIZE]
        retrieved = numer[:, :HEAD_SIZE] / (numer[:, HEAD_SIZE:] + 1.0)
        logit = jnp.full((1, HEAD_SIZE), gate_ref[me * group + parts[p] * heads + h], jnp.float32)
        gate = 1.0 / (1.0 + jnp.exp(-logit))
        mixed = gate * retrieved + (1.0 - gate) * locals_[at * len(parts) + p][:, columns(h)]
        outs[at * len(parts) + p][:, columns(h)] = jnp.where(live, mixed, 0.0).astype(jnp.bfloat16)


def assemble_body(counts, here_ref, *refs):
    parts, out = list(refs[1:-1]), refs[-1]
    width = out.shape[1] // MEMBERS
    for k, count in enumerate(counts):
        for c in range(count):
            at = (here_ref[1] ^ k) * width + c * (width // count)
            out[:, pl.ds(aligned(at), width // count)] = parts.pop(0)[...]


def gate_body(*refs):
    refs[-1][...] = jnp.zeros_like(refs[-1])


def after(array, *others):
    return lax.optimization_barrier((array,) + others)[0]


def shards(sizes, tokens, w_query, w_key, value_weight, gate_bias, block_mask, valid_len):
    n_seg, n_z = sizes
    n_groups = n_seg // MEMBERS
    heads_kv = w_key.shape[1] // HEAD_SIZE
    group = w_query.shape[1] // w_key.shape[1]
    rows = w_query.shape[0]
    length, width = tokens.shape[1], tokens.shape[2]
    assert heads_kv == MEMBERS and group == 4 and length == 2 * BLK
    seg = lax.axis_index("seg")
    z = lax.axis_index("fsdp")
    g, m = seg // MEMBERS, seg % MEMBERS
    here = jnp.stack([g, m, z, g if n_groups == 2 else 1]).astype(jnp.int32)
    bf16, f32 = jnp.bfloat16, jnp.float32
    shape = jax.ShapeDtypeStruct

    def permute(array, to):
        pairs = []
        for gg in range(n_groups):
            for mm in range(MEMBERS):
                for zz in range(n_z):
                    target = to(gg, mm, zz)
                    if target is not None:
                        index = lambda t: (t[0] * MEMBERS + t[1]) * n_z + t[2]
                        pairs.append((index((gg, mm, zz)), index(target)))
        return lax.ppermute(array, AXES, pairs)

    def to_member(array, k):
        return permute(array, lambda gg, mm, zz: (gg, mm ^ k, zz))

    wide = (2 + group) * HEAD_SIZE
    packed = call(
        functools.partial(pack_body, group),
        [shape((rows + META_ROWS, wide), bf16)] * MEMBERS,
        [SMEM] * 3 + [VMEM] * 3,
        limit=56 << 20,
    )(here, valid_len, block_mask, w_query, w_key, value_weight)
    messages = [packed[0], *[to_member(packed[k], k) for k in (1, 2, 3)]]

    def gathered(piece):
        index = lambda gg, mm, zz: (gg * MEMBERS + mm) * n_z + zz
        everything = lax.all_gather(
            piece,
            AXES,
            axis_index_groups=[
                [index(gg, mm, zz) for gg in range(n_groups) for zz in range(n_z)]
                for mm in range(MEMBERS)
            ],
        )
        columns = piece.shape[1]
        natural = everything.reshape(n_groups, n_z, MEMBERS, rows, columns)
        members = jnp.arange(MEMBERS, dtype=jnp.int32) ^ m
        natural = jnp.take(natural, members, axis=2).transpose(0, 2, 1, 3, 4)
        return list(natural.reshape(-1, MEMBERS * HEAD_SIZE, columns))

    pieces = [
        jnp.concatenate([messages[k][:rows] for k in members], axis=0) for members in ((0, 1), (2, 3))
    ]
    n_pieces = width // (MEMBERS * HEAD_SIZE)
    sums, lates = [None] * MEMBERS, [None] * MEMBERS

    def project(segs, early, late, halves, line):
        deep = MEMBERS * HEAD_SIZE // 2
        found = call(
            functools.partial(project_body, early, late, line),
            [shape((length, wide), f32)] * 2 + [shape((length, len(late) * deep), bf16)] * 2,
            [SMEM] + [ANY] * 2 + [VMEM] * len(early),
            flops=2 * 2 * length * len(early) * deep * wide,
            scratch=[pltpu.VMEM((2, length, width), bf16), pltpu.SemaphoreType.DMA((4,))],
        )(here, *[books[s] for s in segs], *[halves[half][piece] for piece, half in early])
        for at, s in enumerate(segs):
            sums[s], lates[s] = found[at], found[2 + at]

    cut = 2 * HEAD_SIZE
    if n_groups == 2 and n_z == 4:
        assert rows == HEAD_SIZE
        inside = (z == 1) | (z == 2)
        over = lambda part: permute(part, lambda gg, mm, zz: (gg ^ 1, mm, zz))
        pair = lambda part: permute(part, lambda gg, mm, zz: (gg, mm, zz ^ 1))
        outward = lambda part: permute(
            part, lambda gg, mm, zz: (gg, mm, zz ^ 1) if zz in (1, 2) else None
        )
        inward = lambda part: permute(
            part, lambda gg, mm, zz: (gg, mm, zz ^ 3) if zz in (1, 2) else None
        )
        locked = lambda *parts: lax.optimization_barrier(parts)
        stage1 = lambda piece: (pair(piece), inward(piece), over(piece))
        stage2 = lambda one, inner: (inward(one), outward(inner), over(one))
        stage3 = lambda middle, two: (outward(middle), over(two))

        a, b, own, sibling = locked(*pieces, tokens[0], to_member(tokens[0], 1))
        across = to_member(own, 2)
        a_one, a_inner, a_far0 = locked(*stage1(a))
        b_one, b_inner, b_far0 = locked(*stage1(b))
        a_middle, a_outer, a_far1 = locked(*stage2(a_one, a_inner))
        b_middle, b_outer, b_far1 = locked(*stage2(b_one, b_inner))
        a_two = jnp.where(inside, a_inner, a_outer)
        a_inner, (a_last, a_far2) = inward(a_far1), stage3(a_middle, a_two)
        b_two = jnp.where(inside, b_inner, b_outer)
        b_last, b_far2 = stage3(b_middle, b_two)
        a_last, a_far2, a_middle, a_inner = locked(a_last, a_far2, a_middle, a_inner)
        a_three = jnp.where(inside, a_middle, a_last)
        books = [own, sibling]
        upper = [a, a_one, a_two, a_three, a_far0, a_far1, a_far2]
        lower = [b, b_one, b_two, None, b_far0, b_far1]
        late = [(3, 1), (6, 1), (7, 0), (7, 1)]
        early = [(k, half) for half in range(2) for k in range(8) if (k, half) not in late]
        project((0, 1), early, late, (upper, lower), n_z)
        b_last, b_far2, b_middle, sums[0], sums[1], across = locked(
            b_last, b_far2, b_middle, sums[0], sums[1], after(across, a_last, a_far2)
        )
        books += [across, to_member(across, 1)]
        project((2, 3), early, late, (upper, lower), n_z)
        b_three = jnp.where(inside, b_middle, b_last)
        pieces = [b_three, b_far2]
        outer_kv, outer_q = [outward(after(a_inner[:, at], b_three)) for at in (slice(0, cut), slice(cut, None))]
        inner = a_inner
        finish = lambda at: over(b_three[:, at])
    else:
        across, sibling = to_member(tokens[0], 2), to_member(tokens[0], 1)
        books = [tokens[0], sibling, across, to_member(across, 1)]
        full = gathered(jnp.concatenate(pieces, axis=0))
        deep = MEMBERS * HEAD_SIZE // 2
        upper, lower = [part[:deep] for part in full], [part[deep:] for part in full]
        late = [(n_pieces - 1, 0), (n_pieces - 1, 1)]
        early = [(k, half) for half in range(2) for k in range(n_pieces - 1)]
        late = [(n_pieces - 2, 1)] + late
        early.remove(late[0])
        for segs in ((0, 1), (2, 3)):
            project(segs, early, late, (upper, lower), 0)
        pieces = [lower[-2]]
        outer_kv, outer_q = upper[-1][:, :cut], upper[-1][:, cut:]
        inner = upper[-1]
        finish = lambda at: lower[-1][:, at]

    halves = [slice(k * HEAD_SIZE, (k + 2) * HEAD_SIZE) for k in (0, 2, 4)]
    lower_kv, lower_q = finish(slice(0, cut)), finish(slice(cut, None))
    found = call(
        functools.partial(kv_body, len(late) + 1),
        [shape((length, 2 * HEAD_SIZE), bf16), shape((HEAD_SIZE, 2 * HEAD_SIZE), f32)] * MEMBERS
        + [shape((HEAD_SIZE, 2 * HEAD_SIZE), bf16)],
        [SMEM] + [VMEM] * (len(late) + 1 + 3 * MEMBERS),
        flops=2 * MEMBERS * length * len(late) * MEMBERS * HEAD_SIZE * HEAD_SIZE,
        scratch=[pltpu.VMEM((MEMBERS * HEAD_SIZE // 2, cut), bf16)],
    )(here, *pieces, inner, outer_kv, lower_kv, *sums, *lates, *messages)
    kvs, deltas, total = found[0:-1:2], found[1:-1:2], found[-1]

    base = None
    for a in range(1, n_groups):
        term = permute(total, lambda gg, mm, zz: (gg ^ a, mm, zz))
        if n_groups > 2:
            term = jnp.where((g ^ a) < g, term, 0).astype(f32)
        base = term if base is None else base + term

    half = group // 2

    def local(segs, part, *others):
        found = call(
            functools.partial(local_body, len(segs), len(late) + 1, halves[1 + part].start, half),
            [shape((length, half * HEAD_SIZE), bf16), shape((length, half * HEAD_SIZE), f32)] * len(segs),
            [SMEM] + [VMEM] * (len(late) + 1 + 4 * len(segs)),
            flops=4 * len(segs) * length * length * half * HEAD_SIZE,
            scratch=[pltpu.VMEM((MEMBERS * HEAD_SIZE // 2, half * HEAD_SIZE), bf16)],
        )(here, *pieces, inner, outer_q, after(lower_q, *others), *[one[s] for one in (kvs, messages, sums, lates) for s in segs])
        return {(s, part): (found[2 * at], found[2 * at + 1]) for at, s in enumerate(segs)}

    def mix(segs, parts, base, ready):
        keys = [(s, part) for s in segs for part in parts]
        return call(
            functools.partial(mix_body, segs, parts, group),
            [shape((length, half * HEAD_SIZE), bf16)] * len(keys),
            [SMEM] * 2 + [VMEM] * (1 + MEMBERS + len(segs) + 2 * len(keys)),
            flops=2 * len(keys) * length * half * HEAD_SIZE * HEAD_SIZE * 6,
        )(
            here, gate_bias, base, *deltas, *[messages[s] for s in segs],
            *[ready[key][0] for key in keys], *[ready[key][1] for key in keys],
        )

    ready = local((2, 3), 0)
    base = after(base, *ready[2, 0])
    two0, three0 = mix((2, 3), (0,), base, ready)
    ready |= local((2, 3), 1, two0, three0)
    two1, three1 = mix((2, 3), (1,), base, ready)
    ready |= local((1, 0), 0, two1, three1)
    ready |= local((1, 0), 1, two1, three1)
    one0, one1, mine0, mine1 = mix((1, 0), (0, 1), after(base, two1, three1), ready)
    sent = [mine0, mine1]
    for k, parts in ((1, (one0, one1)), (2, (two0, two1)), (3, (three0, three1))):
        sent += [to_member(part, k) for part in parts]
    far = sent[4:]
    (gate,) = call(gate_body, [shape((8, HEAD_SIZE), f32)], [ANY] * len(far), moved=16 << 20)(*far)
    (output,) = call(
        functools.partial(assemble_body, (2,) * MEMBERS),
        [shape((length, w_query.shape[1]), bf16)],
        [SMEM] + [VMEM] * (1 + len(sent)),
    )(here, gate, *sent)
    return output[None]


def solution(mesh):
    in_specs = (
        P("fsdp", "seg", None),
        P(("seg", "fsdp"), None),
        P(("seg", "fsdp"), None),
        P(("seg", "fsdp"), None),
        P(),
        P("fsdp", "seg", None, None),
        P("fsdp", "seg"),
    )
    out_specs = P("fsdp", "seg", None)
    body = functools.partial(shards, (mesh.shape["seg"], mesh.shape["fsdp"]))
    return jax.shard_map(body, mesh=mesh, in_specs=in_specs, out_specs=out_specs, check_vma=False)
```

```python
import functools

import jax
import jax.numpy as jnp
from jax import lax
from jax.experimental import pallas as pl
from jax.experimental.pallas import tpu as pltpu
from jax.sharding import PartitionSpec as P

HEAD_SIZE = 128
BLK = 128
MEMBERS = 4
META_ROWS = 16
HALF = META_ROWS // 2
AXES = ("seg", "fsdp")

VMEM = pl.BlockSpec(memory_space=pltpu.VMEM)
SMEM = pl.BlockSpec(memory_space=pltpu.SMEM)
ANY = pl.BlockSpec(memory_space=pl.ANY)
HBM = pl.BlockSpec(memory_space=pltpu.HBM)


def call(body, outs, in_specs, flops=0, scratch=(), out_spec=VMEM, limit=16 << 20, moved=4 << 20):
    return pl.pallas_call(
        body,
        out_shape=outs,
        in_specs=in_specs,
        out_specs=[out_spec] * len(outs),
        scratch_shapes=list(scratch),
        compiler_params=pltpu.CompilerParams(vmem_limit_bytes=limit),
        cost_estimate=pl.CostEstimate(flops=flops, bytes_accessed=moved, transcendentals=0),
    )


def aligned(offset):
    return pl.multiple_of(offset, HEAD_SIZE)


def pack_body(group, here_ref, valid_ref, mask_ref, wq_ref, wk_ref, wv_ref, *outs):
    rows, wide = wk_ref.shape[0], group * HEAD_SIZE
    row = lax.broadcasted_iota(jnp.int32, (META_ROWS, outs[0].shape[1]), 0)
    facts = jnp.where(row < HALF, valid_ref[0, 0], mask_ref[0, 0, 1, 0])
    facts = facts.astype(jnp.float32).astype(jnp.bfloat16)
    for k in range(MEMBERS):
        head, out = here_ref[1] ^ k, outs[k]
        at = aligned(head * HEAD_SIZE)
        out[:rows, :HEAD_SIZE] = wk_ref[:, pl.ds(at, HEAD_SIZE)]
        out[:rows, HEAD_SIZE : 2 * HEAD_SIZE] = wv_ref[:, pl.ds(at, HEAD_SIZE)]
        out[:rows, 2 * HEAD_SIZE :] = wq_ref[:, pl.ds(aligned(head * wide), wide)]
        out[rows:, :] = facts


def columns_of(tokens_ref, here_ref, piece, half, line):
    deep = MEMBERS * HEAD_SIZE // 2
    if not line:
        return tokens_ref[:, pl.ds((2 * piece + half) * deep, deep)]
    g, m, z = here_ref[0] ^ (piece // line), here_ref[1], here_ref[2]
    inside = (z == 1) | (z == 2)
    step = piece % line
    if step < 2:
        z = z ^ step
    else:
        z = jnp.where(inside, z ^ (5 - step), z ^ step)
    parts = [
        tokens_ref[:, pl.ds(aligned(((g * MEMBERS + (m ^ k)) * line + z) * HEAD_SIZE), HEAD_SIZE)]
        for k in (2 * half, 2 * half + 1)
    ]
    return jnp.concatenate(parts, axis=1)


def facts_of(message_ref):
    rows = message_ref.shape[0] - META_ROWS
    facts = message_ref[rows:, : 2 * HEAD_SIZE].astype(jnp.float32)
    return facts[0:1, :], facts[HALF : HALF + 1, :]


def iota(shape, dimension):
    return lax.broadcasted_iota(jnp.int32, shape, dimension).astype(jnp.float32)


def project_body(early, late, line, here_ref, *refs):
    tokens, pieces, outs = refs[:2], refs[2 : 2 + len(early)], refs[2 + len(early) :]
    length = tokens[0].shape[0]
    total = None
    for place, piece in zip(early, pieces):
        columns = jnp.concatenate([columns_of(one, here_ref, *place, line) for one in tokens], axis=0)
        term = jnp.dot(columns, piece[...], preferred_element_type=jnp.float32)
        total = term if total is None else total + term
    for n in range(2):
        outs[n][...] = total[n * length : (n + 1) * length]
        for k, place in enumerate(late):
            columns = columns_of(tokens[n], here_ref, *place, line)
            deep = columns.shape[1]
            outs[2 + n][:, k * deep : (k + 1) * deep] = columns


def sigma_plus(v):
    return jnp.where(v > 0, v + 1.0, jnp.exp(jnp.minimum(v, 0.0)))


def split(values):
    high = values.astype(jnp.bfloat16)
    return high, (values - high.astype(jnp.float32)).astype(jnp.bfloat16)


def late_rows(here_ref, chosen_ref, start, width, *pieces):
    *whole, inner, outer, part = pieces
    lost = inner.shape[1] - outer.shape[1] if start else 0
    at = slice(start - lost, start - lost + width)
    inside = (here_ref[2] == 1) | (here_ref[2] == 2)

    @pl.when(inside)
    def _():
        chosen_ref[...] = inner[:, start : start + width]

    @pl.when(jnp.logical_not(inside))
    def _():
        chosen_ref[...] = outer[:, at]

    rows = [piece[:, start : start + width] for piece in whole]
    return jnp.concatenate(rows + [chosen_ref[...], part[:, at]], axis=0)


def kv_body(n_late, here_ref, *refs):
    pieces, refs, chosen_ref = refs[:n_late], refs[n_late:-1], refs[-1]
    sums, lates, messages = refs[:MEMBERS], refs[MEMBERS : 2 * MEMBERS], refs[2 * MEMBERS : 3 * MEMBERS]
    outs = refs[3 * MEMBERS :]
    rows = late_rows(here_ref, chosen_ref, 0, 2 * HEAD_SIZE, *pieces)
    kvs = []
    for seg in range(MEMBERS):
        total = sums[seg][:, : 2 * HEAD_SIZE]
        total += jnp.dot(lates[seg][...], rows, preferred_element_type=jnp.float32)
        kvs.append(total.astype(jnp.bfloat16))
        outs[2 * seg][...] = kvs[seg]
    whole = None
    for seg, kv in enumerate(kvs):
        length = kv.shape[0]
        valid, _ = facts_of(messages[seg])
        keys = kv[:, :HEAD_SIZE].astype(jnp.float32)
        live = iota((length, HEAD_SIZE), 0) < valid[:, :HEAD_SIZE]
        sig = jnp.where(live, sigma_plus(keys), 0.0)
        wide = jnp.concatenate(
            [kv[:, HEAD_SIZE:], jnp.ones((length, HEAD_SIZE), jnp.bfloat16)], axis=1
        )
        high, low = split(sig)
        over = (((0,), (0,)), ((), ()))
        delta = lax.dot_general(high, wide, over, preferred_element_type=jnp.float32)
        delta += lax.dot_general(low, wide, over, preferred_element_type=jnp.float32)
        outs[2 * seg + 1][...] = delta
        whole = delta if whole is None else whole + delta
    outs[-1][...] = whole.astype(jnp.bfloat16)


def local_body(n, n_late, start, heads, here_ref, *refs):
    pieces, refs, chosen_ref = refs[:n_late], refs[n_late:-1], refs[-1]
    kvs, messages, sums, lates, outs = [refs[k * n : (k + 1) * n] for k in range(4)] + [refs[4 * n :]]
    rows = late_rows(here_ref, chosen_ref, start, heads * HEAD_SIZE, *pieces)
    columns = slice(start, start + heads * HEAD_SIZE)
    queries = []
    for at in range(n):
        total = sums[at][:, columns] + jnp.dot(
            lates[at][...], rows, preferred_element_type=jnp.float32
        )
        queries.append(total.astype(jnp.bfloat16))
        outs[2 * at][...] = queries[at]
    work = [(at, block) for at in range(n) for block in range(queries[0].shape[0] // BLK)]
    span = lambda block: slice(block * BLK, (block + 1) * BLK)
    scores = []
    for at, block in work:
        stacked = jnp.concatenate(
            [queries[at][span(block), h * HEAD_SIZE : (h + 1) * HEAD_SIZE] for h in range(heads)], axis=0
        )
        keys = kvs[at][0 : (block + 1) * BLK, :HEAD_SIZE]
        scores.append(
            lax.dot_general(
                stacked, keys, (((1,), (1,)), ((), ())), preferred_element_type=jnp.float32
            )
        )
    weights = []
    for (at, block), score in zip(work, scores):
        width = (block + 1) * BLK
        valid, seen = facts_of(messages[at])
        i, j = iota((BLK, width), 0) + block * BLK, iota((BLK, width), 1)
        limit = valid[:, :width]
        if block:
            limit = jnp.where((j[0:1] >= block * BLK) | (seen[:, :width] > 0), limit, 0.0)
        allowed = (j <= i) & (j < limit)
        masked = jnp.concatenate(
            [jnp.where(allowed, score[span(h)] * HEAD_SIZE ** (-0.5), -1e30) for h in range(heads)],
            axis=0,
        )
        top = jnp.max(masked, axis=-1, keepdims=True)
        expo = jnp.exp(masked - top)
        total = jnp.maximum(jnp.sum(expo, axis=-1, keepdims=True), 1.0)
        weights.append((expo * (1.0 / total)).astype(jnp.bfloat16))
    for (at, block), weight in zip(work, weights):
        values = kvs[at][0 : (block + 1) * BLK, HEAD_SIZE:]
        local = jnp.dot(weight, values, preferred_element_type=jnp.float32)
        for h in range(heads):
            outs[2 * at + 1][span(block), h * HEAD_SIZE : (h + 1) * HEAD_SIZE] = local[span(h)]


def mix_body(segs, parts, group, here_ref, gate_ref, base_ref, *refs):
    deltas, messages, refs = refs[:MEMBERS], refs[MEMBERS : MEMBERS + len(segs)], refs[MEMBERS + len(segs) :]
    n = len(segs) * len(parts)
    queries, locals_, outs = refs[:n], refs[n : 2 * n], refs[2 * n :]
    me = here_ref[1]
    heads = queries[0].shape[1] // HEAD_SIZE
    length = queries[0].shape[0]
    work = [(at, p, h) for at in range(len(segs)) for p in range(len(parts)) for h in range(heads)]
    memories = []
    for seg in segs:
        memory = jnp.where(here_ref[3] > 0, 1.0, 0.0) * base_ref[...].astype(jnp.float32)
        for other in range(MEMBERS):
            if other != seg:
                earlier = jnp.where((me ^ other) < (me ^ seg), 1.0, 0.0)
                memory = memory + earlier * deltas[other][...]
        memories.append(split(memory))
    columns = lambda h: slice(h * HEAD_SIZE, (h + 1) * HEAD_SIZE)
    numers = []
    for at, p, h in work:
        mem_high, mem_low = memories[at]
        high, low = split(sigma_plus(queries[at * len(parts) + p][:, columns(h)].astype(jnp.float32)))
        numer = jnp.dot(high, mem_high, preferred_element_type=jnp.float32)
        numer += jnp.dot(high, mem_low, preferred_element_type=jnp.float32)
        numer += jnp.dot(low, mem_high, preferred_element_type=jnp.float32)
        numers.append(numer)
    for (at, p, h), numer in zip(work, numers):
        valid, _ = facts_of(messages[at])
        live = iota((length, HEAD_SIZE), 0) < valid[:, :HEAD_SIZE]
        retrieved = numer[:, :HEAD_SIZE] / (numer[:, HEAD_SIZE:] + 1.0)
        logit = jnp.full((1, HEAD_SIZE), gate_ref[me * group + parts[p] * heads + h], jnp.float32)
        gate = 1.0 / (1.0 + jnp.exp(-logit))
        mixed = gate * retrieved + (1.0 - gate) * locals_[at * len(parts) + p][:, columns(h)]
        outs[at * len(parts) + p][:, columns(h)] = jnp.where(live, mixed, 0.0).astype(jnp.bfloat16)


def assemble_body(counts, here_ref, *refs):
    parts, out = list(refs[1:-1]), refs[-1]
    width = out.shape[1] // MEMBERS
    for k, count in enumerate(counts):
        for c in range(count):
            at = (here_ref[1] ^ k) * width + c * (width // count)
            out[:, pl.ds(aligned(at), width // count)] = parts.pop(0)[...]


def gate_body(*refs):
    refs[-1][...] = jnp.zeros_like(refs[-1])


def after(array, *others):
    return lax.optimization_barrier((array,) + others)[0]


def shards(sizes, tokens, w_query, w_key, value_weight, gate_bias, block_mask, valid_len):
    n_seg, n_z = sizes
    n_groups = n_seg // MEMBERS
    heads_kv = w_key.shape[1] // HEAD_SIZE
    group = w_query.shape[1] // w_key.shape[1]
    rows = w_query.shape[0]
    length, width = tokens.shape[1], tokens.shape[2]
    assert heads_kv == MEMBERS and group == 4 and length == 2 * BLK
    seg = lax.axis_index("seg")
    z = lax.axis_index("fsdp")
    g, m = seg // MEMBERS, seg % MEMBERS
    here = jnp.stack([g, m, z, g if n_groups == 2 else 1]).astype(jnp.int32)
    bf16, f32 = jnp.bfloat16, jnp.float32
    shape = jax.ShapeDtypeStruct

    def permute(array, to):
        pairs = []
        for gg in range(n_groups):
            for mm in range(MEMBERS):
                for zz in range(n_z):
                    target = to(gg, mm, zz)
                    if target is not None:
                        index = lambda t: (t[0] * MEMBERS + t[1]) * n_z + t[2]
                        pairs.append((index((gg, mm, zz)), index(target)))
        return lax.ppermute(array, AXES, pairs)

    def to_member(array, k):
        return permute(array, lambda gg, mm, zz: (gg, mm ^ k, zz))

    wide = (2 + group) * HEAD_SIZE
    packed = call(
        functools.partial(pack_body, group),
        [shape((rows + META_ROWS, wide), bf16)] * MEMBERS,
        [SMEM] * 3 + [VMEM] * 3,
        limit=56 << 20,
    )(here, valid_len, block_mask, w_query, w_key, value_weight)
    messages = [packed[0], *[to_member(packed[k], k) for k in (1, 2, 3)]]

    def gathered(piece):
        index = lambda gg, mm, zz: (gg * MEMBERS + mm) * n_z + zz
        everything = lax.all_gather(
            piece,
            AXES,
            axis_index_groups=[
                [index(gg, mm, zz) for gg in range(n_groups) for zz in range(n_z)]
                for mm in range(MEMBERS)
            ],
        )
        columns = piece.shape[1]
        natural = everything.reshape(n_groups, n_z, MEMBERS, rows, columns)
        members = jnp.arange(MEMBERS, dtype=jnp.int32) ^ m
        natural = jnp.take(natural, members, axis=2).transpose(0, 2, 1, 3, 4)
        return list(natural.reshape(-1, MEMBERS * HEAD_SIZE, columns))

    pieces = [
        jnp.concatenate([messages[k][:rows] for k in members], axis=0) for members in ((0, 1), (2, 3))
    ]
    n_pieces = width // (MEMBERS * HEAD_SIZE)
    sums, lates = [None] * MEMBERS, [None] * MEMBERS

    def project(segs, early, late, halves, line):
        deep = MEMBERS * HEAD_SIZE // 2
        found = call(
            functools.partial(project_body, early, late, line),
            [shape((length, wide), f32)] * 2 + [shape((length, len(late) * deep), bf16)] * 2,
            [SMEM] + [VMEM] * (2 + len(early)),
            flops=2 * 2 * length * len(early) * deep * wide,
        )(here, *[books[s] for s in segs], *[halves[half][piece] for piece, half in early])
        for at, s in enumerate(segs):
            sums[s], lates[s] = found[at], found[2 + at]

    cut = 2 * HEAD_SIZE
    if n_groups == 2 and n_z == 4:
        assert rows == HEAD_SIZE
        inside = (z == 1) | (z == 2)
        over = lambda part: permute(part, lambda gg, mm, zz: (gg ^ 1, mm, zz))
        pair = lambda part: permute(part, lambda gg, mm, zz: (gg, mm, zz ^ 1))
        outward = lambda part: permute(
            part, lambda gg, mm, zz: (gg, mm, zz ^ 1) if zz in (1, 2) else None
        )
        inward = lambda part: permute(
            part, lambda gg, mm, zz: (gg, mm, zz ^ 3) if zz in (1, 2) else None
        )
        locked = lambda *parts: lax.optimization_barrier(parts)
        stage1 = lambda piece: (pair(piece), inward(piece), over(piece))
        stage2 = lambda one, inner: (inward(one), outward(inner), over(one))
        stage3 = lambda middle, two: (outward(middle), over(two))

        a, b, own, sibling = locked(*pieces, tokens[0], to_member(tokens[0], 1))
        across = to_member(own, 2)
        a_one, a_inner, a_far0 = locked(*stage1(a))
        b_one, b_inner, b_far0 = locked(*stage1(b))
        a_middle, a_outer, a_far1 = locked(*stage2(a_one, a_inner))
        b_middle, b_outer, b_far1 = locked(*stage2(b_one, b_inner))
        a_two = jnp.where(inside, a_inner, a_outer)
        a_inner, (a_last, a_far2) = inward(a_far1), stage3(a_middle, a_two)
        b_two = jnp.where(inside, b_inner, b_outer)
        b_last, b_far2 = stage3(b_middle, b_two)
        a_last, a_far2, a_middle, a_inner = locked(a_last, a_far2, a_middle, a_inner)
        a_three = jnp.where(inside, a_middle, a_last)
        books = [own, sibling]
        upper = [a, a_one, a_two, a_three, a_far0, a_far1, a_far2]
        lower = [b, b_one, b_two, None, b_far0, b_far1]
        late = [(3, 1), (6, 1), (7, 0), (7, 1)]
        early = [(k, half) for half in range(2) for k in range(8) if (k, half) not in late]
        project((0, 1), early, late, (upper, lower), n_z)
        b_last, b_far2, b_middle, sums[0], sums[1], across = locked(
            b_last, b_far2, b_middle, sums[0], sums[1], after(across, a_last, a_far2)
        )
        books += [across, to_member(across, 1)]
        project((2, 3), early, late, (upper, lower), n_z)
        b_three = jnp.where(inside, b_middle, b_last)
        pieces = [b_three, b_far2]
        outer_kv, outer_q = [outward(a_inner[:, at]) for at in (slice(0, cut), slice(cut, None))]
        inner = a_inner
        finish = lambda at: over(b_three[:, at])
    else:
        across, sibling = to_member(tokens[0], 2), to_member(tokens[0], 1)
        books = [tokens[0], sibling, across, to_member(across, 1)]
        full = gathered(jnp.concatenate(pieces, axis=0))
        deep = MEMBERS * HEAD_SIZE // 2
        upper, lower = [part[:deep] for part in full], [part[deep:] for part in full]
        late = [(n_pieces - 1, 0), (n_pieces - 1, 1)]
        early = [(k, half) for half in range(2) for k in range(n_pieces - 1)]
        late = [(n_pieces - 2, 1)] + late
        early.remove(late[0])
        for segs in ((0, 1), (2, 3)):
            project(segs, early, late, (upper, lower), 0)
        pieces = [lower[-2]]
        outer_kv, outer_q = upper[-1][:, :cut], upper[-1][:, cut:]
        inner = upper[-1]
        finish = lambda at: lower[-1][:, at]

    halves = [slice(k * HEAD_SIZE, (k + 2) * HEAD_SIZE) for k in (0, 2, 4)]
    lower_kv, lower_q = finish(slice(0, cut)), finish(slice(cut, None))
    found = call(
        functools.partial(kv_body, len(late) + 1),
        [shape((length, 2 * HEAD_SIZE), bf16), shape((HEAD_SIZE, 2 * HEAD_SIZE), f32)] * MEMBERS
        + [shape((HEAD_SIZE, 2 * HEAD_SIZE), bf16)],
        [SMEM] + [VMEM] * (len(late) + 1 + 3 * MEMBERS),
        flops=2 * MEMBERS * length * len(late) * MEMBERS * HEAD_SIZE * HEAD_SIZE,
        scratch=[pltpu.VMEM((MEMBERS * HEAD_SIZE // 2, cut), bf16)],
    )(here, *pieces, inner, outer_kv, lower_kv, *sums, *lates, *messages)
    kvs, deltas, total = found[0:-1:2], found[1:-1:2], found[-1]

    base = None
    for a in range(1, n_groups):
        term = permute(total, lambda gg, mm, zz: (gg ^ a, mm, zz))
        if n_groups > 2:
            term = jnp.where((g ^ a) < g, term, 0).astype(f32)
        base = term if base is None else base + term

    half = group // 2

    def local(segs, part, *others):
        found = call(
            functools.partial(local_body, len(segs), len(late) + 1, halves[1 + part].start, half),
            [shape((length, half * HEAD_SIZE), bf16), shape((length, half * HEAD_SIZE), f32)] * len(segs),
            [SMEM] + [VMEM] * (len(late) + 1 + 4 * len(segs)),
            flops=4 * len(segs) * length * length * half * HEAD_SIZE,
            scratch=[pltpu.VMEM((MEMBERS * HEAD_SIZE // 2, half * HEAD_SIZE), bf16)],
        )(here, *pieces, inner, outer_q, after(lower_q, *others), *[one[s] for one in (kvs, messages, sums, lates) for s in segs])
        return {(s, part): (found[2 * at], found[2 * at + 1]) for at, s in enumerate(segs)}

    def mix(segs, parts, base, ready):
        keys = [(s, part) for s in segs for part in parts]
        return call(
            functools.partial(mix_body, segs, parts, group),
            [shape((length, half * HEAD_SIZE), bf16)] * len(keys),
            [SMEM] * 2 + [VMEM] * (1 + MEMBERS + len(segs) + 2 * len(keys)),
            flops=2 * len(keys) * length * half * HEAD_SIZE * HEAD_SIZE * 6,
        )(
            here, gate_bias, base, *deltas, *[messages[s] for s in segs],
            *[ready[key][0] for key in keys], *[ready[key][1] for key in keys],
        )

    ready = local((2, 3), 0)
    base = after(base, *ready[2, 0])
    two0, three0 = mix((2, 3), (0,), base, ready)
    ready |= local((2, 3), 1, two0, three0)
    two1, three1 = mix((2, 3), (1,), base, ready)
    ready |= local((1, 0), 0, two1, three1)
    ready |= local((1, 0), 1, two1, three1)
    one0, one1, mine0, mine1 = mix((1, 0), (0, 1), after(base, two1, three1), ready)
    sent = [mine0, mine1]
    for k, parts in ((1, (one0, one1)), (2, (two0, two1)), (3, (three0, three1))):
        sent += [to_member(part, k) for part in parts]
    far = sent[4:]
    (gate,) = call(gate_body, [shape((8, HEAD_SIZE), f32)], [ANY] * len(far), moved=16 << 20)(*far)
    (output,) = call(
        functools.partial(assemble_body, (2,) * MEMBERS),
        [shape((length, w_query.shape[1]), bf16)],
        [SMEM] + [VMEM] * (1 + len(sent)),
    )(here, gate, *sent)
    return output[None]


def solution(mesh):
    in_specs = (
        P("fsdp", "seg", None),
        P(("seg", "fsdp"), None),
        P(("seg", "fsdp"), None),
        P(("seg", "fsdp"), None),
        P(),
        P("fsdp", "seg", None, None),
        P("fsdp", "seg"),
    )
    out_specs = P("fsdp", "seg", None)
    body = functools.partial(shards, (mesh.shape["seg"], mesh.shape["fsdp"]))
    return jax.shard_map(body, mesh=mesh, in_specs=in_specs, out_specs=out_specs, check_vma=False)
```

```python
import functools

import jax
import jax.numpy as jnp
from jax import lax
from jax.experimental import pallas as pl
from jax.experimental.pallas import tpu as pltpu
from jax.sharding import PartitionSpec as P

HEAD_SIZE = 128
BLK = 128
MEMBERS = 4
META_ROWS = 16
HALF = META_ROWS // 2
AXES = ("seg", "fsdp")

VMEM = pl.BlockSpec(memory_space=pltpu.VMEM)
SMEM = pl.BlockSpec(memory_space=pltpu.SMEM)
ANY = pl.BlockSpec(memory_space=pl.ANY)
HBM = pl.BlockSpec(memory_space=pltpu.HBM)


def call(body, outs, in_specs, flops=0, scratch=(), out_spec=VMEM, limit=16 << 20, moved=4 << 20):
    return pl.pallas_call(
        body,
        out_shape=outs,
        in_specs=in_specs,
        out_specs=[out_spec] * len(outs),
        scratch_shapes=list(scratch),
        compiler_params=pltpu.CompilerParams(vmem_limit_bytes=limit),
        cost_estimate=pl.CostEstimate(flops=flops, bytes_accessed=moved, transcendentals=0),
    )


def aligned(offset):
    return pl.multiple_of(offset, HEAD_SIZE)


def pack_body(group, here_ref, valid_ref, mask_ref, wq_ref, wk_ref, wv_ref, *outs):
    rows, wide = wk_ref.shape[0], group * HEAD_SIZE
    row = lax.broadcasted_iota(jnp.int32, (META_ROWS, outs[0].shape[1]), 0)
    facts = jnp.where(row < HALF, valid_ref[0, 0], mask_ref[0, 0, 1, 0])
    facts = facts.astype(jnp.float32).astype(jnp.bfloat16)
    for k in range(MEMBERS):
        head, out = here_ref[1] ^ k, outs[k]
        at = aligned(head * HEAD_SIZE)
        out[:rows, :HEAD_SIZE] = wk_ref[:, pl.ds(at, HEAD_SIZE)]
        out[:rows, HEAD_SIZE : 2 * HEAD_SIZE] = wv_ref[:, pl.ds(at, HEAD_SIZE)]
        out[:rows, 2 * HEAD_SIZE :] = wq_ref[:, pl.ds(aligned(head * wide), wide)]
        out[rows:, :] = facts


def columns_of(tokens_ref, here_ref, piece, half, line):
    deep = MEMBERS * HEAD_SIZE // 2
    if not line:
        return tokens_ref[:, pl.ds((2 * piece + half) * deep, deep)]
    g, m, z = here_ref[0] ^ (piece // line), here_ref[1], here_ref[2]
    inside = (z == 1) | (z == 2)
    step = piece % line
    if step < 2:
        z = z ^ step
    else:
        z = jnp.where(inside, z ^ (5 - step), z ^ step)
    parts = [
        tokens_ref[:, pl.ds(aligned(((g * MEMBERS + (m ^ k)) * line + z) * HEAD_SIZE), HEAD_SIZE)]
        for k in (2 * half, 2 * half + 1)
    ]
    return jnp.concatenate(parts, axis=1)


def facts_of(message_ref):
    rows = message_ref.shape[0] - META_ROWS
    facts = message_ref[rows:, : 2 * HEAD_SIZE].astype(jnp.float32)
    return facts[0:1, :], facts[HALF : HALF + 1, :]


def iota(shape, dimension):
    return lax.broadcasted_iota(jnp.int32, shape, dimension).astype(jnp.float32)


def project_body(early, late, line, held, here_ref, *refs):
    if held:
        *refs, held_ref, sems = refs
    tokens, pieces, outs = refs[:2], list(refs[2 : 2 + len(early)]), refs[2 + len(early) :]
    length = tokens[0].shape[0]
    copies = [
        pltpu.make_async_copy(pieces[len(early) - held + n], held_ref.at[n], sems.at[n])
        for n in range(held)
    ]
    for n, one in enumerate(copies):
        one.start()
        pieces[len(early) - held + n] = held_ref.at[n]
    total = None
    for at, (place, piece) in enumerate(zip(early, pieces)):
        if at >= len(early) - held:
            copies[at - len(early) + held].wait()
        columns = jnp.concatenate([columns_of(one, here_ref, *place, line) for one in tokens], axis=0)
        term = jnp.dot(columns, piece[...], preferred_element_type=jnp.float32)
        total = term if total is None else total + term
    for n in range(2):
        outs[n][...] = total[n * length : (n + 1) * length]
        for k, place in enumerate(late):
            columns = columns_of(tokens[n], here_ref, *place, line)
            deep = columns.shape[1]
            outs[2 + n][:, k * deep : (k + 1) * deep] = columns


def sigma_plus(v):
    return jnp.where(v > 0, v + 1.0, jnp.exp(jnp.minimum(v, 0.0)))


def split(values):
    high = values.astype(jnp.bfloat16)
    return high, (values - high.astype(jnp.float32)).astype(jnp.bfloat16)


def late_rows(here_ref, chosen_ref, start, width, *pieces):
    *whole, inner, outer, part = pieces
    lost = inner.shape[1] - outer.shape[1] if start else 0
    at = slice(start - lost, start - lost + width)
    inside = (here_ref[2] == 1) | (here_ref[2] == 2)

    @pl.when(inside)
    def _():
        chosen_ref[...] = inner[:, start : start + width]

    @pl.when(jnp.logical_not(inside))
    def _():
        chosen_ref[...] = outer[:, at]

    rows = [piece[:, start : start + width] for piece in whole]
    return jnp.concatenate(rows + [chosen_ref[...], part[:, at]], axis=0)


def kv_body(n_late, here_ref, *refs):
    pieces, refs, chosen_ref = refs[:n_late], refs[n_late:-1], refs[-1]
    sums, lates, messages = refs[:MEMBERS], refs[MEMBERS : 2 * MEMBERS], refs[2 * MEMBERS : 3 * MEMBERS]
    outs = refs[3 * MEMBERS :]
    rows = late_rows(here_ref, chosen_ref, 0, 2 * HEAD_SIZE, *pieces)
    kvs = []
    for seg in range(MEMBERS):
        total = sums[seg][:, : 2 * HEAD_SIZE]
        total += jnp.dot(lates[seg][...], rows, preferred_element_type=jnp.float32)
        kvs.append(total.astype(jnp.bfloat16))
        outs[2 * seg][...] = kvs[seg]
    whole = None
    for seg, kv in enumerate(kvs):
        length = kv.shape[0]
        valid, _ = facts_of(messages[seg])
        keys = kv[:, :HEAD_SIZE].astype(jnp.float32)
        live = iota((length, HEAD_SIZE), 0) < valid[:, :HEAD_SIZE]
        sig = jnp.where(live, sigma_plus(keys), 0.0)
        wide = jnp.concatenate(
            [kv[:, HEAD_SIZE:], jnp.ones((length, HEAD_SIZE), jnp.bfloat16)], axis=1
        )
        high, low = split(sig)
        over = (((0,), (0,)), ((), ()))
        delta = lax.dot_general(high, wide, over, preferred_element_type=jnp.float32)
        delta += lax.dot_general(low, wide, over, preferred_element_type=jnp.float32)
        outs[2 * seg + 1][...] = delta
        whole = delta if whole is None else whole + delta
    outs[-1][...] = whole.astype(jnp.bfloat16)


def local_body(n, n_late, start, heads, here_ref, *refs):
    pieces, refs, chosen_ref = refs[:n_late], refs[n_late:-1], refs[-1]
    kvs, messages, sums, lates, outs = [refs[k * n : (k + 1) * n] for k in range(4)] + [refs[4 * n :]]
    rows = late_rows(here_ref, chosen_ref, start, heads * HEAD_SIZE, *pieces)
    columns = slice(start, start + heads * HEAD_SIZE)
    queries = []
    for at in range(n):
        total = sums[at][:, columns] + jnp.dot(
            lates[at][...], rows, preferred_element_type=jnp.float32
        )
        queries.append(total.astype(jnp.bfloat16))
        outs[2 * at][...] = queries[at]
    work = [(at, block) for at in range(n) for block in range(queries[0].shape[0] // BLK)]
    span = lambda block: slice(block * BLK, (block + 1) * BLK)
    scores = []
    for at, block in work:
        stacked = jnp.concatenate(
            [queries[at][span(block), h * HEAD_SIZE : (h + 1) * HEAD_SIZE] for h in range(heads)], axis=0
        )
        keys = kvs[at][0 : (block + 1) * BLK, :HEAD_SIZE]
        scores.append(
            lax.dot_general(
                stacked, keys, (((1,), (1,)), ((), ())), preferred_element_type=jnp.float32
            )
        )
    weights = []
    for (at, block), score in zip(work, scores):
        width = (block + 1) * BLK
        valid, seen = facts_of(messages[at])
        i, j = iota((BLK, width), 0) + block * BLK, iota((BLK, width), 1)
        limit = valid[:, :width]
        if block:
            limit = jnp.where((j[0:1] >= block * BLK) | (seen[:, :width] > 0), limit, 0.0)
        allowed = (j <= i) & (j < limit)
        masked = jnp.concatenate(
            [jnp.where(allowed, score[span(h)] * HEAD_SIZE ** (-0.5), -1e30) for h in range(heads)],
            axis=0,
        )
        top = jnp.max(masked, axis=-1, keepdims=True)
        expo = jnp.exp(masked - top)
        total = jnp.maximum(jnp.sum(expo, axis=-1, keepdims=True), 1.0)
        weights.append((expo * (1.0 / total)).astype(jnp.bfloat16))
    for (at, block), weight in zip(work, weights):
        values = kvs[at][0 : (block + 1) * BLK, HEAD_SIZE:]
        local = jnp.dot(weight, values, preferred_element_type=jnp.float32)
        for h in range(heads):
            outs[2 * at + 1][span(block), h * HEAD_SIZE : (h + 1) * HEAD_SIZE] = local[span(h)]


def mix_body(segs, parts, group, here_ref, gate_ref, base_ref, *refs):
    deltas, messages, refs = refs[:MEMBERS], refs[MEMBERS : MEMBERS + len(segs)], refs[MEMBERS + len(segs) :]
    n = len(segs) * len(parts)
    queries, locals_, outs = refs[:n], refs[n : 2 * n], refs[2 * n :]
    me = here_ref[1]
    heads = queries[0].shape[1] // HEAD_SIZE
    length = queries[0].shape[0]
    work = [(at, p, h) for at in range(len(segs)) for p in range(len(parts)) for h in range(heads)]
    memories = []
    for seg in segs:
        memory = jnp.where(here_ref[3] > 0, 1.0, 0.0) * base_ref[...].astype(jnp.float32)
        for other in range(MEMBERS):
            if other != seg:
                earlier = jnp.where((me ^ other) < (me ^ seg), 1.0, 0.0)
                memory = memory + earlier * deltas[other][...]
        memories.append(split(memory))
    columns = lambda h: slice(h * HEAD_SIZE, (h + 1) * HEAD_SIZE)
    numers = []
    for at, p, h in work:
        mem_high, mem_low = memories[at]
        high, low = split(sigma_plus(queries[at * len(parts) + p][:, columns(h)].astype(jnp.float32)))
        numer = jnp.dot(high, mem_high, preferred_element_type=jnp.float32)
        numer += jnp.dot(high, mem_low, preferred_element_type=jnp.float32)
        numer += jnp.dot(low, mem_high, preferred_element_type=jnp.float32)
        numers.append(numer)
    for (at, p, h), numer in zip(work, numers):
        valid, _ = facts_of(messages[at])
        live = iota((length, HEAD_SIZE), 0) < valid[:, :HEAD_SIZE]
        retrieved = numer[:, :HEAD_SIZE] / (numer[:, HEAD_SIZE:] + 1.0)
        logit = jnp.full((1, HEAD_SIZE), gate_ref[me * group + parts[p] * heads + h], jnp.float32)
        gate = 1.0 / (1.0 + jnp.exp(-logit))
        mixed = gate * retrieved + (1.0 - gate) * locals_[at * len(parts) + p][:, columns(h)]
        outs[at * len(parts) + p][:, columns(h)] = jnp.where(live, mixed, 0.0).astype(jnp.bfloat16)


def assemble_body(counts, here_ref, *refs):
    parts, out = list(refs[1:-1]), refs[-1]
    width = out.shape[1] // MEMBERS
    for k, count in enumerate(counts):
        for c in range(count):
            at = (here_ref[1] ^ k) * width + c * (width // count)
            out[:, pl.ds(aligned(at), width // count)] = parts.pop(0)[...]


def gate_body(*refs):
    refs[-1][...] = jnp.zeros_like(refs[-1])


def after(array, *others):
    return lax.optimization_barrier((array,) + others)[0]


def shards(sizes, tokens, w_query, w_key, value_weight, gate_bias, block_mask, valid_len):
    n_seg, n_z = sizes
    n_groups = n_seg // MEMBERS
    heads_kv = w_key.shape[1] // HEAD_SIZE
    group = w_query.shape[1] // w_key.shape[1]
    rows = w_query.shape[0]
    length, width = tokens.shape[1], tokens.shape[2]
    assert heads_kv == MEMBERS and group == 4 and length == 2 * BLK
    seg = lax.axis_index("seg")
    z = lax.axis_index("fsdp")
    g, m = seg // MEMBERS, seg % MEMBERS
    here = jnp.stack([g, m, z, g if n_groups == 2 else 1]).astype(jnp.int32)
    bf16, f32 = jnp.bfloat16, jnp.float32
    shape = jax.ShapeDtypeStruct

    def permute(array, to):
        pairs = []
        for gg in range(n_groups):
            for mm in range(MEMBERS):
                for zz in range(n_z):
                    target = to(gg, mm, zz)
                    if target is not None:
                        index = lambda t: (t[0] * MEMBERS + t[1]) * n_z + t[2]
                        pairs.append((index((gg, mm, zz)), index(target)))
        return lax.ppermute(array, AXES, pairs)

    def to_member(array, k):
        return permute(array, lambda gg, mm, zz: (gg, mm ^ k, zz))

    wide = (2 + group) * HEAD_SIZE
    packed = call(
        functools.partial(pack_body, group),
        [shape((rows + META_ROWS, wide), bf16)] * MEMBERS,
        [SMEM] * 3 + [VMEM] * 3,
        limit=56 << 20,
    )(here, valid_len, block_mask, w_query, w_key, value_weight)
    messages = [packed[0], *[to_member(packed[k], k) for k in (1, 2, 3)]]

    def gathered(piece):
        index = lambda gg, mm, zz: (gg * MEMBERS + mm) * n_z + zz
        everything = lax.all_gather(
            piece,
            AXES,
            axis_index_groups=[
                [index(gg, mm, zz) for gg in range(n_groups) for zz in range(n_z)]
                for mm in range(MEMBERS)
            ],
        )
        columns = piece.shape[1]
        natural = everything.reshape(n_groups, n_z, MEMBERS, rows, columns)
        members = jnp.arange(MEMBERS, dtype=jnp.int32) ^ m
        natural = jnp.take(natural, members, axis=2).transpose(0, 2, 1, 3, 4)
        return list(natural.reshape(-1, MEMBERS * HEAD_SIZE, columns))

    pieces = [
        jnp.concatenate([messages[k][:rows] for k in members], axis=0) for members in ((0, 1), (2, 3))
    ]
    n_pieces = width // (MEMBERS * HEAD_SIZE)
    sums, lates = [None] * MEMBERS, [None] * MEMBERS

    def project(segs, early, late, halves, line, held=0):
        deep = MEMBERS * HEAD_SIZE // 2
        found = call(
            functools.partial(project_body, early, late, line, held),
            [shape((length, wide), f32)] * 2 + [shape((length, len(late) * deep), bf16)] * 2,
            [SMEM] + [VMEM] * (2 + len(early) - held) + [ANY] * held,
            flops=2 * 2 * length * len(early) * deep * wide,
            scratch=[pltpu.VMEM((held, deep, wide), bf16), pltpu.SemaphoreType.DMA((held,))] if held else (),
        )(here, *[books[s] for s in segs], *[halves[half][piece] for piece, half in early])
        for at, s in enumerate(segs):
            sums[s], lates[s] = found[at], found[2 + at]

    cut = 2 * HEAD_SIZE
    if n_groups == 2 and n_z == 4:
        assert rows == HEAD_SIZE
        inside = (z == 1) | (z == 2)
        over = lambda part: permute(part, lambda gg, mm, zz: (gg ^ 1, mm, zz))
        pair = lambda part: permute(part, lambda gg, mm, zz: (gg, mm, zz ^ 1))
        outward = lambda part: permute(
            part, lambda gg, mm, zz: (gg, mm, zz ^ 1) if zz in (1, 2) else None
        )
        inward = lambda part: permute(
            part, lambda gg, mm, zz: (gg, mm, zz ^ 3) if zz in (1, 2) else None
        )
        locked = lambda *parts: lax.optimization_barrier(parts)
        stage1 = lambda piece: (pair(piece), inward(piece), over(piece))
        stage2 = lambda one, inner: (inward(one), outward(inner), over(one))
        stage3 = lambda middle, two: (outward(middle), over(two))

        a, b, own, sibling = locked(*pieces, tokens[0], to_member(tokens[0], 1))
        across = to_member(own, 2)
        a_one, a_inner, a_far0 = locked(*stage1(a))
        b_one, b_inner, b_far0 = locked(*stage1(b))
        a_middle, a_outer, a_far1 = locked(*stage2(a_one, a_inner))
        b_middle, b_outer, b_far1 = locked(*stage2(b_one, b_inner))
        a_two = jnp.where(inside, a_inner, a_outer)
        a_inner, (a_last, a_far2) = inward(a_far1), stage3(a_middle, a_two)
        b_two = jnp.where(inside, b_inner, b_outer)
        b_last, b_far2 = stage3(b_middle, b_two)
        a_last, a_far2, a_middle, a_inner = locked(a_last, a_far2, a_middle, a_inner)
        a_three = jnp.where(inside, a_middle, a_last)
        books = [own, sibling]
        upper = [a, a_one, a_two, a_three, a_far0, a_far1, a_far2]
        lower = [b, b_one, b_two, None, b_far0, b_far1]
        late = [(3, 1), (6, 1), (7, 0), (7, 1)]
        early = [(k, half) for half in range(2) for k in range(8) if k != 4 and (k, half) not in late]
        early += [(4, 0), (4, 1)]
        project((0, 1), early, late, (upper, lower), n_z, 2)
        b_last, b_far2, b_middle, sums[0], sums[1], across = locked(
            b_last, b_far2, b_middle, sums[0], sums[1], after(across, a_last, a_far2)
        )
        books += [across, to_member(across, 1)]
        project((2, 3), early, late, (upper, lower), n_z, 2)
        b_three = jnp.where(inside, b_middle, b_last)
        pieces = [b_three, b_far2]
        outer_kv, outer_q = [outward(a_inner[:, at]) for at in (slice(0, cut), slice(cut, None))]
        inner = a_inner
        finish = lambda at: over(b_three[:, at])
    else:
        across, sibling = to_member(tokens[0], 2), to_member(tokens[0], 1)
        books = [tokens[0], sibling, across, to_member(across, 1)]
        full = gathered(jnp.concatenate(pieces, axis=0))
        deep = MEMBERS * HEAD_SIZE // 2
        upper, lower = [part[:deep] for part in full], [part[deep:] for part in full]
        late = [(n_pieces - 1, 0), (n_pieces - 1, 1)]
        early = [(k, half) for half in range(2) for k in range(n_pieces - 1)]
        late = [(n_pieces - 2, 1)] + late
        early.remove(late[0])
        for segs in ((0, 1), (2, 3)):
            project(segs, early, late, (upper, lower), 0)
        pieces = [lower[-2]]
        outer_kv, outer_q = upper[-1][:, :cut], upper[-1][:, cut:]
        inner = upper[-1]
        finish = lambda at: lower[-1][:, at]

    halves = [slice(k * HEAD_SIZE, (k + 2) * HEAD_SIZE) for k in (0, 2, 4)]
    lower_kv, lower_q = finish(slice(0, cut)), finish(slice(cut, None))
    found = call(
        functools.partial(kv_body, len(late) + 1),
        [shape((length, 2 * HEAD_SIZE), bf16), shape((HEAD_SIZE, 2 * HEAD_SIZE), f32)] * MEMBERS
        + [shape((HEAD_SIZE, 2 * HEAD_SIZE), bf16)],
        [SMEM] + [VMEM] * (len(late) + 1 + 3 * MEMBERS),
        flops=2 * MEMBERS * length * len(late) * MEMBERS * HEAD_SIZE * HEAD_SIZE,
        scratch=[pltpu.VMEM((MEMBERS * HEAD_SIZE // 2, cut), bf16)],
    )(here, *pieces, inner, outer_kv, lower_kv, *sums, *lates, *messages)
    kvs, deltas, total = found[0:-1:2], found[1:-1:2], found[-1]

    base = None
    for a in range(1, n_groups):
        term = permute(total, lambda gg, mm, zz: (gg ^ a, mm, zz))
        if n_groups > 2:
            term = jnp.where((g ^ a) < g, term, 0).astype(f32)
        base = term if base is None else base + term

    half = group // 2

    def local(segs, part, *others):
        found = call(
            functools.partial(local_body, len(segs), len(late) + 1, halves[1 + part].start, half),
            [shape((length, half * HEAD_SIZE), bf16), shape((length, half * HEAD_SIZE), f32)] * len(segs),
            [SMEM] + [VMEM] * (len(late) + 1 + 4 * len(segs)),
            flops=4 * len(segs) * length * length * half * HEAD_SIZE,
            scratch=[pltpu.VMEM((MEMBERS * HEAD_SIZE // 2, half * HEAD_SIZE), bf16)],
        )(here, *pieces, inner, outer_q, after(lower_q, *others), *[one[s] for one in (kvs, messages, sums, lates) for s in segs])
        return {(s, part): (found[2 * at], found[2 * at + 1]) for at, s in enumerate(segs)}

    def mix(segs, parts, base, ready):
        keys = [(s, part) for s in segs for part in parts]
        return call(
            functools.partial(mix_body, segs, parts, group),
            [shape((length, half * HEAD_SIZE), bf16)] * len(keys),
            [SMEM] * 2 + [VMEM] * (1 + MEMBERS + len(segs) + 2 * len(keys)),
            flops=2 * len(keys) * length * half * HEAD_SIZE * HEAD_SIZE * 6,
        )(
            here, gate_bias, base, *deltas, *[messages[s] for s in segs],
            *[ready[key][0] for key in keys], *[ready[key][1] for key in keys],
        )

    ready = local((2, 3), 0)
    base = after(base, *ready[2, 0])
    two0, three0 = mix((2, 3), (0,), base, ready)
    ready |= local((2, 3), 1, two0, three0)
    two1, three1 = mix((2, 3), (1,), base, ready)
    ready |= local((1, 0), 0, two1, three1)
    ready |= local((1, 0), 1, two1, three1)
    one0, one1, mine0, mine1 = mix((1, 0), (0, 1), after(base, two1, three1), ready)
    sent = [mine0, mine1]
    for k, parts in ((1, (one0, one1)), (2, (two0, two1)), (3, (three0, three1))):
        sent += [to_member(part, k) for part in parts]
    far = sent[4:]
    (gate,) = call(gate_body, [shape((8, HEAD_SIZE), f32)], [ANY] * len(far), moved=16 << 20)(*far)
    (output,) = call(
        functools.partial(assemble_body, (2,) * MEMBERS),
        [shape((length, w_query.shape[1]), bf16)],
        [SMEM] + [VMEM] * (1 + len(sent)),
    )(here, gate, *sent)
    return output[None]


def solution(mesh):
    in_specs = (
        P("fsdp", "seg", None),
        P(("seg", "fsdp"), None),
        P(("seg", "fsdp"), None),
        P(("seg", "fsdp"), None),
        P(),
        P("fsdp", "seg", None, None),
        P("fsdp", "seg"),
    )
    out_specs = P("fsdp", "seg", None)
    body = functools.partial(shards, (mesh.shape["seg"], mesh.shape["fsdp"]))
    return jax.shard_map(body, mesh=mesh, in_specs=in_specs, out_specs=out_specs, check_vma=False)
```

```python
import functools

import jax
import jax.numpy as jnp
from jax import lax
from jax.experimental import pallas as pl
from jax.experimental.pallas import tpu as pltpu
from jax.sharding import PartitionSpec as P

HEAD_SIZE = 128
BLK = 128
MEMBERS = 4
META_ROWS = 16
HALF = META_ROWS // 2
AXES = ("seg", "fsdp")

VMEM = pl.BlockSpec(memory_space=pltpu.VMEM)
SMEM = pl.BlockSpec(memory_space=pltpu.SMEM)
ANY = pl.BlockSpec(memory_space=pl.ANY)
HBM = pl.BlockSpec(memory_space=pltpu.HBM)


def call(body, outs, in_specs, flops=0, scratch=(), out_spec=VMEM, limit=16 << 20, moved=4 << 20):
    return pl.pallas_call(
        body,
        out_shape=outs,
        in_specs=in_specs,
        out_specs=[out_spec] * len(outs),
        scratch_shapes=list(scratch),
        compiler_params=pltpu.CompilerParams(vmem_limit_bytes=limit),
        cost_estimate=pl.CostEstimate(flops=flops, bytes_accessed=moved, transcendentals=0),
    )


def aligned(offset):
    return pl.multiple_of(offset, HEAD_SIZE)


def pack_body(group, here_ref, valid_ref, mask_ref, wq_ref, wk_ref, wv_ref, *outs):
    rows, wide = wk_ref.shape[0], group * HEAD_SIZE
    row = lax.broadcasted_iota(jnp.int32, (META_ROWS, outs[0].shape[1]), 0)
    facts = jnp.where(row < HALF, valid_ref[0, 0], mask_ref[0, 0, 1, 0])
    facts = facts.astype(jnp.float32).astype(jnp.bfloat16)
    for k in range(MEMBERS):
        head, out = here_ref[1] ^ k, outs[k]
        at = aligned(head * HEAD_SIZE)
        out[:rows, :HEAD_SIZE] = wk_ref[:, pl.ds(at, HEAD_SIZE)]
        out[:rows, HEAD_SIZE : 2 * HEAD_SIZE] = wv_ref[:, pl.ds(at, HEAD_SIZE)]
        out[:rows, 2 * HEAD_SIZE :] = wq_ref[:, pl.ds(aligned(head * wide), wide)]
        out[rows:, :] = facts


def columns_of(tokens_ref, here_ref, piece, half, line):
    deep = MEMBERS * HEAD_SIZE // 2
    if not line:
        return tokens_ref[:, pl.ds((2 * piece + half) * deep, deep)]
    g, m, z = here_ref[0] ^ (piece // line), here_ref[1], here_ref[2]
    inside = (z == 1) | (z == 2)
    step = piece % line
    if step < 2:
        z = z ^ step
    else:
        z = jnp.where(inside, z ^ (5 - step), z ^ step)
    parts = [
        tokens_ref[:, pl.ds(aligned(((g * MEMBERS + (m ^ k)) * line + z) * HEAD_SIZE), HEAD_SIZE)]
        for k in (2 * half, 2 * half + 1)
    ]
    return jnp.concatenate(parts, axis=1)


def facts_of(message_ref):
    rows = message_ref.shape[0] - META_ROWS
    facts = message_ref[rows:, : 2 * HEAD_SIZE].astype(jnp.float32)
    return facts[0:1, :], facts[HALF : HALF + 1, :]


def iota(shape, dimension):
    return lax.broadcasted_iota(jnp.int32, shape, dimension).astype(jnp.float32)


def project_body(early, late, line, here_ref, *refs):
    tokens, pieces, outs = refs[:2], refs[2 : 2 + len(early)], refs[2 + len(early) :]
    length = tokens[0].shape[0]
    total = None
    for place, piece in zip(early, pieces):
        columns = jnp.concatenate([columns_of(one, here_ref, *place, line) for one in tokens], axis=0)
        term = jnp.dot(columns, piece[...], preferred_element_type=jnp.float32)
        total = term if total is None else total + term
    for n in range(2):
        outs[n][...] = total[n * length : (n + 1) * length]
        for k, place in enumerate(late):
            columns = columns_of(tokens[n], here_ref, *place, line)
            deep = columns.shape[1]
            outs[2 + n][:, k * deep : (k + 1) * deep] = columns


def sigma_plus(v):
    return jnp.where(v > 0, v + 1.0, jnp.exp(jnp.minimum(v, 0.0)))


def split(values):
    high = values.astype(jnp.bfloat16)
    return high, (values - high.astype(jnp.float32)).astype(jnp.bfloat16)


def late_rows(here_ref, chosen_ref, start, width, *pieces):
    *whole, inner, outer, part = pieces
    lost = inner.shape[1] - outer.shape[1] if start else 0
    at = slice(start - lost, start - lost + width)
    inside = (here_ref[2] == 1) | (here_ref[2] == 2)

    @pl.when(inside)
    def _():
        chosen_ref[...] = inner[:, start : start + width]

    @pl.when(jnp.logical_not(inside))
    def _():
        chosen_ref[...] = outer[:, at]

    rows = [piece[:, start : start + width] for piece in whole]
    return jnp.concatenate(rows + [chosen_ref[...], part[:, at]], axis=0)


def kv_body(n_late, here_ref, *refs):
    pieces, refs, chosen_ref = refs[:n_late], refs[n_late:-1], refs[-1]
    sums, lates, messages = refs[:MEMBERS], refs[MEMBERS : 2 * MEMBERS], refs[2 * MEMBERS : 3 * MEMBERS]
    outs = refs[3 * MEMBERS :]
    rows = late_rows(here_ref, chosen_ref, 0, 2 * HEAD_SIZE, *pieces)
    kvs = []
    for seg in range(MEMBERS):
        total = sums[seg][:, : 2 * HEAD_SIZE]
        total += jnp.dot(lates[seg][...], rows, preferred_element_type=jnp.float32)
        kvs.append(total.astype(jnp.bfloat16))
        outs[2 * seg][...] = kvs[seg]
    whole = None
    for seg, kv in enumerate(kvs):
        length = kv.shape[0]
        valid, _ = facts_of(messages[seg])
        keys = kv[:, :HEAD_SIZE].astype(jnp.float32)
        live = iota((length, HEAD_SIZE), 0) < valid[:, :HEAD_SIZE]
        sig = jnp.where(live, sigma_plus(keys), 0.0)
        wide = jnp.concatenate(
            [kv[:, HEAD_SIZE:], jnp.ones((length, HEAD_SIZE), jnp.bfloat16)], axis=1
        )
        high, low = split(sig)
        over = (((0,), (0,)), ((), ()))
        delta = lax.dot_general(high, wide, over, preferred_element_type=jnp.float32)
        delta += lax.dot_general(low, wide, over, preferred_element_type=jnp.float32)
        outs[2 * seg + 1][...] = delta
        whole = delta if whole is None else whole + delta
    outs[-1][...] = whole.astype(jnp.bfloat16)


def local_body(n, n_late, start, heads, here_ref, *refs):
    pieces, refs, chosen_ref = refs[:n_late], refs[n_late:-1], refs[-1]
    kvs, messages, sums, lates, outs = [refs[k * n : (k + 1) * n] for k in range(4)] + [refs[4 * n :]]
    rows = late_rows(here_ref, chosen_ref, start, heads * HEAD_SIZE, *pieces)
    columns = slice(start, start + heads * HEAD_SIZE)
    queries = []
    for at in range(n):
        total = sums[at][:, columns] + jnp.dot(
            lates[at][...], rows, preferred_element_type=jnp.float32
        )
        queries.append(total.astype(jnp.bfloat16))
        outs[2 * at][...] = queries[at]
    work = [(at, block) for at in range(n) for block in range(queries[0].shape[0] // BLK)]
    span = lambda block: slice(block * BLK, (block + 1) * BLK)
    scores = []
    for at, block in work:
        stacked = jnp.concatenate(
            [queries[at][span(block), h * HEAD_SIZE : (h + 1) * HEAD_SIZE] for h in range(heads)], axis=0
        )
        keys = kvs[at][0 : (block + 1) * BLK, :HEAD_SIZE]
        scores.append(
            lax.dot_general(
                stacked, keys, (((1,), (1,)), ((), ())), preferred_element_type=jnp.float32
            )
        )
    weights = []
    for (at, block), score in zip(work, scores):
        width = (block + 1) * BLK
        valid, seen = facts_of(messages[at])
        i, j = iota((BLK, width), 0) + block * BLK, iota((BLK, width), 1)
        limit = valid[:, :width]
        if block:
            limit = jnp.where((j[0:1] >= block * BLK) | (seen[:, :width] > 0), limit, 0.0)
        allowed = (j <= i) & (j < limit)
        masked = jnp.concatenate(
            [jnp.where(allowed, score[span(h)] * HEAD_SIZE ** (-0.5), -1e30) for h in range(heads)],
            axis=0,
        )
        top = jnp.max(masked, axis=-1, keepdims=True)
        expo = jnp.exp(masked - top)
        total = jnp.maximum(jnp.sum(expo, axis=-1, keepdims=True), 1.0)
        weights.append((expo * (1.0 / total)).astype(jnp.bfloat16))
    for (at, block), weight in zip(work, weights):
        values = kvs[at][0 : (block + 1) * BLK, HEAD_SIZE:]
        local = jnp.dot(weight, values, preferred_element_type=jnp.float32)
        for h in range(heads):
            outs[2 * at + 1][span(block), h * HEAD_SIZE : (h + 1) * HEAD_SIZE] = local[span(h)]


def mix_body(segs, parts, group, here_ref, gate_ref, base_ref, *refs):
    deltas, messages, refs = refs[:MEMBERS], refs[MEMBERS : MEMBERS + len(segs)], refs[MEMBERS + len(segs) :]
    n = len(segs) * len(parts)
    queries, locals_, outs = refs[:n], refs[n : 2 * n], refs[2 * n :]
    me = here_ref[1]
    heads = queries[0].shape[1] // HEAD_SIZE
    length = queries[0].shape[0]
    work = [(at, p, h) for at in range(len(segs)) for p in range(len(parts)) for h in range(heads)]
    memories = []
    for seg in segs:
        memory = jnp.where(here_ref[3] > 0, 1.0, 0.0) * base_ref[...].astype(jnp.float32)
        for other in range(MEMBERS):
            if other != seg:
                earlier = jnp.where((me ^ other) < (me ^ seg), 1.0, 0.0)
                memory = memory + earlier * deltas[other][...]
        memories.append(split(memory))
    columns = lambda h: slice(h * HEAD_SIZE, (h + 1) * HEAD_SIZE)
    numers = []
    for at, p, h in work:
        mem_high, mem_low = memories[at]
        high, low = split(sigma_plus(queries[at * len(parts) + p][:, columns(h)].astype(jnp.float32)))
        numer = jnp.dot(high, mem_high, preferred_element_type=jnp.float32)
        numer += jnp.dot(high, mem_low, preferred_element_type=jnp.float32)
        numer += jnp.dot(low, mem_high, preferred_element_type=jnp.float32)
        numers.append(numer)
    for (at, p, h), numer in zip(work, numers):
        valid, _ = facts_of(messages[at])
        live = iota((length, HEAD_SIZE), 0) < valid[:, :HEAD_SIZE]
        retrieved = numer[:, :HEAD_SIZE] / (numer[:, HEAD_SIZE:] + 1.0)
        logit = jnp.full((1, HEAD_SIZE), gate_ref[me * group + parts[p] * heads + h], jnp.float32)
        gate = 1.0 / (1.0 + jnp.exp(-logit))
        mixed = gate * retrieved + (1.0 - gate) * locals_[at * len(parts) + p][:, columns(h)]
        outs[at * len(parts) + p][:, columns(h)] = jnp.where(live, mixed, 0.0).astype(jnp.bfloat16)


def assemble_body(counts, here_ref, *refs):
    parts, out = list(refs[1:-1]), refs[-1]
    width = out.shape[1] // MEMBERS
    for k, count in enumerate(counts):
        for c in range(count):
            at = (here_ref[1] ^ k) * width + c * (width // count)
            out[:, pl.ds(aligned(at), width // count)] = parts.pop(0)[...]


def gate_body(*refs):
    refs[-1][...] = jnp.zeros_like(refs[-1])


def after(array, *others):
    return lax.optimization_barrier((array,) + others)[0]


def shards(sizes, tokens, w_query, w_key, value_weight, gate_bias, block_mask, valid_len):
    n_seg, n_z = sizes
    n_groups = n_seg // MEMBERS
    heads_kv = w_key.shape[1] // HEAD_SIZE
    group = w_query.shape[1] // w_key.shape[1]
    rows = w_query.shape[0]
    length, width = tokens.shape[1], tokens.shape[2]
    assert heads_kv == MEMBERS and group == 4 and length == 2 * BLK
    seg = lax.axis_index("seg")
    z = lax.axis_index("fsdp")
    g, m = seg // MEMBERS, seg % MEMBERS
    here = jnp.stack([g, m, z, g if n_groups == 2 else 1]).astype(jnp.int32)
    bf16, f32 = jnp.bfloat16, jnp.float32
    shape = jax.ShapeDtypeStruct

    def permute(array, to):
        pairs = []
        for gg in range(n_groups):
            for mm in range(MEMBERS):
                for zz in range(n_z):
                    target = to(gg, mm, zz)
                    if target is not None:
                        index = lambda t: (t[0] * MEMBERS + t[1]) * n_z + t[2]
                        pairs.append((index((gg, mm, zz)), index(target)))
        return lax.ppermute(array, AXES, pairs)

    def to_member(array, k):
        return permute(array, lambda gg, mm, zz: (gg, mm ^ k, zz))

    wide = (2 + group) * HEAD_SIZE
    packed = call(
        functools.partial(pack_body, group),
        [shape((rows + META_ROWS, wide), bf16)] * MEMBERS,
        [SMEM] * 3 + [VMEM] * 3,
        limit=56 << 20,
    )(here, valid_len, block_mask, w_query, w_key, value_weight)
    messages = [packed[0], *[to_member(packed[k], k) for k in (1, 2, 3)]]

    def gathered(piece):
        index = lambda gg, mm, zz: (gg * MEMBERS + mm) * n_z + zz
        everything = lax.all_gather(
            piece,
            AXES,
            axis_index_groups=[
                [index(gg, mm, zz) for gg in range(n_groups) for zz in range(n_z)]
                for mm in range(MEMBERS)
            ],
        )
        columns = piece.shape[1]
        natural = everything.reshape(n_groups, n_z, MEMBERS, rows, columns)
        members = jnp.arange(MEMBERS, dtype=jnp.int32) ^ m
        natural = jnp.take(natural, members, axis=2).transpose(0, 2, 1, 3, 4)
        return list(natural.reshape(-1, MEMBERS * HEAD_SIZE, columns))

    pieces = [
        jnp.concatenate([messages[k][:rows] for k in members], axis=0) for members in ((0, 1), (2, 3))
    ]
    n_pieces = width // (MEMBERS * HEAD_SIZE)
    sums, lates = [None] * MEMBERS, [None] * MEMBERS

    def project(segs, early, late, halves, line):
        deep = MEMBERS * HEAD_SIZE // 2
        found = call(
            functools.partial(project_body, early, late, line),
            [shape((length, wide), f32)] * 2 + [shape((length, len(late) * deep), bf16)] * 2,
            [SMEM] + [VMEM] * (2 + len(early)),
            flops=2 * 2 * length * len(early) * deep * wide,
        )(here, *[books[s] for s in segs], *[halves[half][piece] for piece, half in early])
        for at, s in enumerate(segs):
            sums[s], lates[s] = found[at], found[2 + at]

    cut = 2 * HEAD_SIZE
    if n_groups == 2 and n_z == 4:
        assert rows == HEAD_SIZE
        inside = (z == 1) | (z == 2)
        over = lambda part: permute(part, lambda gg, mm, zz: (gg ^ 1, mm, zz))
        pair = lambda part: permute(part, lambda gg, mm, zz: (gg, mm, zz ^ 1))
        outward = lambda part: permute(
            part, lambda gg, mm, zz: (gg, mm, zz ^ 1) if zz in (1, 2) else None
        )
        inward = lambda part: permute(
            part, lambda gg, mm, zz: (gg, mm, zz ^ 3) if zz in (1, 2) else None
        )
        locked = lambda *parts: lax.optimization_barrier(parts)
        stage1 = lambda piece: (pair(piece), inward(piece), over(piece))
        stage2 = lambda one, inner: (inward(one), outward(inner), over(one))
        stage3 = lambda middle, two: (outward(middle), over(two))

        a, b, own, sibling = locked(*pieces, tokens[0], to_member(tokens[0], 1))
        across = to_member(own, 2)
        a_one, a_inner, a_far0 = locked(*stage1(a))
        b_one, b_inner, b_far0 = locked(*stage1(b))
        a_middle, a_outer, a_far1 = locked(*stage2(a_one, a_inner))
        b_middle, b_outer, b_far1 = locked(*stage2(b_one, b_inner))
        a_two = jnp.where(inside, a_inner, a_outer)
        a_inner, (a_last, a_far2) = inward(a_far1), stage3(a_middle, a_two)
        b_two = jnp.where(inside, b_inner, b_outer)
        b_last, b_far2 = stage3(b_middle, b_two)
        a_last, a_far2, a_middle, a_inner = locked(a_last, a_far2, a_middle, a_inner)
        a_three = jnp.where(inside, a_middle, a_last)
        books = [own, sibling]
        upper = [a, a_one, a_two, a_three, a_far0, a_far1, a_far2]
        lower = [b, b_one, b_two, None, b_far0, b_far1]
        late = [(3, 1), (6, 1), (7, 0), (7, 1)]
        early = [(k, half) for half in range(2) for k in range(8) if (k, half) not in late]
        project((0, 1), early, late, (upper, lower), n_z)
        b_last, b_far2, b_middle, sums[0], sums[1], across = locked(
            b_last, b_far2, b_middle, sums[0], sums[1], after(across, a_last, a_far2)
        )
        books += [across, to_member(across, 1)]
        project((2, 3), early, late, (upper, lower), n_z)
        b_three = jnp.where(inside, b_middle, b_last)
        pieces = [b_three, b_far2]
        outer_kv, outer_q = [outward(a_inner[:, at]) for at in (slice(0, cut), slice(cut, None))]
        inner = a_inner
        finish = lambda at: over(b_three[:, at])
    else:
        across, sibling = to_member(tokens[0], 2), to_member(tokens[0], 1)
        books = [tokens[0], sibling, across, to_member(across, 1)]
        full = gathered(jnp.concatenate(pieces, axis=0))
        deep = MEMBERS * HEAD_SIZE // 2
        upper, lower = [part[:deep] for part in full], [part[deep:] for part in full]
        late = [(n_pieces - 1, 0), (n_pieces - 1, 1)]
        early = [(k, half) for half in range(2) for k in range(n_pieces - 1)]
        late = [(n_pieces - 2, 1)] + late
        early.remove(late[0])
        for segs in ((0, 1), (2, 3)):
            project(segs, early, late, (upper, lower), 0)
        pieces = [lower[-2]]
        outer_kv, outer_q = upper[-1][:, :cut], upper[-1][:, cut:]
        inner = upper[-1]
        finish = lambda at: lower[-1][:, at]

    halves = [slice(k * HEAD_SIZE, (k + 2) * HEAD_SIZE) for k in (0, 2, 4)]
    lower_kv, lower_q = finish(slice(0, cut)), finish(slice(cut, None))
    found = call(
        functools.partial(kv_body, len(late) + 1),
        [shape((length, 2 * HEAD_SIZE), bf16), shape((HEAD_SIZE, 2 * HEAD_SIZE), f32)] * MEMBERS
        + [shape((HEAD_SIZE, 2 * HEAD_SIZE), bf16)],
        [SMEM] + [VMEM] * (len(late) + 1 + 3 * MEMBERS),
        flops=2 * MEMBERS * length * len(late) * MEMBERS * HEAD_SIZE * HEAD_SIZE,
        scratch=[pltpu.VMEM((MEMBERS * HEAD_SIZE // 2, cut), bf16)],
    )(here, *pieces, inner, outer_kv, lower_kv, *sums, *lates, *messages)
    kvs, deltas, total = found[0:-1:2], found[1:-1:2], found[-1]

    base = None
    for a in range(1, n_groups):
        term = permute(total, lambda gg, mm, zz: (gg ^ a, mm, zz))
        if n_groups > 2:
            term = jnp.where((g ^ a) < g, term, 0).astype(f32)
        base = term if base is None else base + term

    half = group // 2

    def local(segs, part, *others):
        found = call(
            functools.partial(local_body, len(segs), len(late) + 1, halves[1 + part].start, half),
            [shape((length, half * HEAD_SIZE), bf16), shape((length, half * HEAD_SIZE), f32)] * len(segs),
            [SMEM] + [VMEM] * (len(late) + 1 + 4 * len(segs)),
            flops=4 * len(segs) * length * length * half * HEAD_SIZE,
            scratch=[pltpu.VMEM((MEMBERS * HEAD_SIZE // 2, half * HEAD_SIZE), bf16)],
        )(here, *pieces, inner, outer_q, after(lower_q, *others), *[one[s] for one in (kvs, messages, sums, lates) for s in segs])
        return {(s, part): (found[2 * at], found[2 * at + 1]) for at, s in enumerate(segs)}

    def mix(segs, parts, base, ready):
        keys = [(s, part) for s in segs for part in parts]
        return call(
            functools.partial(mix_body, segs, parts, group),
            [shape((length, half * HEAD_SIZE), bf16)] * len(keys),
            [SMEM] * 2 + [VMEM] * (1 + MEMBERS + len(segs) + 2 * len(keys)),
            flops=2 * len(keys) * length * half * HEAD_SIZE * HEAD_SIZE * 6,
        )(
            here, gate_bias, base, *deltas, *[messages[s] for s in segs],
            *[ready[key][0] for key in keys], *[ready[key][1] for key in keys],
        )

    ready = local((2, 3), 0)
    base = after(base, *ready[2, 0])
    (two0,) = mix((2,), (0,), base, ready)
    (three0,) = mix((3,), (0,), after(base, two0), ready)
    ready |= local((2, 3), 1, two0, three0)
    two1, three1 = mix((2, 3), (1,), base, ready)
    ready |= local((1, 0), 0, two1, three1)
    ready |= local((1, 0), 1, two1, three1)
    one0, one1, mine0, mine1 = mix((1, 0), (0, 1), after(base, two1, three1), ready)
    sent = [mine0, mine1]
    for k, parts in ((1, (one0, one1)), (2, (two0, two1)), (3, (three0, three1))):
        sent += [to_member(part, k) for part in parts]
    far = sent[4:]
    (gate,) = call(gate_body, [shape((8, HEAD_SIZE), f32)], [ANY] * len(far), moved=16 << 20)(*far)
    (output,) = call(
        functools.partial(assemble_body, (2,) * MEMBERS),
        [shape((length, w_query.shape[1]), bf16)],
        [SMEM] + [VMEM] * (1 + len(sent)),
    )(here, gate, *sent)
    return output[None]


def solution(mesh):
    in_specs = (
        P("fsdp", "seg", None),
        P(("seg", "fsdp"), None),
        P(("seg", "fsdp"), None),
        P(("seg", "fsdp"), None),
        P(),
        P("fsdp", "seg", None, None),
        P("fsdp", "seg"),
    )
    out_specs = P("fsdp", "seg", None)
    body = functools.partial(shards, (mesh.shape["seg"], mesh.shape["fsdp"]))
    return jax.shard_map(body, mesh=mesh, in_specs=in_specs, out_specs=out_specs, check_vma=False)
```

```python
import functools

import jax
import jax.numpy as jnp
from jax import lax
from jax.experimental import pallas as pl
from jax.experimental.pallas import tpu as pltpu
from jax.sharding import PartitionSpec as P

HEAD_SIZE = 128
BLK = 128
MEMBERS = 4
META_ROWS = 16
HALF = META_ROWS // 2
AXES = ("seg", "fsdp")

VMEM = pl.BlockSpec(memory_space=pltpu.VMEM)
SMEM = pl.BlockSpec(memory_space=pltpu.SMEM)
ANY = pl.BlockSpec(memory_space=pl.ANY)
HBM = pl.BlockSpec(memory_space=pltpu.HBM)


def call(body, outs, in_specs, flops=0, scratch=(), out_spec=VMEM, limit=12 << 20, moved=4 << 20):
    return pl.pallas_call(
        body,
        out_shape=outs,
        in_specs=in_specs,
        out_specs=[out_spec] * len(outs),
        scratch_shapes=list(scratch),
        compiler_params=pltpu.CompilerParams(vmem_limit_bytes=limit),
        cost_estimate=pl.CostEstimate(flops=flops, bytes_accessed=moved, transcendentals=0),
    )


def aligned(offset):
    return pl.multiple_of(offset, HEAD_SIZE)


def pack_body(group, here_ref, valid_ref, mask_ref, wq_ref, wk_ref, wv_ref, *outs):
    rows, wide = wk_ref.shape[0], group * HEAD_SIZE
    row = lax.broadcasted_iota(jnp.int32, (META_ROWS, outs[0].shape[1]), 0)
    facts = jnp.where(row < HALF, valid_ref[0, 0], mask_ref[0, 0, 1, 0])
    facts = facts.astype(jnp.float32).astype(jnp.bfloat16)
    for k in range(MEMBERS):
        head, out = here_ref[1] ^ k, outs[k]
        at = aligned(head * HEAD_SIZE)
        out[:rows, :HEAD_SIZE] = wk_ref[:, pl.ds(at, HEAD_SIZE)]
        out[:rows, HEAD_SIZE : 2 * HEAD_SIZE] = wv_ref[:, pl.ds(at, HEAD_SIZE)]
        out[:rows, 2 * HEAD_SIZE :] = wq_ref[:, pl.ds(aligned(head * wide), wide)]
        out[rows:, :] = facts


def columns_of(tokens_ref, here_ref, piece, half, line):
    deep = MEMBERS * HEAD_SIZE // 2
    if not line:
        return tokens_ref[:, pl.ds((2 * piece + half) * deep, deep)]
    g, m, z = here_ref[0] ^ (piece // line), here_ref[1], here_ref[2]
    inside = (z == 1) | (z == 2)
    step = piece % line
    if step < 2:
        z = z ^ step
    else:
        z = jnp.where(inside, z ^ (5 - step), z ^ step)
    parts = [
        tokens_ref[:, pl.ds(aligned(((g * MEMBERS + (m ^ k)) * line + z) * HEAD_SIZE), HEAD_SIZE)]
        for k in (2 * half, 2 * half + 1)
    ]
    return jnp.concatenate(parts, axis=1)


def facts_of(message_ref):
    rows = message_ref.shape[0] - META_ROWS
    facts = message_ref[rows:, : 2 * HEAD_SIZE].astype(jnp.float32)
    return facts[0:1, :], facts[HALF : HALF + 1, :]


def iota(shape, dimension):
    return lax.broadcasted_iota(jnp.int32, shape, dimension).astype(jnp.float32)


def project_body(early, late, line, here_ref, *refs):
    tokens, pieces, outs = refs[:2], refs[2 : 2 + len(early)], refs[2 + len(early) :]
    length = tokens[0].shape[0]
    total = None
    for place, piece in zip(early, pieces):
        columns = jnp.concatenate([columns_of(one, here_ref, *place, line) for one in tokens], axis=0)
        term = jnp.dot(columns, piece[...], preferred_element_type=jnp.float32)
        total = term if total is None else total + term
    for n in range(2):
        outs[n][...] = total[n * length : (n + 1) * length]
        for k, place in enumerate(late):
            columns = columns_of(tokens[n], here_ref, *place, line)
            deep = columns.shape[1]
            outs[2 + n][:, k * deep : (k + 1) * deep] = columns


def sigma_plus(v):
    return jnp.where(v > 0, v + 1.0, jnp.exp(jnp.minimum(v, 0.0)))


def split(values):
    high = values.astype(jnp.bfloat16)
    return high, (values - high.astype(jnp.float32)).astype(jnp.bfloat16)


def late_rows(here_ref, chosen_ref, start, width, *pieces):
    *whole, inner, outer, part = pieces
    lost = inner.shape[1] - outer.shape[1] if start else 0
    at = slice(start - lost, start - lost + width)
    inside = (here_ref[2] == 1) | (here_ref[2] == 2)

    @pl.when(inside)
    def _():
        chosen_ref[...] = inner[:, start : start + width]

    @pl.when(jnp.logical_not(inside))
    def _():
        chosen_ref[...] = outer[:, at]

    rows = [piece[:, start : start + width] for piece in whole]
    return jnp.concatenate(rows + [chosen_ref[...], part[:, at]], axis=0)


def kv_body(n_late, here_ref, *refs):
    pieces, refs, chosen_ref = refs[:n_late], refs[n_late:-1], refs[-1]
    sums, lates, messages = refs[:MEMBERS], refs[MEMBERS : 2 * MEMBERS], refs[2 * MEMBERS : 3 * MEMBERS]
    outs = refs[3 * MEMBERS :]
    rows = late_rows(here_ref, chosen_ref, 0, 2 * HEAD_SIZE, *pieces)
    kvs = []
    for seg in range(MEMBERS):
        total = sums[seg][:, : 2 * HEAD_SIZE]
        total += jnp.dot(lates[seg][...], rows, preferred_element_type=jnp.float32)
        kvs.append(total.astype(jnp.bfloat16))
        outs[2 * seg][...] = kvs[seg]
    whole = None
    for seg, kv in enumerate(kvs):
        length = kv.shape[0]
        valid, _ = facts_of(messages[seg])
        keys = kv[:, :HEAD_SIZE].astype(jnp.float32)
        live = iota((length, HEAD_SIZE), 0) < valid[:, :HEAD_SIZE]
        sig = jnp.where(live, sigma_plus(keys), 0.0)
        wide = jnp.concatenate(
            [kv[:, HEAD_SIZE:], jnp.ones((length, HEAD_SIZE), jnp.bfloat16)], axis=1
        )
        high, low = split(sig)
        over = (((0,), (0,)), ((), ()))
        delta = lax.dot_general(high, wide, over, preferred_element_type=jnp.float32)
        delta += lax.dot_general(low, wide, over, preferred_element_type=jnp.float32)
        outs[2 * seg + 1][...] = delta
        whole = delta if whole is None else whole + delta
    outs[-1][...] = whole.astype(jnp.bfloat16)


def local_body(n, n_late, start, heads, here_ref, *refs):
    pieces, refs, chosen_ref = refs[:n_late], refs[n_late:-1], refs[-1]
    kvs, messages, sums, lates, outs = [refs[k * n : (k + 1) * n] for k in range(4)] + [refs[4 * n :]]
    rows = late_rows(here_ref, chosen_ref, start, heads * HEAD_SIZE, *pieces)
    columns = slice(start, start + heads * HEAD_SIZE)
    queries = []
    for at in range(n):
        total = sums[at][:, columns] + jnp.dot(
            lates[at][...], rows, preferred_element_type=jnp.float32
        )
        queries.append(total.astype(jnp.bfloat16))
        outs[2 * at][...] = queries[at]
    work = [(at, block) for at in range(n) for block in range(queries[0].shape[0] // BLK)]
    span = lambda block: slice(block * BLK, (block + 1) * BLK)
    scores = []
    for at, block in work:
        stacked = jnp.concatenate(
            [queries[at][span(block), h * HEAD_SIZE : (h + 1) * HEAD_SIZE] for h in range(heads)], axis=0
        )
        keys = kvs[at][0 : (block + 1) * BLK, :HEAD_SIZE]
        scores.append(
            lax.dot_general(
                stacked, keys, (((1,), (1,)), ((), ())), preferred_element_type=jnp.float32
            )
        )
    weights = []
    for (at, block), score in zip(work, scores):
        width = (block + 1) * BLK
        valid, seen = facts_of(messages[at])
        i, j = iota((BLK, width), 0) + block * BLK, iota((BLK, width), 1)
        limit = valid[:, :width]
        if block:
            limit = jnp.where((j[0:1] >= block * BLK) | (seen[:, :width] > 0), limit, 0.0)
        allowed = (j <= i) & (j < limit)
        masked = jnp.concatenate(
            [jnp.where(allowed, score[span(h)] * HEAD_SIZE ** (-0.5), -1e30) for h in range(heads)],
            axis=0,
        )
        top = jnp.max(masked, axis=-1, keepdims=True)
        expo = jnp.exp(masked - top)
        total = jnp.maximum(jnp.sum(expo, axis=-1, keepdims=True), 1.0)
        weights.append((expo * (1.0 / total)).astype(jnp.bfloat16))
    for (at, block), weight in zip(work, weights):
        values = kvs[at][0 : (block + 1) * BLK, HEAD_SIZE:]
        local = jnp.dot(weight, values, preferred_element_type=jnp.float32)
        for h in range(heads):
            outs[2 * at + 1][span(block), h * HEAD_SIZE : (h + 1) * HEAD_SIZE] = local[span(h)]


def mix_body(segs, parts, group, here_ref, gate_ref, base_ref, *refs):
    deltas, messages, refs = refs[:MEMBERS], refs[MEMBERS : MEMBERS + len(segs)], refs[MEMBERS + len(segs) :]
    n = len(segs) * len(parts)
    queries, locals_, outs = refs[:n], refs[n : 2 * n], refs[2 * n :]
    me = here_ref[1]
    heads = queries[0].shape[1] // HEAD_SIZE
    length = queries[0].shape[0]
    work = [(at, p, h) for at in range(len(segs)) for p in range(len(parts)) for h in range(heads)]
    memories = []
    for seg in segs:
        memory = jnp.where(here_ref[3] > 0, 1.0, 0.0) * base_ref[...].astype(jnp.float32)
        for other in range(MEMBERS):
            if other != seg:
                earlier = jnp.where((me ^ other) < (me ^ seg), 1.0, 0.0)
                memory = memory + earlier * deltas[other][...]
        memories.append(split(memory))
    columns = lambda h: slice(h * HEAD_SIZE, (h + 1) * HEAD_SIZE)
    numers = []
    for at, p, h in work:
        mem_high, mem_low = memories[at]
        high, low = split(sigma_plus(queries[at * len(parts) + p][:, columns(h)].astype(jnp.float32)))
        numer = jnp.dot(high, mem_high, preferred_element_type=jnp.float32)
        numer += jnp.dot(high, mem_low, preferred_element_type=jnp.float32)
        numer += jnp.dot(low, mem_high, preferred_element_type=jnp.float32)
        numers.append(numer)
    for (at, p, h), numer in zip(work, numers):
        valid, _ = facts_of(messages[at])
        live = iota((length, HEAD_SIZE), 0) < valid[:, :HEAD_SIZE]
        retrieved = numer[:, :HEAD_SIZE] / (numer[:, HEAD_SIZE:] + 1.0)
        logit = jnp.full((1, HEAD_SIZE), gate_ref[me * group + parts[p] * heads + h], jnp.float32)
        gate = 1.0 / (1.0 + jnp.exp(-logit))
        mixed = gate * retrieved + (1.0 - gate) * locals_[at * len(parts) + p][:, columns(h)]
        outs[at * len(parts) + p][:, columns(h)] = jnp.where(live, mixed, 0.0).astype(jnp.bfloat16)


def assemble_body(counts, here_ref, *refs):
    parts, out = list(refs[1:-1]), refs[-1]
    width = out.shape[1] // MEMBERS
    for k, count in enumerate(counts):
        for c in range(count):
            at = (here_ref[1] ^ k) * width + c * (width // count)
            out[:, pl.ds(aligned(at), width // count)] = parts.pop(0)[...]


def gate_body(*refs):
    refs[-1][...] = jnp.zeros_like(refs[-1])


def after(array, *others):
    return lax.optimization_barrier((array,) + others)[0]


def shards(sizes, tokens, w_query, w_key, value_weight, gate_bias, block_mask, valid_len):
    n_seg, n_z = sizes
    n_groups = n_seg // MEMBERS
    heads_kv = w_key.shape[1] // HEAD_SIZE
    group = w_query.shape[1] // w_key.shape[1]
    rows = w_query.shape[0]
    length, width = tokens.shape[1], tokens.shape[2]
    assert heads_kv == MEMBERS and group == 4 and length == 2 * BLK
    seg = lax.axis_index("seg")
    z = lax.axis_index("fsdp")
    g, m = seg // MEMBERS, seg % MEMBERS
    here = jnp.stack([g, m, z, g if n_groups == 2 else 1]).astype(jnp.int32)
    bf16, f32 = jnp.bfloat16, jnp.float32
    shape = jax.ShapeDtypeStruct

    def permute(array, to):
        pairs = []
        for gg in range(n_groups):
            for mm in range(MEMBERS):
                for zz in range(n_z):
                    target = to(gg, mm, zz)
                    if target is not None:
                        index = lambda t: (t[0] * MEMBERS + t[1]) * n_z + t[2]
                        pairs.append((index((gg, mm, zz)), index(target)))
        return lax.ppermute(array, AXES, pairs)

    def to_member(array, k):
        return permute(array, lambda gg, mm, zz: (gg, mm ^ k, zz))

    wide = (2 + group) * HEAD_SIZE
    packed = call(
        functools.partial(pack_body, group),
        [shape((rows + META_ROWS, wide), bf16)] * MEMBERS,
        [SMEM] * 3 + [VMEM] * 3,
        limit=56 << 20,
    )(here, valid_len, block_mask, w_query, w_key, value_weight)
    messages = [packed[0], *[to_member(packed[k], k) for k in (1, 2, 3)]]

    def gathered(piece):
        index = lambda gg, mm, zz: (gg * MEMBERS + mm) * n_z + zz
        everything = lax.all_gather(
            piece,
            AXES,
            axis_index_groups=[
                [index(gg, mm, zz) for gg in range(n_groups) for zz in range(n_z)]
                for mm in range(MEMBERS)
            ],
        )
        columns = piece.shape[1]
        natural = everything.reshape(n_groups, n_z, MEMBERS, rows, columns)
        members = jnp.arange(MEMBERS, dtype=jnp.int32) ^ m
        natural = jnp.take(natural, members, axis=2).transpose(0, 2, 1, 3, 4)
        return list(natural.reshape(-1, MEMBERS * HEAD_SIZE, columns))

    pieces = [
        jnp.concatenate([messages[k][:rows] for k in members], axis=0) for members in ((0, 1), (2, 3))
    ]
    n_pieces = width // (MEMBERS * HEAD_SIZE)
    sums, lates = [None] * MEMBERS, [None] * MEMBERS

    def project(segs, early, late, halves, line):
        deep = MEMBERS * HEAD_SIZE // 2
        found = call(
            functools.partial(project_body, early, late, line),
            [shape((length, wide), f32)] * 2 + [shape((length, len(late) * deep), bf16)] * 2,
            [SMEM] + [VMEM] * (2 + len(early)),
            flops=2 * 2 * length * len(early) * deep * wide,
        )(here, *[books[s] for s in segs], *[halves[half][piece] for piece, half in early])
        for at, s in enumerate(segs):
            sums[s], lates[s] = found[at], found[2 + at]

    cut = 2 * HEAD_SIZE
    if n_groups == 2 and n_z == 4:
        assert rows == HEAD_SIZE
        inside = (z == 1) | (z == 2)
        over = lambda part: permute(part, lambda gg, mm, zz: (gg ^ 1, mm, zz))
        pair = lambda part: permute(part, lambda gg, mm, zz: (gg, mm, zz ^ 1))
        outward = lambda part: permute(
            part, lambda gg, mm, zz: (gg, mm, zz ^ 1) if zz in (1, 2) else None
        )
        inward = lambda part: permute(
            part, lambda gg, mm, zz: (gg, mm, zz ^ 3) if zz in (1, 2) else None
        )
        locked = lambda *parts: lax.optimization_barrier(parts)
        stage1 = lambda piece: (pair(piece), inward(piece), over(piece))
        stage2 = lambda one, inner: (inward(one), outward(inner), over(one))
        stage3 = lambda middle, two: (outward(middle), over(two))

        a, b, own, sibling = locked(*pieces, tokens[0], to_member(tokens[0], 1))
        across = to_member(own, 2)
        a_one, a_inner, a_far0 = locked(*stage1(a))
        b_one, b_inner, b_far0 = locked(*stage1(b))
        a_middle, a_outer, a_far1 = locked(*stage2(a_one, a_inner))
        b_middle, b_outer, b_far1 = locked(*stage2(b_one, b_inner))
        a_two = jnp.where(inside, a_inner, a_outer)
        a_inner, (a_last, a_far2) = inward(a_far1), stage3(a_middle, a_two)
        b_two = jnp.where(inside, b_inner, b_outer)
        b_last, b_far2 = stage3(b_middle, b_two)
        a_last, a_far2, a_middle, a_inner = locked(a_last, a_far2, a_middle, a_inner)
        a_three = jnp.where(inside, a_middle, a_last)
        books = [own, sibling]
        upper = [a, a_one, a_two, a_three, a_far0, a_far1, a_far2]
        lower = [b, b_one, b_two, None, b_far0, b_far1]
        late = [(3, 1), (6, 1), (7, 0), (7, 1)]
        early = [(k, half) for half in range(2) for k in range(8) if (k, half) not in late]
        project((0, 1), early, late, (upper, lower), n_z)
        b_last, b_far2, b_middle, sums[0], sums[1], across = locked(
            b_last, b_far2, b_middle, sums[0], sums[1], after(across, a_last, a_far2)
        )
        books += [across, to_member(across, 1)]
        project((2, 3), early, late, (upper, lower), n_z)
        b_three = jnp.where(inside, b_middle, b_last)
        pieces = [b_three, b_far2]
        outer_kv, outer_q = [outward(a_inner[:, at]) for at in (slice(0, cut), slice(cut, None))]
        inner = a_inner
        finish = lambda at: over(b_three[:, at])
    else:
        across, sibling = to_member(tokens[0], 2), to_member(tokens[0], 1)
        books = [tokens[0], sibling, across, to_member(across, 1)]
        full = gathered(jnp.concatenate(pieces, axis=0))
        deep = MEMBERS * HEAD_SIZE // 2
        upper, lower = [part[:deep] for part in full], [part[deep:] for part in full]
        late = [(n_pieces - 1, 0), (n_pieces - 1, 1)]
        early = [(k, half) for half in range(2) for k in range(n_pieces - 1)]
        late = [(n_pieces - 2, 1)] + late
        early.remove(late[0])
        for segs in ((0, 1), (2, 3)):
            project(segs, early, late, (upper, lower), 0)
        pieces = [lower[-2]]
        outer_kv, outer_q = upper[-1][:, :cut], upper[-1][:, cut:]
        inner = upper[-1]
        finish = lambda at: lower[-1][:, at]

    halves = [slice(k * HEAD_SIZE, (k + 2) * HEAD_SIZE) for k in (0, 2, 4)]
    lower_kv, lower_q = finish(slice(0, cut)), finish(slice(cut, None))
    found = call(
        functools.partial(kv_body, len(late) + 1),
        [shape((length, 2 * HEAD_SIZE), bf16), shape((HEAD_SIZE, 2 * HEAD_SIZE), f32)] * MEMBERS
        + [shape((HEAD_SIZE, 2 * HEAD_SIZE), bf16)],
        [SMEM] + [VMEM] * (len(late) + 1 + 3 * MEMBERS),
        flops=2 * MEMBERS * length * len(late) * MEMBERS * HEAD_SIZE * HEAD_SIZE,
        scratch=[pltpu.VMEM((MEMBERS * HEAD_SIZE // 2, cut), bf16)],
    )(here, *pieces, inner, outer_kv, lower_kv, *sums, *lates, *messages)
    kvs, deltas, total = found[0:-1:2], found[1:-1:2], found[-1]

    base = None
    for a in range(1, n_groups):
        term = permute(total, lambda gg, mm, zz: (gg ^ a, mm, zz))
        if n_groups > 2:
            term = jnp.where((g ^ a) < g, term, 0).astype(f32)
        base = term if base is None else base + term

    half = group // 2

    def local(segs, part, *others):
        found = call(
            functools.partial(local_body, len(segs), len(late) + 1, halves[1 + part].start, half),
            [shape((length, half * HEAD_SIZE), bf16), shape((length, half * HEAD_SIZE), f32)] * len(segs),
            [SMEM] + [VMEM] * (len(late) + 1 + 4 * len(segs)),
            flops=4 * len(segs) * length * length * half * HEAD_SIZE,
            scratch=[pltpu.VMEM((MEMBERS * HEAD_SIZE // 2, half * HEAD_SIZE), bf16)],
        )(here, *pieces, inner, outer_q, after(lower_q, *others), *[one[s] for one in (kvs, messages, sums, lates) for s in segs])
        return {(s, part): (found[2 * at], found[2 * at + 1]) for at, s in enumerate(segs)}

    def mix(segs, parts, base, ready):
        keys = [(s, part) for s in segs for part in parts]
        return call(
            functools.partial(mix_body, segs, parts, group),
            [shape((length, half * HEAD_SIZE), bf16)] * len(keys),
            [SMEM] * 2 + [VMEM] * (1 + MEMBERS + len(segs) + 2 * len(keys)),
            flops=2 * len(keys) * length * half * HEAD_SIZE * HEAD_SIZE * 6,
        )(
            here, gate_bias, base, *deltas, *[messages[s] for s in segs],
            *[ready[key][0] for key in keys], *[ready[key][1] for key in keys],
        )

    ready = local((2, 3), 0)
    base = after(base, *ready[2, 0])
    two0, three0 = mix((2, 3), (0,), base, ready)
    ready |= local((2, 3), 1, two0, three0)
    two1, three1 = mix((2, 3), (1,), base, ready)
    ready |= local((1, 0), 0, two1, three1)
    ready |= local((1, 0), 1, two1, three1)
    one0, one1, mine0, mine1 = mix((1, 0), (0, 1), after(base, two1, three1), ready)
    sent = [mine0, mine1]
    for k, parts in ((1, (one0, one1)), (2, (two0, two1)), (3, (three0, three1))):
        sent += [to_member(part, k) for part in parts]
    far = sent[4:]
    (gate,) = call(gate_body, [shape((8, HEAD_SIZE), f32)], [ANY] * len(far), moved=16 << 20)(*far)
    (output,) = call(
        functools.partial(assemble_body, (2,) * MEMBERS),
        [shape((length, w_query.shape[1]), bf16)],
        [SMEM] + [VMEM] * (1 + len(sent)),
    )(here, gate, *sent)
    return output[None]


def solution(mesh):
    in_specs = (
        P("fsdp", "seg", None),
        P(("seg", "fsdp"), None),
        P(("seg", "fsdp"), None),
        P(("seg", "fsdp"), None),
        P(),
        P("fsdp", "seg", None, None),
        P("fsdp", "seg"),
    )
    out_specs = P("fsdp", "seg", None)
    body = functools.partial(shards, (mesh.shape["seg"], mesh.shape["fsdp"]))
    return jax.shard_map(body, mesh=mesh, in_specs=in_specs, out_specs=out_specs, check_vma=False)
```
